32 devices in a mesh: items: 4 (over y, x), seq: 8 (over z, core).
Axes of the slice: x: 2, y: 2, z: 4, core: 2. Of those that a mesh axis runs over, the one named last changes fastest.
Arguments:
- token_ids: int32 [16, 1024], P('items', 'seq'), may hold values from 0 to 127
- masked: int32 [16, 1024], P('items', 'seq'), may hold values 0 or 1
- item_flag: int32 [16], P('items'), may hold values 0 or 1
- prefix: int32 [16], P('items'), may hold values from 1 to 1024
- cotangent: bfloat16 [16, 1024, 2048], P('items', 'seq'), may hold values from -6 to 6
- embedding: bfloat16 [2048, 128], P(('items', 'seq')), may hold values from -6 to 6
- heads_weight: bfloat16 [2048, 6144], P(('items', 'seq')), may hold values from -0.21875 to 0.21875
- heads_bias: bfloat16 [6144], P(('items', 'seq')), may hold values from -4 to 4
- dense_weight: bfloat16 [2048, 2048], P(('items', 'seq')), may hold values from -0.75 to 0.75
- dense_bias: bfloat16 [2048], P(('items', 'seq')), may hold values from -6 to 6
- first_gain: bfloat16 [2048], P(('items', 'seq')), may hold values from 0.5 to 1.5
- first_bias: bfloat16 [2048], P(('items', 'seq')), may hold values from -4 to 4
- up_weight: bfloat16 [2048, 10922], P(('items', 'seq')), may hold values from -0.125 to 0.125
- up_bias: bfloat16 [10922], replicated, may hold values from -4 to 4
- down_weight: bfloat16 [5461, 2048], P(None, ('items', 'seq')), may hold values from -0.625 to 0.625
- down_bias: bfloat16 [2048], P(('items', 'seq')), may hold values from -6 to 6
- second_gain: bfloat16 [2048], P(('items', 'seq')), may hold values from 0.5 to 1.5
- second_bias: bfloat16 [2048], P(('items', 'seq')), may hold values from -4 to 4
Outputs:
- layer_out: bfloat16 [16, 1024, 2048], P('items', 'seq')
- input_grad: float32 [16, 1024, 2048], P('items', 'seq')
- embed_grad: float32 [2048, 128], P(('items', 'seq'))
- grad_heads_weight: float32 [2048, 6144], P(('items', 'seq'))
- grad_heads_bias: float32 [6144], P(('items', 'seq'))
- grad_dense_weight: float32 [2048, 2048], P(('items', 'seq'))
- grad_dense_bias: float32 [2048], P(('items', 'seq'))
- grad_first_gain: float32 [2048], P(('items', 'seq'))
- grad_first_bias: float32 [2048], P(('items', 'seq'))
- grad_up_weight: float32 [2048, 10922], P(('items', 'seq'))
- grad_up_bias: float32 [10922], replicated
- grad_down_weight: float32 [5461, 2048], P(None, ('items', 'seq'))
- grad_down_bias: float32 [2048], P(('items', 'seq'))
- grad_second_gain: float32 [2048], P(('items', 'seq'))
- grad_second_bias: float32 [2048], P(('items', 'seq'))
The draws below stay inside these ranges and needn't reach their ends.
All inputs are finite; a program needn't handle non-finite values. No bound on the sum of `masked` or of `item_flag` on one device may be relied on, other than what follows from the above.
Results may differ from the reference program's by a relative error of at most 0.015.
Values may be sent and summed in bfloat16 or wider, within the bound.
A program may use at most 384 MiB of HBM per device.

```python
import math
import jax
import jax.numpy as jnp
from jax import lax

HEADS = 16
HEAD = 128
D = 2048
FF = 5461
VOCAB = 128
LEN = 1024
ITEMS = 16


def with_ends(values, rng, smallest, high):
    spot = [jax.random.randint(jax.random.fold_in(rng, axis), (), 0, length) for axis, length in enumerate(values.shape)]
    main_axis = values.shape.index(max(values.shape))
    next_to = spot[:main_axis] + [(spot[main_axis] + 1) % values.shape[main_axis]] + spot[main_axis + 1:]
    return values.at[tuple(spot)].set(smallest).at[tuple(next_to)].set(high)


def block_scale(key, dims, cuts, least, high):
    level, own = 1.0, jax.random.fold_in(key, 6)
    for dim, parts in cuts:
        heights = jnp.exp(jax.random.uniform(jax.random.fold_in(own, dim), (parts,), jnp.float32, least / len(cuts), high / len(cuts)))
        level = level * jnp.repeat(heights, dims[dim] // parts).reshape([-1 if axis == dim else 1 for axis in range(len(dims))])
    return level


def centred(own_key, extent, scale, most, shards=(), kind=jnp.bfloat16):
    factor_of = block_scale(own_key, extent, shards, -0.22, 0.18) if shards else 1.0
    entries = jax.random.normal(own_key, extent, jnp.float32) * scale * factor_of
    return jnp.minimum(jnp.maximum(entries, -most), most).astype(kind)


def setup_inputs(seed: int = 0) -> dict:
    key_of = jax.random.split(jax.random.key(seed), 19)
    return {
        "token_ids": with_ends(jax.random.randint(key_of[0], (ITEMS, LEN), 0, VOCAB), jax.random.fold_in(key_of[0], 1), 0, VOCAB - 1).astype(jnp.int32),
        "masked": with_ends((jax.random.randint(key_of[1], (ITEMS, LEN), 0, 20) < 3).astype(jnp.int32), jax.random.fold_in(key_of[1], 1), 0, 1),
        "item_flag": with_ends((jax.random.randint(key_of[2], (ITEMS,), 0, 5) < 1).astype(jnp.int32), jax.random.fold_in(key_of[2], 1), 0, 1),
        "prefix": with_ends(jax.random.randint(key_of[3], (ITEMS,), 1, LEN + 1), jax.random.fold_in(key_of[3], 1), 1, LEN).astype(jnp.int32),
        "cotangent": centred(key_of[4], (ITEMS, LEN, D), 1.0, 6.0, ((0, 4), (1, 8))),
        "embedding": centred(key_of[5], (D, VOCAB), 1.0, 6.0, ((0, 32),)),
        "heads_weight": centred(key_of[6], (D, 3 * D), (D // 3) ** -0.5, 0.21875, ((0, 32),)),
        "heads_bias": centred(key_of[7], (3 * D,), 0.3, 4.0, ((0, 32),)),
        "dense_weight": centred(key_of[8], (D, D), (D // 32) ** -0.5, 0.75, ((0, 32),)),
        "dense_bias": centred(key_of[9], (D,), 1.0, 6.0, ((0, 32),)),
        "first_gain": jnp.clip(1.0 + 0.1 * jax.random.normal(key_of[10], (D,), jnp.float32), 0.5, 1.5).astype(jnp.bfloat16),
        "first_bias": centred(key_of[11], (D,), 0.3, 4.0, ((0, 32),)),
        "up_weight": centred(key_of[12], (D, 2 * FF), D ** -0.5, 0.125, ((0, 32),)),
        "up_bias": centred(key_of[13], (2 * FF,), 0.3, 4.0),
        "down_weight": centred(key_of[14], (FF, D), (FF // 64) ** -0.5, 0.625, ((1, 32),)),
        "down_bias": centred(key_of[15], (D,), 1.0, 6.0, ((0, 32),)),
        "second_gain": jnp.clip(1.0 + 0.1 * jax.random.normal(key_of[16], (D,), jnp.float32), 0.5, 1.5).astype(jnp.bfloat16),
        "second_bias": centred(key_of[17], (D,), 0.3, 4.0, ((0, 32),)),
    }


@jax.custom_vjp
def low(v):
    return lax.optimization_barrier(v.astype(jnp.bfloat16)).astype(jnp.float32)

@jax.custom_vjp
def low_back(v):
    return v

def low_keep(v):
    return (low(v), None)

def low_pass(kept, grad):
    return (grad,)

def back_keep(v):
    return (v, None)

def back_low(kept, grad):
    return (low(grad),)
low.defvjp(low_keep, low_pass)
low_back.defvjp(back_keep, back_low)
deep_alpha = math.sqrt(48.0)
epsilon = 1e-05
mask_token = 3
highest = lax.Precision.HIGHEST

def rotary(values, positions):
    half_width = values.shape[-1] // 2
    frequency = jnp.exp(jnp.arange(half_width, dtype=jnp.float32) * (-2.0 * math.log(10000.0) / values.shape[-1]))
    angles = positions[:, None] * frequency[None, :]
    cosine = jnp.cos(angles)[:, None, :]
    sine_part = jnp.sin(angles)[:, None, :]
    first = values[..., :half_width]
    second = values[..., half_width:]
    return jnp.concatenate([first * cosine - second * sine_part, second * cosine + first * sine_part], axis=-1)

def normalize(residual, gain_vec, bias_vec):
    center = residual - lax.optimization_barrier(jnp.mean(residual, axis=-1, keepdims=True))
    spread = lax.optimization_barrier(jnp.mean(center * center, axis=-1, keepdims=True))
    return center * lax.rsqrt(spread + epsilon) * gain_vec + bias_vec

def linear(left, right):
    return jnp.dot(left, right, precision=highest)

def forward(shift, embedding, heads_weight, heads_bias, dense_weight, dense_bias, first_gain, first_bias, up_weight, up_bias, down_weight, down_bias, second_gain, second_bias, onehot, allowed, positions):
    total_length = onehot.shape[0]
    inputs = jnp.dot(onehot, embedding.T, precision=highest) + shift
    mixed_rows = low_back(linear(low(inputs), low(heads_weight)) + heads_bias)
    mixed_rows = mixed_rows.reshape(total_length, HEADS, 3 * HEAD)
    queries = rotary(mixed_rows[..., :HEAD], positions)
    keys_all = rotary(mixed_rows[..., HEAD:2 * HEAD], positions)
    packed = low_back(low(jnp.concatenate([queries, keys_all, mixed_rows[..., 2 * HEAD:]], axis=-1)))
    scores = low_back(jnp.einsum('qhd,khd->hqk', packed[..., :HEAD], packed[..., HEAD:2 * HEAD], precision=highest) * HEAD ** (-0.5))
    scores = jnp.where(allowed[None], scores, -jnp.inf)
    row_peak = lax.optimization_barrier(jnp.max(scores, axis=-1, keepdims=True))
    expos = jnp.exp(scores - row_peak)
    weights = expos / lax.optimization_barrier(jnp.sum(expos, axis=-1, keepdims=True))
    context = jnp.einsum('hqk,khd->qhd', low(weights), packed[..., 2 * HEAD:], precision=highest)
    context = low_back(low(context)).reshape(total_length, HEADS * HEAD)
    branch = low_back(linear(context, low(dense_weight)) + dense_bias)
    hidden = normalize(deep_alpha * inputs + branch, first_gain, first_bias)
    gate_up = low_back(linear(low(hidden), low(up_weight)) + up_bias)
    product = low(gate_up[:, :FF] * jax.nn.gelu(gate_up[:, FF:], approximate=False))
    mlp_branch = low_back(linear(product, low(down_weight)) + down_bias)
    return normalize(deep_alpha * hidden + mlp_branch, second_gain, second_bias)

def reference(token_ids, masked, item_flag, prefix, cotangent, embedding, heads_weight, heads_bias, dense_weight, dense_bias, first_gain, first_bias, up_weight, up_bias, down_weight, down_bias, second_gain, second_bias):
    params = tuple((array_in.astype(jnp.float32) for array_in in (embedding, heads_weight, heads_bias, dense_weight, dense_bias, first_gain, first_bias, up_weight, up_bias, down_weight, down_bias, second_gain, second_bias)))
    input_ids = jnp.where(masked == 1, mask_token, token_ids).astype(jnp.int32)
    positions = jnp.arange(LEN, dtype=jnp.float32)
    key_index = jnp.arange(LEN, dtype=jnp.int32)
    vocab_index = jnp.arange(VOCAB, dtype=jnp.int32)

    def one_item(carry, sliced):
        token_row, flag_value, prefix_value, grad_row = sliced
        onehot = (token_row[:, None] == vocab_index[None, :]).astype(jnp.float32)
        visible = jnp.where(flag_value == 1, LEN, prefix_value).astype(jnp.int32)
        allowed = (key_index[None, :] <= key_index[:, None]) | (key_index[None, :] < visible)
        shift = jnp.zeros((LEN, D), jnp.float32)

        def local_forward(*weight_list):
            return forward(*weight_list, onehot, allowed, positions)
        result, pullback = jax.vjp(local_forward, shift, *params)
        grads = pullback(grad_row.astype(jnp.float32))
        carry = tuple((summed + extra for summed, extra in zip(carry, grads[1:])))
        return (carry, (result.astype(jnp.bfloat16), grads[0]))
    initial = tuple((jnp.zeros(array_in.shape, jnp.float32) for array_in in params))
    totals, (layer_out, input_grad) = lax.scan(one_item, initial, (input_ids, item_flag, prefix, cotangent))
    return (layer_out, input_grad, 0.1 * totals[0], totals[1], totals[2], totals[3], totals[4], totals[5], totals[6], totals[7], totals[8], totals[9], totals[10], totals[11], totals[12])
```

```python
import math

import jax
import jax.numpy as jnp
from jax import lax
from jax.sharding import PartitionSpec as P

HEADS = 16
HEAD = 128


deep_alpha = math.sqrt(48.0)
epsilon = 1e-05
mask_token = 3
both = ("items", "seq")
bf16 = jnp.bfloat16
f32 = jnp.float32


def swap(part, axis, bit):
    return lax.ppermute(part, axis, [(j, j ^ bit) for j in range(lax.axis_size(axis))])


def bits_of(axis):
    found = []
    bit = 1
    while bit < lax.axis_size(axis):
        found.append((axis, bit))
        bit *= 2
    return found


def my_bit(axis, bit):
    return (lax.axis_index(axis) // bit) % 2


def in_order(own, got, place, dim):
    return jnp.where(
        place == 0, jnp.concatenate([own, got], axis=dim), jnp.concatenate([got, own], axis=dim)
    )


def pick(whole, place, dim):
    return lax.dynamic_index_in_dim(whole, place, dim, keepdims=False)


def gather_pieces(own, steps):
    pieces = [(0, 0, own)]
    for axis, bit in steps:
        pieces = pieces + [
            (
                mask_i ^ (bit if axis == "items" else 0),
                mask_s ^ (bit if axis == "seq" else 0),
                swap(piece, axis, bit),
            )
            for mask_i, mask_s, piece in pieces
        ]
    return pieces


def place_pieces(buffer, pieces, group, column):
    seq_size = lax.axis_size("seq")
    for mask_i, mask_s, piece in pieces:
        index = (
            (lax.axis_index("items") ^ mask_i) * seq_size + (lax.axis_index("seq") ^ mask_s)
        ) // group
        buffer = lax.dynamic_update_slice(buffer, piece[None], (index, 0, column))
    return buffer


def gather_merge(own, steps):
    for axis, bit in steps:
        own = in_order(own, swap(own, axis, bit), my_bit(axis, bit), 0)
    return own


def halve(whole, dim, axis, bit):
    place = my_bit(axis, bit)
    mine = pick(whole, place, dim)
    got = swap(pick(whole, 1 - place, dim), axis, bit)
    return (mine.astype(f32) + got.astype(f32)).astype(whole.dtype)


def butterfly(part, steps):
    for axis, bit in steps:
        part = part + swap(part, axis, bit)
    return part


def member_exchange(parts):
    for dim, bit in ((0, 2), (1, 1)):
        place = my_bit("seq", bit)
        mine = jnp.expand_dims(pick(parts, place, dim), dim)
        got = jnp.expand_dims(swap(pick(parts, 1 - place, dim), "seq", bit), dim)
        parts = in_order(mine, got, place, dim)
    return parts


def gather_four(own):
    far = swap(own, "seq", 2)
    near = swap(own, "seq", 1)
    return jnp.concatenate([own, near, far, swap(far, "seq", 1)], axis=0)


def sum_four(parts):
    own, near, far, cross = jnp.split(parts, 4, axis=0)
    far = (far.astype(f32) + swap(cross, "seq", 1).astype(f32)).astype(bf16)
    own = own.astype(f32) + swap(near, "seq", 1).astype(f32)
    return own + swap(far, "seq", 2).astype(f32)


def contract_rows(left, right):
    return lax.dot_general(
        left, right, (((0,), (0,)), ((), ())), preferred_element_type=f32
    )


def contract_cols(left, right):
    return lax.dot_general(
        left, right, (((1,), (1,)), ((), ())), preferred_element_type=f32
    )


def dot(left, right):
    return jnp.dot(left, right, preferred_element_type=f32)


def rotate(values, cosine, sine_part):
    half_width = values.shape[-1] // 2
    first = values[..., :half_width]
    second = values[..., half_width:]
    cosine = cosine[:, None, :]
    sine_part = sine_part[:, None, :]
    return jnp.concatenate(
        [first * cosine - second * sine_part, second * cosine + first * sine_part], axis=-1
    )


def norm_forward(residual, gain_vec, bias_vec):
    center = residual - jnp.mean(residual, axis=-1, keepdims=True)
    inverse = lax.rsqrt(jnp.mean(center * center, axis=-1, keepdims=True) + epsilon)
    normed = center * inverse
    return (normed * gain_vec + bias_vec, normed, inverse)


def norm_backward(grad_out, normed, inverse, gain_vec):
    scaled = grad_out * gain_vec
    grad_in = inverse * (
        scaled
        - jnp.mean(scaled, axis=-1, keepdims=True)
        - normed * jnp.mean(scaled * normed, axis=-1, keepdims=True)
    )
    return (grad_in, jnp.sum(grad_out * normed, axis=0), jnp.sum(grad_out, axis=0))


def visible_mask(offset, block_rows, total_length, visible):
    query_pos = offset + jnp.arange(block_rows, dtype=jnp.int32)[:, None]
    key_pos = jnp.arange(total_length, dtype=jnp.int32)[None, :]
    return (key_pos <= query_pos) | (key_pos < visible)


def block_scores(query_block, keys_all, offset, visible):
    block_rows = query_block.shape[0]
    total_length = keys_all.shape[0]
    scores = jnp.einsum(
        "qhd,khd->hqk", query_block, keys_all, preferred_element_type=f32
    ) * HEAD ** (-0.5)
    return jnp.where(
        visible_mask(offset, block_rows, total_length, visible)[None], scores, -jnp.inf
    )


def attend(unit, visible):
    total_length = unit.shape[0]
    block_rows = min(512, total_length)
    queries = unit[..., :HEAD]
    keys_all = unit[..., HEAD : 2 * HEAD]
    values = unit[..., 2 * HEAD :]
    contexts = []
    log_sums = []
    for offset in range(0, total_length, block_rows):
        scores = block_scores(queries[offset : offset + block_rows], keys_all, offset, visible)
        row_peak = jnp.max(scores, axis=-1, keepdims=True)
        expos = jnp.exp(scores - row_peak)
        row_total = jnp.sum(expos, axis=-1, keepdims=True)
        weights_low = (expos / row_total).astype(bf16)
        contexts.append(
            jnp.einsum(
                "hqk,khd->qhd", weights_low, values, preferred_element_type=f32
            ).astype(bf16)
        )
        log_sums.append((row_peak + jnp.log(row_total))[..., 0])
    return (jnp.concatenate(contexts, axis=0), jnp.concatenate(log_sums, axis=1))


def attend_back(unit, grad_context, log_sums, visible):
    total_length = unit.shape[0]
    block_rows = min(512, total_length)
    queries = unit[..., :HEAD]
    keys_all = unit[..., HEAD : 2 * HEAD]
    values = unit[..., 2 * HEAD :]
    grad_queries = []
    grad_keys = jnp.zeros(keys_all.shape, f32)
    grad_values = jnp.zeros(values.shape, f32)
    for offset in range(0, total_length, block_rows):
        query_block = queries[offset : offset + block_rows]
        grad_block = grad_context[offset : offset + block_rows]
        scores = block_scores(query_block, keys_all, offset, visible)
        weights = jnp.exp(scores - log_sums[:, offset : offset + block_rows, None])
        weights_low = weights.astype(bf16)
        grad_values = grad_values + jnp.einsum(
            "hqk,qhd->khd", weights_low, grad_block, preferred_element_type=f32
        )
        grad_weights = jnp.einsum(
            "qhd,khd->hqk", grad_block, values, preferred_element_type=f32
        )
        inner = jnp.sum(weights * grad_weights, axis=-1, keepdims=True)
        grad_scores = (weights * (grad_weights - inner)).astype(bf16)
        grad_queries.append(
            jnp.einsum("hqk,khd->qhd", grad_scores, keys_all, preferred_element_type=f32)
            * HEAD ** (-0.5)
        )
        grad_keys = grad_keys + jnp.einsum(
            "hqk,qhd->khd", grad_scores, query_block, preferred_element_type=f32
        ) * HEAD ** (-0.5)
    return jnp.concatenate(
        [jnp.concatenate(grad_queries, axis=0), grad_keys, grad_values], axis=-1
    ).astype(bf16)


def on_device(
    token_ids,
    masked,
    item_flag,
    prefix,
    cotangent,
    embedding,
    heads_weight,
    heads_bias,
    dense_weight,
    dense_bias,
    first_gain,
    first_bias,
    up_weight,
    up_bias,
    down_weight,
    down_bias,
    second_gain,
    second_bias,
):
    items_here, span = token_ids.shape
    items_size, seq_size = lax.axis_size("items"), lax.axis_size("seq")
    item_place, seq_place = lax.axis_index("items"), lax.axis_index("seq")
    count = items_size * seq_size
    length = span * seq_size
    local_rows = items_here * span
    width = embedding.shape[0] * count
    vocab = embedding.shape[1]
    heads_here = HEADS // seq_size
    packed_width = heads_here * 3 * HEAD
    weight_rows = up_weight.shape[0]
    ff_width = down_weight.shape[0]
    members = 4
    groups = count // members
    member = seq_place % members
    ff_part = -(-ff_width // (members * 128)) * 128

    item_bits, seq_bits = bits_of("items"), bits_of("seq")
    outer_bits = seq_bits[2:]

    input_ids = jnp.where(masked == 1, mask_token, token_ids)
    small = [
        embedding.reshape(-1),
        input_ids.astype(bf16).reshape(-1),
        heads_bias,
        dense_bias,
        first_gain,
        first_bias,
        down_bias,
        second_gain,
        second_bias,
    ]
    ends = [0]
    for part in small:
        ends.append(ends[-1] + part.shape[0])
    flat = jnp.concatenate(small)
    flat = jnp.pad(flat, (0, -flat.shape[0] % 1024)).reshape(1, -1, 128)
    everyone = lax.all_gather(flat, both, axis=0, tiled=True).reshape(count, -1)
    pieces = [everyone[:, a:b] for a, b in zip(ends[:-1], ends[1:])]
    table = pieces[0].reshape(width, vocab)
    ids_here = pick(pieces[1].reshape(items_size, seq_size, items_here, span), item_place, 0)
    ids_here = jnp.transpose(ids_here, (1, 0, 2)).reshape(items_here, length).astype(jnp.int32)
    b_heads, b_dense, gain_one, shift_one, b_down, gain_two, shift_two = (
        part.reshape(-1).astype(f32) for part in pieces[2:]
    )

    w_block = lax.all_to_all(
        jnp.transpose(heads_weight.reshape(weight_rows, seq_size, packed_width), (1, 0, 2)),
        "seq",
        split_axis=0,
        concat_axis=0,
        tiled=True,
    ).reshape(seq_size * weight_rows, packed_width)
    table_block = lax.dynamic_slice_in_dim(
        table, item_place * seq_size * weight_rows, seq_size * weight_rows, 0
    )
    mixed_table = butterfly(contract_rows(table_block, w_block), item_bits)
    mixed_table = mixed_table + lax.dynamic_slice_in_dim(
        b_heads, seq_place * packed_width, packed_width, 0
    )

    def by_member(part):
        padded = jnp.pad(part, ((0, 0), (0, members * ff_part - ff_width)))
        parts = jnp.transpose(padded.reshape(weight_rows, 2, 2, ff_part), (1, 2, 0, 3))
        return member_exchange(parts).reshape(members * weight_rows, ff_part)

    w_dense = dense_weight
    w_dense = gather_merge(w_dense, seq_bits[1:][::-1][::-1])
    dense_pieces = gather_pieces(w_dense, item_bits[1:] + item_bits[:1] + seq_bits[:1])
    dense_buffer = jnp.zeros((items_size, 2, seq_size // 2, weight_rows, width), bf16)
    for mask_i, mask_s, piece in dense_pieces:
        dense_buffer = lax.dynamic_update_slice(
            dense_buffer,
            piece.reshape(1, 1, seq_size // 2, weight_rows, width),
            (item_place ^ mask_i, (seq_place ^ mask_s) % 2, 0, 0, 0),
        )
    w_dense = jnp.transpose(dense_buffer, (0, 2, 1, 3, 4)).reshape(width, width)

    order_a = outer_bits + item_bits[:1] + item_bits[1:]
    order_b = outer_bits + item_bits[1:] + item_bits[:1]
    w_in = jnp.zeros((groups, members * weight_rows, 2 * ff_part), bf16)
    w_in = place_pieces(
        w_in, gather_pieces(by_member(up_weight[:, :ff_width]), order_a), members, 0
    )
    w_in = place_pieces(
        w_in, gather_pieces(by_member(up_weight[:, ff_width:]), order_b), members, ff_part
    )
    w_in = w_in.reshape(width, 2 * ff_part)
    w_out = jnp.zeros((2 * groups, members * weight_rows // 2, ff_part), bf16)
    out_first, out_second = jnp.split(by_member(down_weight.T), 2, axis=0)

    def place_half(buffer, found, which):
        for mask_i, mask_s, piece in found:
            index = ((item_place ^ mask_i) * seq_size + (seq_place ^ mask_s)) // members
            buffer = lax.dynamic_update_slice(buffer, piece[None], (2 * index + which, 0, 0))
        return buffer

    w_out = place_half(w_out, gather_pieces(out_first, order_a), 0)
    w_out = place_half(w_out, gather_pieces(out_second, order_b), 1)
    w_out = w_out.reshape(width, ff_part)
    in_bias = jnp.pad(
        up_bias.astype(f32).reshape(2, ff_width), ((0, 0), (0, members * ff_part - ff_width))
    )
    in_bias = lax.dynamic_slice(in_bias, (0, member * ff_part), (2, ff_part)).reshape(-1)

    vocab_index = jnp.arange(vocab, dtype=jnp.int32)
    positions = jnp.arange(length, dtype=f32)
    frequency = jnp.exp(
        jnp.arange(HEAD // 2, dtype=f32) * (-2.0 * math.log(10000.0) / HEAD)
    )
    angles = positions[:, None] * frequency[None, :]
    cosine, sine_part = jnp.cos(angles), jnp.sin(angles)
    visible = jnp.where(item_flag == 1, length, prefix)
    packed, log_sums, onehots, context_rows = [], [], [], []
    for item in range(items_here):
        onehot = (ids_here[item][:, None] == vocab_index[None, :]).astype(bf16)
        mixed = jnp.dot(onehot.astype(f32), mixed_table, precision=lax.Precision.HIGHEST).reshape(
            length, heads_here, 3 * HEAD
        )
        unit = jnp.concatenate(
            [
                rotate(mixed[..., :HEAD], cosine, sine_part),
                rotate(mixed[..., HEAD : 2 * HEAD], cosine, sine_part),
                mixed[..., 2 * HEAD :],
            ],
            axis=-1,
        ).astype(bf16)
        context, log_sum = attend(unit, visible[item])
        onehots.append(onehot)
        packed.append(unit)
        log_sums.append(log_sum)
        rows = lax.all_to_all(
            context.reshape(seq_size, span, heads_here * HEAD),
            "seq",
            split_axis=0,
            concat_axis=0,
            tiled=True,
        )
        context_rows.append(jnp.transpose(rows, (1, 0, 2)).reshape(span, HEADS * HEAD))

    halves = 2 if items_here % 2 == 0 else 1
    per_half = items_here // halves
    kept = []
    for half in range(halves):
        chosen = range(half * per_half, (half + 1) * per_half)
        context = jnp.concatenate([context_rows[item] for item in chosen], axis=0)
        own_ids = input_ids[half * per_half : (half + 1) * per_half].reshape(-1)
        onehot = (own_ids[:, None] == vocab_index[None, :]).astype(bf16)
        inputs = contract_cols(onehot, table)
        branch = dot(context, w_dense) + b_dense
        hidden, normed_one, inverse_one = norm_forward(
            deep_alpha * inputs + branch, gain_one, shift_one
        )
        shared = gather_four(hidden.astype(bf16))
        gate_up = dot(shared, w_in) + in_bias
        up_part, gate = gate_up[:, :ff_part], gate_up[:, ff_part:]
        below = 0.5 * (1.0 + lax.erf(gate * (0.5**0.5)))
        activated = gate * below
        slope = below + gate * jnp.exp(-0.5 * gate * gate) * (1.0 / math.sqrt(2.0 * math.pi))
        product_low = (up_part * activated).astype(bf16)
        act_low = activated.astype(bf16)
        slope_low = (up_part * slope).astype(bf16)
        mlp_branch = sum_four(contract_cols(product_low, w_out).astype(bf16)) + b_down
        layer_out, normed_two, inverse_two = norm_forward(
            deep_alpha * hidden + mlp_branch, gain_two, shift_two
        )
        grad_top = (
            cotangent[half * per_half : (half + 1) * per_half]
            .reshape(per_half * span, width)
            .astype(f32)
        )
        grad_resid_two, grad_gain_two, grad_shift_two = norm_backward(
            grad_top, normed_two, inverse_two, gain_two
        )
        grad_mlp_low = grad_resid_two.astype(bf16)
        grad_shared = gather_four(grad_mlp_low)
        grad_product = dot(grad_shared, w_out)
        grad_in_low = jnp.concatenate(
            [grad_product * act_low.astype(f32), grad_product * slope_low.astype(f32)], axis=1
        ).astype(bf16)
        grad_hidden = (
            sum_four(contract_cols(grad_in_low, w_in).astype(bf16)) + deep_alpha * grad_resid_two
        )
        grad_resid_one, grad_gain_one, grad_shift_one = norm_backward(
            grad_hidden, normed_one, inverse_one, gain_one
        )
        grad_branch_low = grad_resid_one.astype(bf16)
        grad_context = contract_cols(grad_branch_low, w_dense).astype(bf16)
        kept.append(
            dict(
                layer_out=layer_out.astype(bf16),
                context=context,
                shared=shared,
                product=product_low,
                grad_shared=grad_shared,
                grad_in=grad_in_low,
                grad_branch=grad_branch_low,
                grad_resid_one=grad_resid_one,
                grad_context=grad_context,
                vectors=jnp.stack(
                    [
                        grad_gain_one,
                        grad_shift_one,
                        jnp.sum(grad_branch_low.astype(f32), axis=0),
                        grad_gain_two,
                        grad_shift_two,
                        jnp.sum(grad_mlp_low.astype(f32), axis=0),
                    ]
                ),
                in_sum=jnp.sum(grad_in_low.astype(f32), axis=0),
                token_sum=lax.dot_general(
                    grad_resid_one,
                    onehot.astype(f32),
                    (((0,), (0,)), ((), ())),
                    precision=lax.Precision.HIGHEST,
                    preferred_element_type=f32,
                ),
            )
        )

    def total(function):
        result = function(kept[0])
        for one in kept[1:]:
            result = result + function(one)
        return result

    def to_owner(whole, order):
        dims = [("items", bit) for _, bit in item_bits[::-1]] + outer_bits[::-1]
        whole = whole.reshape((2,) * len(dims) + (members * weight_rows, -1))
        for step in order[::-1]:
            place = dims.index(step)
            whole = halve(whole, place, *step)
            dims.pop(place)
        return whole

    grad_in_weight = total(lambda one: contract_rows(one["shared"], one["grad_in"])).astype(bf16)
    grad_out_weight = total(lambda one: contract_rows(one["grad_shared"], one["product"])).astype(
        bf16
    )
    sums = [
        to_owner(grad_in_weight[:, :ff_part], order_a),
        to_owner(grad_in_weight[:, ff_part:], order_b),
        to_owner(grad_out_weight, order_a),
    ]

    def from_members(part):
        parts = member_exchange(part.reshape(2, 2, weight_rows, ff_part))
        parts = jnp.transpose(parts, (2, 0, 1, 3)).reshape(weight_rows, members * ff_part)
        return parts[:, :ff_width].astype(f32)

    grad_up, grad_gate, grad_down = (from_members(part) for part in sums)

    def sum_rows(whole):
        dims = item_bits[::-1] + seq_bits[::-1]
        whole = whole.reshape((2,) * len(dims) + (weight_rows, -1))
        for step in seq_bits[:1] + item_bits + seq_bits[1:]:
            place = dims.index(step)
            whole = halve(whole, place, *step)
            dims.pop(place)
        return whole

    grad_dense = sum_rows(
        total(lambda one: contract_rows(one["context"], one["grad_branch"])).astype(bf16)
    ).astype(f32)
    token_sum = sum_rows(total(lambda one: one["token_sum"]))

    in_sum = total(lambda one: one["in_sum"]).reshape(2, ff_part)
    in_all = lax.dynamic_update_slice(
        jnp.zeros((2, members * ff_part), f32), in_sum, (0, member * ff_part)
    )
    vectors = jnp.concatenate([total(lambda one: one["vectors"]).reshape(-1), in_all.reshape(-1)])
    vectors = jnp.pad(vectors, (0, -vectors.shape[0] % 1024)).reshape(-1, 128)
    vectors = butterfly(vectors, seq_bits + item_bits).reshape(-1)
    in_all = vectors[6 * width :][: 2 * members * ff_part].reshape(2, members * ff_part)
    grad_up_bias = in_all[:, :ff_width].reshape(-1)
    vectors = vectors[: 6 * width].reshape(6, count, weight_rows)
    own_vectors = pick(vectors, item_place * seq_size + seq_place, 1)

    w_slices = jnp.zeros((items_size, seq_size * weight_rows, packed_width), bf16)
    w_slices = place_pieces(w_slices, gather_pieces(w_block, item_bits), seq_size, 0)
    w_slice = w_slices.reshape(width, packed_width)
    token_mixed = jnp.zeros((vocab, packed_width), f32)
    input_grads = []
    for item in range(items_here):
        half, row = item // per_half, (item % per_half) * span
        grad_context = kept[half]["grad_context"][row : row + span]
        grad_context = lax.all_to_all(
            jnp.transpose(grad_context.reshape(span, seq_size, heads_here * HEAD), (1, 0, 2)),
            "seq",
            split_axis=0,
            concat_axis=0,
            tiled=True,
        ).reshape(length, heads_here, HEAD)
        grad_packed = attend_back(packed[item], grad_context, log_sums[item], visible[item])
        grad_packed = grad_packed.astype(f32)
        grad_mixed = jnp.concatenate(
            [
                rotate(grad_packed[..., :HEAD], cosine, -sine_part),
                rotate(grad_packed[..., HEAD : 2 * HEAD], cosine, -sine_part),
                grad_packed[..., 2 * HEAD :],
            ],
            axis=-1,
        )
        grad_mixed = grad_mixed.reshape(length, packed_width).astype(bf16)
        token_mixed = token_mixed + contract_rows(onehots[item], grad_mixed)
        part = contract_cols(grad_mixed, w_slice).astype(bf16).reshape(seq_size, span, width)
        for step in seq_bits:
            part = halve(part.reshape(-1, 2, span, width), 1, *step)
        input_grads.append(
            part.reshape(span, width).astype(f32)
            + deep_alpha * kept[half]["grad_resid_one"][row : row + span]
        )

    token_mixed = butterfly(token_mixed, item_bits)
    token_all = token_mixed[None]
    token_all = gather_merge(token_all, seq_bits)
    token_all = jnp.transpose(token_all, (1, 0, 2)).reshape(vocab, -1)
    grad_heads = jnp.dot(embedding.astype(f32), token_all, precision=lax.Precision.HIGHEST)
    grad_heads_bias = lax.dynamic_slice_in_dim(
        jnp.sum(token_all, axis=0),
        (item_place * seq_size + seq_place) * heads_bias.shape[0],
        heads_bias.shape[0],
        0,
    )
    embed_grad = 0.1 * (
        lax.dot_general(
            heads_weight.astype(f32),
            token_all,
            (((1,), (1,)), ((), ())),
            precision=lax.Precision.HIGHEST,
            preferred_element_type=f32,
        )
        + deep_alpha * token_sum
    )
    return (
        jnp.concatenate([one["layer_out"] for one in kept], axis=0).reshape(
            items_here, span, width
        ),
        jnp.stack(input_grads),
        embed_grad,
        grad_heads,
        grad_heads_bias,
        grad_dense,
        own_vectors[2],
        own_vectors[0],
        own_vectors[1],
        jnp.concatenate([grad_up, grad_gate], axis=1),
        grad_up_bias,
        grad_down.T,
        own_vectors[5],
        own_vectors[3],
        own_vectors[4],
    )


def solution(mesh):
    in_specs = (
        P("items", "seq"),
        P("items", "seq"),
        P("items"),
        P("items"),
        P("items", "seq", None),
        P(("items", "seq"), None),
        P(("items", "seq"), None),
        P(("items", "seq")),
        P(("items", "seq"), None),
        P(("items", "seq")),
        P(("items", "seq")),
        P(("items", "seq")),
        P(("items", "seq"), None),
        P(),
        P(None, ("items", "seq")),
        P(("items", "seq")),
        P(("items", "seq")),
        P(("items", "seq")),
    )
    out_specs = (
        P("items", "seq", None),
        P("items", "seq", None),
        P(("items", "seq"), None),
        P(("items", "seq"), None),
        P(("items", "seq")),
        P(("items", "seq"), None),
        P(("items", "seq")),
        P(("items", "seq")),
        P(("items", "seq")),
        P(("items", "seq"), None),
        P(),
        P(None, ("items", "seq")),
        P(("items", "seq")),
        P(("items", "seq")),
        P(("items", "seq")),
    )
    return jax.shard_map(
        on_device, mesh=mesh, in_specs=in_specs, out_specs=out_specs, check_vma=False
    )
```

```python
import functools
import math

import jax
import jax.numpy as jnp
import numpy as np
from jax import lax
from jax.experimental import pallas as pl
from jax.experimental.pallas import tpu as pltpu
from jax.sharding import PartitionSpec as P

HEADS = 16
HEAD = 128


deep_alpha = math.sqrt(48.0)
epsilon = 1e-05
mask_token = 3
both = ("items", "seq")
bf16 = jnp.bfloat16
f32 = jnp.float32
score_scale = HEAD ** (-0.5)
exponent_scale = score_scale * math.log2(math.e)


class Lines:
    def __init__(self):
        self.last = {}

    def swap(self, part, axis, bit):
        if (axis, bit) in self.last:
            part, _ = lax.optimization_barrier((part, self.last[axis, bit]))
        size = lax.axis_size(axis)
        got = lax.ppermute(part, axis, [(j, j ^ bit) for j in range(size)])
        self.last[axis, bit] = got
        return got


def bits_of(axis):
    found = []
    bit = 1
    while bit < lax.axis_size(axis):
        found.append((axis, bit))
        bit *= 2
    return found


def my_bit(axis, bit):
    return (lax.axis_index(axis) // bit) % 2


def in_order(own, got, place, dim):
    return jnp.where(
        place == 0, jnp.concatenate([own, got], axis=dim), jnp.concatenate([got, own], axis=dim)
    )


def pick(whole, place, dim):
    return lax.dynamic_index_in_dim(whole, place, dim, keepdims=False)


def gather_merge(lines, own, steps):
    for axis, bit in steps:
        own = in_order(own, lines.swap(own, axis, bit), my_bit(axis, bit), 0)
    return own


def halve(lines, whole, dim, axis, bit):
    place = my_bit(axis, bit)
    mine = pick(whole, place, dim)
    got = lines.swap(pick(whole, 1 - place, dim), axis, bit)
    return (mine.astype(f32) + got.astype(f32)).astype(whole.dtype)


def moved(masks, axis, bit):
    return (masks[0] ^ (bit if axis == "items" else 0), masks[1] ^ (bit if axis == "seq" else 0))


def gather_four(lines, own):
    chip = jnp.concatenate([own, lines.swap(own, "seq", 2)], axis=0)
    return jnp.concatenate([chip, lines.swap(chip, "seq", 1)], axis=0)


def sum_four(lines, parts):
    mine, other = jnp.split(parts, 2, axis=0)
    mine = mine.astype(f32) + lines.swap(other, "seq", 1).astype(f32)
    own, far = jnp.split(mine, 2, axis=0)
    return own + lines.swap(far.astype(bf16), "seq", 2).astype(f32)


def contract_rows(left, right):
    return lax.dot_general(left, right, (((0,), (0,)), ((), ())), preferred_element_type=f32)


def contract_cols(left, right):
    return lax.dot_general(left, right, (((1,), (1,)), ((), ())), preferred_element_type=f32)


def dot(left, right):
    return jnp.dot(left, right, preferred_element_type=f32)


def turn(values, cosine, sine_part):
    return values * cosine + pltpu.roll(values, HEAD // 2, 1) * sine_part


def head_parts(onehot_ref, table_ref, cosine, sine_part):
    onehot = onehot_ref[...]
    mixed = dot(jnp.concatenate([onehot, onehot], axis=1), table_ref[...])
    query = turn(mixed[:, :HEAD], cosine, sine_part).astype(bf16)
    key = turn(mixed[:, HEAD : 2 * HEAD], cosine, sine_part).astype(bf16)
    return query, key, mixed[:, 2 * HEAD :].astype(bf16)


def visible_scores(key, query, offset, visible):
    scores = contract_cols(key, query)
    place = offset + lax.broadcasted_iota(jnp.int32, (1, query.shape[0]), 1)
    seen = lax.broadcasted_iota(jnp.int32, scores.shape, 0) < jnp.maximum(place + 1, visible)
    return jnp.where(seen, scores, -1e30)


def table_halves(mixed_table):
    vocab = mixed_table.shape[0]
    by_head = jnp.transpose(mixed_table.reshape(vocab, -1, 3 * HEAD), (1, 0, 2))
    high = lax.reduce_precision(by_head, 8, 7)
    return jnp.concatenate([high.astype(bf16), (by_head - high).astype(bf16)], axis=1)


MESH = pl.DeviceIdType.MESH


class Copies:
    def __init__(self, send_sems, recv_sems, local_sems):
        self.sems = send_sems, recv_sems, local_sems
        self.sent = {}
        self.moved = 0
        self.count = 0
        self.here = lax.axis_index("items"), lax.axis_index("seq")

    def send(self, source, target, masks):
        order = self.count
        self.count += 1
        copy = pltpu.make_async_remote_copy(
            src_ref=source,
            dst_ref=target,
            send_sem=self.sems[0].at[order],
            recv_sem=self.sems[1].at[order],
            device_id=(self.here[0] ^ masks[0], self.here[1] ^ masks[1]),
            device_id_type=MESH,
        )
        copy.start()
        self.sent[id(copy)] = copy
        return copy

    def move(self, source, target):
        copy = pltpu.make_async_copy(source, target, self.sems[2].at[self.moved])
        self.moved += 1
        copy.start()
        return copy

    def sent_now(self, copy):
        self.sent.pop(id(copy)).wait_send()

    def end(self):
        for copy in self.sent.values():
            copy.wait_send()


def wait_all(copies):
    for copy in copies:
        copy.wait_recv()


def mask_of(step):
    return moved((0, 0), *step)


def greet(masks):
    barrier = pltpu.get_barrier_semaphore()
    here = lax.axis_index("items"), lax.axis_index("seq")
    for mask_i, mask_s in masks:
        pl.semaphore_signal(
            barrier,
            inc=1,
            device_id=(here[0] ^ mask_i, here[1] ^ mask_s),
            device_id_type=MESH,
        )
    pl.semaphore_wait(barrier, len(masks))


def partners(seq_size, item_bits):
    return [(0, mask) for mask in range(1, seq_size)] + [mask_of(step) for step in item_bits]


def aligned(place, size):
    return pl.ds(place // size * size, size)


def first_kernel(
    item_bits,
    seq_bits,
    row_count,
    small_ref,
    heads_ref,
    dense_ref,
    in_ref,
    out_ref,
    everyone_ref,
    table_ref,
    block_ref,
    dense_all_ref,
    own_in_ref,
    own_out_ref,
    embed_scr,
    block_scr,
    sum_scr,
    got_scr,
    send_sems,
    recv_sems,
    local_sems,
):
    items_size, seq_size = everyone_ref.shape[:2]
    item_place, seq_place = lax.axis_index("items"), lax.axis_index("seq")
    core, chip = seq_place % 2, seq_place // 2
    member = seq_place % 4
    rows = dense_ref.shape[0]
    columns = block_scr.shape[2]
    greet(partners(seq_size, item_bits))
    copies = Copies(send_sems, recv_sems, local_sems)

    def head_columns(place):
        return heads_ref.at[:, pl.ds(pl.multiple_of(place * columns, 128), columns)]

    small = [copies.send(small_ref, everyone_ref.at[item_place, seq_place], mask_of(seq_bits[0]))]
    heads = [
        copies.send(head_columns(seq_place ^ mask), block_scr.at[seq_place], (0, mask))
        for mask in range(1, seq_size)
    ]
    dense = [
        copies.send(dense_ref, dense_all_ref.at[item_place, chip, core], mask_of(seq_bits[1]))
    ]
    shares = []
    for source, target in ((in_ref, own_in_ref), (out_ref, own_out_ref)):
        mine = pl.ds(pl.multiple_of(member * rows, rows), rows)
        for mask in range(1, 4):
            other = member ^ mask
            shares.append(
                copies.send(source.at[other // 2, other % 2], target.at[mine], (0, mask))
            )
    local = [
        copies.move(small_ref, everyone_ref.at[item_place, seq_place]),
        copies.move(dense_ref, dense_all_ref.at[item_place, chip, core]),
        copies.move(head_columns(seq_place), block_scr.at[seq_place]),
        copies.move(in_ref.at[member // 2, core], own_in_ref.at[mine]),
        copies.move(out_ref.at[member // 2, core], own_out_ref.at[mine]),
    ]
    for copy in local:
        copy.wait()

    for order in range(1, len(seq_bits)):
        wait_all(small[-1:])
        part = everyone_ref.at[item_place, aligned(seq_place, 2**order)]
        small.append(copies.send(part, part, mask_of(seq_bits[order])))
        if order > 1:
            wait_all(dense[-1:])
            part = dense_all_ref.at[item_place, aligned(chip, 2 ** (order - 1)), core]
            dense.append(copies.send(part, part, mask_of(seq_bits[order])))
    wait_all(small[-1:])
    embed = copies.move(everyone_ref.at[item_place, :, pl.ds(0, row_count)], embed_scr)
    part = everyone_ref.at[item_place]
    small.append(copies.send(part, part, mask_of(item_bits[0])))
    wait_all(dense[-1:])

    def dense_part(mask):
        return dense_all_ref.at[item_place ^ mask, :, core]

    known = [0]
    waves = []
    for step in item_bits[::-1]:
        waves.append([(mask, step) for mask in known])
        known = known + [mask ^ step[1] for mask in known]
    arrived = {}
    for wave in waves:
        part = dense_part(0)
        arrived[wave[0][1][1]] = copies.send(part, part, mask_of(wave[0][1]))
    near = [copies.send(dense_part(0), dense_part(0), mask_of(seq_bits[0]))]

    wait_all(heads)
    embed.wait()
    sum_scr[0] = lax.dot_general(
        embed_scr[...].reshape(seq_size * row_count, -1),
        block_scr[...].reshape(seq_size * row_count, columns),
        (((0,), (0,)), ((), ())),
        preferred_element_type=f32,
    )
    block_out = copies.move(block_scr, block_ref)
    for order, step in enumerate(item_bits):
        one = copies.send(sum_scr.at[order], got_scr.at[order], mask_of(step))
        if order + 1 < len(item_bits):
            wait_all(small[-1:])
            part = everyone_ref.at[aligned(item_place, 2 ** (order + 1))]
            small.append(copies.send(part, part, mask_of(item_bits[order + 1])))
        one.wait_recv()
        sum_scr[order + 1] = sum_scr[order] + got_scr[order]
    table_ref[...] = sum_scr[len(item_bits)]

    for wave in waves:
        for mask, step in wave:
            if mask:
                part = dense_part(mask)
                arrived[mask ^ step[1]] = copies.send(part, part, mask_of(step))
        for mask, step in wave:
            arrived[mask ^ step[1]].wait_recv()
            part = dense_part(mask ^ step[1])
            near.append(copies.send(part, part, mask_of(seq_bits[0])))
    wait_all(near)
    wait_all(shares)
    wait_all(small[-1:])
    block_out.wait()
    copies.end()


def first_call(item_bits, seq_bits, small, heads, dense, parts_in, parts_out):
    items_size, seq_size = 2 ** len(item_bits), 2 ** len(seq_bits)
    row_count = heads.shape[0]
    rows, width = dense.shape
    vocab = small.shape[1]
    columns = heads.shape[1] // seq_size
    any_space = pl.BlockSpec(memory_space=pl.ANY)
    spare = 8 * (len(item_bits) + len(seq_bits)) + 2 * seq_size + 2 ** (len(item_bits) + 1)
    return pl.pallas_call(
        functools.partial(first_kernel, item_bits, seq_bits, row_count),
        in_specs=[any_space] * 5,
        out_specs=[any_space, pl.BlockSpec(memory_space=pltpu.VMEM)] + [any_space] * 4,
        out_shape=[
            jax.ShapeDtypeStruct((items_size, seq_size) + small.shape, bf16),
            jax.ShapeDtypeStruct((vocab, columns), f32),
            jax.ShapeDtypeStruct((seq_size, row_count, columns), bf16),
            jax.ShapeDtypeStruct((items_size, seq_size // 2, 2, rows, width), bf16),
            jax.ShapeDtypeStruct((4 * rows, parts_in.shape[3]), bf16),
            jax.ShapeDtypeStruct((4 * rows, parts_out.shape[3]), bf16),
        ],
        scratch_shapes=[
            pltpu.VMEM((seq_size, row_count, vocab), bf16),
            pltpu.VMEM((seq_size, row_count, columns), bf16),
            pltpu.VMEM((len(item_bits) + 1, vocab, columns), f32),
            pltpu.VMEM((len(item_bits), vocab, columns), f32),
            pltpu.SemaphoreType.DMA((spare,)),
            pltpu.SemaphoreType.DMA((spare,)),
            pltpu.SemaphoreType.DMA((8,)),
        ],
        compiler_params=pltpu.CompilerParams(
            collective_id=0, has_side_effects=True, vmem_limit_bytes=24 * 2**20
        ),
        name="first",
    )(small, heads, dense, parts_in, parts_out)


class Spread:
    def __init__(self, copies, own, whole, outer_bits, item_bits):
        self.copies, self.own, self.whole = copies, own, whole
        self.outer_bits, self.item_bits = outer_bits, item_bits
        self.half = own.shape[0] // 2

    def part(self, masks):
        place = (self.copies.here[0] ^ masks[0]) * lax.axis_size("seq")
        return self.whole.at[(place + (self.copies.here[1] ^ masks[1])) // 4]

    def over(self, masks, step, rows=None):
        source = self.own if masks == (0, 0) else self.part(masks)
        target = self.part(masks)
        if rows is not None:
            source, target = source.at[rows], target.at[rows]
        return self.copies.send(source, target, mask_of(step))

    def start(self):
        self.local = self.copies.move(self.own, self.part((0, 0)))
        self.first = [self.over((0, 0), step) for step in self.item_bits]
        self.outer = self.over((0, 0), self.outer_bits[0])

    def cross(self, masks, first):
        one, two = self.item_bits
        first[0].wait_recv()
        found = [self.over(moved(masks, *one), two, pl.ds(0, self.half))]
        first[1].wait_recv()
        found.append(self.over(moved(masks, *two), one, pl.ds(self.half, self.half)))
        return found

    def cross_own(self):
        self.last = self.cross((0, 0), self.first)

    def spread_outer(self):
        self.outer.wait_recv()
        masks = mask_of(self.outer_bits[0])
        self.second = [self.over(masks, step) for step in self.item_bits]

    def cross_outer(self):
        self.last += self.cross(mask_of(self.outer_bits[0]), self.second)

    def plain(self):
        self.local = self.copies.move(self.own, self.part((0, 0)))
        known = [(0, 0)]
        for step in self.outer_bits + self.item_bits:
            wait_all([self.over(masks, step) for masks in known])
            known = known + [moved(masks, *step) for masks in known]
        self.last = []

    def end(self):
        wait_all(self.last)
        self.local.wait()


def attend_unit(block, visible, onehot_ref, table_ref, cosine_ref, sine_ref, context_ref, lse_ref):
    query, key, value = head_parts(onehot_ref, table_ref, cosine_ref[...], sine_ref[...])
    value_turned = value.T
    for offset in range(0, query.shape[0], block):
        scores = visible_scores(key, query[offset : offset + block], offset, visible)
        peak = jnp.max(scores, axis=0, keepdims=True)
        expos = jnp.exp2((scores - peak) * exponent_scale)
        total = jnp.sum(expos, axis=0, keepdims=True)
        context = dot(value_turned, expos.astype(bf16)) / total
        context_ref[offset : offset + block, :] = context.T.astype(bf16)
        lse_ref[:, offset : offset + block] = peak * exponent_scale + jnp.log2(total)


def second_kernel(
    item_bits,
    seq_bits,
    visible_ref,
    onehot_ref,
    table_ref,
    cosine_ref,
    sine_ref,
    own_in_ref,
    own_out_ref,
    context_ref,
    lse_ref,
    in_ref,
    out_ref,
    context_scr,
    send_sems,
    recv_sems,
    local_sems,
):
    seq_size = 2 ** len(seq_bits)
    items_here, length, features = context_scr.shape
    heads_here = features // HEAD
    span = length // seq_size
    seq_place = lax.axis_index("seq")
    outer_bits = seq_bits[2:]
    greet(partners(seq_size, item_bits))
    copies = Copies(send_sems, recv_sems, local_sems)
    spreads = [
        Spread(copies, own_in_ref, in_ref, outer_bits, item_bits),
        Spread(copies, own_out_ref, out_ref, outer_bits, item_bits),
    ]
    stepwise = len(outer_bits) == 1 and len(item_bits) == 2
    if stepwise:
        for one in spreads:
            one.start()
    arrivals, local = [], []
    for item in range(items_here):

        @pl.loop(0, heads_here)
        def _(head):
            place = pl.ds(pl.multiple_of(head * HEAD, HEAD), HEAD)
            attend_unit(
                min(256, length),
                visible_ref[item],
                onehot_ref.at[item],
                table_ref.at[head],
                cosine_ref,
                sine_ref,
                context_scr.at[item, :, place],
                lse_ref.at[item, head],
            )

        target = context_ref.at[
            item, :, pl.ds(pl.multiple_of(seq_place * features, HEAD), features)
        ]
        for mask in range(seq_size):
            rows = pl.ds(pl.multiple_of((seq_place ^ mask) * span, span), span)
            source = context_scr.at[item, rows]
            if mask:
                arrivals.append(copies.send(source, target, (0, mask)))
            else:
                local.append(copies.move(source, target))
    if stepwise:
        for one in spreads:
            one.cross_own()
        for one in spreads:
            one.spread_outer()
        for one in spreads:
            one.cross_outer()
    else:
        for one in spreads:
            one.plain()
    for one in spreads:
        one.end()
    wait_all(arrivals)
    for copy in local:
        copy.wait()
    copies.end()


def second_call(item_bits, seq_bits, visible, onehots, tables, cosine, sine_part, own_in, own_out):
    items_here, length, vocab = onehots.shape
    heads_here = tables.shape[0]
    features = heads_here * HEAD
    seq_size = 2 ** len(seq_bits)
    groups = 2 ** (len(item_bits) + len(seq_bits)) // 4
    any_space = pl.BlockSpec(memory_space=pl.ANY)
    near_space = pl.BlockSpec(memory_space=pltpu.VMEM)
    spare = 4 * groups + items_here * seq_size
    return pl.pallas_call(
        functools.partial(second_kernel, item_bits, seq_bits),
        in_specs=[pl.BlockSpec(memory_space=pltpu.SMEM)] + [near_space] * 4 + [any_space] * 2,
        out_specs=[any_space, near_space, any_space, any_space],
        out_shape=[
            jax.ShapeDtypeStruct((items_here, length // seq_size, features * seq_size), bf16),
            jax.ShapeDtypeStruct((items_here, heads_here, 1, length), f32),
            jax.ShapeDtypeStruct((groups,) + own_in.shape, bf16),
            jax.ShapeDtypeStruct((groups,) + own_out.shape, bf16),
        ],
        scratch_shapes=[
            pltpu.VMEM((items_here, length, features), bf16),
            pltpu.SemaphoreType.DMA((spare,)),
            pltpu.SemaphoreType.DMA((spare,)),
            pltpu.SemaphoreType.DMA((8,)),
        ],
        compiler_params=pltpu.CompilerParams(
            collective_id=1, has_side_effects=True, vmem_limit_bytes=48 * 2**20
        ),
        name="second",
    )(visible, onehots, tables, cosine, sine_part, own_in, own_out)


def leading(ref):
    return [index for index in np.ndindex(*ref.shape[:-2])]


def add_into(target, source):
    rows = target.shape[-2]
    for index in leading(target):

        @pl.loop(0, rows // 16)
        def _(order):
            place = index + (pl.ds(pl.multiple_of(order * 16, 16), 16),)
            total = target[place].astype(f32) + source[place].astype(f32)
            target[place] = total.astype(target.dtype)


def copy_into(target, source):
    @pl.loop(0, target.shape[0] // 16)
    def _(order):
        place = pl.ds(pl.multiple_of(order * 16, 16), 16)
        target[place] = source[place]


class Reduce:
    def __init__(self, copies, whole, rows, dims, steps, got, stage, stage_sems):
        self.copies, self.whole, self.rows = copies, whole, rows
        self.steps, self.got = steps, got
        self.place = dims.index(steps[0])
        self.stage, self.stage_sems = stage, stage_sems
        self.order = 0

    def first(self, bit, index=()):
        full = (slice(None),) * self.place
        if index:
            full = index[: self.place]
        rest = index[self.place :] if index else ()
        if index:
            return self.whole.at[full + (bit,) + rest + (self.rows,)]
        spare = len(self.whole.shape) - 3 - self.place
        return self.whole.at[full + (bit,) + (slice(None),) * spare + (self.rows,)]

    def start(self):
        step = self.steps[0]
        self.copy = self.copies.send(self.first(1 - my_bit(*step)), self.got[0], mask_of(step))

    def advance(self):
        step = self.steps[self.order]
        self.copy.wait_recv()
        if self.order == 0:
            self.kept = self.got[0]
            rows, columns = self.kept.shape[-2:]
            places = leading(self.kept)

            def load(order):
                return pltpu.make_async_copy(
                    self.first(my_bit(*step), places[order]),
                    self.stage.at[order % 2, pl.ds(0, rows), pl.ds(0, columns)],
                    self.stage_sems.at[order % 2],
                )

            load(0).start()
            for order, place in enumerate(places):
                if order + 1 < len(places):
                    load(order + 1).start()
                load(order).wait()
                add_into(
                    self.kept.at[place],
                    self.stage.at[order % 2, pl.ds(0, rows), pl.ds(0, columns)],
                )
        else:
            self.kept = self.kept.at[my_bit(*step)]
            add_into(self.kept, self.got[self.order])
        self.order += 1
        if self.order < len(self.steps):
            step = self.steps[self.order]
            self.copy = self.copies.send(
                self.kept.at[1 - my_bit(*step)], self.got[self.order], mask_of(step)
            )


def attend_back_unit(
    block,
    visible,
    onehot_ref,
    table_ref,
    cosine_ref,
    sine_ref,
    lse_ref,
    grad_ref,
    mixed_ref,
    sums_ref,
):
    cosine, sine_part = cosine_ref[...], sine_ref[...]
    query, key, value = head_parts(onehot_ref, table_ref, cosine, sine_part)
    key_turned = key.T
    length = query.shape[0]
    grad_key = jnp.zeros((length, HEAD), f32)
    grad_value = jnp.zeros((length, HEAD), f32)
    grad_query = []
    for offset in range(0, length, block):
        query_block = query[offset : offset + block]
        grad_block = grad_ref[offset : offset + block, :]
        scores = visible_scores(key, query_block, offset, visible)
        weights = jnp.exp2(scores * exponent_scale - lse_ref[:, offset : offset + block])
        grad_weights = contract_cols(value, grad_block)
        inner = jnp.sum(weights * grad_weights, axis=0, keepdims=True)
        grad_scores = (weights * (grad_weights - inner)).astype(bf16)
        grad_value = grad_value + dot(weights.astype(bf16), grad_block)
        grad_key = grad_key + dot(grad_scores, query_block)
        grad_query.append(dot(key_turned, grad_scores).T)
    grad_query = jnp.concatenate(grad_query, axis=0)

    def back(grad):
        return turn((grad * score_scale).astype(bf16).astype(f32), cosine, -sine_part).astype(bf16)

    mixed = jnp.concatenate([back(grad_query), back(grad_key), grad_value.astype(bf16)], axis=1)
    mixed_ref[...] = mixed.reshape(mixed_ref.shape)
    sums_ref[...] += dot(onehot_ref[...].T, mixed)


def third_kernel(
    item_bits,
    seq_bits,
    visible_ref,
    onehot_ref,
    table_ref,
    cosine_ref,
    sine_ref,
    lse_ref,
    slice_ref,
    grad_ref,
    in_ref,
    out_ref,
    dense_ref,
    bias_ref,
    spread_ref,
    sums_all_ref,
    in_part_ref,
    out_part_ref,
    dense_part_ref,
    bias_sum_ref,
    mixed_scr,
    other_scr,
    kept_scr,
    step_scrs,
    sums_scr,
    sums_got,
    bias_scr,
    bias_got,
    in_got,
    out_got,
    dense_got,
    in_final,
    out_final,
    stage_scr,
    stage_sems,
    send_sems,
    recv_sems,
    local_sems,
):
    seq_size = 2 ** len(seq_bits)
    items_here, length, features = grad_ref.shape
    heads_here = features // HEAD
    seq_place = lax.axis_index("seq")
    member = seq_place % 4
    outer_bits = seq_bits[2:]
    width = slice_ref.shape[1]
    greet(partners(seq_size, item_bits))
    copies = Copies(send_sems, recv_sems, local_sems)
    dims = item_bits[::-1] + outer_bits[::-1]

    def reducers(whole, got):
        rows = whole.shape[-2]
        if len(item_bits) == 2:
            one, two = item_bits
            ways = [
                (pl.ds(0, rows // 2), [two, one] + outer_bits[::-1]),
                (pl.ds(rows // 2, rows // 2), [one, two] + outer_bits[::-1]),
            ]
        else:
            ways = [(pl.ds(0, rows), dims)]
        return [
            Reduce(copies, whole, part, dims, steps, list(got[order]), stage_scr, stage_sems)
            for order, (part, steps) in enumerate(ways)
        ]

    in_sums = reducers(in_ref, in_got)
    out_sums = reducers(out_ref, out_got)
    dense_steps = item_bits[::-1] + seq_bits[:0:-1]
    dense_sum = Reduce(
        copies,
        dense_ref,
        pl.ds(0, dense_ref.shape[-2]),
        dense_steps,
        dense_steps,
        list(dense_got),
        stage_scr,
        stage_sems,
    )
    for one in in_sums:
        one.start()
    sums_scr[...] = jnp.zeros_like(sums_scr)
    tile = 256
    flying = {}
    for stage in range(items_here + len(seq_bits)):
        if stage < items_here:

            @pl.loop(0, heads_here)
            def _(head):
                place = pl.ds(pl.multiple_of(head * HEAD, HEAD), HEAD)
                packed = pl.ds(pl.multiple_of(head * 3 * HEAD, HEAD), 3 * HEAD)
                attend_back_unit(
                    min(256, length),
                    visible_ref[stage],
                    onehot_ref.at[stage],
                    table_ref.at[head],
                    cosine_ref,
                    sine_ref,
                    lse_ref.at[stage, head],
                    grad_ref.at[stage, :, place],
                    mixed_scr.at[:, :, :, packed],
                    sums_scr.at[0, head],
                )

        for order in range(len(seq_bits) - 1, -1, -1):
            item = stage - 1 - order
            if not 0 <= item < items_here:
                continue
            copy, kept = flying[item]
            copy.wait_recv()
            got = step_scrs[order].at[item % 2]
            if order:
                full = (slice(None),) * (len(kept.shape) - 3)
                kept = kept.at[full + (my_bit(*seq_bits[order]),)]
            if order + 1 < len(seq_bits):
                add_into(kept, got)
                step = seq_bits[order + 1]
                full = (slice(None),) * (len(kept.shape) - 3)
                copy = copies.send(
                    kept.at[full + (1 - my_bit(*step),)],
                    step_scrs[order + 1].at[item % 2],
                    mask_of(step),
                )
                flying[item] = copy, kept
                flying["later", item].append(copy)
            else:

                @pl.loop(0, kept.shape[0] // 16)
                def _(block):
                    place = (pl.ds(pl.multiple_of(block * 16, 16), 16),)
                    total = kept[place].astype(f32) + got[place].astype(f32)
                    spread_ref[(item,) + place] = total.astype(bf16)

        if stage < items_here:
            core = my_bit(*seq_bits[0])
            slot = stage % 2
            if stage >= 2:
                copies.sent_now(flying["first", stage - 2])
            kept_slot = stage % len(seq_bits)
            if stage >= len(seq_bits):
                for copy in flying["later", stage - len(seq_bits)]:
                    copies.sent_now(copy)
            half = mixed_scr.shape[0] * mixed_scr.shape[2]
            other = mixed_scr[:, 1 - core].reshape(half, -1)
            mine = mixed_scr[:, core].reshape(half, -1)

            @pl.loop(0, width // tile)
            def _(order):
                place = pl.ds(pl.multiple_of(order * tile, tile), tile)
                weights = slice_ref[:, place]
                target = other_scr.at[slot]
                target[..., place] = dot(other, weights).astype(bf16).reshape(
                    target.shape[:-1] + (tile,)
                )
                target = kept_scr.at[kept_slot]
                target[..., place] = dot(mine, weights).astype(bf16).reshape(
                    target.shape[:-1] + (tile,)
                )

            copy = copies.send(
                other_scr.at[slot], step_scrs[0].at[slot], mask_of(seq_bits[0])
            )
            flying[stage] = copy, kept_scr.at[kept_slot]
            flying["first", stage] = copy
            flying["later", stage] = []
        if stage == 0:
            for one in out_sums:
                one.start()
        if stage == 2:
            dense_sum.start()
        if stage == items_here:
            for one in in_sums:
                one.advance()

    for one in out_sums:
        one.advance()
    for order, step in enumerate(item_bits):
        copy = copies.send(sums_scr.at[order], sums_got.at[order], mask_of(step))
        copy.wait_recv()
        sums_scr[order + 1] = sums_scr[order] + sums_got[order]
    sums_all_ref[seq_place] = sums_scr[len(item_bits)].astype(bf16)
    for one in in_sums + out_sums:
        one.advance()
    known = [0]
    for axis, bit in seq_bits[::-1]:
        arrivals = []
        for mask in known:
            part = sums_all_ref.at[seq_place ^ mask]
            arrivals.append(copies.send(part, part, (0, bit)))
        if bit == seq_bits[-1][1]:
            dense_sum.advance()
        wait_all(arrivals)
        known = known + [mask ^ bit for mask in known]
    bias_scr[0] = bias_ref[...]
    for order, step in enumerate(seq_bits + item_bits):
        copy = copies.send(bias_scr.at[order], bias_got.at[order], mask_of(step))
        copy.wait_recv()
        bias_scr[order + 1] = bias_scr[order] + bias_got[order]
    bias_sum_ref[...] = bias_scr[len(seq_bits) + len(item_bits)]

    while in_sums[0].order < len(dims):
        for one in in_sums + out_sums:
            one.advance()
        if dense_sum.order < len(dense_steps):
            dense_sum.advance()
    shares, local = [], []
    for sums, final, target in (
        (in_sums, in_final, in_part_ref),
        (out_sums, out_final, out_part_ref),
    ):
        rows = target.shape[1]
        first = 0
        for one in sums:
            copy_into(final.at[pl.ds(first, one.kept.shape[0])], one.kept)
            first += one.kept.shape[0]
        for mask in range(4):
            source = final.at[pl.ds(pl.multiple_of((member ^ mask) * rows, 16), rows)]
            if mask:
                shares.append(copies.send(source, target.at[member], (0, mask)))
            else:
                local.append(copies.move(source, target.at[member]))
    while dense_sum.order < len(dense_steps):
        dense_sum.advance()
    dense_part_ref[...] = dense_sum.kept[...]
    wait_all(shares)
    for copy in local:
        copy.wait()
    copies.end()


def third_call(
    item_bits,
    seq_bits,
    visible,
    onehots,
    tables,
    cosine,
    sine_part,
    log_sums,
    w_slice,
    grad_context,
    grad_in,
    grad_out,
    by_rows,
    in_sum,
):
    items_here, length, vocab = onehots.shape
    heads_here = tables.shape[0]
    seq_size = 2 ** len(seq_bits)
    span = length // seq_size
    width = w_slice.shape[1]
    packed = heads_here * 3 * HEAD
    outer = len(seq_bits) - 2
    levels = len(item_bits) + outer
    any_space = pl.BlockSpec(memory_space=pl.ANY)
    near_space = pl.BlockSpec(memory_space=pltpu.VMEM)

    def got_shapes(whole, ways, depth):
        rows, columns = whole.shape[-2:]
        one = tuple(
            pltpu.VMEM((2,) * order + (rows // ways, columns), bf16)
            for order in range(depth - 1, -1, -1)
        )
        return one

    ways = 2 if len(item_bits) == 2 else 1
    group_rows = grad_in.shape[-2]
    rows = group_rows // 4
    dense_depth = len(item_bits) + len(seq_bits) - 1
    spread = (2,) * (len(seq_bits) - 1) + (span, width)
    all_bits = len(item_bits) + len(seq_bits)
    spare = 8 * items_here + 8 * levels + 16 * all_bits
    stage_rows = max(group_rows // ways, by_rows.shape[-2])
    return pl.pallas_call(
        functools.partial(third_kernel, item_bits, seq_bits),
        in_specs=[pl.BlockSpec(memory_space=pltpu.SMEM)]
        + [near_space] * 7
        + [any_space] * 3
        + [near_space],
        out_specs=[near_space, near_space, any_space, any_space, near_space, near_space],
        out_shape=[
            jax.ShapeDtypeStruct((items_here, span, width), bf16),
            jax.ShapeDtypeStruct((seq_size, heads_here, vocab, 3 * HEAD), bf16),
            jax.ShapeDtypeStruct((4, rows, grad_in.shape[-1]), bf16),
            jax.ShapeDtypeStruct((4, rows, grad_out.shape[-1]), bf16),
            jax.ShapeDtypeStruct(by_rows.shape[-2:], bf16),
            jax.ShapeDtypeStruct(in_sum.shape, f32),
        ],
        scratch_shapes=[
            pltpu.VMEM((seq_size // 2, 2, span, packed), bf16),
            pltpu.VMEM((2,) + spread, bf16),
            pltpu.VMEM((len(seq_bits),) + spread, bf16),
            tuple(pltpu.VMEM((2,) + spread[order:], bf16) for order in range(len(seq_bits))),
            pltpu.VMEM((len(item_bits) + 1, heads_here, vocab, 3 * HEAD), f32),
            pltpu.VMEM((len(item_bits), heads_here, vocab, 3 * HEAD), f32),
            pltpu.VMEM((all_bits + 1,) + in_sum.shape, f32),
            pltpu.VMEM((all_bits,) + in_sum.shape, f32),
            tuple(got_shapes(grad_in, ways, levels) for _ in range(ways)),
            tuple(got_shapes(grad_out, ways, levels) for _ in range(ways)),
            got_shapes(by_rows, 1, dense_depth),
            pltpu.VMEM((group_rows, grad_in.shape[-1]), bf16),
            pltpu.VMEM((group_rows, grad_out.shape[-1]), bf16),
            pltpu.VMEM((2, stage_rows, grad_in.shape[-1]), bf16),
            pltpu.SemaphoreType.DMA((2,)),
            pltpu.SemaphoreType.DMA((spare,)),
            pltpu.SemaphoreType.DMA((spare,)),
            pltpu.SemaphoreType.DMA((8,)),
        ],
        compiler_params=pltpu.CompilerParams(
            collective_id=2, has_side_effects=True, vmem_limit_bytes=60 * 2**20
        ),
        name="third",
    )(
        visible,
        onehots,
        tables,
        cosine,
        sine_part,
        log_sums,
        w_slice,
        grad_context,
        grad_in,
        grad_out,
        by_rows,
        in_sum,
    )


def norm_forward(residual, gain_vec, bias_vec):
    center = residual - jnp.mean(residual, axis=-1, keepdims=True)
    inverse = lax.rsqrt(jnp.mean(center * center, axis=-1, keepdims=True) + epsilon)
    normed = center * inverse
    return (normed * gain_vec + bias_vec, normed, inverse)


def norm_backward(grad_out, normed, inverse, gain_vec):
    scaled = grad_out * gain_vec
    grad_in = inverse * (
        scaled
        - jnp.mean(scaled, axis=-1, keepdims=True)
        - normed * jnp.mean(scaled * normed, axis=-1, keepdims=True)
    )
    return (grad_in, jnp.sum(grad_out * normed, axis=0), jnp.sum(grad_out, axis=0))


def on_device(
    token_ids,
    masked,
    item_flag,
    prefix,
    cotangent,
    embedding,
    heads_weight,
    heads_bias,
    dense_weight,
    dense_bias,
    first_gain,
    first_bias,
    up_weight,
    up_bias,
    down_weight,
    down_bias,
    second_gain,
    second_bias,
):
    lines = Lines()
    items_here, span = token_ids.shape
    items_size, seq_size = lax.axis_size("items"), lax.axis_size("seq")
    item_place, seq_place = lax.axis_index("items"), lax.axis_index("seq")
    count = items_size * seq_size
    length = span * seq_size
    width = embedding.shape[0] * count
    vocab = embedding.shape[1]
    heads_here = HEADS // seq_size
    packed_width = heads_here * 3 * HEAD
    rows_here = up_weight.shape[0]
    ff_width = down_weight.shape[0]
    members = 4
    groups = count // members
    member = seq_place % members
    ff_part = -(-ff_width // (members * 128)) * 128
    ff_all = members * ff_part

    item_bits, seq_bits = bits_of("items"), bits_of("seq")
    outer_bits = seq_bits[2:]

    input_ids = jnp.where(masked == 1, mask_token, token_ids)
    flat_place = item_place * seq_size + seq_place
    row_count = rows_here + 16
    bias_row = lax.dynamic_update_slice(
        jnp.zeros((16, heads_weight.shape[1]), bf16),
        heads_bias[None],
        (0, flat_place * heads_bias.shape[0]),
    )
    ones_row = jnp.zeros((16, vocab), bf16).at[0].set(1.0)
    small = [
        embedding.reshape(-1),
        ones_row.reshape(-1),
        input_ids.astype(bf16).reshape(-1),
        dense_bias,
        first_gain,
        first_bias,
        down_bias,
        second_gain,
        second_bias,
    ]
    ends = [0]
    for part in small:
        ends.append(ends[-1] + part.shape[0])
    flat = jnp.concatenate(small)
    flat = jnp.pad(flat, (0, -flat.shape[0] % 2048)).reshape(-1, 128)

    def by_member(part):
        padded = jnp.pad(part, ((0, 0), (0, ff_all - ff_width)))
        return jnp.transpose(padded.reshape(rows_here, 2, 2, ff_part), (1, 2, 0, 3))

    parts_in = jnp.concatenate(
        [by_member(up_weight[:, :ff_width]), by_member(up_weight[:, ff_width:])], axis=3
    )
    parts_out = by_member(down_weight.T)
    everyone, mixed_table, w_block, w_dense, own_in, own_out = first_call(
        item_bits,
        seq_bits,
        flat,
        jnp.concatenate([heads_weight, bias_row], axis=0),
        dense_weight,
        parts_in,
        parts_out,
    )
    w_dense = w_dense.reshape(width, width)
    w_block = w_block[:, :rows_here].reshape(seq_size * rows_here, packed_width)
    everyone = everyone.reshape(count, -1)
    pieces = [everyone[:, a:b] for a, b in zip(ends[:-1], ends[1:])]
    table = pieces[0].reshape(width, vocab)
    b_dense, gain_one, shift_one, b_down, gain_two, shift_two = (
        part.reshape(-1).astype(f32) for part in pieces[3:]
    )
    ids_here = pick(pieces[2].reshape(items_size, seq_size, items_here, span), item_place, 0)
    ids_here = jnp.transpose(ids_here, (1, 0, 2)).reshape(items_here, length).astype(jnp.int32)
    in_bias = jnp.pad(
        up_bias.astype(f32).reshape(2, ff_width), ((0, 0), (0, ff_all - ff_width))
    )
    in_bias = lax.dynamic_slice(in_bias, (0, member * ff_part), (2, ff_part)).reshape(-1)

    vocab_index = jnp.arange(vocab, dtype=jnp.int32)
    positions = jnp.arange(length, dtype=f32)
    frequency = jnp.exp(jnp.arange(HEAD // 2, dtype=f32) * (-2.0 * math.log(10000.0) / HEAD))
    angles = positions[:, None] * frequency[None, :]
    cosine = jnp.cos(angles)
    sine_part = jnp.sin(angles)
    cosine = jnp.concatenate([cosine, cosine], axis=1)
    sine_part = jnp.concatenate([-sine_part, sine_part], axis=1)
    visible = jnp.where(item_flag == 1, length, prefix)
    tables = table_halves(mixed_table)
    onehots = (ids_here[:, :, None] == vocab_index).astype(bf16)
    halves = 2 if items_here % 2 == 0 else 1
    per_half = items_here // halves
    chosen = [slice(half * per_half, (half + 1) * per_half) for half in range(halves)]
    context_rows, log_sums, w_in, w_out = second_call(
        item_bits, seq_bits, visible, onehots, tables, cosine, sine_part, own_in, own_out
    )
    w_in = w_in.reshape(width, 2 * ff_part)
    w_out = w_out.reshape(width, ff_part)
    contexts = [context_rows[part].reshape(per_half * span, width) for part in chosen]

    kept = []
    for half, part in enumerate(chosen):
        own_ids = input_ids[part].reshape(-1)
        onehot = (own_ids[:, None] == vocab_index[None, :]).astype(bf16)
        inputs = contract_cols(onehot, table)
        branch = dot(contexts[half], w_dense) + b_dense
        hidden, normed_one, inverse_one = norm_forward(
            deep_alpha * inputs + branch, gain_one, shift_one
        )
        kept.append(
            dict(
                onehot=onehot,
                hidden=hidden,
                normed_one=normed_one,
                inverse_one=inverse_one,
                shared=gather_four(lines, hidden.astype(bf16)),
            )
        )
    for half, part in enumerate(chosen):
        one = kept[half]
        gate_up = dot(one["shared"], w_in) + in_bias
        up_part, gate = gate_up[:, :ff_part], gate_up[:, ff_part:]
        below = 0.5 * (1.0 + lax.erf(gate * (0.5**0.5)))
        activated = gate * below
        slope = below + gate * jnp.exp(-0.5 * gate * gate) * (1.0 / math.sqrt(2.0 * math.pi))
        product_low = (up_part * activated).astype(bf16)
        one["act"] = activated.astype(bf16)
        one["slope"] = (up_part * slope).astype(bf16)
        one["product"] = product_low
        mlp_branch = sum_four(lines, contract_cols(product_low, w_out).astype(bf16)) + b_down
        layer_out, normed_two, inverse_two = norm_forward(
            deep_alpha * one["hidden"] + mlp_branch, gain_two, shift_two
        )
        one["layer_out"] = layer_out.astype(bf16)
        grad_top = cotangent[part].reshape(per_half * span, width).astype(f32)
        grad_resid_two, one["gain_two"], one["shift_two"] = norm_backward(
            grad_top, normed_two, inverse_two, gain_two
        )
        grad_mlp_low = grad_resid_two.astype(bf16)
        one["grad_resid_two"] = grad_resid_two
        one["down_sum"] = jnp.sum(grad_mlp_low.astype(f32), axis=0)
        one["grad_shared"] = gather_four(lines, grad_mlp_low)

    def total(function):
        result = function(kept[0])
        for one in kept[1:]:
            result = result + function(one)
        return result

    for one in kept:
        grad_product = dot(one["grad_shared"], w_out)
        one["grad_in"] = jnp.concatenate(
            [
                grad_product * one["act"].astype(f32),
                grad_product * one["slope"].astype(f32),
            ],
            axis=1,
        ).astype(bf16)
        one["in_sum"] = jnp.sum(one["grad_in"].astype(f32), axis=0)
        grad_hidden = (
            sum_four(lines, contract_cols(one["grad_in"], w_in).astype(bf16))
            + deep_alpha * one["grad_resid_two"]
        )
        grad_resid_one, one["gain_one"], one["shift_one"] = norm_backward(
            grad_hidden, one["normed_one"], one["inverse_one"], gain_one
        )
        grad_branch_low = grad_resid_one.astype(bf16)
        one["grad_branch"] = grad_branch_low
        one["grad_resid_one"] = grad_resid_one
        one["branch_sum"] = jnp.sum(grad_branch_low.astype(f32), axis=0)
        grad_context = contract_cols(grad_branch_low, w_dense).astype(bf16)
        grad_context = lax.all_to_all(
            jnp.transpose(
                grad_context.reshape(per_half, span, seq_size, heads_here * HEAD), (0, 2, 1, 3)
            ),
            "seq",
            split_axis=1,
            concat_axis=1,
            tiled=True,
        )
        one["grad_context"] = grad_context.reshape(per_half, length, heads_here * HEAD)

    vectors = jnp.stack(
        [
            total(lambda one: one[name])
            for name in ("gain_one", "shift_one", "branch_sum", "gain_two", "shift_two", "down_sum")
        ],
        axis=1,
    )
    token_sum = total(
        lambda one: lax.dot_general(
            one["grad_resid_one"],
            one["onehot"].astype(f32),
            (((0,), (0,)), ((), ())),
            precision=lax.Precision.HIGHEST,
            preferred_element_type=f32,
        )
    )
    grad_dense = sum(
        contract_rows(contexts[half], one["grad_branch"]) for half, one in enumerate(kept)
    )
    by_rows = jnp.concatenate(
        [grad_dense, token_sum, jnp.pad(vectors, ((0, 0), (0, 128 - vectors.shape[1])))], axis=1
    ).astype(bf16)
    row_dims = item_bits[::-1] + seq_bits[::-1]
    by_rows = by_rows.reshape((2,) * len(row_dims) + (rows_here, -1))
    by_rows = halve(lines, by_rows, len(row_dims) - 1, *seq_bits[0])
    grad_out_weight = total(lambda one: contract_rows(one["grad_shared"], one["product"]))
    grad_in_weight = total(lambda one: contract_rows(one["shared"], one["grad_in"]))
    group_dims = (2,) * (len(item_bits) + len(outer_bits)) + (members * rows_here, -1)
    in_sum = total(lambda one: one["in_sum"]).reshape(2, ff_part)
    in_all = lax.dynamic_update_slice(
        jnp.zeros((2, ff_all), f32), in_sum, (0, member * ff_part)
    ).reshape(-1, 128)
    w_slice = gather_merge(lines, w_block[None], item_bits).reshape(width, packed_width)
    spread, token_all, in_part, out_part, by_rows, in_all = third_call(
        item_bits,
        seq_bits,
        visible,
        onehots,
        tables,
        cosine,
        sine_part,
        log_sums,
        w_slice.T,
        jnp.concatenate([one["grad_context"] for one in kept], axis=0),
        grad_in_weight.astype(bf16).reshape(group_dims),
        grad_out_weight.astype(bf16).reshape(group_dims),
        by_rows,
        in_all,
    )
    grad_resid_one = jnp.concatenate([one["grad_resid_one"] for one in kept], axis=0)
    input_grads = spread.astype(f32) + deep_alpha * grad_resid_one.reshape(spread.shape)
    token_all = jnp.transpose(token_all, (2, 0, 1, 3)).reshape(vocab, -1)

    def from_members(part):
        taken = jnp.transpose(part, (1, 0, 2)).reshape(rows_here, ff_all)
        return taken[:, :ff_width].astype(f32)

    grad_up = from_members(in_part[..., :ff_part])
    grad_gate = from_members(in_part[..., ff_part:])
    grad_down = from_members(out_part)
    by_rows = by_rows.astype(f32)
    grad_dense = by_rows[:, :width]
    token_sum = by_rows[:, width : width + vocab]
    own_vectors = by_rows[:, width + vocab :].T
    in_all = in_all.reshape(2, ff_all)
    grad_up_bias = in_all[:, :ff_width].reshape(-1)

    grad_heads = dot(embedding, token_all)
    grad_heads_bias = lax.dynamic_slice_in_dim(
        jnp.sum(token_all.astype(f32), axis=0),
        (item_place * seq_size + seq_place) * heads_bias.shape[0],
        heads_bias.shape[0],
        0,
    )
    embed_grad = 0.1 * (contract_cols(heads_weight, token_all) + deep_alpha * token_sum)
    return (
        jnp.concatenate([one["layer_out"] for one in kept], axis=0).reshape(
            items_here, span, width
        ),
        input_grads,
        embed_grad,
        grad_heads,
        grad_heads_bias,
        grad_dense,
        own_vectors[2],
        own_vectors[0],
        own_vectors[1],
        jnp.concatenate([grad_up, grad_gate], axis=1),
        grad_up_bias,
        grad_down.T,
        own_vectors[5],
        own_vectors[3],
        own_vectors[4],
    )


def solution(mesh):
    in_specs = (
        P("items", "seq"),
        P("items", "seq"),
        P("items"),
        P("items"),
        P("items", "seq", None),
        P(("items", "seq"), None),
        P(("items", "seq"), None),
        P(("items", "seq")),
        P(("items", "seq"), None),
        P(("items", "seq")),
        P(("items", "seq")),
        P(("items", "seq")),
        P(("items", "seq"), None),
        P(),
        P(None, ("items", "seq")),
        P(("items", "seq")),
        P(("items", "seq")),
        P(("items", "seq")),
    )
    out_specs = (
        P("items", "seq", None),
        P("items", "seq", None),
        P(("items", "seq"), None),
        P(("items", "seq"), None),
        P(("items", "seq")),
        P(("items", "seq"), None),
        P(("items", "seq")),
        P(("items", "seq")),
        P(("items", "seq")),
        P(("items", "seq"), None),
        P(),
        P(None, ("items", "seq")),
        P(("items", "seq")),
        P(("items", "seq")),
        P(("items", "seq")),
    )
    return jax.shard_map(
        on_device, mesh=mesh, in_specs=in_specs, out_specs=out_specs, check_vma=False
    )
```

```python
import functools
import math

import jax
import jax.numpy as jnp
import numpy as np
from jax import lax
from jax.experimental import pallas as pl
from jax.experimental.pallas import tpu as pltpu
from jax.sharding import PartitionSpec as P

HEADS = 16
HEAD = 128


deep_alpha = math.sqrt(48.0)
epsilon = 1e-05
mask_token = 3
both = ("items", "seq")
bf16 = jnp.bfloat16
f32 = jnp.float32
score_scale = HEAD ** (-0.5)
exponent_scale = score_scale * math.log2(math.e)


class Lines:
    def __init__(self):
        self.last = {}

    def swap(self, part, axis, bit):
        if (axis, bit) in self.last:
            part, _ = lax.optimization_barrier((part, self.last[axis, bit]))
        size = lax.axis_size(axis)
        got = lax.ppermute(part, axis, [(j, j ^ bit) for j in range(size)])
        self.last[axis, bit] = got
        return got


def bits_of(axis):
    found = []
    bit = 1
    while bit < lax.axis_size(axis):
        found.append((axis, bit))
        bit *= 2
    return found


def my_bit(axis, bit):
    return (lax.axis_index(axis) // bit) % 2


def in_order(own, got, place, dim):
    return jnp.where(
        place == 0, jnp.concatenate([own, got], axis=dim), jnp.concatenate([got, own], axis=dim)
    )


def pick(whole, place, dim):
    return lax.dynamic_index_in_dim(whole, place, dim, keepdims=False)


def gather_merge(lines, own, steps):
    for axis, bit in steps:
        own = in_order(own, lines.swap(own, axis, bit), my_bit(axis, bit), 0)
    return own


def halve(lines, whole, dim, axis, bit):
    place = my_bit(axis, bit)
    mine = pick(whole, place, dim)
    got = lines.swap(pick(whole, 1 - place, dim), axis, bit)
    return (mine.astype(f32) + got.astype(f32)).astype(whole.dtype)


def moved(masks, axis, bit):
    return (masks[0] ^ (bit if axis == "items" else 0), masks[1] ^ (bit if axis == "seq" else 0))


def contract_rows(left, right):
    return lax.dot_general(left, right, (((0,), (0,)), ((), ())), preferred_element_type=f32)


def contract_cols(left, right):
    return lax.dot_general(left, right, (((1,), (1,)), ((), ())), preferred_element_type=f32)


def dot(left, right):
    return jnp.dot(left, right, preferred_element_type=f32)


def turn(values, cosine, sine_part):
    return values * cosine + pltpu.roll(values, HEAD // 2, 1) * sine_part


def head_parts(onehot_ref, table_ref, cosine, sine_part):
    onehot = onehot_ref[...]
    mixed = dot(jnp.concatenate([onehot, onehot], axis=1), table_ref[...])
    query = turn(mixed[:, :HEAD], cosine, sine_part).astype(bf16)
    key = turn(mixed[:, HEAD : 2 * HEAD], cosine, sine_part).astype(bf16)
    return query, key, mixed[:, 2 * HEAD :].astype(bf16)


def visible_scores(key, query, offset, visible):
    scores = contract_cols(key, query)
    place = offset + lax.broadcasted_iota(jnp.int32, (1, query.shape[0]), 1)
    seen = lax.broadcasted_iota(jnp.int32, scores.shape, 0) < jnp.maximum(place + 1, visible)
    return jnp.where(seen, scores, -1e30)


def table_halves(mixed_table):
    vocab = mixed_table.shape[0]
    by_head = jnp.transpose(mixed_table.reshape(vocab, -1, 3 * HEAD), (1, 0, 2))
    high = lax.reduce_precision(by_head, 8, 7)
    return jnp.concatenate([high.astype(bf16), (by_head - high).astype(bf16)], axis=1)


def norm_rows(rows):
    center = rows - jnp.mean(rows, axis=-1, keepdims=True)
    inverse = lax.rsqrt(jnp.mean(center * center, axis=-1, keepdims=True) + epsilon)
    return center * inverse, inverse


def norm_rows_back(grad, normed, inverse, gain):
    scaled = grad * gain
    return inverse * (
        scaled
        - jnp.mean(scaled, axis=-1, keepdims=True)
        - normed * jnp.mean(scaled * normed, axis=-1, keepdims=True)
    )


MESH = pl.DeviceIdType.MESH


class Copies:
    def __init__(self, send_sems, recv_sems, local_sems):
        self.sems = send_sems, recv_sems, local_sems
        self.sent = {}
        self.moved = 0
        self.count = 0
        self.here = lax.axis_index("items"), lax.axis_index("seq")

    def send(self, source, target, masks):
        order = self.count
        self.count += 1
        copy = pltpu.make_async_remote_copy(
            src_ref=source,
            dst_ref=target,
            send_sem=self.sems[0].at[order],
            recv_sem=self.sems[1].at[order],
            device_id=(self.here[0] ^ masks[0], self.here[1] ^ masks[1]),
            device_id_type=MESH,
        )
        copy.start()
        self.sent[id(copy)] = copy
        return copy

    def move(self, source, target):
        copy = pltpu.make_async_copy(source, target, self.sems[2].at[self.moved])
        self.moved += 1
        copy.start()
        return copy

    def sent_now(self, copy):
        self.sent.pop(id(copy)).wait_send()

    def end(self):
        for copy in self.sent.values():
            copy.wait_send()


def wait_all(copies):
    for copy in copies:
        copy.wait_recv()


def mask_of(step):
    return moved((0, 0), *step)


def greet(masks):
    barrier = pltpu.get_barrier_semaphore()
    here = lax.axis_index("items"), lax.axis_index("seq")
    for mask_i, mask_s in masks:
        pl.semaphore_signal(
            barrier,
            inc=1,
            device_id=(here[0] ^ mask_i, here[1] ^ mask_s),
            device_id_type=MESH,
        )
    pl.semaphore_wait(barrier, len(masks))


def partners(seq_size, item_bits):
    return [(0, mask) for mask in range(1, seq_size)] + [mask_of(step) for step in item_bits]


def aligned(place, size):
    return pl.ds(place // size * size, size)


def first_kernel(
    item_bits,
    seq_bits,
    row_count,
    small_ref,
    heads_ref,
    dense_ref,
    in_ref,
    out_ref,
    everyone_ref,
    table_ref,
    block_ref,
    dense_all_ref,
    own_in_ref,
    own_out_ref,
    embed_scr,
    block_scr,
    sum_scr,
    got_scr,
    send_sems,
    recv_sems,
    local_sems,
):
    items_size, seq_size = everyone_ref.shape[:2]
    item_place, seq_place = lax.axis_index("items"), lax.axis_index("seq")
    core, chip = seq_place % 2, seq_place // 2
    member = seq_place % 4
    rows = dense_ref.shape[0]
    columns = block_scr.shape[2]
    greet(partners(seq_size, item_bits))
    copies = Copies(send_sems, recv_sems, local_sems)

    def head_columns(place):
        return heads_ref.at[:, pl.ds(pl.multiple_of(place * columns, 128), columns)]

    small = [copies.send(small_ref, everyone_ref.at[item_place, seq_place], mask_of(seq_bits[0]))]
    heads = [
        copies.send(head_columns(seq_place ^ mask), block_scr.at[seq_place], (0, mask))
        for mask in range(1, seq_size)
    ]
    dense = [
        copies.send(dense_ref, dense_all_ref.at[item_place, chip, core], mask_of(seq_bits[1]))
    ]
    shares = []
    for source, target in ((in_ref, own_in_ref), (out_ref, own_out_ref)):
        mine = pl.ds(pl.multiple_of(member * rows, rows), rows)
        for mask in range(1, 4):
            other = member ^ mask
            shares.append(
                copies.send(source.at[other // 2, other % 2], target.at[mine], (0, mask))
            )
    local = [
        copies.move(small_ref, everyone_ref.at[item_place, seq_place]),
        copies.move(dense_ref, dense_all_ref.at[item_place, chip, core]),
        copies.move(head_columns(seq_place), block_scr.at[seq_place]),
        copies.move(in_ref.at[member // 2, core], own_in_ref.at[mine]),
        copies.move(out_ref.at[member // 2, core], own_out_ref.at[mine]),
    ]
    for copy in local:
        copy.wait()

    for order in range(1, len(seq_bits)):
        wait_all(small[-1:])
        part = everyone_ref.at[item_place, aligned(seq_place, 2**order)]
        small.append(copies.send(part, part, mask_of(seq_bits[order])))
        if order > 1:
            wait_all(dense[-1:])
            part = dense_all_ref.at[item_place, aligned(chip, 2 ** (order - 1)), core]
            dense.append(copies.send(part, part, mask_of(seq_bits[order])))
    wait_all(small[-1:])
    embed = copies.move(everyone_ref.at[item_place, :, pl.ds(0, row_count)], embed_scr)
    part = everyone_ref.at[item_place]
    small.append(copies.send(part, part, mask_of(item_bits[0])))
    wait_all(dense[-1:])

    def dense_part(mask):
        return dense_all_ref.at[item_place ^ mask, :, core]

    known = [0]
    waves = []
    for step in item_bits[::-1]:
        waves.append([(mask, step) for mask in known])
        known = known + [mask ^ step[1] for mask in known]
    arrived = {}
    for wave in waves:
        part = dense_part(0)
        arrived[wave[0][1][1]] = copies.send(part, part, mask_of(wave[0][1]))
    near = [copies.send(dense_part(0), dense_part(0), mask_of(seq_bits[0]))]

    wait_all(heads)
    embed.wait()
    sum_scr[0] = lax.dot_general(
        embed_scr[...].reshape(seq_size * row_count, -1),
        block_scr[...].reshape(seq_size * row_count, columns),
        (((0,), (0,)), ((), ())),
        preferred_element_type=f32,
    )
    block_out = copies.move(block_scr, block_ref)
    for order, step in enumerate(item_bits):
        one = copies.send(sum_scr.at[order], got_scr.at[order], mask_of(step))
        if order + 1 < len(item_bits):
            wait_all(small[-1:])
            part = everyone_ref.at[aligned(item_place, 2 ** (order + 1))]
            small.append(copies.send(part, part, mask_of(item_bits[order + 1])))
        one.wait_recv()
        sum_scr[order + 1] = sum_scr[order] + got_scr[order]
    table_ref[...] = sum_scr[len(item_bits)]

    for wave in waves:
        for mask, step in wave:
            if mask:
                part = dense_part(mask)
                arrived[mask ^ step[1]] = copies.send(part, part, mask_of(step))
        for mask, step in wave:
            arrived[mask ^ step[1]].wait_recv()
            part = dense_part(mask ^ step[1])
            near.append(copies.send(part, part, mask_of(seq_bits[0])))
    wait_all(near)
    wait_all(shares)
    wait_all(small[-1:])
    block_out.wait()
    copies.end()


def first_call(item_bits, seq_bits, small, heads, dense, parts_in, parts_out):
    items_size, seq_size = 2 ** len(item_bits), 2 ** len(seq_bits)
    row_count = heads.shape[0]
    rows, width = dense.shape
    vocab = small.shape[1]
    columns = heads.shape[1] // seq_size
    any_space = pl.BlockSpec(memory_space=pl.ANY)
    spare = 8 * (len(item_bits) + len(seq_bits)) + 2 * seq_size + 2 ** (len(item_bits) + 1)
    return pl.pallas_call(
        functools.partial(first_kernel, item_bits, seq_bits, row_count),
        in_specs=[any_space] * 5,
        out_specs=[any_space, pl.BlockSpec(memory_space=pltpu.VMEM)] + [any_space] * 4,
        out_shape=[
            jax.ShapeDtypeStruct((items_size, seq_size) + small.shape, bf16),
            jax.ShapeDtypeStruct((vocab, columns), f32),
            jax.ShapeDtypeStruct((seq_size, row_count, columns), bf16),
            jax.ShapeDtypeStruct((items_size, seq_size // 2, 2, rows, width), bf16),
            jax.ShapeDtypeStruct((4 * rows, parts_in.shape[3]), bf16),
            jax.ShapeDtypeStruct((4 * rows, parts_out.shape[3]), bf16),
        ],
        scratch_shapes=[
            pltpu.VMEM((seq_size, row_count, vocab), bf16),
            pltpu.VMEM((seq_size, row_count, columns), bf16),
            pltpu.VMEM((len(item_bits) + 1, vocab, columns), f32),
            pltpu.VMEM((len(item_bits), vocab, columns), f32),
            pltpu.SemaphoreType.DMA((spare,)),
            pltpu.SemaphoreType.DMA((spare,)),
            pltpu.SemaphoreType.DMA((8,)),
        ],
        compiler_params=pltpu.CompilerParams(
            collective_id=0, has_side_effects=True, vmem_limit_bytes=24 * 2**20
        ),
        name="first",
    )(small, heads, dense, parts_in, parts_out)


class Spread:
    def __init__(self, copies, own, whole, outer_bits, item_bits):
        self.copies, self.own, self.whole = copies, own, whole
        self.outer_bits, self.item_bits = outer_bits, item_bits
        self.half = own.shape[0] // 2

    def part(self, masks):
        place = (self.copies.here[0] ^ masks[0]) * lax.axis_size("seq")
        return self.whole.at[(place + (self.copies.here[1] ^ masks[1])) // 4]

    def over(self, masks, step, rows=None):
        source = self.own if masks == (0, 0) else self.part(masks)
        target = self.part(masks)
        if rows is not None:
            source, target = source.at[rows], target.at[rows]
        return self.copies.send(source, target, mask_of(step))

    def start(self):
        self.local = self.copies.move(self.own, self.part((0, 0)))
        self.first = [self.over((0, 0), step) for step in self.item_bits]
        self.outer = self.over((0, 0), self.outer_bits[0])

    def cross(self, masks, first):
        one, two = self.item_bits
        first[0].wait_recv()
        found = [self.over(moved(masks, *one), two, pl.ds(0, self.half))]
        first[1].wait_recv()
        found.append(self.over(moved(masks, *two), one, pl.ds(self.half, self.half)))
        return found

    def cross_own(self):
        self.last = self.cross((0, 0), self.first)

    def spread_outer(self):
        self.outer.wait_recv()
        masks = mask_of(self.outer_bits[0])
        self.second = [self.over(masks, step) for step in self.item_bits]

    def cross_outer(self):
        self.last += self.cross(mask_of(self.outer_bits[0]), self.second)

    def plain(self):
        self.local = self.copies.move(self.own, self.part((0, 0)))
        known = [(0, 0)]
        for step in self.outer_bits + self.item_bits:
            wait_all([self.over(masks, step) for masks in known])
            known = known + [moved(masks, *step) for masks in known]
        self.last = []

    def end(self):
        wait_all(self.last)
        self.local.wait()


def attend_unit(block, visible, onehot_ref, table_ref, cosine_ref, sine_ref, context_ref, lse_ref):
    query, key, value = head_parts(onehot_ref, table_ref, cosine_ref[...], sine_ref[...])
    value_turned = value.T
    for offset in range(0, query.shape[0], block):
        scores = visible_scores(key, query[offset : offset + block], offset, visible)
        peak = jnp.max(scores, axis=0, keepdims=True)
        expos = jnp.exp2((scores - peak) * exponent_scale)
        total = jnp.sum(expos, axis=0, keepdims=True)
        context = dot(value_turned, expos.astype(bf16)) / total
        context_ref[offset : offset + block, :] = context.T.astype(bf16)
        lse_ref[:, offset : offset + block] = peak * exponent_scale + jnp.log2(total)


def second_kernel(
    item_bits,
    seq_bits,
    visible_ref,
    onehot_ref,
    table_ref,
    cosine_ref,
    sine_ref,
    own_onehot_ref,
    embed_ref,
    vector_ref,
    dense_ref,
    own_in_ref,
    own_out_ref,
    context_ref,
    lse_ref,
    in_ref,
    out_ref,
    shared_ref,
    normed_ref,
    inverse_ref,
    context_scr,
    dense_scr,
    resid_scr,
    low_scr,
    send_sems,
    recv_sems,
    local_sems,
):
    seq_size = 2 ** len(seq_bits)
    items_here, length, features = context_scr.shape
    heads_here = features // HEAD
    span = length // seq_size
    width = dense_ref.shape[0]
    seq_place = lax.axis_index("seq")
    outer_bits = seq_bits[2:]
    greet(partners(seq_size, item_bits))
    copies = Copies(send_sems, recv_sems, local_sems)
    dense_copy = copies.move(dense_ref, dense_scr)
    spreads = [
        Spread(copies, own_in_ref, in_ref, outer_bits, item_bits),
        Spread(copies, own_out_ref, out_ref, outer_bits, item_bits),
    ]
    stepwise = len(outer_bits) == 1 and len(item_bits) == 2
    if stepwise:
        for one in spreads:
            one.start()
    arrivals, local = [], []
    for item in range(items_here):

        @pl.loop(0, heads_here)
        def _(head):
            place = pl.ds(pl.multiple_of(head * HEAD, HEAD), HEAD)
            attend_unit(
                min(256, length),
                visible_ref[item],
                onehot_ref.at[item],
                table_ref.at[head],
                cosine_ref,
                sine_ref,
                context_scr.at[item, :, place],
                lse_ref.at[item, head],
            )

        target = context_ref.at[
            item, :, pl.ds(pl.multiple_of(seq_place * features, HEAD), features)
        ]
        for mask in range(seq_size):
            rows = pl.ds(pl.multiple_of((seq_place ^ mask) * span, span), span)
            source = context_scr.at[item, rows]
            if mask:
                arrivals.append(copies.send(source, target, (0, mask)))
            else:
                local.append(copies.move(source, target))
    wait_all(arrivals)
    for copy in local:
        copy.wait()
    if stepwise:
        for one in spreads:
            one.cross_own()

    dense_copy.wait()
    rows_all = items_here * span
    tile = 256

    @pl.loop(0, width // tile)
    def _(order):
        place = pl.ds(pl.multiple_of(order * tile, tile), tile)
        branch = dot(context_ref[...].reshape(rows_all, width), dense_scr[:, place])
        inputs = contract_cols(own_onehot_ref[...], embed_ref[place, :])
        resid_scr[:, place] = deep_alpha * inputs + (branch + vector_ref[5:6, place])

    block = 32
    near, far = ("seq", 1), ("seq", 2)
    far_copies, near_copies, own_copies = [], [], []
    for item in range(items_here):

        @pl.loop(0, span // block)
        def _(order):
            start = pl.multiple_of(order * block, block)
            rows = pl.ds(pl.multiple_of(item * span + start, block), block)
            normed, inverse = norm_rows(resid_scr[rows, :])
            normed_ref[rows, :] = normed
            inverse_ref[rows, :] = jnp.broadcast_to(inverse, (block, 128))
            hidden = normed * vector_ref[0:1, :] + vector_ref[1:2, :]
            low_scr[item, pl.ds(start, block), :] = hidden.astype(bf16)

        source = low_scr.at[item]
        far_copies.append(copies.send(source, shared_ref.at[item, 1], mask_of(far)))
        near_copies.append(copies.send(source, shared_ref.at[item, 2], mask_of(near)))
        own_copies.append(copies.move(source, shared_ref.at[item, 0]))

    def pass_on(item):
        far_copies[item].wait_recv()
        part = shared_ref.at[item, 1]
        near_copies.append(copies.send(part, shared_ref.at[item, 3], mask_of(near)))

    if stepwise:
        spreads[0].spread_outer()
    pass_on(0)
    if stepwise:
        spreads[1].spread_outer()
    for item in range(1, items_here):
        pass_on(item)
    if stepwise:
        for one in spreads:
            one.cross_outer()
    else:
        for one in spreads:
            one.plain()
    for one in spreads:
        one.end()
    wait_all(near_copies)
    for copy in own_copies:
        copy.wait()
    copies.end()


def second_call(
    item_bits,
    seq_bits,
    visible,
    onehots,
    tables,
    cosine,
    sine_part,
    own_onehot,
    embed,
    vectors,
    w_dense,
    own_in,
    own_out,
):
    items_here, length, vocab = onehots.shape
    heads_here = tables.shape[0]
    features = heads_here * HEAD
    seq_size = 2 ** len(seq_bits)
    span = length // seq_size
    width = w_dense.shape[0]
    groups = 2 ** (len(item_bits) + len(seq_bits)) // 4
    any_space = pl.BlockSpec(memory_space=pl.ANY)
    near_space = pl.BlockSpec(memory_space=pltpu.VMEM)
    spare = 4 * groups + items_here * (seq_size + 4)
    return pl.pallas_call(
        functools.partial(second_kernel, item_bits, seq_bits),
        in_specs=[pl.BlockSpec(memory_space=pltpu.SMEM)] + [near_space] * 7 + [any_space] * 3,
        out_specs=[near_space] * 2 + [any_space] * 3 + [near_space] * 2,
        out_shape=[
            jax.ShapeDtypeStruct((items_here, span, width), bf16),
            jax.ShapeDtypeStruct((items_here, heads_here, 1, length), f32),
            jax.ShapeDtypeStruct((groups,) + own_in.shape, bf16),
            jax.ShapeDtypeStruct((groups,) + own_out.shape, bf16),
            jax.ShapeDtypeStruct((items_here, 4, span, width), bf16),
            jax.ShapeDtypeStruct((items_here * span, width), f32),
            jax.ShapeDtypeStruct((items_here * span, 128), f32),
        ],
        scratch_shapes=[
            pltpu.VMEM((items_here, length, features), bf16),
            pltpu.VMEM((width, width), bf16),
            pltpu.VMEM((items_here * span, width), f32),
            pltpu.VMEM((items_here, span, width), bf16),
            pltpu.SemaphoreType.DMA((spare,)),
            pltpu.SemaphoreType.DMA((spare,)),
            pltpu.SemaphoreType.DMA((16,)),
        ],
        compiler_params=pltpu.CompilerParams(
            collective_id=1, has_side_effects=True, vmem_limit_bytes=56 * 2**20
        ),
        name="second",
    )(
        visible,
        onehots,
        tables,
        cosine,
        sine_part,
        own_onehot,
        embed,
        vectors,
        w_dense,
        own_in,
        own_out,
    )


def leading(ref):
    return [index for index in np.ndindex(*ref.shape[:-2])]


def add_into(target, source):
    rows = target.shape[-2]
    for index in leading(target):

        @pl.loop(0, rows // 16)
        def _(order):
            place = index + (pl.ds(pl.multiple_of(order * 16, 16), 16),)
            total = target[place].astype(f32) + source[place].astype(f32)
            target[place] = total.astype(target.dtype)


def copy_into(target, source):
    @pl.loop(0, target.shape[0] // 16)
    def _(order):
        place = pl.ds(pl.multiple_of(order * 16, 16), 16)
        target[place] = source[place]


class Reduce:
    def __init__(self, copies, whole, rows, dims, steps, got, stage, stage_sems):
        self.copies, self.whole, self.rows = copies, whole, rows
        self.steps, self.got = steps, got
        self.place = dims.index(steps[0])
        self.stage, self.stage_sems = stage, stage_sems
        self.order = 0

    def first(self, bit, index=()):
        full = (slice(None),) * self.place
        if index:
            full = index[: self.place]
        rest = index[self.place :] if index else ()
        if index:
            return self.whole.at[full + (bit,) + rest + (self.rows,)]
        spare = len(self.whole.shape) - 3 - self.place
        return self.whole.at[full + (bit,) + (slice(None),) * spare + (self.rows,)]

    def start(self):
        step = self.steps[0]
        self.copy = self.copies.send(self.first(1 - my_bit(*step)), self.got[0], mask_of(step))

    def advance(self):
        step = self.steps[self.order]
        self.copy.wait_recv()
        if self.order == 0:
            self.kept = self.got[0]
            rows, columns = self.kept.shape[-2:]
            places = leading(self.kept)

            def load(order):
                return pltpu.make_async_copy(
                    self.first(my_bit(*step), places[order]),
                    self.stage.at[order % 2, pl.ds(0, rows), pl.ds(0, columns)],
                    self.stage_sems.at[order % 2],
                )

            load(0).start()
            for order, place in enumerate(places):
                if order + 1 < len(places):
                    load(order + 1).start()
                load(order).wait()
                add_into(
                    self.kept.at[place],
                    self.stage.at[order % 2, pl.ds(0, rows), pl.ds(0, columns)],
                )
        else:
            self.kept = self.kept.at[my_bit(*step)]
            add_into(self.kept, self.got[self.order])
        self.order += 1
        if self.order < len(self.steps):
            step = self.steps[self.order]
            self.copy = self.copies.send(
                self.kept.at[1 - my_bit(*step)], self.got[self.order], mask_of(step)
            )


def attend_back_unit(
    block,
    visible,
    onehot_ref,
    table_ref,
    cosine_ref,
    sine_ref,
    lse_ref,
    grad_ref,
    mixed_ref,
    sums_ref,
):
    cosine, sine_part = cosine_ref[...], sine_ref[...]
    query, key, value = head_parts(onehot_ref, table_ref, cosine, sine_part)
    key_turned = key.T
    length = query.shape[0]
    grad_key = jnp.zeros((length, HEAD), f32)
    grad_value = jnp.zeros((length, HEAD), f32)
    grad_query = []
    for offset in range(0, length, block):
        query_block = query[offset : offset + block]
        grad_block = grad_ref[offset : offset + block, :]
        scores = visible_scores(key, query_block, offset, visible)
        weights = jnp.exp2(scores * exponent_scale - lse_ref[:, offset : offset + block])
        grad_weights = contract_cols(value, grad_block)
        inner = jnp.sum(weights * grad_weights, axis=0, keepdims=True)
        grad_scores = (weights * (grad_weights - inner)).astype(bf16)
        grad_value = grad_value + dot(weights.astype(bf16), grad_block)
        grad_key = grad_key + dot(grad_scores, query_block)
        grad_query.append(dot(key_turned, grad_scores).T)
    grad_query = jnp.concatenate(grad_query, axis=0)

    def back(grad):
        return turn((grad * score_scale).astype(bf16).astype(f32), cosine, -sine_part).astype(bf16)

    mixed = jnp.concatenate([back(grad_query), back(grad_key), grad_value.astype(bf16)], axis=1)
    mixed_ref[...] = mixed.reshape(mixed_ref.shape)
    sums_ref[...] += dot(onehot_ref[...].T, mixed)


def third_kernel(
    item_bits,
    seq_bits,
    visible_ref,
    onehot_ref,
    table_ref,
    cosine_ref,
    sine_ref,
    lse_ref,
    slice_ref,
    grad_ref,
    in_ref,
    out_ref,
    dense_ref,
    bias_ref,
    spread_ref,
    sums_all_ref,
    in_part_ref,
    out_part_ref,
    dense_part_ref,
    bias_sum_ref,
    mixed_scr,
    other_scr,
    kept_scr,
    step_scrs,
    sums_scr,
    sums_got,
    bias_scr,
    bias_got,
    in_got,
    out_got,
    dense_got,
    in_final,
    out_final,
    stage_scr,
    stage_sems,
    send_sems,
    recv_sems,
    local_sems,
):
    seq_size = 2 ** len(seq_bits)
    items_here, length, features = grad_ref.shape
    heads_here = features // HEAD
    seq_place = lax.axis_index("seq")
    member = seq_place % 4
    outer_bits = seq_bits[2:]
    width = slice_ref.shape[1]
    greet(partners(seq_size, item_bits))
    copies = Copies(send_sems, recv_sems, local_sems)
    dims = item_bits[::-1] + outer_bits[::-1]

    def reducers(whole, got):
        rows = whole.shape[-2]
        if len(item_bits) == 2:
            one, two = item_bits
            ways = [
                (pl.ds(0, rows // 2), [two, one] + outer_bits[::-1]),
                (pl.ds(rows // 2, rows // 2), [one, two] + outer_bits[::-1]),
            ]
        else:
            ways = [(pl.ds(0, rows), dims)]
        return [
            Reduce(copies, whole, part, dims, steps, list(got[order]), stage_scr, stage_sems)
            for order, (part, steps) in enumerate(ways)
        ]

    in_sums = reducers(in_ref, in_got)
    out_sums = reducers(out_ref, out_got)
    dense_steps = item_bits[::-1] + seq_bits[:0:-1]
    dense_sum = Reduce(
        copies,
        dense_ref,
        pl.ds(0, dense_ref.shape[-2]),
        dense_steps,
        dense_steps,
        list(dense_got),
        stage_scr,
        stage_sems,
    )
    for one in in_sums:
        one.start()
    sums_scr[...] = jnp.zeros_like(sums_scr)
    tile = 256
    flying = {}
    bias_scr[0] = bias_ref[...]
    bias_steps = seq_bits + item_bits
    bias_copies = [copies.send(bias_scr.at[0], bias_got.at[0], mask_of(bias_steps[0]))]
    for stage in range(items_here + len(seq_bits)):
        if stage < items_here:

            @pl.loop(0, heads_here)
            def _(head):
                place = pl.ds(pl.multiple_of(head * HEAD, HEAD), HEAD)
                packed = pl.ds(pl.multiple_of(head * 3 * HEAD, HEAD), 3 * HEAD)
                attend_back_unit(
                    min(256, length),
                    visible_ref[stage],
                    onehot_ref.at[stage],
                    table_ref.at[head],
                    cosine_ref,
                    sine_ref,
                    lse_ref.at[stage, head],
                    grad_ref.at[stage, :, place],
                    mixed_scr.at[:, :, :, packed],
                    sums_scr.at[0, head],
                )

        for order in range(len(seq_bits) - 1, -1, -1):
            item = stage - 1 - order
            if not 0 <= item < items_here:
                continue
            copy, kept = flying[item]
            copy.wait_recv()
            got = step_scrs[order].at[item % 2]
            if order:
                full = (slice(None),) * (len(kept.shape) - 3)
                kept = kept.at[full + (my_bit(*seq_bits[order]),)]
            if order + 1 < len(seq_bits):
                add_into(kept, got)
                step = seq_bits[order + 1]
                full = (slice(None),) * (len(kept.shape) - 3)
                copy = copies.send(
                    kept.at[full + (1 - my_bit(*step),)],
                    step_scrs[order + 1].at[item % 2],
                    mask_of(step),
                )
                flying[item] = copy, kept
                flying["later", item].append(copy)
            else:

                @pl.loop(0, kept.shape[0] // 16)
                def _(block):
                    place = (pl.ds(pl.multiple_of(block * 16, 16), 16),)
                    total = kept[place].astype(f32) + got[place].astype(f32)
                    spread_ref[(item,) + place] = total.astype(bf16)

        if stage < items_here:
            core = my_bit(*seq_bits[0])
            slot = stage % 2
            if stage >= 2:
                copies.sent_now(flying["first", stage - 2])
            kept_slot = stage % len(seq_bits)
            if stage >= len(seq_bits):
                for copy in flying["later", stage - len(seq_bits)]:
                    copies.sent_now(copy)
            half = mixed_scr.shape[0] * mixed_scr.shape[2]
            other = mixed_scr[:, 1 - core].reshape(half, -1)
            mine = mixed_scr[:, core].reshape(half, -1)

            @pl.loop(0, width // tile)
            def _(order):
                place = pl.ds(pl.multiple_of(order * tile, tile), tile)
                weights = slice_ref[:, place]
                target = other_scr.at[slot]
                target[..., place] = dot(other, weights).astype(bf16).reshape(
                    target.shape[:-1] + (tile,)
                )
                target = kept_scr.at[kept_slot]
                target[..., place] = dot(mine, weights).astype(bf16).reshape(
                    target.shape[:-1] + (tile,)
                )

            copy = copies.send(
                other_scr.at[slot], step_scrs[0].at[slot], mask_of(seq_bits[0])
            )
            flying[stage] = copy, kept_scr.at[kept_slot]
            flying["first", stage] = copy
            flying["later", stage] = []
        if stage == 0:
            for one in out_sums:
                one.start()
        if stage == items_here:
            for one in in_sums:
                one.advance()
            dense_sum.start()
            sums_copy = copies.send(sums_scr.at[0], sums_got.at[0], mask_of(item_bits[0]))
        if stage == items_here + 1:
            for one in out_sums:
                one.advance()
        if stage == items_here + 2:
            for one in in_sums:
                one.advance()
        bias_done = len(bias_copies)
        if bias_done <= len(bias_steps):
            bias_copies[-1].wait_recv()
            bias_scr[bias_done] = bias_scr[bias_done - 1] + bias_got[bias_done - 1]
            if bias_done < len(bias_steps):
                bias_copies.append(
                    copies.send(
                        bias_scr.at[bias_done],
                        bias_got.at[bias_done],
                        mask_of(bias_steps[bias_done]),
                    )
                )
            else:
                bias_copies.append(None)
                bias_sum_ref[...] = bias_scr[bias_done]

    for order, step in enumerate(item_bits):
        sums_copy.wait_recv()
        sums_scr[order + 1] = sums_scr[order] + sums_got[order]
        if order + 1 < len(item_bits):
            sums_copy = copies.send(
                sums_scr.at[order + 1], sums_got.at[order + 1], mask_of(item_bits[order + 1])
            )
    sums_all_ref[seq_place] = sums_scr[len(item_bits)].astype(bf16)
    known = [0]
    arrivals = []
    for axis, bit in seq_bits[::-1]:
        wait_all(arrivals)
        arrivals = []
        for mask in known:
            part = sums_all_ref.at[seq_place ^ mask]
            arrivals.append(copies.send(part, part, (0, bit)))
        known = known + [mask ^ bit for mask in known]
        for one in out_sums:
            if one.order < 2:
                one.advance()
        if dense_sum.order == 0:
            dense_sum.advance()

    while in_sums[0].order < len(dims):
        for one in in_sums + out_sums:
            if one.order < len(dims):
                one.advance()
        if dense_sum.order < len(dense_steps):
            dense_sum.advance()
    while out_sums[0].order < len(dims):
        for one in out_sums:
            one.advance()
    wait_all(arrivals)
    shares, local = [], []
    for sums, final, target in (
        (in_sums, in_final, in_part_ref),
        (out_sums, out_final, out_part_ref),
    ):
        rows = target.shape[1]
        first = 0
        for one in sums:
            copy_into(final.at[pl.ds(first, one.kept.shape[0])], one.kept)
            first += one.kept.shape[0]
        for mask in range(4):
            source = final.at[pl.ds(pl.multiple_of((member ^ mask) * rows, 16), rows)]
            if mask:
                shares.append(copies.send(source, target.at[member], (0, mask)))
            else:
                local.append(copies.move(source, target.at[member]))
    while dense_sum.order < len(dense_steps):
        dense_sum.advance()
    dense_part_ref[...] = dense_sum.kept[...]
    wait_all(shares)
    for copy in local:
        copy.wait()
    copies.end()


def third_call(
    item_bits,
    seq_bits,
    visible,
    onehots,
    tables,
    cosine,
    sine_part,
    log_sums,
    w_slice,
    grad_context,
    grad_in,
    grad_out,
    by_rows,
    in_sum,
):
    items_here, length, vocab = onehots.shape
    heads_here = tables.shape[0]
    seq_size = 2 ** len(seq_bits)
    span = length // seq_size
    width = w_slice.shape[1]
    packed = heads_here * 3 * HEAD
    outer = len(seq_bits) - 2
    levels = len(item_bits) + outer
    any_space = pl.BlockSpec(memory_space=pl.ANY)
    near_space = pl.BlockSpec(memory_space=pltpu.VMEM)

    def got_shapes(whole, ways, depth):
        rows, columns = whole.shape[-2:]
        one = tuple(
            pltpu.VMEM((2,) * order + (rows // ways, columns), bf16)
            for order in range(depth - 1, -1, -1)
        )
        return one

    ways = 2 if len(item_bits) == 2 else 1
    group_rows = grad_in.shape[-2]
    rows = group_rows // 4
    dense_depth = len(item_bits) + len(seq_bits) - 1
    spread = (2,) * (len(seq_bits) - 1) + (span, width)
    all_bits = len(item_bits) + len(seq_bits)
    spare = 8 * items_here + 8 * levels + 16 * all_bits
    stage_rows = max(group_rows // ways, by_rows.shape[-2])
    return pl.pallas_call(
        functools.partial(third_kernel, item_bits, seq_bits),
        in_specs=[pl.BlockSpec(memory_space=pltpu.SMEM)]
        + [near_space] * 7
        + [any_space] * 3
        + [near_space],
        out_specs=[near_space, near_space, any_space, any_space, near_space, near_space],
        out_shape=[
            jax.ShapeDtypeStruct((items_here, span, width), bf16),
            jax.ShapeDtypeStruct((seq_size, heads_here, vocab, 3 * HEAD), bf16),
            jax.ShapeDtypeStruct((4, rows, grad_in.shape[-1]), bf16),
            jax.ShapeDtypeStruct((4, rows, grad_out.shape[-1]), bf16),
            jax.ShapeDtypeStruct(by_rows.shape[-2:], bf16),
            jax.ShapeDtypeStruct(in_sum.shape, f32),
        ],
        scratch_shapes=[
            pltpu.VMEM((seq_size // 2, 2, span, packed), bf16),
            pltpu.VMEM((2,) + spread, bf16),
            pltpu.VMEM((len(seq_bits),) + spread, bf16),
            tuple(pltpu.VMEM((2,) + spread[order:], bf16) for order in range(len(seq_bits))),
            pltpu.VMEM((len(item_bits) + 1, heads_here, vocab, 3 * HEAD), f32),
            pltpu.VMEM((len(item_bits), heads_here, vocab, 3 * HEAD), f32),
            pltpu.VMEM((all_bits + 1,) + in_sum.shape, f32),
            pltpu.VMEM((all_bits,) + in_sum.shape, f32),
            tuple(got_shapes(grad_in, ways, levels) for _ in range(ways)),
            tuple(got_shapes(grad_out, ways, levels) for _ in range(ways)),
            got_shapes(by_rows, 1, dense_depth),
            pltpu.VMEM((group_rows, grad_in.shape[-1]), bf16),
            pltpu.VMEM((group_rows, grad_out.shape[-1]), bf16),
            pltpu.VMEM((2, stage_rows, grad_in.shape[-1]), bf16),
            pltpu.SemaphoreType.DMA((2,)),
            pltpu.SemaphoreType.DMA((spare,)),
            pltpu.SemaphoreType.DMA((spare,)),
            pltpu.SemaphoreType.DMA((8,)),
        ],
        compiler_params=pltpu.CompilerParams(
            collective_id=2, has_side_effects=True, vmem_limit_bytes=60 * 2**20
        ),
        name="third",
    )(
        visible,
        onehots,
        tables,
        cosine,
        sine_part,
        log_sums,
        w_slice,
        grad_context,
        grad_in,
        grad_out,
        by_rows,
        in_sum,
    )


def ff_kernel(
    shared_ref,
    normed_ref,
    inverse_ref,
    cotangent_ref,
    in_ref,
    out_ref,
    vector_ref,
    bias_ref,
    product_ref,
    saved_ref,
    grad_shared_ref,
    grad_in_ref,
    layer_ref,
    resid_ref,
    sums_ref,
    in_sum_ref,
    rows_scr,
    product_scr,
    save_scr,
    parts_scr,
    near_got,
    far_got,
    low_scr,
    grad_in_scr,
    resid_scr,
    normed_scr,
    gate_scr,
    send_sems,
    recv_sems,
    load_sems,
    keep_sems,
):
    chunks, blocks, span, width = shared_ref.shape
    group_rows = blocks * span
    tiles = product_scr.shape[-1] // 128
    tile = 256
    near, far = ("seq", 1), ("seq", 2)
    greet([mask_of(near), mask_of(far)])
    copies = Copies(send_sems, recv_sems, None)
    keeps, loads = {}, {}
    state = {}
    gain_one, shift_one, b_down, gain_two, shift_two = range(5)
    for line in range(sums_ref.shape[0]):
        sums_ref[line : line + 1, :] = jnp.zeros((1, width), f32)
    in_sum_ref[...] = jnp.zeros_like(in_sum_ref)

    def load(name, slot, source, target):
        copy = pltpu.make_async_copy(source, target, load_sems.at[slot])
        copy.start()
        loads[name] = copy

    def loaded(name):
        loads.pop(name).wait()

    def keep(name, slot, source, target):
        copy = pltpu.make_async_copy(source, target, keep_sems.at[slot])
        copy.start()
        keeps[name] = copy

    def keep_done(name):
        if name in keeps:
            keeps.pop(name).wait()

    def load_shared(chunk):
        slot = chunk % 2
        load(("rows", slot), slot, shared_ref.at[chunk], rows_scr.at[slot])

    def load_normed(chunk):
        slot = chunk % 2
        rows = pl.ds(chunk * span, span)
        load(("normed", slot), 2 + slot, normed_ref.at[rows], normed_scr.at[slot])

    def forward_gate(chunk):
        slot = chunk % 2
        loaded(("rows", slot))
        if chunk + 1 < chunks:
            load_shared(chunk + 1)
        keep_done(("product", slot))
        keep_done(("save", slot))
        rows = rows_scr.at[slot]

        def multiply(order, place):
            columns = pl.ds(pl.multiple_of(order * tile, tile), tile)
            gate_scr[place] = (
                dot(rows[...].reshape(group_rows, width), in_ref[:, columns])
                + bias_ref[:, columns]
            )

        def finish(order, place):
            gate_up = gate_scr[place]
            up_part, gate = gate_up[:, :128], gate_up[:, 128:]
            below = 0.5 * (1.0 + lax.erf(gate * (0.5**0.5)))
            activated = gate * below
            slope = below + gate * jnp.exp(-0.5 * gate * gate) * (1.0 / math.sqrt(2.0 * math.pi))
            columns = pl.ds(pl.multiple_of(order * 128, 128), 128)
            product_scr[slot, :, columns] = (up_part * activated).astype(bf16)
            save_scr[slot, 0, :, columns] = activated.astype(bf16)
            save_scr[slot, 1, :, columns] = (up_part * slope).astype(bf16)

        multiply(0, 0)

        @pl.loop(0, (tiles - 1) // 2)
        def _(pair):
            finish(2 * pair, 0)
            multiply(2 * pair + 1, 1)
            finish(2 * pair + 1, 1)
            multiply(2 * pair + 2, 0)

        if tiles % 2 == 0:
            multiply(tiles - 1, 1)
            finish(tiles - 2, 0)
            finish(tiles - 1, 1)
        else:
            finish(tiles - 1, 0)
        keep(("product", slot), slot, product_scr.at[slot], product_ref.at[chunk])
        keep(("save", slot), 2 + slot, save_scr.at[slot], saved_ref.at[chunk])

    def send_near(name, slot):
        source = parts_scr.at[slot, pl.ds(2, 2)]
        state["near", name] = copies.send(source, near_got.at[slot], mask_of(near))

    def free_parts(slot):
        for key in ("near", "far"):
            copy = state.pop((key, "of", slot), None)
            if copy is not None:
                copies.sent_now(copy)

    def times_turned(name, slot, left, weights_ref):
        free_parts(slot)

        @pl.loop(0, width // tile)
        def _(order):
            place = pl.ds(pl.multiple_of(order * tile, tile), tile)
            total = contract_cols(left[...], weights_ref[place, :])
            parts_scr[slot, :, :, place] = total.astype(bf16).reshape(blocks, span, tile)

        send_near(name, slot)
        state["near", "of", slot] = state["near", name]

    def forward_out(chunk):
        times_turned(chunk, chunk % 2, product_scr.at[chunk % 2], out_ref)

    def sum_near(name, chunk):
        slot = chunk % 2
        state["near", name].wait_recv()
        add_into(parts_scr.at[slot, pl.ds(0, 2)], near_got.at[slot])
        copy = copies.send(parts_scr.at[slot, 1], far_got.at[chunk], mask_of(far))
        state["far", name] = copy
        state["far", "of", slot] = copy

    block = 32

    def row_blocks(function):
        @pl.loop(0, span // block)
        def _(order):
            function(pl.ds(pl.multiple_of(order * block, block), block))

    def line(index):
        return vector_ref[index : index + 1, :]

    def add_sum(index, rows):
        sums_ref[index : index + 1, :] += jnp.sum(rows, axis=0, keepdims=True)

    def second_norm(chunk):
        slot = chunk % 2
        state["far", chunk].wait_recv()
        loaded(("normed", slot))
        for key in ("low near", "low far"):
            copy = state.pop((key, slot), None)
            if copy is not None:
                copies.sent_now(copy)
        keep_done(("low", slot))

        def body(rows):
            hidden = normed_scr[slot, rows] * line(gain_one) + line(shift_one)
            mlp_branch = parts_scr[slot, 0, rows].astype(f32) + far_got[chunk, rows].astype(f32)
            normed, inverse = norm_rows(deep_alpha * hidden + mlp_branch + line(b_down))
            layer_ref[chunk, rows] = (normed * line(gain_two) + line(shift_two)).astype(bf16)
            grad = cotangent_ref[chunk, rows].astype(f32)
            resid = norm_rows_back(grad, normed, inverse, line(gain_two))
            low = resid.astype(bf16)
            resid_scr[chunk, rows] = resid
            low_scr[slot, rows] = low
            add_sum(3, grad * normed)
            add_sum(4, grad)
            add_sum(5, low.astype(f32))

        row_blocks(body)
        if chunk + 2 < chunks:
            load_normed(chunk + 2)
        source = low_scr.at[slot]
        keep(("low", slot), 4 + slot, source, grad_shared_ref.at[chunk, 0])
        state["low far", slot] = copies.send(source, grad_shared_ref.at[chunk, 1], mask_of(far))
        state["low near", slot] = copies.send(source, grad_shared_ref.at[chunk, 2], mask_of(near))
        state["grad far", chunk] = state["low far", slot]
        state["grad near", chunk] = state["low near", slot]

    def pass_on(chunk):
        state["grad far", chunk].wait_recv()
        part = grad_shared_ref.at[chunk, 1]
        state["grad cross", chunk] = copies.send(
            part, grad_shared_ref.at[chunk, 3], mask_of(near)
        )

    def load_grads(chunk):
        slot = chunk % 2
        keep_done(("low", slot))
        state["grad near", chunk].wait_recv()
        state["grad cross", chunk].wait_recv()
        load(("rows", slot), slot, grad_shared_ref.at[chunk], rows_scr.at[slot])
        keep_done(("save", slot))
        load(("save", slot), 4 + slot, saved_ref.at[chunk], save_scr.at[slot])

    def backward_gate(chunk):
        slot = chunk % 2
        loaded(("rows", slot))
        loaded(("save", slot))
        keep_done("grad in")
        rows = rows_scr.at[slot]

        def columns_of(first, count):
            columns = pl.ds(pl.multiple_of(first * 128, 128), count * 128)
            grad = dot(rows[...].reshape(group_rows, width), out_ref[:, columns])
            for order in range(count):
                part = grad[:, order * 128 : (order + 1) * 128]
                saved = pl.ds(pl.multiple_of((first + order) * 128, 128), 128)
                for which in range(2):
                    low = (part * save_scr[slot, which, :, saved].astype(f32)).astype(bf16)
                    place = pl.ds(
                        pl.multiple_of((2 * (first + order) + which) * 128, 128), 128
                    )
                    grad_in_scr[:, place] = low
                    in_sum_ref[:, place] += jnp.sum(low.astype(f32), axis=0, keepdims=True)

        @pl.loop(0, tiles // 2)
        def _(pair):
            columns_of(2 * pair, 2)

        if tiles % 2:
            columns_of(tiles - 1, 1)
        keep("grad in", 6, grad_in_scr, grad_in_ref.at[chunk])

    def backward_in(chunk):
        times_turned(("back", chunk), chunk % 2, grad_in_scr, in_ref)

    def first_norm(chunk):
        slot = chunk % 2
        state["far", ("back", chunk)].wait_recv()
        loaded(("normed", slot))

        def body(rows):
            grad = parts_scr[slot, 0, rows].astype(f32) + far_got[chunk, rows].astype(f32)
            grad = grad + deep_alpha * resid_scr[chunk, rows]
            normed = normed_scr[slot, rows]
            place = pl.ds(pl.multiple_of(chunk * span + rows.start, block), block)
            resid = norm_rows_back(grad, normed, inverse_ref[place, 0:1], line(gain_one))
            resid_scr[chunk, rows] = resid
            add_sum(0, grad * normed)
            add_sum(1, grad)
            add_sum(2, resid.astype(bf16).astype(f32))

        row_blocks(body)
        if chunk + 2 < chunks:
            load_normed(chunk + 2)
        keep(("resid", chunk), 7 + chunk, resid_scr.at[chunk], resid_ref.at[chunk])

    load_shared(0)
    load_normed(0)
    load_normed(1)
    last = chunks - 1
    for chunk in range(chunks):
        forward_gate(chunk)
        if chunk >= 1:
            sum_near(chunk - 1, chunk - 1)
        if chunk >= 2:
            second_norm(chunk - 2)
        if chunk >= 3:
            pass_on(chunk - 3)
        forward_out(chunk)
    sum_near(last, last)
    second_norm(last - 1)
    pass_on(last - 2)
    waiting = [("norm", last), ("pass", last - 1), ("pass", last)]
    for chunk in range(chunks):
        if chunk == 0:
            load_grads(0)
        backward_gate(chunk)
        if waiting and waiting[0][0] == "norm":
            second_norm(waiting.pop(0)[1])
            load_normed(0)
            load_normed(1)
        if waiting:
            pass_on(waiting.pop(0)[1])
        if chunk >= 1:
            sum_near(("back", chunk - 1), chunk - 1)
        if chunk >= 2:
            first_norm(chunk - 2)
        if chunk + 1 < chunks:
            if chunk + 1 == last and waiting:
                pass_on(waiting.pop(0)[1])
            load_grads(chunk + 1)
        backward_in(chunk)
    sum_near(("back", last), last)
    first_norm(last - 1)
    first_norm(last)
    for name in list(keeps):
        keep_done(name)
    copies.end()


def ff_call(shared, normed, inverse, cotangent, w_in, w_out, vectors, in_bias):
    chunks, blocks, span, width = shared.shape
    group_rows = blocks * span
    ff_part = w_out.shape[1]
    any_space = pl.BlockSpec(memory_space=pl.ANY)
    near_space = pl.BlockSpec(memory_space=pltpu.VMEM)
    spare = 8 * chunks
    return pl.pallas_call(
        ff_kernel,
        in_specs=[any_space, any_space] + [near_space] * 6,
        out_specs=[any_space] * 4 + [near_space, any_space, near_space, near_space],
        out_shape=[
            jax.ShapeDtypeStruct((chunks, group_rows, ff_part), bf16),
            jax.ShapeDtypeStruct((chunks, 2, group_rows, ff_part), bf16),
            jax.ShapeDtypeStruct((chunks, blocks, span, width), bf16),
            jax.ShapeDtypeStruct((chunks, group_rows, 2 * ff_part), bf16),
            jax.ShapeDtypeStruct((chunks, span, width), bf16),
            jax.ShapeDtypeStruct((chunks, span, width), f32),
            jax.ShapeDtypeStruct((8, width), f32),
            jax.ShapeDtypeStruct((1, 2 * ff_part), f32),
        ],
        scratch_shapes=[
            pltpu.VMEM((2, blocks, span, width), bf16),
            pltpu.VMEM((2, group_rows, ff_part), bf16),
            pltpu.VMEM((2, 2, group_rows, ff_part), bf16),
            pltpu.VMEM((2, blocks, span, width), bf16),
            pltpu.VMEM((2, 2, span, width), bf16),
            pltpu.VMEM((chunks, span, width), bf16),
            pltpu.VMEM((2, span, width), bf16),
            pltpu.VMEM((group_rows, 2 * ff_part), bf16),
            pltpu.VMEM((chunks, span, width), f32),
            pltpu.VMEM((2, span, width), f32),
            pltpu.VMEM((2, group_rows, 256), f32),
            pltpu.SemaphoreType.DMA((spare,)),
            pltpu.SemaphoreType.DMA((spare,)),
            pltpu.SemaphoreType.DMA((6,)),
            pltpu.SemaphoreType.DMA((7 + chunks,)),
        ],
        compiler_params=pltpu.CompilerParams(
            collective_id=3, has_side_effects=True, vmem_limit_bytes=60 * 2**20
        ),
        name="feed_forward",
    )(shared, normed, inverse, cotangent, w_in, w_out, vectors, in_bias)


def on_device(
    token_ids,
    masked,
    item_flag,
    prefix,
    cotangent,
    embedding,
    heads_weight,
    heads_bias,
    dense_weight,
    dense_bias,
    first_gain,
    first_bias,
    up_weight,
    up_bias,
    down_weight,
    down_bias,
    second_gain,
    second_bias,
):
    lines = Lines()
    items_here, span = token_ids.shape
    items_size, seq_size = lax.axis_size("items"), lax.axis_size("seq")
    item_place, seq_place = lax.axis_index("items"), lax.axis_index("seq")
    count = items_size * seq_size
    length = span * seq_size
    width = embedding.shape[0] * count
    vocab = embedding.shape[1]
    heads_here = HEADS // seq_size
    packed_width = heads_here * 3 * HEAD
    rows_here = up_weight.shape[0]
    ff_width = down_weight.shape[0]
    members = 4
    groups = count // members
    member = seq_place % members
    ff_part = -(-ff_width // (members * 128)) * 128
    ff_all = members * ff_part

    item_bits, seq_bits = bits_of("items"), bits_of("seq")
    outer_bits = seq_bits[2:]

    input_ids = jnp.where(masked == 1, mask_token, token_ids)
    flat_place = item_place * seq_size + seq_place
    row_count = rows_here + 16
    bias_row = lax.dynamic_update_slice(
        jnp.zeros((16, heads_weight.shape[1]), bf16),
        heads_bias[None],
        (0, flat_place * heads_bias.shape[0]),
    )
    ones_row = jnp.zeros((16, vocab), bf16).at[0].set(1.0)
    small = [
        embedding.reshape(-1),
        ones_row.reshape(-1),
        input_ids.astype(bf16).reshape(-1),
        dense_bias,
        first_gain,
        first_bias,
        down_bias,
        second_gain,
        second_bias,
    ]
    ends = [0]
    for part in small:
        ends.append(ends[-1] + part.shape[0])
    flat = jnp.concatenate(small)
    flat = jnp.pad(flat, (0, -flat.shape[0] % 2048)).reshape(-1, 128)

    def by_member(part):
        padded = jnp.pad(part, ((0, 0), (0, ff_all - ff_width)))
        return jnp.transpose(padded.reshape(rows_here, 2, 2, ff_part), (1, 2, 0, 3))

    tiles = ff_part // 128

    def woven(up, gate):
        shape = up.shape[:-1] + (tiles, 128)
        return jnp.stack([up.reshape(shape), gate.reshape(shape)], axis=-2).reshape(
            up.shape[:-1] + (2 * ff_part,)
        )

    def unwoven(both_parts):
        parts = both_parts.reshape(both_parts.shape[:-1] + (tiles, 2, 128))
        shape = both_parts.shape[:-1] + (ff_part,)
        return parts[..., 0, :].reshape(shape), parts[..., 1, :].reshape(shape)

    parts_in = woven(by_member(up_weight[:, :ff_width]), by_member(up_weight[:, ff_width:]))
    parts_out = by_member(down_weight.T)
    everyone, mixed_table, w_block, w_dense, own_in, own_out = first_call(
        item_bits,
        seq_bits,
        flat,
        jnp.concatenate([heads_weight, bias_row], axis=0),
        dense_weight,
        parts_in,
        parts_out,
    )
    w_dense = w_dense.reshape(width, width)
    w_block = w_block[:, :rows_here].reshape(seq_size * rows_here, packed_width)
    everyone = everyone.reshape(count, -1)
    pieces = [everyone[:, a:b] for a, b in zip(ends[:-1], ends[1:])]
    table = pieces[0].reshape(width, vocab)
    b_dense, gain_one, shift_one, b_down, gain_two, shift_two = (
        part.reshape(-1).astype(f32) for part in pieces[3:]
    )
    ids_here = pick(pieces[2].reshape(items_size, seq_size, items_here, span), item_place, 0)
    ids_here = jnp.transpose(ids_here, (1, 0, 2)).reshape(items_here, length).astype(jnp.int32)
    in_bias = jnp.pad(
        up_bias.astype(f32).reshape(2, ff_width), ((0, 0), (0, ff_all - ff_width))
    )
    in_bias = lax.dynamic_slice(in_bias, (0, member * ff_part), (2, ff_part))
    in_bias = woven(in_bias[:1], in_bias[1:])

    vocab_index = jnp.arange(vocab, dtype=jnp.int32)
    positions = jnp.arange(length, dtype=f32)
    frequency = jnp.exp(jnp.arange(HEAD // 2, dtype=f32) * (-2.0 * math.log(10000.0) / HEAD))
    angles = positions[:, None] * frequency[None, :]
    cosine = jnp.cos(angles)
    sine_part = jnp.sin(angles)
    cosine = jnp.concatenate([cosine, cosine], axis=1)
    sine_part = jnp.concatenate([-sine_part, sine_part], axis=1)
    visible = jnp.where(item_flag == 1, length, prefix)
    tables = table_halves(mixed_table)
    onehots = (ids_here[:, :, None] == vocab_index).astype(bf16)
    own_onehot = (input_ids.reshape(-1)[:, None] == vocab_index[None, :]).astype(bf16)
    vectors = jnp.stack([gain_one, shift_one, b_down, gain_two, shift_two, b_dense])
    vectors = jnp.pad(vectors, ((0, 2), (0, 0)))
    context, log_sums, w_in, w_out, shared, normed, inverse = second_call(
        item_bits,
        seq_bits,
        visible,
        onehots,
        tables,
        cosine,
        sine_part,
        own_onehot,
        table,
        vectors,
        w_dense,
        own_in,
        own_out,
    )
    product, _, grad_shared, grad_in, layer_out, grad_resid, sums, in_sum = ff_call(
        shared,
        normed,
        inverse,
        cotangent,
        w_in.reshape(width, 2 * ff_part),
        w_out.reshape(width, ff_part),
        vectors,
        in_bias,
    )
    rows_all = items_here * span
    group_all = members * rows_all
    context = context.reshape(rows_all, width)
    grad_resid = grad_resid.reshape(rows_all, width)
    grad_branch = grad_resid.astype(bf16)
    grad_context = contract_cols(grad_branch, w_dense).astype(bf16)
    grad_context = lax.all_to_all(
        jnp.transpose(
            grad_context.reshape(items_here, span, seq_size, heads_here * HEAD), (0, 2, 1, 3)
        ),
        "seq",
        split_axis=1,
        concat_axis=1,
        tiled=True,
    ).reshape(items_here, length, heads_here * HEAD)

    vector_sums = sums[:6].T
    token_sum = lax.dot_general(
        grad_resid,
        own_onehot.astype(f32),
        (((0,), (0,)), ((), ())),
        precision=lax.Precision.HIGHEST,
        preferred_element_type=f32,
    )
    grad_dense = contract_rows(context, grad_branch)
    by_rows = jnp.concatenate(
        [grad_dense, token_sum, jnp.pad(vector_sums, ((0, 0), (0, 122)))], axis=1
    ).astype(bf16)
    row_dims = item_bits[::-1] + seq_bits[::-1]
    by_rows = by_rows.reshape((2,) * len(row_dims) + (rows_here, -1))
    by_rows = halve(lines, by_rows, len(row_dims) - 1, *seq_bits[0])
    grad_out_weight = contract_rows(
        grad_shared.reshape(group_all, width), product.reshape(group_all, ff_part)
    )
    grad_in_weight = contract_rows(
        shared.reshape(group_all, width), grad_in.reshape(group_all, 2 * ff_part)
    )
    group_dims = (2,) * (len(item_bits) + len(outer_bits)) + (members * rows_here, -1)
    in_sum = jnp.concatenate(unwoven(in_sum), axis=0)
    in_all = lax.dynamic_update_slice(
        jnp.zeros((2, ff_all), f32), in_sum, (0, member * ff_part)
    ).reshape(-1, 128)
    w_slice = gather_merge(lines, w_block[None], item_bits).reshape(width, packed_width)
    spread, token_all, in_part, out_part, by_rows, in_all = third_call(
        item_bits,
        seq_bits,
        visible,
        onehots,
        tables,
        cosine,
        sine_part,
        log_sums,
        w_slice.T,
        grad_context,
        grad_in_weight.astype(bf16).reshape(group_dims),
        grad_out_weight.astype(bf16).reshape(group_dims),
        by_rows,
        in_all,
    )
    input_grads = spread.astype(f32) + deep_alpha * grad_resid.reshape(spread.shape)
    token_all = jnp.transpose(token_all, (2, 0, 1, 3)).reshape(vocab, -1)

    def from_members(part):
        taken = jnp.transpose(part, (1, 0, 2)).reshape(rows_here, ff_all)
        return taken[:, :ff_width].astype(f32)

    grad_up, grad_gate = (from_members(part) for part in unwoven(in_part))
    grad_down = from_members(out_part)
    by_rows = by_rows.astype(f32)
    grad_dense = by_rows[:, :width]
    token_sum = by_rows[:, width : width + vocab]
    own_vectors = by_rows[:, width + vocab :].T
    in_all = in_all.reshape(2, ff_all)
    grad_up_bias = in_all[:, :ff_width].reshape(-1)

    grad_heads = dot(embedding, token_all)
    grad_heads_bias = lax.dynamic_slice_in_dim(
        jnp.sum(token_all.astype(f32), axis=0),
        (item_place * seq_size + seq_place) * heads_bias.shape[0],
        heads_bias.shape[0],
        0,
    )
    embed_grad = 0.1 * (contract_cols(heads_weight, token_all) + deep_alpha * token_sum)
    return (
        layer_out,
        input_grads,
        embed_grad,
        grad_heads,
        grad_heads_bias,
        grad_dense,
        own_vectors[2],
        own_vectors[0],
        own_vectors[1],
        jnp.concatenate([grad_up, grad_gate], axis=1),
        grad_up_bias,
        grad_down.T,
        own_vectors[5],
        own_vectors[3],
        own_vectors[4],
    )


def solution(mesh):
    in_specs = (
        P("items", "seq"),
        P("items", "seq"),
        P("items"),
        P("items"),
        P("items", "seq", None),
        P(("items", "seq"), None),
        P(("items", "seq"), None),
        P(("items", "seq")),
        P(("items", "seq"), None),
        P(("items", "seq")),
        P(("items", "seq")),
        P(("items", "seq")),
        P(("items", "seq"), None),
        P(),
        P(None, ("items", "seq")),
        P(("items", "seq")),
        P(("items", "seq")),
        P(("items", "seq")),
    )
    out_specs = (
        P("items", "seq", None),
        P("items", "seq", None),
        P(("items", "seq"), None),
        P(("items", "seq"), None),
        P(("items", "seq")),
        P(("items", "seq"), None),
        P(("items", "seq")),
        P(("items", "seq")),
        P(("items", "seq")),
        P(("items", "seq"), None),
        P(),
        P(None, ("items", "seq")),
        P(("items", "seq")),
        P(("items", "seq")),
        P(("items", "seq")),
    )
    return jax.shard_map(
        on_device, mesh=mesh, in_specs=in_specs, out_specs=out_specs, check_vma=False
    )
```

```python
import functools
import math

import jax
import jax.numpy as jnp
import numpy as np
from jax import lax
from jax.experimental import pallas as pl
from jax.experimental.pallas import tpu as pltpu
from jax.sharding import PartitionSpec as P

HEADS = 16
HEAD = 128


deep_alpha = math.sqrt(48.0)
epsilon = 1e-05
mask_token = 3
both = ("items", "seq")
bf16 = jnp.bfloat16
f32 = jnp.float32
score_scale = HEAD ** (-0.5)
exponent_scale = score_scale * math.log2(math.e)


class Lines:
    def __init__(self):
        self.last = {}

    def swap(self, part, axis, bit):
        if (axis, bit) in self.last:
            part, _ = lax.optimization_barrier((part, self.last[axis, bit]))
        size = lax.axis_size(axis)
        got = lax.ppermute(part, axis, [(j, j ^ bit) for j in range(size)])
        self.last[axis, bit] = got
        return got


def bits_of(axis):
    found = []
    bit = 1
    while bit < lax.axis_size(axis):
        found.append((axis, bit))
        bit *= 2
    return found


def my_bit(axis, bit):
    return (lax.axis_index(axis) // bit) % 2


def pick(whole, place, dim):
    return lax.dynamic_index_in_dim(whole, place, dim, keepdims=False)


def halve(lines, whole, dim, axis, bit):
    place = my_bit(axis, bit)
    mine = pick(whole, place, dim)
    got = lines.swap(pick(whole, 1 - place, dim), axis, bit)
    return (mine.astype(f32) + got.astype(f32)).astype(whole.dtype)


def moved(masks, axis, bit):
    return (masks[0] ^ (bit if axis == "items" else 0), masks[1] ^ (bit if axis == "seq" else 0))


def contract_rows(left, right):
    return lax.dot_general(left, right, (((0,), (0,)), ((), ())), preferred_element_type=f32)


def contract_cols(left, right):
    return lax.dot_general(left, right, (((1,), (1,)), ((), ())), preferred_element_type=f32)


def dot(left, right):
    return jnp.dot(left, right, preferred_element_type=f32)


def turn(values, cosine, sine_part):
    return values * cosine + pltpu.roll(values, HEAD // 2, 1) * sine_part


def head_parts(onehot_ref, table_ref, cosine, sine_part):
    onehot = onehot_ref[...]
    mixed = dot(jnp.concatenate([onehot, onehot], axis=1), table_ref[...])
    query = turn(mixed[:, :HEAD], cosine, sine_part).astype(bf16)
    key = turn(mixed[:, HEAD : 2 * HEAD], cosine, sine_part).astype(bf16)
    return query, key, mixed[:, 2 * HEAD :].astype(bf16)


def visible_scores(key, query, offset, visible):
    scores = contract_cols(key, query)
    place = offset + lax.broadcasted_iota(jnp.int32, (1, query.shape[0]), 1)
    seen = lax.broadcasted_iota(jnp.int32, scores.shape, 0) < jnp.maximum(place + 1, visible)
    return jnp.where(seen, scores, -1e30)


def table_halves(mixed_table):
    vocab = mixed_table.shape[0]
    by_head = jnp.transpose(mixed_table.reshape(vocab, -1, 3 * HEAD), (1, 0, 2))
    high = lax.reduce_precision(by_head, 8, 7)
    return jnp.concatenate([high.astype(bf16), (by_head - high).astype(bf16)], axis=1)


def norm_rows(rows):
    center = rows - jnp.mean(rows, axis=-1, keepdims=True)
    inverse = lax.rsqrt(jnp.mean(center * center, axis=-1, keepdims=True) + epsilon)
    return center * inverse, inverse


def norm_rows_back(grad, normed, inverse, gain):
    scaled = grad * gain
    return inverse * (
        scaled
        - jnp.mean(scaled, axis=-1, keepdims=True)
        - normed * jnp.mean(scaled * normed, axis=-1, keepdims=True)
    )


MESH = pl.DeviceIdType.MESH


class Copies:
    def __init__(self, send_sems, recv_sems, local_sems):
        self.sems = send_sems, recv_sems, local_sems
        self.sent = {}
        self.moved = 0
        self.count = 0
        self.here = lax.axis_index("items"), lax.axis_index("seq")

    def send(self, source, target, masks):
        order = self.count
        self.count += 1
        copy = pltpu.make_async_remote_copy(
            src_ref=source,
            dst_ref=target,
            send_sem=self.sems[0].at[order],
            recv_sem=self.sems[1].at[order],
            device_id=(self.here[0] ^ masks[0], self.here[1] ^ masks[1]),
            device_id_type=MESH,
        )
        copy.start()
        self.sent[id(copy)] = copy
        return copy

    def move(self, source, target):
        copy = pltpu.make_async_copy(source, target, self.sems[2].at[self.moved])
        self.moved += 1
        copy.start()
        return copy

    def sent_now(self, copy):
        self.sent.pop(id(copy)).wait_send()

    def end(self):
        for copy in self.sent.values():
            copy.wait_send()


def wait_all(copies):
    for copy in copies:
        copy.wait_recv()


def mask_of(step):
    return moved((0, 0), *step)


def greet(masks):
    barrier = pltpu.get_barrier_semaphore()
    here = lax.axis_index("items"), lax.axis_index("seq")
    for mask_i, mask_s in masks:
        pl.semaphore_signal(
            barrier,
            inc=1,
            device_id=(here[0] ^ mask_i, here[1] ^ mask_s),
            device_id_type=MESH,
        )
    pl.semaphore_wait(barrier, len(masks))


def partners(seq_size, item_bits):
    return [(0, mask) for mask in range(1, seq_size)] + [mask_of(step) for step in item_bits]


def aligned(place, size):
    return pl.ds(place // size * size, size)


def first_kernel(
    item_bits,
    seq_bits,
    row_count,
    small_ref,
    heads_ref,
    head_bias_ref,
    dense_ref,
    in_ref,
    out_ref,
    everyone_ref,
    table_ref,
    block_ref,
    dense_all_ref,
    own_in_ref,
    own_out_ref,
    embed_scr,
    block_scr,
    sum_scr,
    got_scr,
    send_sems,
    recv_sems,
    local_sems,
):
    items_size, seq_size = everyone_ref.shape[:2]
    item_place, seq_place = lax.axis_index("items"), lax.axis_index("seq")
    core, chip = seq_place % 2, seq_place // 2
    member = seq_place % 4
    rows = dense_ref.shape[0]
    columns = block_scr.shape[2]
    greet(partners(seq_size, item_bits))
    copies = Copies(send_sems, recv_sems, local_sems)

    def head_columns(place, source):
        return source.at[:, pl.ds(pl.multiple_of(place * columns, 128), columns)]

    head_rows = [
        (heads_ref, pl.ds(0, rows)),
        (head_bias_ref, pl.ds(rows, row_count - rows)),
    ]

    small = [copies.send(small_ref, everyone_ref.at[item_place, seq_place], mask_of(seq_bits[0]))]
    heads = [
        copies.send(
            head_columns(seq_place ^ mask, source), block_scr.at[seq_place, place], (0, mask)
        )
        for mask in range(1, seq_size)
        for source, place in head_rows
    ]
    dense = [
        copies.send(dense_ref, dense_all_ref.at[item_place, chip, core], mask_of(seq_bits[1]))
    ]
    mine = pl.ds(pl.multiple_of(member * rows, rows), rows)
    shares = []

    def share(source, target):
        for mask in range(1, 4):
            other = member ^ mask
            shares.append(
                copies.send(source.at[other // 2, other % 2], target.at[mine], (0, mask))
            )

    local = [
        copies.move(small_ref, everyone_ref.at[item_place, seq_place]),
        copies.move(dense_ref, dense_all_ref.at[item_place, chip, core]),
        copies.move(head_columns(seq_place, heads_ref), block_scr.at[seq_place, head_rows[0][1]]),
        copies.move(
            head_columns(seq_place, head_bias_ref), block_scr.at[seq_place, head_rows[1][1]]
        ),
        copies.move(in_ref.at[member // 2, core], own_in_ref.at[0, mine]),
        copies.move(out_ref.at[member // 2, core], own_out_ref.at[mine]),
    ]
    for copy in local:
        copy.wait()

    for order in range(1, len(seq_bits)):
        if order > 1:
            wait_all(dense[-1:])
            part = dense_all_ref.at[item_place, aligned(chip, 2 ** (order - 1)), core]
            dense.append(copies.send(part, part, mask_of(seq_bits[order])))
        wait_all(small[-1:])
        part = everyone_ref.at[item_place, aligned(seq_place, 2**order)]
        small.append(copies.send(part, part, mask_of(seq_bits[order])))
        if order == 1:
            share(in_ref, own_in_ref.at[0])
    wait_all(small[-1:])
    embed = copies.move(everyone_ref.at[item_place, :, pl.ds(0, row_count)], embed_scr)

    wait_all(heads)
    embed.wait()
    sum_scr[0] = lax.dot_general(
        embed_scr[...].reshape(seq_size * row_count, -1),
        block_scr[...].reshape(seq_size * row_count, columns),
        (((0,), (0,)), ((), ())),
        preferred_element_type=f32,
    )
    sums = copies.send(sum_scr.at[0], got_scr.at[0], mask_of(item_bits[0]))
    block_out = copies.move(block_scr, block_ref)
    part = everyone_ref.at[item_place]
    small.append(copies.send(part, part, mask_of(item_bits[0])))
    share(out_ref, own_out_ref)
    wait_all(dense[-1:])

    def dense_part(mask):
        return dense_all_ref.at[item_place ^ mask, :, core]

    known = [0]
    waves = []
    for step in item_bits[::-1]:
        waves.append([(mask, step) for mask in known])
        known = known + [mask ^ step[1] for mask in known]
    arrived = {}
    for wave in waves:
        part = dense_part(0)
        arrived[wave[0][1][1]] = copies.send(part, part, mask_of(wave[0][1]))
    near = [copies.send(dense_part(0), dense_part(0), mask_of(seq_bits[0]))]
    wait_all(shares[:3])
    outer = []
    if len(seq_bits) == 3:
        first = pl.ds(0, 2 * rows)
        outer.append(
            copies.send(own_in_ref.at[0, first], own_in_ref.at[1, first], mask_of(seq_bits[2]))
        )
    for order, step in enumerate(item_bits):
        sums.wait_recv()
        sum_scr[order + 1] = sum_scr[order] + got_scr[order]
        if order + 1 < len(item_bits):
            sums = copies.send(
                sum_scr.at[order + 1], got_scr.at[order + 1], mask_of(item_bits[order + 1])
            )
            wait_all(small[-1:])
            part = everyone_ref.at[aligned(item_place, 2 ** (order + 1))]
            small.append(copies.send(part, part, mask_of(item_bits[order + 1])))
        if order < len(waves) and order + 1 < len(item_bits):
            wave = waves[order]
            for mask, step in wave:
                arrived[mask ^ step[1]].wait_recv()
                part = dense_part(mask ^ step[1])
                for later in waves[order + 1 :]:
                    arrived[mask ^ step[1] ^ later[0][1][1]] = copies.send(
                        part, part, mask_of(later[0][1])
                    )
                near.append(copies.send(part, part, mask_of(seq_bits[0])))
    table_ref[...] = sum_scr[len(item_bits)]

    for mask, step in waves[-1]:
        arrived[mask ^ step[1]].wait_recv()
        part = dense_part(mask ^ step[1])
        near.append(copies.send(part, part, mask_of(seq_bits[0])))
    wait_all(near)
    wait_all(shares[3:])
    wait_all(outer)
    wait_all(small[-1:])
    block_out.wait()
    copies.end()


def first_call(item_bits, seq_bits, small, heads, head_bias, dense, parts_in, parts_out):
    items_size, seq_size = 2 ** len(item_bits), 2 ** len(seq_bits)
    row_count = heads.shape[0] + head_bias.shape[0]
    rows, width = dense.shape
    vocab = small.shape[1]
    columns = heads.shape[1] // seq_size
    any_space = pl.BlockSpec(memory_space=pl.ANY)
    spare = 8 * (len(item_bits) + len(seq_bits)) + 4 * seq_size + 2 ** (len(item_bits) + 2)
    return pl.pallas_call(
        functools.partial(first_kernel, item_bits, seq_bits, row_count),
        in_specs=[any_space] * 6,
        out_specs=[any_space, pl.BlockSpec(memory_space=pltpu.VMEM)] + [any_space] * 4,
        out_shape=[
            jax.ShapeDtypeStruct((items_size, seq_size) + small.shape, bf16),
            jax.ShapeDtypeStruct((vocab, columns), f32),
            jax.ShapeDtypeStruct((seq_size, row_count, columns), bf16),
            jax.ShapeDtypeStruct((items_size, seq_size // 2, 2, rows, width), bf16),
            jax.ShapeDtypeStruct((2, 4 * rows, parts_in.shape[3]), bf16),
            jax.ShapeDtypeStruct((4 * rows, parts_out.shape[3]), bf16),
        ],
        scratch_shapes=[
            pltpu.VMEM((seq_size, row_count, vocab), bf16),
            pltpu.VMEM((seq_size, row_count, columns), bf16),
            pltpu.VMEM((len(item_bits) + 1, vocab, columns), f32),
            pltpu.VMEM((len(item_bits), vocab, columns), f32),
            pltpu.SemaphoreType.DMA((spare,)),
            pltpu.SemaphoreType.DMA((spare,)),
            pltpu.SemaphoreType.DMA((8,)),
        ],
        compiler_params=pltpu.CompilerParams(
            collective_id=0, has_side_effects=True, vmem_limit_bytes=24 * 2**20
        ),
        name="first",
    )(small, heads, head_bias, dense, parts_in, parts_out)


class Spread:
    def __init__(self, copies, own, whole, outer_bits, item_bits, given=None):
        self.copies, self.own, self.whole, self.given = copies, own, whole, given
        self.outer_bits, self.item_bits = outer_bits, item_bits
        half = own.shape[0] // 2
        self.halves = pl.ds(0, half), pl.ds(half, half)
        self.last = []

    def part(self, masks):
        place = (self.copies.here[0] ^ masks[0]) * lax.axis_size("seq")
        return self.whole.at[(place + (self.copies.here[1] ^ masks[1])) // 4]

    def over(self, masks, step, rows=None):
        source = self.own if masks == (0, 0) else self.part(masks)
        target = self.part(masks)
        if rows is not None:
            source, target = source.at[rows], target.at[rows]
        return self.copies.send(source, target, mask_of(step))

    def start(self):
        self.local = self.copies.move(self.own, self.part((0, 0)))
        self.first = [self.over((0, 0), step) for step in self.item_bits]

    def start_given(self):
        masks = mask_of(self.outer_bits[0])
        target = self.part(masks).at[self.halves[0]]
        self.local_given = self.copies.move(self.given, target)
        self.second = [
            [self.copies.send(self.given, target, mask_of(step)) for step in self.item_bits],
            [],
        ]
        self.outer = [None, self.over((0, 0), self.outer_bits[0], self.halves[1])]

    def start_outer(self):
        self.outer = [self.over((0, 0), self.outer_bits[0], rows) for rows in self.halves]
        self.second = [[], []]

    def cross_own(self):
        one, two = self.item_bits
        self.first[0].wait_recv()
        self.last.append(self.over(moved((0, 0), *one), two, self.halves[0]))
        self.first[1].wait_recv()
        self.last.append(self.over(moved((0, 0), *two), one, self.halves[1]))

    def spread_outer(self, which):
        self.outer[which].wait_recv()
        masks = mask_of(self.outer_bits[0])
        self.second[which] = [
            self.over(masks, step, self.halves[which]) for step in self.item_bits
        ]

    def cross_outer(self, which):
        masks = mask_of(self.outer_bits[0])
        steps = self.item_bits if which == 0 else self.item_bits[::-1]
        copies = self.second[which] if which == 0 else self.second[which][::-1]
        copies[0].wait_recv()
        self.last.append(self.over(moved(masks, *steps[0]), steps[1], self.halves[which]))
        self.last.append(copies[1])

    def plain(self):
        self.local = self.copies.move(self.own, self.part((0, 0)))
        known = [(0, 0)]
        for step in self.outer_bits + self.item_bits:
            wait_all([self.over(masks, step) for masks in known])
            known = known + [moved(masks, *step) for masks in known]

    def end(self):
        wait_all(self.last)
        self.local.wait()
        if self.given is not None:
            self.local_given.wait()


def attend_unit(block, visible, onehot_ref, table_ref, cosine_ref, sine_ref, context_ref, lse_ref):
    query, key, value = head_parts(onehot_ref, table_ref, cosine_ref[...], sine_ref[...])
    value_turned = value.T
    for offset in range(0, query.shape[0], block):
        scores = visible_scores(key, query[offset : offset + block], offset, visible)
        peak = jnp.max(scores, axis=0, keepdims=True)
        expos = jnp.exp2((scores - peak) * exponent_scale)
        total = jnp.sum(expos, axis=0, keepdims=True)
        context = dot(value_turned, expos.astype(bf16)) / total
        context_ref[offset : offset + block, :] = context.T.astype(bf16)
        lse_ref[:, offset : offset + block] = peak * exponent_scale + jnp.log2(total)


def second_kernel(
    item_bits,
    seq_bits,
    visible_ref,
    onehot_ref,
    table_ref,
    cosine_ref,
    sine_ref,
    own_onehot_ref,
    embed_ref,
    vector_ref,
    dense_ref,
    own_in_ref,
    own_out_ref,
    context_ref,
    lse_ref,
    in_ref,
    out_ref,
    shared_ref,
    normed_ref,
    inverse_ref,
    context_scr,
    dense_scr,
    resid_scr,
    low_scr,
    send_sems,
    recv_sems,
    local_sems,
):
    seq_size = 2 ** len(seq_bits)
    items_here, length, features = context_scr.shape
    heads_here = features // HEAD
    span = length // seq_size
    width = dense_ref.shape[0]
    seq_place = lax.axis_index("seq")
    outer_bits = seq_bits[2:]
    greet(partners(seq_size, item_bits))
    copies = Copies(send_sems, recv_sems, local_sems)
    dense_copy = copies.move(dense_ref, dense_scr)
    stepwise = len(outer_bits) == 1 and len(item_bits) == 2
    given = own_in_ref.at[1, pl.ds(0, own_in_ref.shape[1] // 2)] if stepwise else None
    spreads = [
        Spread(copies, own_in_ref.at[0], in_ref, outer_bits, item_bits, given),
        Spread(copies, own_out_ref, out_ref, outer_bits, item_bits),
    ]
    if stepwise:
        spreads[0].start()
        spreads[0].start_given()
    arrivals, local = [], []
    for item in range(items_here):

        @pl.loop(0, heads_here)
        def _(head):
            place = pl.ds(pl.multiple_of(head * HEAD, HEAD), HEAD)
            attend_unit(
                min(256, length),
                visible_ref[item],
                onehot_ref.at[item],
                table_ref.at[head],
                cosine_ref,
                sine_ref,
                context_scr.at[item, :, place],
                lse_ref.at[item, head],
            )

        target = context_ref.at[
            item, :, pl.ds(pl.multiple_of(seq_place * features, HEAD), features)
        ]
        for mask in range(seq_size):
            rows = pl.ds(pl.multiple_of((seq_place ^ mask) * span, span), span)
            source = context_scr.at[item, rows]
            if mask:
                arrivals.append(copies.send(source, target, (0, mask)))
            else:
                local.append(copies.move(source, target))
    if stepwise:
        spreads[0].cross_own()
        spreads[0].cross_outer(0)
        spreads[1].start()
        spreads[0].spread_outer(1)
    wait_all(arrivals)
    for copy in local:
        copy.wait()

    if stepwise:
        spreads[1].start_outer()

    dense_copy.wait()
    rows_all = items_here * span
    tile = 256

    @pl.loop(0, width // tile)
    def _(order):
        place = pl.ds(pl.multiple_of(order * tile, tile), tile)
        branch = dot(context_ref[...].reshape(rows_all, width), dense_scr[:, place])
        inputs = contract_cols(own_onehot_ref[...], embed_ref[place, :])
        resid_scr[:, place] = deep_alpha * inputs + (branch + vector_ref[5:6, place])

    block = 32
    near, far = ("seq", 1), ("seq", 2)
    far_copies, near_copies, own_copies = [], [], []
    for item in range(items_here):

        @pl.loop(0, span // block)
        def _(order):
            start = pl.multiple_of(order * block, block)
            rows = pl.ds(pl.multiple_of(item * span + start, block), block)
            normed, inverse = norm_rows(resid_scr[rows, :])
            normed_ref[rows, :] = normed
            inverse_ref[rows, :] = jnp.broadcast_to(inverse, (block, 128))
            hidden = normed * vector_ref[0:1, :] + vector_ref[1:2, :]
            low_scr[item, pl.ds(start, block), :] = hidden.astype(bf16)

        source = low_scr.at[item]
        far_copies.append(copies.send(source, shared_ref.at[item, 1], mask_of(far)))
        near_copies.append(copies.send(source, shared_ref.at[item, 2], mask_of(near)))
        own_copies.append(copies.move(source, shared_ref.at[item, 0]))

    def pass_on(item):
        far_copies[item].wait_recv()
        part = shared_ref.at[item, 1]
        near_copies.append(copies.send(part, shared_ref.at[item, 3], mask_of(near)))

    if stepwise:
        spreads[1].cross_own()
        spreads[0].cross_outer(1)
    pass_on(0)
    if stepwise:
        spreads[1].spread_outer(0)
    pass_on(1)
    if stepwise:
        spreads[1].spread_outer(1)
        spreads[1].cross_outer(0)
    for item in range(2, items_here):
        pass_on(item)
    if stepwise:
        spreads[1].cross_outer(1)
    else:
        for one in spreads:
            one.plain()
    for one in spreads:
        one.end()
    wait_all(near_copies)
    for copy in own_copies:
        copy.wait()
    copies.end()


def second_call(
    item_bits,
    seq_bits,
    visible,
    onehots,
    tables,
    cosine,
    sine_part,
    own_onehot,
    embed,
    vectors,
    w_dense,
    own_in,
    own_out,
):
    items_here, length, vocab = onehots.shape
    heads_here = tables.shape[0]
    features = heads_here * HEAD
    seq_size = 2 ** len(seq_bits)
    span = length // seq_size
    width = w_dense.shape[0]
    groups = 2 ** (len(item_bits) + len(seq_bits)) // 4
    any_space = pl.BlockSpec(memory_space=pl.ANY)
    near_space = pl.BlockSpec(memory_space=pltpu.VMEM)
    spare = 4 * groups + items_here * (seq_size + 4)
    return pl.pallas_call(
        functools.partial(second_kernel, item_bits, seq_bits),
        in_specs=[pl.BlockSpec(memory_space=pltpu.SMEM)] + [near_space] * 7 + [any_space] * 3,
        out_specs=[near_space] * 2 + [any_space] * 3 + [near_space] * 2,
        out_shape=[
            jax.ShapeDtypeStruct((items_here, span, width), bf16),
            jax.ShapeDtypeStruct((items_here, heads_here, 1, length), f32),
            jax.ShapeDtypeStruct((groups,) + own_in.shape[1:], bf16),
            jax.ShapeDtypeStruct((groups,) + own_out.shape, bf16),
            jax.ShapeDtypeStruct((items_here, 4, span, width), bf16),
            jax.ShapeDtypeStruct((items_here * span, width), f32),
            jax.ShapeDtypeStruct((items_here * span, 128), f32),
        ],
        scratch_shapes=[
            pltpu.VMEM((items_here, length, features), bf16),
            pltpu.VMEM((width, width), bf16),
            pltpu.VMEM((items_here * span, width), f32),
            pltpu.VMEM((items_here, span, width), bf16),
            pltpu.SemaphoreType.DMA((spare,)),
            pltpu.SemaphoreType.DMA((spare,)),
            pltpu.SemaphoreType.DMA((16,)),
        ],
        compiler_params=pltpu.CompilerParams(
            collective_id=1, has_side_effects=True, vmem_limit_bytes=56 * 2**20
        ),
        name="second",
    )(
        visible,
        onehots,
        tables,
        cosine,
        sine_part,
        own_onehot,
        embed,
        vectors,
        w_dense,
        own_in,
        own_out,
    )


def leading(ref):
    return [index for index in np.ndindex(*ref.shape[:-2])]


def add_into(target, source):
    rows = target.shape[-2]
    for index in leading(target):

        @pl.loop(0, rows // 16)
        def _(order):
            place = index + (pl.ds(pl.multiple_of(order * 16, 16), 16),)
            total = target[place].astype(f32) + source[place].astype(f32)
            target[place] = total.astype(target.dtype)


def copy_into(target, source):
    @pl.loop(0, target.shape[0] // 16)
    def _(order):
        place = pl.ds(pl.multiple_of(order * 16, 16), 16)
        target[place] = source[place]


class Reduce:
    def __init__(self, copies, whole, rows, dims, steps, got, stage, stage_sems):
        self.copies, self.whole, self.rows = copies, whole, rows
        self.steps, self.got = steps, got
        self.place = dims.index(steps[0])
        self.stage, self.stage_sems = stage, stage_sems
        self.order = 0

    def first(self, bit, index=()):
        full = (slice(None),) * self.place
        if index:
            full = index[: self.place]
        rest = index[self.place :] if index else ()
        if index:
            return self.whole.at[full + (bit,) + rest + (self.rows,)]
        spare = len(self.whole.shape) - 3 - self.place
        return self.whole.at[full + (bit,) + (slice(None),) * spare + (self.rows,)]

    def start(self):
        step = self.steps[0]
        self.copy = self.copies.send(self.first(1 - my_bit(*step)), self.got[0], mask_of(step))

    def advance(self):
        step = self.steps[self.order]
        self.copy.wait_recv()
        if self.order == 0:
            self.kept = self.got[0]
            rows, columns = self.kept.shape[-2:]
            places = leading(self.kept)

            def load(order):
                return pltpu.make_async_copy(
                    self.first(my_bit(*step), places[order]),
                    self.stage.at[order % 2, pl.ds(0, rows), pl.ds(0, columns)],
                    self.stage_sems.at[order % 2],
                )

            load(0).start()
            for order, place in enumerate(places):
                if order + 1 < len(places):
                    load(order + 1).start()
                load(order).wait()
                add_into(
                    self.kept.at[place],
                    self.stage.at[order % 2, pl.ds(0, rows), pl.ds(0, columns)],
                )
        else:
            self.kept = self.kept.at[my_bit(*step)]
            add_into(self.kept, self.got[self.order])
        self.order += 1
        if self.order < len(self.steps):
            step = self.steps[self.order]
            self.copy = self.copies.send(
                self.kept.at[1 - my_bit(*step)], self.got[self.order], mask_of(step)
            )


def attend_back_unit(
    block,
    visible,
    onehot_ref,
    table_ref,
    cosine_ref,
    sine_ref,
    lse_ref,
    grad_ref,
    mixed_ref,
    sums_ref,
):
    cosine, sine_part = cosine_ref[...], sine_ref[...]
    query, key, value = head_parts(onehot_ref, table_ref, cosine, sine_part)
    key_turned = key.T
    length = query.shape[0]
    grad_key = jnp.zeros((length, HEAD), f32)
    grad_value = jnp.zeros((length, HEAD), f32)
    grad_query = []
    for offset in range(0, length, block):
        query_block = query[offset : offset + block]
        grad_block = grad_ref[offset : offset + block, :]
        scores = visible_scores(key, query_block, offset, visible)
        weights = jnp.exp2(scores * exponent_scale - lse_ref[:, offset : offset + block])
        grad_weights = contract_cols(value, grad_block)
        inner = jnp.sum(weights * grad_weights, axis=0, keepdims=True)
        grad_scores = (weights * (grad_weights - inner)).astype(bf16)
        grad_value = grad_value + dot(weights.astype(bf16), grad_block)
        grad_key = grad_key + dot(grad_scores, query_block)
        grad_query.append(dot(key_turned, grad_scores).T)
    grad_query = jnp.concatenate(grad_query, axis=0)

    def back(grad):
        return turn((grad * score_scale).astype(bf16).astype(f32), cosine, -sine_part).astype(bf16)

    mixed = jnp.concatenate([back(grad_query), back(grad_key), grad_value.astype(bf16)], axis=1)
    mixed_ref[...] = mixed.reshape(mixed_ref.shape)
    sums_ref[...] += dot(onehot_ref[...].T, mixed)


def third_kernel(
    item_bits,
    seq_bits,
    visible_ref,
    onehot_ref,
    table_ref,
    cosine_ref,
    sine_ref,
    lse_ref,
    slice_ref,
    grad_ref,
    in_ref,
    out_ref,
    dense_ref,
    bias_ref,
    spread_ref,
    sums_all_ref,
    in_part_ref,
    out_part_ref,
    dense_part_ref,
    bias_sum_ref,
    mixed_scr,
    other_scr,
    kept_scr,
    step_scrs,
    sums_scr,
    sums_got,
    bias_scr,
    bias_got,
    in_got,
    out_got,
    dense_got,
    in_final,
    out_final,
    stage_scr,
    stage_sems,
    send_sems,
    recv_sems,
    local_sems,
):
    seq_size = 2 ** len(seq_bits)
    items_here, length, features = grad_ref.shape
    heads_here = features // HEAD
    seq_place = lax.axis_index("seq")
    member = seq_place % 4
    outer_bits = seq_bits[2:]
    width = slice_ref.shape[1]
    greet(partners(seq_size, item_bits))
    copies = Copies(send_sems, recv_sems, local_sems)
    dims = item_bits[::-1] + outer_bits[::-1]

    def reducers(whole, got):
        rows = whole.shape[-2]
        if len(item_bits) == 2:
            one, two = item_bits
            ways = [
                (pl.ds(0, rows // 2), [two, one] + outer_bits[::-1]),
                (pl.ds(rows // 2, rows // 2), [one, two] + outer_bits[::-1]),
            ]
        else:
            ways = [(pl.ds(0, rows), dims)]
        return [
            Reduce(copies, whole, part, dims, steps, list(got[order]), stage_scr, stage_sems)
            for order, (part, steps) in enumerate(ways)
        ]

    in_sums = reducers(in_ref, in_got)
    out_sums = reducers(out_ref, out_got)
    dense_steps = (item_bits[::-1] + seq_bits[:0:-1])[1:]
    dense_sum = Reduce(
        copies,
        dense_ref,
        pl.ds(0, dense_ref.shape[-2]),
        dense_steps,
        dense_steps,
        list(dense_got),
        stage_scr,
        stage_sems,
    )
    for one in in_sums + out_sums:
        one.start()
    sums_scr[...] = jnp.zeros_like(sums_scr)
    tile = 256
    flying = {}
    sums_copy = None

    def next_sum(order):
        nonlocal sums_copy
        sums_copy.wait_recv()
        sums_scr[order + 1] = sums_scr[order] + sums_got[order]
        if order + 1 < len(item_bits):
            sums_copy = copies.send(
                sums_scr.at[order + 1], sums_got.at[order + 1], mask_of(item_bits[order + 1])
            )

    bias_scr[0] = bias_ref[...]
    bias_steps = seq_bits + item_bits
    bias_copies = [copies.send(bias_scr.at[0], bias_got.at[0], mask_of(bias_steps[0]))]
    for stage in range(items_here + len(seq_bits)):
        if stage < items_here:

            @pl.loop(0, heads_here)
            def _(head):
                place = pl.ds(pl.multiple_of(head * HEAD, HEAD), HEAD)
                packed = pl.ds(pl.multiple_of(head * 3 * HEAD, HEAD), 3 * HEAD)
                attend_back_unit(
                    min(256, length),
                    visible_ref[stage],
                    onehot_ref.at[stage],
                    table_ref.at[head],
                    cosine_ref,
                    sine_ref,
                    lse_ref.at[stage, head],
                    grad_ref.at[stage, :, place],
                    mixed_scr.at[:, :, :, packed],
                    sums_scr.at[0, head],
                )

        for order in range(len(seq_bits) - 1, -1, -1):
            item = stage - 1 - order
            if not 0 <= item < items_here:
                continue
            copy, kept = flying[item]
            copy.wait_recv()
            got = step_scrs[order].at[item % 2]
            if order:
                full = (slice(None),) * (len(kept.shape) - 3)
                kept = kept.at[full + (my_bit(*seq_bits[order]),)]
            if order + 1 < len(seq_bits):
                add_into(kept, got)
                step = seq_bits[order + 1]
                full = (slice(None),) * (len(kept.shape) - 3)
                copy = copies.send(
                    kept.at[full + (1 - my_bit(*step),)],
                    step_scrs[order + 1].at[item % 2],
                    mask_of(step),
                )
                flying[item] = copy, kept
                flying["later", item].append(copy)
            else:

                @pl.loop(0, kept.shape[0] // 16)
                def _(block):
                    place = (pl.ds(pl.multiple_of(block * 16, 16), 16),)
                    total = kept[place].astype(f32) + got[place].astype(f32)
                    spread_ref[(item,) + place] = total.astype(bf16)

        if stage < items_here:
            core = my_bit(*seq_bits[0])
            slot = stage % 2
            if stage >= 2:
                copies.sent_now(flying["first", stage - 2])
            kept_slot = stage % len(seq_bits)
            if stage >= len(seq_bits):
                for copy in flying["later", stage - len(seq_bits)]:
                    copies.sent_now(copy)
            half = mixed_scr.shape[0] * mixed_scr.shape[2]
            other = mixed_scr[:, 1 - core].reshape(half, -1)
            mine = mixed_scr[:, core].reshape(half, -1)

            @pl.loop(0, width // tile)
            def _(order):
                place = pl.ds(pl.multiple_of(order * tile, tile), tile)
                weights = slice_ref[:, place]
                target = other_scr.at[slot]
                target[..., place] = dot(other, weights).astype(bf16).reshape(
                    target.shape[:-1] + (tile,)
                )
                target = kept_scr.at[kept_slot]
                target[..., place] = dot(mine, weights).astype(bf16).reshape(
                    target.shape[:-1] + (tile,)
                )

            copy = copies.send(
                other_scr.at[slot], step_scrs[0].at[slot], mask_of(seq_bits[0])
            )
            flying[stage] = copy, kept_scr.at[kept_slot]
            flying["first", stage] = copy
            flying["later", stage] = []
        if stage == 1:
            dense_sum.start()
        if stage == items_here - 1:
            sums_copy = copies.send(sums_scr.at[0], sums_got.at[0], mask_of(item_bits[0]))
        if stage == items_here:
            for one in in_sums:
                one.advance()
        if stage == items_here + 1:
            next_sum(0)
            for one in in_sums:
                one.advance()
            for one in out_sums:
                one.advance()
        if stage == items_here + 2:
            for order in range(1, len(item_bits)):
                next_sum(order)
            for one in out_sums:
                one.advance()

        bias_done = len(bias_copies)
        if bias_done <= len(bias_steps):
            bias_copies[-1].wait_recv()
            bias_scr[bias_done] = bias_scr[bias_done - 1] + bias_got[bias_done - 1]
            if bias_done < len(bias_steps):
                bias_copies.append(
                    copies.send(
                        bias_scr.at[bias_done],
                        bias_got.at[bias_done],
                        mask_of(bias_steps[bias_done]),
                    )
                )
            else:
                bias_copies.append(None)
                bias_sum_ref[...] = bias_scr[bias_done]

    sums_all_ref[seq_place] = sums_scr[len(item_bits)].astype(bf16)
    known = [0]
    arrivals = []
    for axis, bit in seq_bits[::-1]:
        wait_all(arrivals)
        arrivals = []
        for mask in known:
            part = sums_all_ref.at[seq_place ^ mask]
            arrivals.append(copies.send(part, part, (0, bit)))
        known = known + [mask ^ bit for mask in known]
        if dense_sum.order < len(dense_steps):
            dense_sum.advance()

    while in_sums[0].order < len(dims):
        for one in in_sums + out_sums:
            if one.order < len(dims):
                one.advance()
        if dense_sum.order < len(dense_steps):
            dense_sum.advance()
    while out_sums[0].order < len(dims):
        for one in out_sums:
            one.advance()
    wait_all(arrivals)
    shares, local = [], []
    for sums, final, target in (
        (in_sums, in_final, in_part_ref),
        (out_sums, out_final, out_part_ref),
    ):
        rows = target.shape[1]
        first = 0
        for one in sums:
            copy_into(final.at[pl.ds(first, one.kept.shape[0])], one.kept)
            first += one.kept.shape[0]
        for mask in range(4):
            source = final.at[pl.ds(pl.multiple_of((member ^ mask) * rows, 16), rows)]
            if mask:
                shares.append(copies.send(source, target.at[member], (0, mask)))
            else:
                local.append(copies.move(source, target.at[member]))
    while dense_sum.order < len(dense_steps):
        dense_sum.advance()
    dense_part_ref[...] = dense_sum.kept[...]
    wait_all(shares)
    for copy in local:
        copy.wait()
    copies.end()


def third_call(
    item_bits,
    seq_bits,
    visible,
    onehots,
    tables,
    cosine,
    sine_part,
    log_sums,
    w_slice,
    grad_context,
    grad_in,
    grad_out,
    by_rows,
    in_sum,
):
    items_here, length, vocab = onehots.shape
    heads_here = tables.shape[0]
    seq_size = 2 ** len(seq_bits)
    span = length // seq_size
    width = w_slice.shape[1]
    packed = heads_here * 3 * HEAD
    outer = len(seq_bits) - 2
    levels = len(item_bits) + outer
    any_space = pl.BlockSpec(memory_space=pl.ANY)
    near_space = pl.BlockSpec(memory_space=pltpu.VMEM)

    def got_shapes(whole, ways, depth):
        rows, columns = whole.shape[-2:]
        one = tuple(
            pltpu.VMEM((2,) * order + (rows // ways, columns), bf16)
            for order in range(depth - 1, -1, -1)
        )
        return one

    ways = 2 if len(item_bits) == 2 else 1
    group_rows = grad_in.shape[-2]
    rows = group_rows // 4
    dense_depth = len(item_bits) + len(seq_bits) - 2
    spread = (2,) * (len(seq_bits) - 1) + (span, width)
    all_bits = len(item_bits) + len(seq_bits)
    spare = 8 * items_here + 8 * levels + 16 * all_bits
    stage_rows = max(group_rows // ways, by_rows.shape[-2])
    return pl.pallas_call(
        functools.partial(third_kernel, item_bits, seq_bits),
        in_specs=[pl.BlockSpec(memory_space=pltpu.SMEM)]
        + [near_space] * 7
        + [any_space] * 3
        + [near_space],
        out_specs=[near_space, near_space, any_space, any_space, near_space, near_space],
        out_shape=[
            jax.ShapeDtypeStruct((items_here, span, width), bf16),
            jax.ShapeDtypeStruct((seq_size, heads_here, vocab, 3 * HEAD), bf16),
            jax.ShapeDtypeStruct((4, rows, grad_in.shape[-1]), bf16),
            jax.ShapeDtypeStruct((4, rows, grad_out.shape[-1]), bf16),
            jax.ShapeDtypeStruct(by_rows.shape[-2:], bf16),
            jax.ShapeDtypeStruct(in_sum.shape, f32),
        ],
        scratch_shapes=[
            pltpu.VMEM((seq_size // 2, 2, span, packed), bf16),
            pltpu.VMEM((2,) + spread, bf16),
            pltpu.VMEM((len(seq_bits),) + spread, bf16),
            tuple(pltpu.VMEM((2,) + spread[order:], bf16) for order in range(len(seq_bits))),
            pltpu.VMEM((len(item_bits) + 1, heads_here, vocab, 3 * HEAD), f32),
            pltpu.VMEM((len(item_bits), heads_here, vocab, 3 * HEAD), f32),
            pltpu.VMEM((all_bits + 1,) + in_sum.shape, f32),
            pltpu.VMEM((all_bits,) + in_sum.shape, f32),
            tuple(got_shapes(grad_in, ways, levels) for _ in range(ways)),
            tuple(got_shapes(grad_out, ways, levels) for _ in range(ways)),
            got_shapes(by_rows, 1, dense_depth),
            pltpu.VMEM((group_rows, grad_in.shape[-1]), bf16),
            pltpu.VMEM((group_rows, grad_out.shape[-1]), bf16),
            pltpu.VMEM((2, stage_rows, grad_in.shape[-1]), bf16),
            pltpu.SemaphoreType.DMA((2,)),
            pltpu.SemaphoreType.DMA((spare,)),
            pltpu.SemaphoreType.DMA((spare,)),
            pltpu.SemaphoreType.DMA((8,)),
        ],
        compiler_params=pltpu.CompilerParams(
            collective_id=2, has_side_effects=True, vmem_limit_bytes=60 * 2**20
        ),
        name="third",
    )(
        visible,
        onehots,
        tables,
        cosine,
        sine_part,
        log_sums,
        w_slice,
        grad_context,
        grad_in,
        grad_out,
        by_rows,
        in_sum,
    )


def ff_kernel(
    item_bits,
    shared_ref,
    normed_ref,
    inverse_ref,
    cotangent_ref,
    in_ref,
    out_ref,
    vector_ref,
    bias_ref,
    block_ref,
    product_ref,
    saved_ref,
    grad_shared_ref,
    grad_in_ref,
    layer_ref,
    resid_ref,
    sums_ref,
    in_sum_ref,
    slices_ref,
    rows_scr,
    product_scr,
    save_scr,
    parts_scr,
    near_got,
    far_got,
    low_scr,
    grad_in_scr,
    resid_scr,
    normed_scr,
    gate_scr,
    send_sems,
    recv_sems,
    load_sems,
    keep_sems,
):
    chunks, blocks, span, width = shared_ref.shape
    group_rows = blocks * span
    tiles = product_scr.shape[-1] // 128
    tile = 256
    near, far = ("seq", 1), ("seq", 2)
    greet([mask_of(near), mask_of(far)] + [mask_of(step) for step in item_bits])
    copies = Copies(send_sems, recv_sems, keep_sems)
    item_place = copies.here[0]
    slices = copies.move(block_ref, slices_ref.at[item_place])
    slices.wait()
    spread = []

    def spread_block():
        order = len(spread)
        if order < len(item_bits):
            wait_all(spread[-1:])
            part = slices_ref.at[aligned(item_place, 2**order)]
            spread.append(copies.send(part, part, mask_of(item_bits[order])))

    spread_block()
    keeps, loads = {}, {}
    state = {}
    gain_one, shift_one, b_down, gain_two, shift_two = range(5)
    for line in range(sums_ref.shape[0]):
        sums_ref[line : line + 1, :] = jnp.zeros((1, width), f32)
    in_sum_ref[...] = jnp.zeros_like(in_sum_ref)

    def load(name, slot, source, target):
        copy = pltpu.make_async_copy(source, target, load_sems.at[slot])
        copy.start()
        loads[name] = copy

    def loaded(name):
        loads.pop(name).wait()

    def keep(name, slot, source, target):
        copy = pltpu.make_async_copy(source, target, keep_sems.at[1 + slot])
        copy.start()
        keeps[name] = copy

    def keep_done(name):
        if name in keeps:
            keeps.pop(name).wait()

    def load_shared(chunk):
        slot = chunk % 2
        load(("rows", slot), slot, shared_ref.at[chunk], rows_scr.at[slot])

    def load_normed(chunk):
        slot = chunk % 2
        rows = pl.ds(chunk * span, span)
        load(("normed", slot), 2 + slot, normed_ref.at[rows], normed_scr.at[slot])

    def forward_gate(chunk):
        slot = chunk % 2
        loaded(("rows", slot))
        if chunk + 1 < chunks:
            load_shared(chunk + 1)
        keep_done(("product", slot))
        keep_done(("save", slot))
        rows = rows_scr.at[slot]

        def multiply(order, place):
            columns = pl.ds(pl.multiple_of(order * tile, tile), tile)
            gate_scr[place] = (
                dot(rows[...].reshape(group_rows, width), in_ref[:, columns])
                + bias_ref[:, columns]
            )

        def finish(order, place):
            gate_up = gate_scr[place]
            up_part, gate = gate_up[:, :128], gate_up[:, 128:]
            below = 0.5 * (1.0 + lax.erf(gate * (0.5**0.5)))
            activated = gate * below
            slope = below + gate * jnp.exp(-0.5 * gate * gate) * (1.0 / math.sqrt(2.0 * math.pi))
            columns = pl.ds(pl.multiple_of(order * 128, 128), 128)
            product_scr[slot, :, columns] = (up_part * activated).astype(bf16)
            save_scr[slot, 0, :, columns] = activated.astype(bf16)
            save_scr[slot, 1, :, columns] = (up_part * slope).astype(bf16)

        multiply(0, 0)

        @pl.loop(0, (tiles - 1) // 2)
        def _(pair):
            finish(2 * pair, 0)
            multiply(2 * pair + 1, 1)
            finish(2 * pair + 1, 1)
            multiply(2 * pair + 2, 0)

        if tiles % 2 == 0:
            multiply(tiles - 1, 1)
            finish(tiles - 2, 0)
            finish(tiles - 1, 1)
        else:
            finish(tiles - 1, 0)
        keep(("product", slot), slot, product_scr.at[slot], product_ref.at[chunk])
        keep(("save", slot), 2 + slot, save_scr.at[slot], saved_ref.at[chunk])

    def send_near(name, slot):
        source = parts_scr.at[slot, pl.ds(2, 2)]
        state["near", name] = copies.send(source, near_got.at[slot], mask_of(near))

    def free_parts(slot):
        for key in ("near", "far"):
            copy = state.pop((key, "of", slot), None)
            if copy is not None:
                copies.sent_now(copy)

    def times_turned(name, slot, left, weights_ref):
        free_parts(slot)

        @pl.loop(0, width // tile)
        def _(order):
            place = pl.ds(pl.multiple_of(order * tile, tile), tile)
            total = contract_cols(left[...], weights_ref[place, :])
            parts_scr[slot, :, :, place] = total.astype(bf16).reshape(blocks, span, tile)

        send_near(name, slot)
        state["near", "of", slot] = state["near", name]

    def forward_out(chunk):
        times_turned(chunk, chunk % 2, product_scr.at[chunk % 2], out_ref)

    def sum_near(name, chunk):
        slot = chunk % 2
        state["near", name].wait_recv()
        add_into(parts_scr.at[slot, pl.ds(0, 2)], near_got.at[slot])
        copy = copies.send(parts_scr.at[slot, 1], far_got.at[chunk], mask_of(far))
        state["far", name] = copy
        state["far", "of", slot] = copy

    block = 32

    def row_blocks(function):
        @pl.loop(0, span // block)
        def _(order):
            function(pl.ds(pl.multiple_of(order * block, block), block))

    def line(index):
        return vector_ref[index : index + 1, :]

    def add_sum(index, rows):
        sums_ref[index : index + 1, :] += jnp.sum(rows, axis=0, keepdims=True)

    def second_norm(chunk):
        slot = chunk % 2
        state["far", chunk].wait_recv()
        loaded(("normed", slot))
        for key in ("low near", "low far"):
            copy = state.pop((key, slot), None)
            if copy is not None:
                copies.sent_now(copy)
        keep_done(("low", slot))

        def body(rows):
            hidden = normed_scr[slot, rows] * line(gain_one) + line(shift_one)
            mlp_branch = parts_scr[slot, 0, rows].astype(f32) + far_got[chunk, rows].astype(f32)
            normed, inverse = norm_rows(deep_alpha * hidden + mlp_branch + line(b_down))
            layer_ref[chunk, rows] = (normed * line(gain_two) + line(shift_two)).astype(bf16)
            grad = cotangent_ref[chunk, rows].astype(f32)
            resid = norm_rows_back(grad, normed, inverse, line(gain_two))
            low = resid.astype(bf16)
            resid_scr[chunk, rows] = resid
            low_scr[slot, rows] = low
            add_sum(3, grad * normed)
            add_sum(4, grad)
            add_sum(5, low.astype(f32))

        row_blocks(body)
        if chunk + 2 < chunks:
            load_normed(chunk + 2)
        source = low_scr.at[slot]
        keep(("low", slot), 4 + slot, source, grad_shared_ref.at[chunk, 0])
        state["low far", slot] = copies.send(source, grad_shared_ref.at[chunk, 1], mask_of(far))
        state["low near", slot] = copies.send(source, grad_shared_ref.at[chunk, 2], mask_of(near))
        state["grad far", chunk] = state["low far", slot]
        state["grad near", chunk] = state["low near", slot]

    def pass_on(chunk):
        state["grad far", chunk].wait_recv()
        part = grad_shared_ref.at[chunk, 1]
        state["grad cross", chunk] = copies.send(
            part, grad_shared_ref.at[chunk, 3], mask_of(near)
        )

    def load_grads(chunk):
        slot = chunk % 2
        keep_done(("low", slot))
        state["grad near", chunk].wait_recv()
        state["grad cross", chunk].wait_recv()
        load(("rows", slot), slot, grad_shared_ref.at[chunk], rows_scr.at[slot])
        keep_done(("save", slot))
        load(("save", slot), 4 + slot, saved_ref.at[chunk], save_scr.at[slot])

    def backward_gate(chunk):
        slot = chunk % 2
        loaded(("rows", slot))
        loaded(("save", slot))
        keep_done("grad in")
        rows = rows_scr.at[slot]

        def columns_of(first, count):
            columns = pl.ds(pl.multiple_of(first * 128, 128), count * 128)
            grad = dot(rows[...].reshape(group_rows, width), out_ref[:, columns])
            for order in range(count):
                part = grad[:, order * 128 : (order + 1) * 128]
                saved = pl.ds(pl.multiple_of((first + order) * 128, 128), 128)
                for which in range(2):
                    low = (part * save_scr[slot, which, :, saved].astype(f32)).astype(bf16)
                    place = pl.ds(
                        pl.multiple_of((2 * (first + order) + which) * 128, 128), 128
                    )
                    grad_in_scr[:, place] = low
                    in_sum_ref[:, place] += jnp.sum(low.astype(f32), axis=0, keepdims=True)

        @pl.loop(0, tiles // 2)
        def _(pair):
            columns_of(2 * pair, 2)

        if tiles % 2:
            columns_of(tiles - 1, 1)
        keep("grad in", 6, grad_in_scr, grad_in_ref.at[chunk])

    def backward_in(chunk):
        times_turned(("back", chunk), chunk % 2, grad_in_scr, in_ref)

    def first_norm(chunk):
        slot = chunk % 2
        state["far", ("back", chunk)].wait_recv()
        loaded(("normed", slot))

        def body(rows):
            grad = parts_scr[slot, 0, rows].astype(f32) + far_got[chunk, rows].astype(f32)
            grad = grad + deep_alpha * resid_scr[chunk, rows]
            normed = normed_scr[slot, rows]
            place = pl.ds(pl.multiple_of(chunk * span + rows.start, block), block)
            resid = norm_rows_back(grad, normed, inverse_ref[place, 0:1], line(gain_one))
            resid_scr[chunk, rows] = resid
            add_sum(0, grad * normed)
            add_sum(1, grad)
            add_sum(2, resid.astype(bf16).astype(f32))

        row_blocks(body)
        if chunk + 2 < chunks:
            load_normed(chunk + 2)
        keep(("resid", chunk), 7 + chunk, resid_scr.at[chunk], resid_ref.at[chunk])

    load_shared(0)
    load_normed(0)
    load_normed(1)
    last = chunks - 1
    for chunk in range(chunks):
        forward_gate(chunk)
        if chunk >= 1:
            sum_near(chunk - 1, chunk - 1)
        if chunk >= 2:
            second_norm(chunk - 2)
        if chunk >= 3:
            pass_on(chunk - 3)
        forward_out(chunk)
    sum_near(last, last)
    second_norm(last - 1)
    pass_on(last - 2)
    waiting = [("norm", last), ("pass", last - 1), ("pass", last)]
    for chunk in range(chunks):
        if chunk == 0:
            load_grads(0)
        backward_gate(chunk)
        spread_block()
        if waiting and waiting[0][0] == "norm":
            second_norm(waiting.pop(0)[1])
            load_normed(0)
            load_normed(1)
        if waiting:
            pass_on(waiting.pop(0)[1])
        if chunk >= 1:
            sum_near(("back", chunk - 1), chunk - 1)
        if chunk >= 2:
            first_norm(chunk - 2)
        if chunk + 1 < chunks:
            if chunk + 1 == last and waiting:
                pass_on(waiting.pop(0)[1])
            load_grads(chunk + 1)
        backward_in(chunk)
    sum_near(("back", last), last)
    first_norm(last - 1)
    first_norm(last)
    wait_all(spread[-1:])
    for name in list(keeps):
        keep_done(name)
    copies.end()


def ff_call(
    item_bits, shared, normed, inverse, cotangent, w_in, w_out, vectors, in_bias, block
):
    chunks, blocks, span, width = shared.shape
    group_rows = blocks * span
    ff_part = w_out.shape[1]
    any_space = pl.BlockSpec(memory_space=pl.ANY)
    near_space = pl.BlockSpec(memory_space=pltpu.VMEM)
    spare = 8 * chunks
    return pl.pallas_call(
        functools.partial(ff_kernel, item_bits),
        in_specs=[any_space, any_space] + [near_space] * 6 + [any_space],
        out_specs=[any_space] * 4 + [near_space, any_space, near_space, near_space, any_space],
        out_shape=[
            jax.ShapeDtypeStruct((chunks, group_rows, ff_part), bf16),
            jax.ShapeDtypeStruct((chunks, 2, group_rows, ff_part), bf16),
            jax.ShapeDtypeStruct((chunks, blocks, span, width), bf16),
            jax.ShapeDtypeStruct((chunks, group_rows, 2 * ff_part), bf16),
            jax.ShapeDtypeStruct((chunks, span, width), bf16),
            jax.ShapeDtypeStruct((chunks, span, width), f32),
            jax.ShapeDtypeStruct((8, width), f32),
            jax.ShapeDtypeStruct((1, 2 * ff_part), f32),
            jax.ShapeDtypeStruct((2 ** len(item_bits),) + block.shape, bf16),
        ],
        scratch_shapes=[
            pltpu.VMEM((2, blocks, span, width), bf16),
            pltpu.VMEM((2, group_rows, ff_part), bf16),
            pltpu.VMEM((2, 2, group_rows, ff_part), bf16),
            pltpu.VMEM((2, blocks, span, width), bf16),
            pltpu.VMEM((2, 2, span, width), bf16),
            pltpu.VMEM((chunks, span, width), bf16),
            pltpu.VMEM((2, span, width), bf16),
            pltpu.VMEM((group_rows, 2 * ff_part), bf16),
            pltpu.VMEM((chunks, span, width), f32),
            pltpu.VMEM((2, span, width), f32),
            pltpu.VMEM((2, group_rows, 256), f32),
            pltpu.SemaphoreType.DMA((spare,)),
            pltpu.SemaphoreType.DMA((spare,)),
            pltpu.SemaphoreType.DMA((6,)),
            pltpu.SemaphoreType.DMA((8 + chunks,)),
        ],
        compiler_params=pltpu.CompilerParams(
            collective_id=3, has_side_effects=True, vmem_limit_bytes=60 * 2**20
        ),
        name="feed_forward",
    )(shared, normed, inverse, cotangent, w_in, w_out, vectors, in_bias, block)


def on_device(
    token_ids,
    masked,
    item_flag,
    prefix,
    cotangent,
    embedding,
    heads_weight,
    heads_bias,
    dense_weight,
    dense_bias,
    first_gain,
    first_bias,
    up_weight,
    up_bias,
    down_weight,
    down_bias,
    second_gain,
    second_bias,
):
    lines = Lines()
    items_here, span = token_ids.shape
    items_size, seq_size = lax.axis_size("items"), lax.axis_size("seq")
    item_place, seq_place = lax.axis_index("items"), lax.axis_index("seq")
    count = items_size * seq_size
    length = span * seq_size
    width = embedding.shape[0] * count
    vocab = embedding.shape[1]
    heads_here = HEADS // seq_size
    packed_width = heads_here * 3 * HEAD
    rows_here = up_weight.shape[0]
    ff_width = down_weight.shape[0]
    members = 4
    groups = count // members
    member = seq_place % members
    ff_part = -(-ff_width // (members * 128)) * 128
    ff_all = members * ff_part

    item_bits, seq_bits = bits_of("items"), bits_of("seq")
    outer_bits = seq_bits[2:]

    input_ids = jnp.where(masked == 1, mask_token, token_ids)
    flat_place = item_place * seq_size + seq_place
    row_count = rows_here + 16
    bias_row = lax.dynamic_update_slice(
        jnp.zeros((16, heads_weight.shape[1]), bf16),
        heads_bias[None],
        (0, flat_place * heads_bias.shape[0]),
    )
    ones_row = jnp.zeros((16, vocab), bf16).at[0].set(1.0)
    small = [
        embedding.reshape(-1),
        ones_row.reshape(-1),
        input_ids.astype(bf16).reshape(-1),
        dense_bias,
        first_gain,
        first_bias,
        down_bias,
        second_gain,
        second_bias,
    ]
    ends = [0]
    for part in small:
        ends.append(ends[-1] + part.shape[0])
    flat = jnp.concatenate(small)
    flat = jnp.pad(flat, (0, -flat.shape[0] % 2048)).reshape(-1, 128)

    def by_member(part):
        padded = jnp.pad(part, ((0, 0), (0, ff_all - ff_width)))
        return jnp.transpose(padded.reshape(rows_here, 2, 2, ff_part), (1, 2, 0, 3))

    tiles = ff_part // 128

    def woven(up, gate):
        shape = up.shape[:-1] + (tiles, 128)
        return jnp.stack([up.reshape(shape), gate.reshape(shape)], axis=-2).reshape(
            up.shape[:-1] + (2 * ff_part,)
        )

    def unwoven(both_parts):
        parts = both_parts.reshape(both_parts.shape[:-1] + (tiles, 2, 128))
        shape = both_parts.shape[:-1] + (ff_part,)
        return parts[..., 0, :].reshape(shape), parts[..., 1, :].reshape(shape)

    parts_in = woven(by_member(up_weight[:, :ff_width]), by_member(up_weight[:, ff_width:]))
    parts_out = by_member(down_weight.T)
    everyone, mixed_table, w_block, w_dense, own_in, own_out = first_call(
        item_bits,
        seq_bits,
        flat,
        heads_weight,
        bias_row,
        dense_weight,
        parts_in,
        parts_out,
    )
    w_dense = w_dense.reshape(width, width)
    w_block = w_block[:, :rows_here].reshape(seq_size * rows_here, packed_width)
    everyone = everyone.reshape(count, -1)
    pieces = [everyone[:, a:b] for a, b in zip(ends[:-1], ends[1:])]
    table = pieces[0].reshape(width, vocab)
    b_dense, gain_one, shift_one, b_down, gain_two, shift_two = (
        part.reshape(-1).astype(f32) for part in pieces[3:]
    )
    ids_here = pick(pieces[2].reshape(items_size, seq_size, items_here, span), item_place, 0)
    ids_here = jnp.transpose(ids_here, (1, 0, 2)).reshape(items_here, length).astype(jnp.int32)
    in_bias = jnp.pad(
        up_bias.astype(f32).reshape(2, ff_width), ((0, 0), (0, ff_all - ff_width))
    )
    in_bias = lax.dynamic_slice(in_bias, (0, member * ff_part), (2, ff_part))
    in_bias = woven(in_bias[:1], in_bias[1:])

    vocab_index = jnp.arange(vocab, dtype=jnp.int32)
    positions = jnp.arange(length, dtype=f32)
    frequency = jnp.exp(jnp.arange(HEAD // 2, dtype=f32) * (-2.0 * math.log(10000.0) / HEAD))
    angles = positions[:, None] * frequency[None, :]
    cosine = jnp.cos(angles)
    sine_part = jnp.sin(angles)
    cosine = jnp.concatenate([cosine, cosine], axis=1)
    sine_part = jnp.concatenate([-sine_part, sine_part], axis=1)
    visible = jnp.where(item_flag == 1, length, prefix)
    tables = table_halves(mixed_table)
    onehots = (ids_here[:, :, None] == vocab_index).astype(bf16)
    own_onehot = (input_ids.reshape(-1)[:, None] == vocab_index[None, :]).astype(bf16)
    vectors = jnp.stack([gain_one, shift_one, b_down, gain_two, shift_two, b_dense])
    vectors = jnp.pad(vectors, ((0, 2), (0, 0)))
    context, log_sums, w_in, w_out, shared, normed, inverse = second_call(
        item_bits,
        seq_bits,
        visible,
        onehots,
        tables,
        cosine,
        sine_part,
        own_onehot,
        table,
        vectors,
        w_dense,
        own_in,
        own_out,
    )
    product, _, grad_shared, grad_in, layer_out, grad_resid, sums, in_sum, w_slice = ff_call(
        item_bits,
        shared,
        normed,
        inverse,
        cotangent,
        w_in.reshape(width, 2 * ff_part),
        w_out.reshape(width, ff_part),
        vectors,
        in_bias,
        w_block,
    )
    rows_all = items_here * span
    group_all = members * rows_all
    context = context.reshape(rows_all, width)
    grad_resid = grad_resid.reshape(rows_all, width)
    grad_branch = grad_resid.astype(bf16)
    grad_context = contract_cols(grad_branch, w_dense).astype(bf16)
    grad_context = lax.all_to_all(
        jnp.transpose(
            grad_context.reshape(items_here, span, seq_size, heads_here * HEAD), (0, 2, 1, 3)
        ),
        "seq",
        split_axis=1,
        concat_axis=1,
        tiled=True,
    ).reshape(items_here, length, heads_here * HEAD)

    vector_sums = sums[:6].T
    token_sum = contract_rows(grad_branch, own_onehot)
    grad_dense = contract_rows(context, grad_branch)
    by_rows = jnp.concatenate(
        [grad_dense, token_sum, jnp.pad(vector_sums, ((0, 0), (0, 122)))], axis=1
    ).astype(bf16)
    row_dims = item_bits[::-1] + seq_bits[::-1]
    by_rows = by_rows.reshape((2,) * len(row_dims) + (rows_here, -1))
    by_rows = halve(lines, by_rows, len(row_dims) - 1, *seq_bits[0])
    by_rows = halve(lines, by_rows, 0, *row_dims[0])
    grad_out_weight = contract_rows(
        grad_shared.reshape(group_all, width), product.reshape(group_all, ff_part)
    )
    grad_in_weight = contract_rows(
        shared.reshape(group_all, width), grad_in.reshape(group_all, 2 * ff_part)
    )
    group_dims = (2,) * (len(item_bits) + len(outer_bits)) + (members * rows_here, -1)
    in_sum = jnp.concatenate(unwoven(in_sum), axis=0)
    in_all = lax.dynamic_update_slice(
        jnp.zeros((2, ff_all), f32), in_sum, (0, member * ff_part)
    ).reshape(-1, 128)
    w_slice = w_slice.reshape(width, packed_width)
    spread, token_all, in_part, out_part, by_rows, in_all = third_call(
        item_bits,
        seq_bits,
        visible,
        onehots,
        tables,
        cosine,
        sine_part,
        log_sums,
        w_slice.T,
        grad_context,
        grad_in_weight.astype(bf16).reshape(group_dims),
        grad_out_weight.astype(bf16).reshape(group_dims),
        by_rows,
        in_all,
    )
    input_grads = spread.astype(f32) + deep_alpha * grad_resid.reshape(spread.shape)
    token_all = jnp.transpose(token_all, (2, 0, 1, 3)).reshape(vocab, -1)

    def from_members(part):
        taken = jnp.transpose(part, (1, 0, 2)).reshape(rows_here, ff_all)
        return taken[:, :ff_width].astype(f32)

    grad_up, grad_gate = (from_members(part) for part in unwoven(in_part))
    grad_down = from_members(out_part)
    by_rows = by_rows.astype(f32)
    grad_dense = by_rows[:, :width]
    token_sum = by_rows[:, width : width + vocab]
    own_vectors = by_rows[:, width + vocab :].T
    in_all = in_all.reshape(2, ff_all)
    grad_up_bias = in_all[:, :ff_width].reshape(-1)

    grad_heads = dot(embedding, token_all)
    grad_heads_bias = lax.dynamic_slice_in_dim(
        jnp.sum(token_all.astype(f32), axis=0),
        (item_place * seq_size + seq_place) * heads_bias.shape[0],
        heads_bias.shape[0],
        0,
    )
    embed_grad = 0.1 * (contract_cols(heads_weight, token_all) + deep_alpha * token_sum)
    return (
        layer_out,
        input_grads,
        embed_grad,
        grad_heads,
        grad_heads_bias,
        grad_dense,
        own_vectors[2],
        own_vectors[0],
        own_vectors[1],
        jnp.concatenate([grad_up, grad_gate], axis=1),
        grad_up_bias,
        grad_down.T,
        own_vectors[5],
        own_vectors[3],
        own_vectors[4],
    )


def solution(mesh):
    in_specs = (
        P("items", "seq"),
        P("items", "seq"),
        P("items"),
        P("items"),
        P("items", "seq", None),
        P(("items", "seq"), None),
        P(("items", "seq"), None),
        P(("items", "seq")),
        P(("items", "seq"), None),
        P(("items", "seq")),
        P(("items", "seq")),
        P(("items", "seq")),
        P(("items", "seq"), None),
        P(),
        P(None, ("items", "seq")),
        P(("items", "seq")),
        P(("items", "seq")),
        P(("items", "seq")),
    )
    out_specs = (
        P("items", "seq", None),
        P("items", "seq", None),
        P(("items", "seq"), None),
        P(("items", "seq"), None),
        P(("items", "seq")),
        P(("items", "seq"), None),
        P(("items", "seq")),
        P(("items", "seq")),
        P(("items", "seq")),
        P(("items", "seq"), None),
        P(),
        P(None, ("items", "seq")),
        P(("items", "seq")),
        P(("items", "seq")),
        P(("items", "seq")),
    )
    return jax.shard_map(
        on_device, mesh=mesh, in_specs=in_specs, out_specs=out_specs, check_vma=False
    )
```

```python
import functools
import math

import jax
import jax.numpy as jnp
import numpy as np
from jax import lax
from jax.experimental import pallas as pl
from jax.experimental.pallas import tpu as pltpu
from jax.sharding import PartitionSpec as P

HEADS = 16
HEAD = 128


deep_alpha = math.sqrt(48.0)
epsilon = 1e-05
mask_token = 3
both = ("items", "seq")
bf16 = jnp.bfloat16
f32 = jnp.float32
score_scale = HEAD ** (-0.5)
exponent_scale = score_scale * math.log2(math.e)


class Lines:
    def __init__(self):
        self.last = {}

    def swap(self, part, axis, bit):
        if (axis, bit) in self.last:
            part, _ = lax.optimization_barrier((part, self.last[axis, bit]))
        size = lax.axis_size(axis)
        got = lax.ppermute(part, axis, [(j, j ^ bit) for j in range(size)])
        self.last[axis, bit] = got
        return got


def bits_of(axis):
    found = []
    bit = 1
    while bit < lax.axis_size(axis):
        found.append((axis, bit))
        bit *= 2
    return found


def my_bit(axis, bit):
    return (lax.axis_index(axis) // bit) % 2


def pick(whole, place, dim):
    return lax.dynamic_index_in_dim(whole, place, dim, keepdims=False)


def moved(masks, axis, bit):
    return (masks[0] ^ (bit if axis == "items" else 0), masks[1] ^ (bit if axis == "seq" else 0))


def contract_rows(left, right):
    return lax.dot_general(left, right, (((0,), (0,)), ((), ())), preferred_element_type=f32)


def contract_cols(left, right):
    return lax.dot_general(left, right, (((1,), (1,)), ((), ())), preferred_element_type=f32)


def dot(left, right):
    return jnp.dot(left, right, preferred_element_type=f32)


def turn(values, cosine, sine_part):
    return values * cosine + pltpu.roll(values, HEAD // 2, 1) * sine_part


def head_parts(onehot_ref, table_ref, cosine, sine_part):
    onehot = onehot_ref[...]
    mixed = dot(jnp.concatenate([onehot, onehot], axis=1), table_ref[...])
    query = turn(mixed[:, :HEAD], cosine, sine_part).astype(bf16)
    key = turn(mixed[:, HEAD : 2 * HEAD], cosine, sine_part).astype(bf16)
    return query, key, mixed[:, 2 * HEAD :].astype(bf16)


def visible_scores(key, query, offset, visible):
    scores = contract_cols(key, query)
    place = offset + lax.broadcasted_iota(jnp.int32, (1, query.shape[0]), 1)
    seen = lax.broadcasted_iota(jnp.int32, scores.shape, 0) < jnp.maximum(place + 1, visible)
    return jnp.where(seen, scores, -1e30)


def table_halves(mixed_table):
    vocab = mixed_table.shape[0]
    by_head = jnp.transpose(mixed_table.reshape(vocab, -1, 3 * HEAD), (1, 0, 2))
    high = lax.reduce_precision(by_head, 8, 7)
    return jnp.concatenate([high.astype(bf16), (by_head - high).astype(bf16)], axis=1)


def norm_rows(rows):
    center = rows - jnp.mean(rows, axis=-1, keepdims=True)
    inverse = lax.rsqrt(jnp.mean(center * center, axis=-1, keepdims=True) + epsilon)
    return center * inverse, inverse


def norm_rows_back(grad, normed, inverse, gain):
    scaled = grad * gain
    return inverse * (
        scaled
        - jnp.mean(scaled, axis=-1, keepdims=True)
        - normed * jnp.mean(scaled * normed, axis=-1, keepdims=True)
    )


MESH = pl.DeviceIdType.MESH


class Copies:
    def __init__(self, send_sems, recv_sems, local_sems):
        self.sems = send_sems, recv_sems, local_sems
        self.sent = {}
        self.moved = 0
        self.count = 0
        self.here = lax.axis_index("items"), lax.axis_index("seq")

    def send(self, source, target, masks):
        order = self.count
        self.count += 1
        copy = pltpu.make_async_remote_copy(
            src_ref=source,
            dst_ref=target,
            send_sem=self.sems[0].at[order],
            recv_sem=self.sems[1].at[order],
            device_id=(self.here[0] ^ masks[0], self.here[1] ^ masks[1]),
            device_id_type=MESH,
        )
        copy.start()
        self.sent[id(copy)] = copy
        return copy

    def move(self, source, target):
        copy = pltpu.make_async_copy(source, target, self.sems[2].at[self.moved])
        self.moved += 1
        copy.start()
        return copy

    def sent_now(self, copy):
        self.sent.pop(id(copy)).wait_send()

    def end(self):
        for copy in self.sent.values():
            copy.wait_send()


def wait_all(copies):
    for copy in copies:
        copy.wait_recv()


def mask_of(step):
    return moved((0, 0), *step)


def greet(masks):
    barrier = pltpu.get_barrier_semaphore()
    here = lax.axis_index("items"), lax.axis_index("seq")
    for mask_i, mask_s in masks:
        pl.semaphore_signal(
            barrier,
            inc=1,
            device_id=(here[0] ^ mask_i, here[1] ^ mask_s),
            device_id_type=MESH,
        )
    pl.semaphore_wait(barrier, len(masks))


def partners(seq_size, item_bits):
    return [(0, mask) for mask in range(1, seq_size)] + [mask_of(step) for step in item_bits]


def aligned(place, size):
    return pl.ds(place // size * size, size)


def first_kernel(
    item_bits,
    seq_bits,
    row_count,
    small_ref,
    heads_ref,
    head_bias_ref,
    dense_ref,
    in_ref,
    out_ref,
    everyone_ref,
    table_ref,
    block_ref,
    dense_all_ref,
    own_in_ref,
    own_out_ref,
    embed_scr,
    block_scr,
    sum_scr,
    got_scr,
    send_sems,
    recv_sems,
    local_sems,
):
    items_size, seq_size = everyone_ref.shape[:2]
    item_place, seq_place = lax.axis_index("items"), lax.axis_index("seq")
    core, chip = seq_place % 2, seq_place // 2
    member = seq_place % 4
    rows = dense_ref.shape[0]
    columns = block_scr.shape[2]
    greet(partners(seq_size, item_bits))
    copies = Copies(send_sems, recv_sems, local_sems)

    def head_columns(place, source):
        return source.at[:, pl.ds(pl.multiple_of(place * columns, 128), columns)]

    head_rows = [
        (heads_ref, pl.ds(0, rows)),
        (head_bias_ref, pl.ds(rows, row_count - rows)),
    ]

    small = [copies.send(small_ref, everyone_ref.at[item_place, seq_place], mask_of(seq_bits[0]))]
    heads = [
        copies.send(
            head_columns(seq_place ^ mask, source), block_scr.at[seq_place, place], (0, mask)
        )
        for mask in range(1, seq_size)
        for source, place in head_rows
    ]
    dense = [
        copies.send(dense_ref, dense_all_ref.at[item_place, chip, core], mask_of(seq_bits[1]))
    ]
    mine = pl.ds(pl.multiple_of(member * rows, rows), rows)
    shares = []

    def share(source, target):
        for mask in range(1, 4):
            other = member ^ mask
            shares.append(
                copies.send(source.at[other // 2, other % 2], target.at[mine], (0, mask))
            )

    local = [
        copies.move(small_ref, everyone_ref.at[item_place, seq_place]),
        copies.move(dense_ref, dense_all_ref.at[item_place, chip, core]),
        copies.move(head_columns(seq_place, heads_ref), block_scr.at[seq_place, head_rows[0][1]]),
        copies.move(
            head_columns(seq_place, head_bias_ref), block_scr.at[seq_place, head_rows[1][1]]
        ),
        copies.move(in_ref.at[member // 2, core], own_in_ref.at[0, mine]),
        copies.move(out_ref.at[member // 2, core], own_out_ref.at[mine]),
    ]
    for copy in local:
        copy.wait()

    for order in range(1, len(seq_bits)):
        if order > 1:
            wait_all(dense[-1:])
            part = dense_all_ref.at[item_place, aligned(chip, 2 ** (order - 1)), core]
            dense.append(copies.send(part, part, mask_of(seq_bits[order])))
        wait_all(small[-1:])
        part = everyone_ref.at[item_place, aligned(seq_place, 2**order)]
        small.append(copies.send(part, part, mask_of(seq_bits[order])))
        if order == 1:
            share(in_ref, own_in_ref.at[0])
    wait_all(small[-1:])
    embed = copies.move(everyone_ref.at[item_place, :, pl.ds(0, row_count)], embed_scr)

    wait_all(heads)
    embed.wait()
    sum_scr[0] = lax.dot_general(
        embed_scr[...].reshape(seq_size * row_count, -1),
        block_scr[...].reshape(seq_size * row_count, columns),
        (((0,), (0,)), ((), ())),
        preferred_element_type=f32,
    )
    sums = copies.send(sum_scr.at[0], got_scr.at[0], mask_of(item_bits[0]))
    block_out = copies.move(block_scr, block_ref)
    part = everyone_ref.at[item_place]
    small.append(copies.send(part, part, mask_of(item_bits[0])))
    share(out_ref, own_out_ref)
    wait_all(dense[-1:])

    def dense_part(mask):
        return dense_all_ref.at[item_place ^ mask, :, core]

    known = [0]
    waves = []
    for step in item_bits[::-1]:
        waves.append([(mask, step) for mask in known])
        known = known + [mask ^ step[1] for mask in known]
    arrived = {}
    for wave in waves:
        part = dense_part(0)
        arrived[wave[0][1][1]] = copies.send(part, part, mask_of(wave[0][1]))
    near = [copies.send(dense_part(0), dense_part(0), mask_of(seq_bits[0]))]
    wait_all(shares[:3])
    outer = []
    if len(seq_bits) == 3:
        first = pl.ds(0, 2 * rows)
        outer.append(
            copies.send(own_in_ref.at[0, first], own_in_ref.at[1, first], mask_of(seq_bits[2]))
        )
    for order, step in enumerate(item_bits):
        sums.wait_recv()
        sum_scr[order + 1] = sum_scr[order] + got_scr[order]
        if order + 1 < len(item_bits):
            sums = copies.send(
                sum_scr.at[order + 1], got_scr.at[order + 1], mask_of(item_bits[order + 1])
            )
            wait_all(small[-1:])
            part = everyone_ref.at[aligned(item_place, 2 ** (order + 1))]
            small.append(copies.send(part, part, mask_of(item_bits[order + 1])))
        if order < len(waves) and order + 1 < len(item_bits):
            wave = waves[order]
            for mask, step in wave:
                arrived[mask ^ step[1]].wait_recv()
                part = dense_part(mask ^ step[1])
                for later in waves[order + 1 :]:
                    arrived[mask ^ step[1] ^ later[0][1][1]] = copies.send(
                        part, part, mask_of(later[0][1])
                    )
                near.append(copies.send(part, part, mask_of(seq_bits[0])))
    table_ref[...] = sum_scr[len(item_bits)]

    for mask, step in waves[-1]:
        arrived[mask ^ step[1]].wait_recv()
        part = dense_part(mask ^ step[1])
        near.append(copies.send(part, part, mask_of(seq_bits[0])))
    wait_all(near)
    wait_all(shares[3:])
    wait_all(outer)
    wait_all(small[-1:])
    block_out.wait()
    copies.end()


def first_call(item_bits, seq_bits, small, heads, head_bias, dense, parts_in, parts_out):
    items_size, seq_size = 2 ** len(item_bits), 2 ** len(seq_bits)
    row_count = heads.shape[0] + head_bias.shape[0]
    rows, width = dense.shape
    vocab = small.shape[1]
    columns = heads.shape[1] // seq_size
    any_space = pl.BlockSpec(memory_space=pl.ANY)
    spare = 8 * (len(item_bits) + len(seq_bits)) + 4 * seq_size + 2 ** (len(item_bits) + 2)
    return pl.pallas_call(
        functools.partial(first_kernel, item_bits, seq_bits, row_count),
        in_specs=[any_space] * 6,
        out_specs=[any_space, pl.BlockSpec(memory_space=pltpu.VMEM)] + [any_space] * 4,
        out_shape=[
            jax.ShapeDtypeStruct((items_size, seq_size) + small.shape, bf16),
            jax.ShapeDtypeStruct((vocab, columns), f32),
            jax.ShapeDtypeStruct((seq_size, row_count, columns), bf16),
            jax.ShapeDtypeStruct((items_size, seq_size // 2, 2, rows, width), bf16),
            jax.ShapeDtypeStruct((2, 4 * rows, parts_in.shape[3]), bf16),
            jax.ShapeDtypeStruct((4 * rows, parts_out.shape[3]), bf16),
        ],
        scratch_shapes=[
            pltpu.VMEM((seq_size, row_count, vocab), bf16),
            pltpu.VMEM((seq_size, row_count, columns), bf16),
            pltpu.VMEM((len(item_bits) + 1, vocab, columns), f32),
            pltpu.VMEM((len(item_bits), vocab, columns), f32),
            pltpu.SemaphoreType.DMA((spare,)),
            pltpu.SemaphoreType.DMA((spare,)),
            pltpu.SemaphoreType.DMA((8,)),
        ],
        compiler_params=pltpu.CompilerParams(
            collective_id=0, has_side_effects=True, vmem_limit_bytes=24 * 2**20
        ),
        name="first",
    )(small, heads, head_bias, dense, parts_in, parts_out)


class Spread:
    def __init__(self, copies, own, whole, outer_bits, item_bits, given=None):
        self.copies, self.own, self.whole, self.given = copies, own, whole, given
        self.outer_bits, self.item_bits = outer_bits, item_bits
        half = own.shape[0] // 2
        self.halves = pl.ds(0, half), pl.ds(half, half)
        self.last = []

    def part(self, masks):
        place = (self.copies.here[0] ^ masks[0]) * lax.axis_size("seq")
        return self.whole.at[(place + (self.copies.here[1] ^ masks[1])) // 4]

    def over(self, masks, step, rows=None):
        source = self.own if masks == (0, 0) else self.part(masks)
        target = self.part(masks)
        if rows is not None:
            source, target = source.at[rows], target.at[rows]
        return self.copies.send(source, target, mask_of(step))

    def start(self):
        self.local = self.copies.move(self.own, self.part((0, 0)))
        self.first = [self.over((0, 0), step) for step in self.item_bits]

    def start_given(self):
        masks = mask_of(self.outer_bits[0])
        target = self.part(masks).at[self.halves[0]]
        self.local_given = self.copies.move(self.given, target)
        self.second = [
            [self.copies.send(self.given, target, mask_of(step)) for step in self.item_bits],
            [],
        ]
        self.outer = [None, self.over((0, 0), self.outer_bits[0], self.halves[1])]

    def start_outer(self):
        self.outer = [self.over((0, 0), self.outer_bits[0], rows) for rows in self.halves]
        self.second = [[], []]

    def cross_own(self):
        one, two = self.item_bits
        self.first[0].wait_recv()
        self.last.append(self.over(moved((0, 0), *one), two, self.halves[0]))
        self.first[1].wait_recv()
        self.last.append(self.over(moved((0, 0), *two), one, self.halves[1]))

    def spread_outer(self, which):
        self.outer[which].wait_recv()
        masks = mask_of(self.outer_bits[0])
        self.second[which] = [
            self.over(masks, step, self.halves[which]) for step in self.item_bits
        ]

    def cross_outer(self, which):
        masks = mask_of(self.outer_bits[0])
        steps = self.item_bits if which == 0 else self.item_bits[::-1]
        copies = self.second[which] if which == 0 else self.second[which][::-1]
        copies[0].wait_recv()
        self.last.append(self.over(moved(masks, *steps[0]), steps[1], self.halves[which]))
        self.last.append(copies[1])

    def plain(self):
        self.local = self.copies.move(self.own, self.part((0, 0)))
        known = [(0, 0)]
        for step in self.outer_bits + self.item_bits:
            wait_all([self.over(masks, step) for masks in known])
            known = known + [moved(masks, *step) for masks in known]

    def end(self):
        wait_all(self.last)
        self.local.wait()
        if self.given is not None:
            self.local_given.wait()


def attend_unit(block, visible, onehot_ref, table_ref, cosine_ref, sine_ref, context_ref, lse_ref):
    query, key, value = head_parts(onehot_ref, table_ref, cosine_ref[...], sine_ref[...])
    value_turned = value.T
    for offset in range(0, query.shape[0], block):
        scores = visible_scores(key, query[offset : offset + block], offset, visible)
        peak = jnp.max(scores, axis=0, keepdims=True)
        expos = jnp.exp2((scores - peak) * exponent_scale)
        total = jnp.sum(expos, axis=0, keepdims=True)
        context = dot(value_turned, expos.astype(bf16)) / total
        context_ref[offset : offset + block, :] = context.T.astype(bf16)
        lse_ref[:, offset : offset + block] = peak * exponent_scale + jnp.log2(total)


def second_kernel(
    item_bits,
    seq_bits,
    visible_ref,
    onehot_ref,
    table_ref,
    cosine_ref,
    sine_ref,
    own_onehot_ref,
    embed_ref,
    vector_ref,
    dense_ref,
    own_in_ref,
    own_out_ref,
    context_ref,
    lse_ref,
    in_ref,
    out_ref,
    shared_ref,
    normed_ref,
    inverse_ref,
    context_scr,
    dense_scr,
    resid_scr,
    low_scr,
    send_sems,
    recv_sems,
    local_sems,
):
    seq_size = 2 ** len(seq_bits)
    items_here, length, features = context_scr.shape
    heads_here = features // HEAD
    span = length // seq_size
    width = dense_ref.shape[0]
    seq_place = lax.axis_index("seq")
    outer_bits = seq_bits[2:]
    greet(partners(seq_size, item_bits))
    copies = Copies(send_sems, recv_sems, local_sems)
    dense_copy = copies.move(dense_ref, dense_scr)
    stepwise = len(outer_bits) == 1 and len(item_bits) == 2
    given = own_in_ref.at[1, pl.ds(0, own_in_ref.shape[1] // 2)] if stepwise else None
    spreads = [
        Spread(copies, own_in_ref.at[0], in_ref, outer_bits, item_bits, given),
        Spread(copies, own_out_ref, out_ref, outer_bits, item_bits),
    ]
    if stepwise:
        spreads[0].start()
        spreads[0].start_given()
    arrivals, local = [], []
    for item in range(items_here):

        @pl.loop(0, heads_here)
        def _(head):
            place = pl.ds(pl.multiple_of(head * HEAD, HEAD), HEAD)
            attend_unit(
                min(256, length),
                visible_ref[item],
                onehot_ref.at[item],
                table_ref.at[head],
                cosine_ref,
                sine_ref,
                context_scr.at[item, :, place],
                lse_ref.at[item, head],
            )

        target = context_ref.at[
            item, :, pl.ds(pl.multiple_of(seq_place * features, HEAD), features)
        ]
        for mask in range(seq_size):
            rows = pl.ds(pl.multiple_of((seq_place ^ mask) * span, span), span)
            source = context_scr.at[item, rows]
            if mask:
                arrivals.append(copies.send(source, target, (0, mask)))
            else:
                local.append(copies.move(source, target))
    if stepwise:
        spreads[0].cross_own()
        spreads[0].cross_outer(0)
        spreads[1].start()
        spreads[0].spread_outer(1)
    wait_all(arrivals)
    for copy in local:
        copy.wait()

    if stepwise:
        spreads[1].start_outer()

    dense_copy.wait()
    rows_all = items_here * span
    tile = 256

    @pl.loop(0, width // tile)
    def _(order):
        place = pl.ds(pl.multiple_of(order * tile, tile), tile)
        branch = dot(context_ref[...].reshape(rows_all, width), dense_scr[:, place])
        inputs = contract_cols(own_onehot_ref[...], embed_ref[place, :])
        resid_scr[:, place] = deep_alpha * inputs + (branch + vector_ref[5:6, place])

    block = 32
    near, far = ("seq", 1), ("seq", 2)
    far_copies, near_copies, own_copies = [], [], []
    for item in range(items_here):

        @pl.loop(0, span // block)
        def _(order):
            start = pl.multiple_of(order * block, block)
            rows = pl.ds(pl.multiple_of(item * span + start, block), block)
            normed, inverse = norm_rows(resid_scr[rows, :])
            normed_ref[rows, :] = normed
            inverse_ref[rows, :] = jnp.broadcast_to(inverse, (block, 128))
            hidden = normed * vector_ref[0:1, :] + vector_ref[1:2, :]
            low_scr[item, pl.ds(start, block), :] = hidden.astype(bf16)

        source = low_scr.at[item]
        far_copies.append(copies.send(source, shared_ref.at[item, 1], mask_of(far)))
        near_copies.append(copies.send(source, shared_ref.at[item, 2], mask_of(near)))
        own_copies.append(copies.move(source, shared_ref.at[item, 0]))

    def pass_on(item):
        far_copies[item].wait_recv()
        part = shared_ref.at[item, 1]
        near_copies.append(copies.send(part, shared_ref.at[item, 3], mask_of(near)))

    if stepwise:
        spreads[1].cross_own()
        spreads[0].cross_outer(1)
    pass_on(0)
    if stepwise:
        spreads[1].spread_outer(0)
    pass_on(1)
    if stepwise:
        spreads[1].spread_outer(1)
        spreads[1].cross_outer(0)
    for item in range(2, items_here):
        pass_on(item)
    if stepwise:
        spreads[1].cross_outer(1)
    else:
        for one in spreads:
            one.plain()
    for one in spreads:
        one.end()
    wait_all(near_copies)
    for copy in own_copies:
        copy.wait()
    copies.end()


def second_call(
    item_bits,
    seq_bits,
    visible,
    onehots,
    tables,
    cosine,
    sine_part,
    own_onehot,
    embed,
    vectors,
    w_dense,
    own_in,
    own_out,
):
    items_here, length, vocab = onehots.shape
    heads_here = tables.shape[0]
    features = heads_here * HEAD
    seq_size = 2 ** len(seq_bits)
    span = length // seq_size
    width = w_dense.shape[0]
    groups = 2 ** (len(item_bits) + len(seq_bits)) // 4
    any_space = pl.BlockSpec(memory_space=pl.ANY)
    near_space = pl.BlockSpec(memory_space=pltpu.VMEM)
    spare = 4 * groups + items_here * (seq_size + 4)
    return pl.pallas_call(
        functools.partial(second_kernel, item_bits, seq_bits),
        in_specs=[pl.BlockSpec(memory_space=pltpu.SMEM)] + [near_space] * 7 + [any_space] * 3,
        out_specs=[near_space] * 2 + [any_space] * 3 + [near_space] * 2,
        out_shape=[
            jax.ShapeDtypeStruct((items_here, span, width), bf16),
            jax.ShapeDtypeStruct((items_here, heads_here, 1, length), f32),
            jax.ShapeDtypeStruct((groups,) + own_in.shape[1:], bf16),
            jax.ShapeDtypeStruct((groups,) + own_out.shape, bf16),
            jax.ShapeDtypeStruct((items_here, 4, span, width), bf16),
            jax.ShapeDtypeStruct((items_here * span, width), f32),
            jax.ShapeDtypeStruct((items_here * span, 128), f32),
        ],
        scratch_shapes=[
            pltpu.VMEM((items_here, length, features), bf16),
            pltpu.VMEM((width, width), bf16),
            pltpu.VMEM((items_here * span, width), f32),
            pltpu.VMEM((items_here, span, width), bf16),
            pltpu.SemaphoreType.DMA((spare,)),
            pltpu.SemaphoreType.DMA((spare,)),
            pltpu.SemaphoreType.DMA((16,)),
        ],
        compiler_params=pltpu.CompilerParams(
            collective_id=1, has_side_effects=True, vmem_limit_bytes=56 * 2**20
        ),
        name="second",
    )(
        visible,
        onehots,
        tables,
        cosine,
        sine_part,
        own_onehot,
        embed,
        vectors,
        w_dense,
        own_in,
        own_out,
    )


def leading(ref):
    return [index for index in np.ndindex(*ref.shape[:-2])]


def add_into(target, source):
    rows = target.shape[-2]
    for index in leading(target):

        @pl.loop(0, rows // 16)
        def _(order):
            place = index + (pl.ds(pl.multiple_of(order * 16, 16), 16),)
            total = target[place].astype(f32) + source[place].astype(f32)
            target[place] = total.astype(target.dtype)


def copy_into(target, source):
    @pl.loop(0, target.shape[0] // 16)
    def _(order):
        place = pl.ds(pl.multiple_of(order * 16, 16), 16)
        target[place] = source[place]


class Reduce:
    def __init__(self, copies, whole, rows, dims, steps, got, stage, stage_sems):
        self.copies, self.whole, self.rows = copies, whole, rows
        self.steps, self.got = steps, got
        self.place = dims.index(steps[0])
        self.stage, self.stage_sems = stage, stage_sems
        self.order = 0

    def first(self, bit, index=()):
        full = (slice(None),) * self.place
        if index:
            full = index[: self.place]
        rest = index[self.place :] if index else ()
        if index:
            return self.whole.at[full + (bit,) + rest + (self.rows,)]
        spare = len(self.whole.shape) - 3 - self.place
        return self.whole.at[full + (bit,) + (slice(None),) * spare + (self.rows,)]

    def start(self):
        step = self.steps[0]
        self.copy = self.copies.send(self.first(1 - my_bit(*step)), self.got[0], mask_of(step))

    def advance(self):
        step = self.steps[self.order]
        self.copy.wait_recv()
        if self.order == 0:
            self.kept = self.got[0]
            rows, columns = self.kept.shape[-2:]
            places = leading(self.kept)

            def load(order):
                return pltpu.make_async_copy(
                    self.first(my_bit(*step), places[order]),
                    self.stage.at[order % 2, pl.ds(0, rows), pl.ds(0, columns)],
                    self.stage_sems.at[order % 2],
                )

            load(0).start()
            for order, place in enumerate(places):
                if order + 1 < len(places):
                    load(order + 1).start()
                load(order).wait()
                add_into(
                    self.kept.at[place],
                    self.stage.at[order % 2, pl.ds(0, rows), pl.ds(0, columns)],
                )
        else:
            self.kept = self.kept.at[my_bit(*step)]
            add_into(self.kept, self.got[self.order])
        self.order += 1
        if self.order < len(self.steps):
            step = self.steps[self.order]
            self.copy = self.copies.send(
                self.kept.at[1 - my_bit(*step)], self.got[self.order], mask_of(step)
            )


def attend_back_unit(
    block,
    visible,
    onehot_ref,
    table_ref,
    cosine_ref,
    sine_ref,
    lse_ref,
    grad_ref,
    mixed_ref,
    sums_ref,
):
    cosine, sine_part = cosine_ref[...], sine_ref[...]
    query, key, value = head_parts(onehot_ref, table_ref, cosine, sine_part)
    key_turned = key.T
    length = query.shape[0]
    grad_key = jnp.zeros((length, HEAD), f32)
    grad_value = jnp.zeros((length, HEAD), f32)
    grad_query = []
    for offset in range(0, length, block):
        query_block = query[offset : offset + block]
        grad_block = grad_ref[offset : offset + block, :]
        scores = visible_scores(key, query_block, offset, visible)
        weights = jnp.exp2(scores * exponent_scale - lse_ref[:, offset : offset + block])
        grad_weights = contract_cols(value, grad_block)
        inner = jnp.sum(weights * grad_weights, axis=0, keepdims=True)
        grad_scores = (weights * (grad_weights - inner)).astype(bf16)
        grad_value = grad_value + dot(weights.astype(bf16), grad_block)
        grad_key = grad_key + dot(grad_scores, query_block)
        grad_query.append(dot(key_turned, grad_scores).T)
    grad_query = jnp.concatenate(grad_query, axis=0)

    def back(grad):
        return turn((grad * score_scale).astype(bf16).astype(f32), cosine, -sine_part).astype(bf16)

    mixed = jnp.concatenate([back(grad_query), back(grad_key), grad_value.astype(bf16)], axis=1)
    mixed_ref[...] = mixed.reshape(mixed_ref.shape)
    sums_ref[...] += dot(onehot_ref[...].T, mixed)


def third_kernel(
    item_bits,
    seq_bits,
    visible_ref,
    onehot_ref,
    table_ref,
    cosine_ref,
    sine_ref,
    lse_ref,
    slice_ref,
    grad_ref,
    in_ref,
    out_ref,
    dense_ref,
    bias_ref,
    spread_ref,
    sums_all_ref,
    in_part_ref,
    out_part_ref,
    dense_part_ref,
    bias_sum_ref,
    mixed_scr,
    other_scr,
    kept_scr,
    step_scrs,
    sums_scr,
    sums_got,
    bias_scr,
    bias_got,
    in_got,
    out_got,
    dense_got,
    in_final,
    out_final,
    stage_scr,
    stage_sems,
    send_sems,
    recv_sems,
    local_sems,
):
    seq_size = 2 ** len(seq_bits)
    items_here, length, features = grad_ref.shape
    heads_here = features // HEAD
    seq_place = lax.axis_index("seq")
    member = seq_place % 4
    outer_bits = seq_bits[2:]
    width = slice_ref.shape[1]
    greet(partners(seq_size, item_bits))
    copies = Copies(send_sems, recv_sems, local_sems)
    dims = item_bits[::-1] + outer_bits[::-1]

    def reducers(whole, got):
        rows = whole.shape[-2]
        if len(item_bits) == 2:
            one, two = item_bits
            ways = [
                (pl.ds(0, rows // 2), [two, one] + outer_bits[::-1]),
                (pl.ds(rows // 2, rows // 2), [one, two] + outer_bits[::-1]),
            ]
        else:
            ways = [(pl.ds(0, rows), dims)]
        return [
            Reduce(copies, whole, part, dims, steps, list(got[order]), stage_scr, stage_sems)
            for order, (part, steps) in enumerate(ways)
        ]

    in_sums = reducers(in_ref, in_got)
    out_sums = reducers(out_ref, out_got)
    dense_steps = item_bits[::-1] + seq_bits[:0:-1]
    dense_sum = Reduce(
        copies,
        dense_ref,
        pl.ds(0, dense_ref.shape[-2]),
        dense_steps,
        dense_steps,
        list(dense_got),
        stage_scr,
        stage_sems,
    )
    for one in in_sums + out_sums:
        one.start()
    sums_scr[...] = jnp.zeros_like(sums_scr)
    tile = 256
    flying = {}
    sums_copy = None

    def next_sum(order):
        nonlocal sums_copy
        sums_copy.wait_recv()
        sums_scr[order + 1] = sums_scr[order] + sums_got[order]
        if order + 1 < len(item_bits):
            sums_copy = copies.send(
                sums_scr.at[order + 1], sums_got.at[order + 1], mask_of(item_bits[order + 1])
            )

    bias_scr[0] = bias_ref[...]
    bias_steps = seq_bits + item_bits
    bias_copies = [copies.send(bias_scr.at[0], bias_got.at[0], mask_of(bias_steps[0]))]
    for stage in range(items_here + len(seq_bits)):
        if stage < items_here:

            @pl.loop(0, heads_here)
            def _(head):
                place = pl.ds(pl.multiple_of(head * HEAD, HEAD), HEAD)
                packed = pl.ds(pl.multiple_of(head * 3 * HEAD, HEAD), 3 * HEAD)
                attend_back_unit(
                    min(256, length),
                    visible_ref[stage],
                    onehot_ref.at[stage],
                    table_ref.at[head],
                    cosine_ref,
                    sine_ref,
                    lse_ref.at[stage, head],
                    grad_ref.at[stage, :, place],
                    mixed_scr.at[:, :, :, packed],
                    sums_scr.at[0, head],
                )

        for order in range(len(seq_bits) - 1, -1, -1):
            item = stage - 1 - order
            if not 0 <= item < items_here:
                continue
            copy, kept = flying[item]
            copy.wait_recv()
            got = step_scrs[order].at[item % 2]
            if order:
                full = (slice(None),) * (len(kept.shape) - 3)
                kept = kept.at[full + (my_bit(*seq_bits[order]),)]
            if order + 1 < len(seq_bits):
                add_into(kept, got)
                step = seq_bits[order + 1]
                full = (slice(None),) * (len(kept.shape) - 3)
                copy = copies.send(
                    kept.at[full + (1 - my_bit(*step),)],
                    step_scrs[order + 1].at[item % 2],
                    mask_of(step),
                )
                flying[item] = copy, kept
                flying["later", item].append(copy)
            else:

                @pl.loop(0, kept.shape[0] // 16)
                def _(block):
                    place = (pl.ds(pl.multiple_of(block * 16, 16), 16),)
                    total = kept[place].astype(f32) + got[place].astype(f32)
                    spread_ref[(item,) + place] = total.astype(bf16)

        if stage < items_here:
            core = my_bit(*seq_bits[0])
            slot = stage % 2
            if stage >= 2:
                copies.sent_now(flying["first", stage - 2])
            kept_slot = stage % len(seq_bits)
            if stage >= len(seq_bits):
                for copy in flying["later", stage - len(seq_bits)]:
                    copies.sent_now(copy)
            half = mixed_scr.shape[0] * mixed_scr.shape[2]
            other = mixed_scr[:, 1 - core].reshape(half, -1)
            mine = mixed_scr[:, core].reshape(half, -1)

            @pl.loop(0, width // tile)
            def _(order):
                place = pl.ds(pl.multiple_of(order * tile, tile), tile)
                weights = slice_ref[:, place]
                target = other_scr.at[slot]
                target[..., place] = dot(other, weights).astype(bf16).reshape(
                    target.shape[:-1] + (tile,)
                )
                target = kept_scr.at[kept_slot]
                target[..., place] = dot(mine, weights).astype(bf16).reshape(
                    target.shape[:-1] + (tile,)
                )

            copy = copies.send(
                other_scr.at[slot], step_scrs[0].at[slot], mask_of(seq_bits[0])
            )
            flying[stage] = copy, kept_scr.at[kept_slot]
            flying["first", stage] = copy
            flying["later", stage] = []
        if stage == 1:
            dense_sum.start()
        if stage == items_here - 1:
            sums_copy = copies.send(sums_scr.at[0], sums_got.at[0], mask_of(item_bits[0]))
        if stage == items_here:
            for one in in_sums:
                one.advance()
        if stage == items_here + 1:
            next_sum(0)
            for one in in_sums:
                one.advance()
            for one in out_sums:
                one.advance()
        if stage == items_here + 2:
            for order in range(1, len(item_bits)):
                next_sum(order)
            for one in out_sums:
                one.advance()

        bias_done = len(bias_copies)
        if bias_done <= len(bias_steps):
            bias_copies[-1].wait_recv()
            bias_scr[bias_done] = bias_scr[bias_done - 1] + bias_got[bias_done - 1]
            if bias_done < len(bias_steps):
                bias_copies.append(
                    copies.send(
                        bias_scr.at[bias_done],
                        bias_got.at[bias_done],
                        mask_of(bias_steps[bias_done]),
                    )
                )
            else:
                bias_copies.append(None)
                bias_sum_ref[...] = bias_scr[bias_done]

    sums_all_ref[seq_place] = sums_scr[len(item_bits)].astype(bf16)
    known = [0]
    arrivals = []
    for axis, bit in seq_bits[::-1]:
        wait_all(arrivals)
        arrivals = []
        for mask in known:
            part = sums_all_ref.at[seq_place ^ mask]
            arrivals.append(copies.send(part, part, (0, bit)))
        known = known + [mask ^ bit for mask in known]
        if dense_sum.order < len(dense_steps):
            dense_sum.advance()

    while in_sums[0].order < len(dims):
        for one in in_sums + out_sums:
            if one.order < len(dims):
                one.advance()
        if dense_sum.order < len(dense_steps):
            dense_sum.advance()
    while out_sums[0].order < len(dims):
        for one in out_sums:
            one.advance()
    wait_all(arrivals)
    shares, local = [], []
    for sums, final, target in (
        (in_sums, in_final, in_part_ref),
        (out_sums, out_final, out_part_ref),
    ):
        rows = target.shape[1]
        first = 0
        for one in sums:
            copy_into(final.at[pl.ds(first, one.kept.shape[0])], one.kept)
            first += one.kept.shape[0]
        for mask in range(4):
            source = final.at[pl.ds(pl.multiple_of((member ^ mask) * rows, 16), rows)]
            if mask:
                shares.append(copies.send(source, target.at[member], (0, mask)))
            else:
                local.append(copies.move(source, target.at[member]))
    while dense_sum.order < len(dense_steps):
        dense_sum.advance()
    dense_part_ref[...] = dense_sum.kept[...]
    wait_all(shares)
    for copy in local:
        copy.wait()
    copies.end()


def third_call(
    item_bits,
    seq_bits,
    visible,
    onehots,
    tables,
    cosine,
    sine_part,
    log_sums,
    w_slice,
    grad_context,
    grad_in,
    grad_out,
    by_rows,
    in_sum,
):
    items_here, length, vocab = onehots.shape
    heads_here = tables.shape[0]
    seq_size = 2 ** len(seq_bits)
    span = length // seq_size
    width = w_slice.shape[1]
    packed = heads_here * 3 * HEAD
    outer = len(seq_bits) - 2
    levels = len(item_bits) + outer
    any_space = pl.BlockSpec(memory_space=pl.ANY)
    near_space = pl.BlockSpec(memory_space=pltpu.VMEM)

    def got_shapes(whole, ways, depth):
        rows, columns = whole.shape[-2:]
        one = tuple(
            pltpu.VMEM((2,) * order + (rows // ways, columns), bf16)
            for order in range(depth - 1, -1, -1)
        )
        return one

    ways = 2 if len(item_bits) == 2 else 1
    group_rows = grad_in.shape[-2]
    rows = group_rows // 4
    dense_depth = len(item_bits) + len(seq_bits) - 1
    spread = (2,) * (len(seq_bits) - 1) + (span, width)
    all_bits = len(item_bits) + len(seq_bits)
    spare = 8 * items_here + 8 * levels + 16 * all_bits
    stage_rows = max(group_rows // ways, by_rows.shape[-2])
    return pl.pallas_call(
        functools.partial(third_kernel, item_bits, seq_bits),
        in_specs=[pl.BlockSpec(memory_space=pltpu.SMEM)]
        + [near_space] * 7
        + [any_space] * 3
        + [near_space],
        out_specs=[near_space, near_space, any_space, any_space, near_space, near_space],
        out_shape=[
            jax.ShapeDtypeStruct((items_here, span, width), bf16),
            jax.ShapeDtypeStruct((seq_size, heads_here, vocab, 3 * HEAD), bf16),
            jax.ShapeDtypeStruct((4, rows, grad_in.shape[-1]), bf16),
            jax.ShapeDtypeStruct((4, rows, grad_out.shape[-1]), bf16),
            jax.ShapeDtypeStruct(by_rows.shape[-2:], bf16),
            jax.ShapeDtypeStruct(in_sum.shape, f32),
        ],
        scratch_shapes=[
            pltpu.VMEM((seq_size // 2, 2, span, packed), bf16),
            pltpu.VMEM((2,) + spread, bf16),
            pltpu.VMEM((len(seq_bits),) + spread, bf16),
            tuple(pltpu.VMEM((2,) + spread[order:], bf16) for order in range(len(seq_bits))),
            pltpu.VMEM((len(item_bits) + 1, heads_here, vocab, 3 * HEAD), f32),
            pltpu.VMEM((len(item_bits), heads_here, vocab, 3 * HEAD), f32),
            pltpu.VMEM((all_bits + 1,) + in_sum.shape, f32),
            pltpu.VMEM((all_bits,) + in_sum.shape, f32),
            tuple(got_shapes(grad_in, ways, levels) for _ in range(ways)),
            tuple(got_shapes(grad_out, ways, levels) for _ in range(ways)),
            got_shapes(by_rows, 1, dense_depth),
            pltpu.VMEM((group_rows, grad_in.shape[-1]), bf16),
            pltpu.VMEM((group_rows, grad_out.shape[-1]), bf16),
            pltpu.VMEM((2, stage_rows, grad_in.shape[-1]), bf16),
            pltpu.SemaphoreType.DMA((2,)),
            pltpu.SemaphoreType.DMA((spare,)),
            pltpu.SemaphoreType.DMA((spare,)),
            pltpu.SemaphoreType.DMA((8,)),
        ],
        compiler_params=pltpu.CompilerParams(
            collective_id=2, has_side_effects=True, vmem_limit_bytes=60 * 2**20
        ),
        name="third",
    )(
        visible,
        onehots,
        tables,
        cosine,
        sine_part,
        log_sums,
        w_slice,
        grad_context,
        grad_in,
        grad_out,
        by_rows,
        in_sum,
    )


def merged_kernel(
    item_bits,
    seq_bits,
    visible_ref,
    onehot_ref,
    table_ref,
    cosine_ref,
    sine_ref,
    lse_ref,
    slice_ref,
    grad_ref,
    shared_ref,
    grad_in_ref,
    grad_shared_ref,
    product_ref,
    dense_ref,
    bias_ref,
    spread_ref,
    sums_all_ref,
    parts_ref,
    dense_part_ref,
    bias_sum_ref,
    land_one_ref,
    land_two_ref,
    land_three_ref,
    mixed_scr,
    other_scr,
    kept_scr,
    step_scrs,
    sums_scr,
    sums_got,
    bias_scr,
    bias_got,
    dense_got,
    rhs_scr,
    lhs_scr,
    turned_scr,
    slot_scr,
    sum_scr,
    stage_scr,
    dense_scr,
    grad_scr,
    stage_sems,
    load_sems,
    send_sems,
    recv_sems,
    local_sems,
):
    seq_size = 2 ** len(seq_bits)
    items_here, length, features = grad_scr.shape
    span = length // seq_size
    heads_here = features // HEAD
    seq_place = lax.axis_index("seq")
    member = seq_place % 4
    outer_bits = seq_bits[2:]
    width = slice_ref.shape[1]
    greet(partners(seq_size, item_bits))
    copies = Copies(send_sems, recv_sems, local_sems)

    one, two = item_bits
    high = outer_bits[0]
    ways = [[two, one, high], [one, two, high]]
    blocks = [(grad_shared_ref, product_ref, 0)]
    ff_part = product_ref.shape[1]
    blocks += [(shared_ref, grad_in_ref, 0), (shared_ref, grad_in_ref, ff_part)]
    group_rows = lhs_scr.shape[2]
    half_rows = group_rows // 2
    pairs = [(two, one), (two,), (one,), ()]

    def masks_of(steps):
        masks = (0, 0)
        for step in steps:
            masks = moved(masks, *step)
        return masks

    def load_rhs(block):
        _, rhs, first = blocks[block]
        return pltpu.make_async_copy(
            rhs.at[:, pl.ds(first, ff_part)], rhs_scr, load_sems.at[0]
        )

    def load_lhs(block, pair, which):
        masks = masks_of(pairs[pair] + ((high,) if which == 0 else ()))
        group = ((copies.here[0] ^ masks[0]) * seq_size + (copies.here[1] ^ masks[1])) // 4
        columns = pl.ds(pl.multiple_of(group * group_rows, 128), group_rows)
        return pltpu.make_async_copy(
            blocks[block][0].at[:, columns], lhs_scr.at[which], load_sems.at[1 + which]
        )

    landed, slots, sends = {}, {}, {}

    def products(block):
        load_rhs(block).wait()
        for pair, steps in enumerate(pairs):
            for which in range(2):
                load_lhs(block, pair, which).wait()
                rows = pl.ds(which * group_rows, group_rows)
                turned_scr[rows, :] = lhs_scr[which].T
            follow = (block, pair + 1) if pair + 1 < len(pairs) else (block + 1, 0)
            if follow[0] < len(blocks):
                for which in range(2):
                    load_lhs(*follow, which).start()
            targets = []
            for which in range(2):
                for way in range(2):
                    away, other = ways[way][:2]
                    place = 2 * (other in steps) + 1 - which
                    if away in steps:
                        if (way, place) in slots:
                            copies.sent_now(slots.pop((way, place)))
                        targets.append(slot_scr.at[way, place])
                    else:
                        targets.append(sum_scr.at[block, way, place])

            def multiply(columns):
                total = dot(turned_scr[...], rhs_scr[:, columns]).astype(bf16)
                for order, target in enumerate(targets):
                    target[:, columns] = total[order * half_rows : (order + 1) * half_rows]

            @pl.loop(0, ff_part // 256)
            def _(order):
                multiply(pl.ds(pl.multiple_of(order * 256, 256), 256))

            if ff_part % 256:
                multiply(pl.ds(ff_part // 256 * 256, ff_part % 256))
            for which in range(2):
                for way in range(2):
                    away, other = ways[way][:2]
                    place = 2 * (other in steps) + 1 - which
                    if away in steps:
                        copy = copies.send(
                            slot_scr.at[way, place],
                            land_one_ref.at[block, way, place],
                            mask_of(away),
                        )
                        slots[way, place] = copy
                        landed[1, block, way, place] = copy
        if block + 1 < len(blocks):
            load_rhs(block + 1).start()

    lands = {1: land_one_ref, 2: land_two_ref, 3: land_three_ref}

    def absorb(level, block):
        count = 2 ** (3 - level)
        pending = []

        def finish():
            load, way, place, slot = pending.pop(0)
            load.wait()
            add_into(sum_scr.at[block, way, place], stage_scr.at[slot])
            if level < 3 and place >= count // 2:
                left = place - count // 2
                landed[level + 1, block, way, left] = copies.send(
                    sum_scr.at[block, way, place],
                    lands[level + 1].at[block, way, left],
                    mask_of(ways[way][level]),
                )

        order = 0
        for place in range(count - 1, -1, -1):
            for way in range(2):
                landed[level, block, way, place].wait_recv()
                slot = order % 2
                load = pltpu.make_async_copy(
                    lands[level].at[block, way, place], stage_scr.at[slot], stage_sems.at[slot]
                )
                load.start()
                if pending:
                    finish()
                pending.append((load, way, place, slot))
                order += 1
        finish()

    shares, local = [], []

    def to_members(block):
        rows = parts_ref.shape[2]
        for mask in range(4):
            other = member ^ mask
            source = sum_scr.at[
                block, other // 2, 0, pl.ds(pl.multiple_of(other % 2 * rows, 16), rows)
            ]
            if mask:
                shares.append(copies.send(source, parts_ref.at[block, member], (0, mask)))
            else:
                local.append(copies.move(source, parts_ref.at[block, member]))

    grads = {}

    def send_grads(item):
        target = grad_scr.at[item, pl.ds(pl.multiple_of(seq_place * span, span), span)]
        arriving = []
        for mask in range(seq_size):
            columns = pl.ds(pl.multiple_of((seq_place ^ mask) * features, HEAD), features)
            source = grad_ref.at[item, :, columns]
            if mask:
                arriving.append(copies.send(source, target, (0, mask)))
            else:
                own = copies.move(source, target)
        grads[item] = arriving, own

    send_grads(0)
    load_rhs(0).start()
    for which in range(2):
        load_lhs(0, 0, which).start()
    dense_steps = item_bits[::-1] + seq_bits[:0:-1]
    dense_sum = Reduce(
        copies,
        dense_ref,
        pl.ds(0, dense_ref.shape[-2]),
        dense_steps,
        dense_steps,
        list(dense_got),
        dense_scr,
        stage_sems,
    )
    sums_scr[...] = jnp.zeros_like(sums_scr)
    tile = 256
    flying = {}
    sums_copy = None

    def next_sum(order):
        nonlocal sums_copy
        sums_copy.wait_recv()
        sums_scr[order + 1] = sums_scr[order] + sums_got[order]
        if order + 1 < len(item_bits):
            sums_copy = copies.send(
                sums_scr.at[order + 1], sums_got.at[order + 1], mask_of(item_bits[order + 1])
            )

    known, arrivals = [0], []

    def spread_sums():
        nonlocal known, arrivals
        wait_all(arrivals)
        arrivals = []
        bit = seq_size // 2 // len(known)
        for mask in known:
            part = sums_all_ref.at[seq_place ^ mask]
            arrivals.append(copies.send(part, part, (0, bit)))
        known = known + [mask ^ bit for mask in known]

    bias_scr[0] = bias_ref[...]
    bias_steps = seq_bits + item_bits
    bias_copies = [copies.send(bias_scr.at[0], bias_got.at[0], mask_of(bias_steps[0]))]

    def attention(item):
        arriving, own = grads[item]
        wait_all(arriving)
        own.wait()

        @pl.loop(0, heads_here)
        def _(head):
            place = pl.ds(pl.multiple_of(head * HEAD, HEAD), HEAD)
            packed = pl.ds(pl.multiple_of(head * 3 * HEAD, HEAD), 3 * HEAD)
            attend_back_unit(
                min(256, length),
                visible_ref[item],
                onehot_ref.at[item],
                table_ref.at[head],
                cosine_ref,
                sine_ref,
                lse_ref.at[item, head],
                grad_scr.at[item, :, place],
                mixed_scr.at[:, :, :, packed],
                sums_scr.at[0, head],
            )

    def step_on(item, order):
        copy, kept = flying[item]
        copy.wait_recv()
        got = step_scrs[order].at[item % step_scrs[order].shape[0]]
        full = (slice(None),) * (len(kept.shape) - 3)
        if order:
            kept = kept.at[full + (my_bit(*seq_bits[order]),)]
            full = full[1:]
        if order + 1 < len(seq_bits):
            add_into(kept, got)
            step = seq_bits[order + 1]
            target = step_scrs[order + 1]
            copy = copies.send(
                kept.at[full + (1 - my_bit(*step),)],
                target.at[item % target.shape[0]],
                mask_of(step),
            )
            flying[item] = copy, kept
            flying["later", item].append(copy)
        else:
            add_into(kept, got)
            flying["out", item] = copies.move(kept, spread_ref.at[item])

    def partial(item):
        core = my_bit(*seq_bits[0])
        slot = item % 2
        if item >= 1:
            copies.sent_now(flying["first", item - 1])
        kept_slot = item % len(seq_bits)
        if item >= len(seq_bits):
            for copy in flying["later", item - len(seq_bits)]:
                copies.sent_now(copy)
            flying.pop(("out", item - len(seq_bits))).wait()
        half = mixed_scr.shape[0] * mixed_scr.shape[2]
        other = mixed_scr[:, 1 - core].reshape(half, -1)
        mine = mixed_scr[:, core].reshape(half, -1)

        @pl.loop(0, width // tile)
        def _(order):
            place = pl.ds(pl.multiple_of(order * tile, tile), tile)
            weights = slice_ref[:, place]
            target = other_scr
            target[..., place] = dot(other, weights).astype(bf16).reshape(
                target.shape[:-1] + (tile,)
            )
            target = kept_scr.at[kept_slot]
            target[..., place] = dot(mine, weights).astype(bf16).reshape(
                target.shape[:-1] + (tile,)
            )

        copy = copies.send(other_scr, step_scrs[0].at[slot], mask_of(seq_bits[0]))
        flying[item] = copy, kept_scr.at[kept_slot]
        flying["first", item] = copy
        flying["later", item] = []

    def bias_step():
        done = len(bias_copies)
        bias_copies[-1].wait_recv()
        bias_scr[done] = bias_scr[done - 1] + bias_got[done - 1]
        if done < len(bias_steps):
            bias_copies.append(
                copies.send(bias_scr.at[done], bias_got.at[done], mask_of(bias_steps[done]))
            )
        else:
            bias_sum_ref[...] = bias_scr[done]

    dense_sum.start()
    products(0)
    send_grads(1)
    attention(0)
    partial(0)
    send_grads(2)
    bias_step()
    attention(1)
    step_on(0, 0)
    partial(1)
    products(1)
    send_grads(3)
    step_on(1, 0)
    bias_step()
    attention(2)
    step_on(0, 1)
    partial(2)
    absorb(1, 0)
    bias_step()
    dense_sum.advance()
    attention(3)
    step_on(2, 0)
    step_on(1, 1)
    step_on(0, 2)
    partial(3)
    sums_copy = copies.send(sums_scr.at[0], sums_got.at[0], mask_of(item_bits[0]))
    products(2)
    step_on(3, 0)
    absorb(1, 1)
    step_on(2, 1)
    absorb(2, 0)
    next_sum(0)
    bias_step()
    dense_sum.advance()
    step_on(1, 2)
    absorb(1, 2)
    step_on(3, 1)
    next_sum(1)
    bias_step()
    sums_all_ref[seq_place] = sums_scr[len(item_bits)].astype(bf16)
    spread_sums()
    absorb(2, 1)
    step_on(2, 2)
    absorb(3, 0)
    to_members(0)
    absorb(2, 2)
    spread_sums()
    dense_sum.advance()
    step_on(3, 2)
    absorb(3, 1)
    to_members(1)
    spread_sums()
    while dense_sum.order < len(dense_steps):
        dense_sum.advance()
    absorb(3, 2)
    to_members(2)
    wait_all(arrivals)
    while dense_sum.order < len(dense_steps):
        dense_sum.advance()
    dense_part_ref[...] = dense_sum.kept[...]
    wait_all(shares)
    for item in range(items_here):
        if ("out", item) in flying:
            flying["out", item].wait()
    for copy in local:
        copy.wait()
    copies.end()


def merged_call(
    item_bits,
    seq_bits,
    visible,
    onehots,
    tables,
    cosine,
    sine_part,
    log_sums,
    w_slice,
    grad_context,
    shared,
    grad_in,
    grad_shared,
    product,
    by_rows,
    in_sum,
):
    items_here, length, vocab = onehots.shape
    heads_here = tables.shape[0]
    seq_size = 2 ** len(seq_bits)
    span = length // seq_size
    width = w_slice.shape[1]
    packed = heads_here * 3 * HEAD
    any_space = pl.BlockSpec(memory_space=pl.ANY)
    near_space = pl.BlockSpec(memory_space=pltpu.VMEM)
    ff_part = product.shape[1]
    group_rows = width * 4 // 2 ** (len(item_bits) + len(seq_bits))
    rows = group_rows // 4
    dense_depth = len(item_bits) + len(seq_bits) - 1
    spread = (2,) * (len(seq_bits) - 1) + (span, width)
    all_bits = len(item_bits) + len(seq_bits)
    spare = (8 + seq_size) * items_here + 64 + 16 * all_bits
    half = (group_rows // 2, ff_part)
    return pl.pallas_call(
        functools.partial(merged_kernel, item_bits, seq_bits),
        in_specs=[pl.BlockSpec(memory_space=pltpu.SMEM)]
        + [near_space] * 6
        + [any_space] * 6
        + [near_space],
        out_specs=[any_space, near_space, any_space, near_space, near_space] + [any_space] * 3,
        out_shape=[
            jax.ShapeDtypeStruct((items_here, span, width), bf16),
            jax.ShapeDtypeStruct((seq_size, heads_here, vocab, 3 * HEAD), bf16),
            jax.ShapeDtypeStruct((3, 4, rows, ff_part), bf16),
            jax.ShapeDtypeStruct(by_rows.shape[-2:], bf16),
            jax.ShapeDtypeStruct(in_sum.shape, f32),
            jax.ShapeDtypeStruct((3, 2, 4) + half, bf16),
            jax.ShapeDtypeStruct((3, 2, 2) + half, bf16),
            jax.ShapeDtypeStruct((3, 2, 1) + half, bf16),
        ],
        scratch_shapes=[
            pltpu.VMEM((seq_size // 2, 2, span, packed), bf16),
            pltpu.VMEM(spread, bf16),
            pltpu.VMEM((len(seq_bits),) + spread, bf16),
            tuple(
                pltpu.VMEM((2 if order == 0 else items_here,) + spread[order:], bf16)
                for order in range(len(seq_bits))
            ),
            pltpu.VMEM((len(item_bits) + 1, heads_here, vocab, 3 * HEAD), f32),
            pltpu.VMEM((len(item_bits), heads_here, vocab, 3 * HEAD), f32),
            pltpu.VMEM((all_bits + 1,) + in_sum.shape, f32),
            pltpu.VMEM((all_bits,) + in_sum.shape, f32),
            tuple(
                pltpu.VMEM((2,) * order + by_rows.shape[-2:], bf16)
                for order in range(dense_depth - 1, -1, -1)
            ),
            pltpu.VMEM((product.shape[0], ff_part), bf16),
            pltpu.VMEM((2, product.shape[0], group_rows), bf16),
            pltpu.VMEM((2 * group_rows, product.shape[0]), bf16),
            pltpu.VMEM((2, 4) + half, bf16),
            pltpu.VMEM((3, 2, 4) + half, bf16),
            pltpu.VMEM((2,) + half, bf16),
            pltpu.VMEM((2,) + by_rows.shape[-2:], bf16),
            pltpu.VMEM((items_here, length, heads_here * HEAD), bf16),
            pltpu.SemaphoreType.DMA((2,)),
            pltpu.SemaphoreType.DMA((3,)),
            pltpu.SemaphoreType.DMA((spare,)),
            pltpu.SemaphoreType.DMA((spare,)),
            pltpu.SemaphoreType.DMA((16,)),
        ],
        compiler_params=pltpu.CompilerParams(
            collective_id=4, has_side_effects=True, vmem_limit_bytes=62 * 2**20
        ),
        name="merged",
    )(
        visible,
        onehots,
        tables,
        cosine,
        sine_part,
        log_sums,
        w_slice,
        grad_context,
        shared,
        grad_in,
        grad_shared,
        product,
        by_rows,
        in_sum,
    )


def ff_kernel(
    item_bits,
    shared_ref,
    normed_ref,
    inverse_ref,
    cotangent_ref,
    in_ref,
    out_ref,
    vector_ref,
    bias_ref,
    block_ref,
    product_ref,
    saved_ref,
    grad_shared_ref,
    grad_in_ref,
    layer_ref,
    resid_ref,
    sums_ref,
    in_sum_ref,
    slices_ref,
    rows_scr,
    product_scr,
    save_scr,
    parts_scr,
    near_got,
    far_got,
    low_scr,
    grad_in_scr,
    resid_scr,
    normed_scr,
    gate_scr,
    send_sems,
    recv_sems,
    load_sems,
    keep_sems,
):
    chunks, blocks, span, width = shared_ref.shape
    group_rows = blocks * span
    tiles = product_scr.shape[-1] // 128
    tile = 256
    near, far = ("seq", 1), ("seq", 2)
    greet([mask_of(near), mask_of(far)] + [mask_of(step) for step in item_bits])
    copies = Copies(send_sems, recv_sems, keep_sems)
    item_place = copies.here[0]
    slices = copies.move(block_ref, slices_ref.at[item_place])
    slices.wait()
    spread = []

    def spread_block():
        order = len(spread)
        if order < len(item_bits):
            wait_all(spread[-1:])
            part = slices_ref.at[aligned(item_place, 2**order)]
            spread.append(copies.send(part, part, mask_of(item_bits[order])))

    spread_block()
    keeps, loads = {}, {}
    state = {}
    gain_one, shift_one, b_down, gain_two, shift_two = range(5)
    for line in range(sums_ref.shape[0]):
        sums_ref[line : line + 1, :] = jnp.zeros((1, width), f32)
    in_sum_ref[...] = jnp.zeros_like(in_sum_ref)

    def load(name, slot, source, target):
        copy = pltpu.make_async_copy(source, target, load_sems.at[slot])
        copy.start()
        loads[name] = copy

    def loaded(name):
        loads.pop(name).wait()

    def keep(name, slot, source, target):
        copy = pltpu.make_async_copy(source, target, keep_sems.at[1 + slot])
        copy.start()
        keeps[name] = copy

    def keep_done(name):
        if name in keeps:
            keeps.pop(name).wait()

    def load_shared(chunk):
        slot = chunk % 2
        load(("rows", slot), slot, shared_ref.at[chunk], rows_scr.at[slot])

    def load_normed(chunk):
        slot = chunk % 2
        rows = pl.ds(chunk * span, span)
        load(("normed", slot), 2 + slot, normed_ref.at[rows], normed_scr.at[slot])

    def forward_gate(chunk):
        slot = chunk % 2
        loaded(("rows", slot))
        if chunk + 1 < chunks:
            load_shared(chunk + 1)
        keep_done(("product", slot))
        keep_done(("save", slot))
        rows = rows_scr.at[slot]

        def multiply(order, place):
            columns = pl.ds(pl.multiple_of(order * tile, tile), tile)
            gate_scr[place] = (
                dot(rows[...].reshape(group_rows, width), in_ref[:, columns])
                + bias_ref[:, columns]
            )

        def finish(order, place):
            gate_up = gate_scr[place]
            up_part, gate = gate_up[:, :128], gate_up[:, 128:]
            below = 0.5 * (1.0 + lax.erf(gate * (0.5**0.5)))
            activated = gate * below
            slope = below + gate * jnp.exp(-0.5 * gate * gate) * (1.0 / math.sqrt(2.0 * math.pi))
            columns = pl.ds(pl.multiple_of(order * 128, 128), 128)
            product_scr[slot, :, columns] = (up_part * activated).astype(bf16)
            save_scr[slot, 0, :, columns] = activated.astype(bf16)
            save_scr[slot, 1, :, columns] = (up_part * slope).astype(bf16)

        multiply(0, 0)

        @pl.loop(0, (tiles - 1) // 2)
        def _(pair):
            finish(2 * pair, 0)
            multiply(2 * pair + 1, 1)
            finish(2 * pair + 1, 1)
            multiply(2 * pair + 2, 0)

        if tiles % 2 == 0:
            multiply(tiles - 1, 1)
            finish(tiles - 2, 0)
            finish(tiles - 1, 1)
        else:
            finish(tiles - 1, 0)
        keep(("product", slot), slot, product_scr.at[slot], product_ref.at[chunk])
        keep(("save", slot), 2 + slot, save_scr.at[slot], saved_ref.at[chunk])

    def send_near(name, slot):
        source = parts_scr.at[slot, pl.ds(2, 2)]
        state["near", name] = copies.send(source, near_got.at[slot], mask_of(near))

    def free_parts(slot):
        for key in ("near", "far"):
            copy = state.pop((key, "of", slot), None)
            if copy is not None:
                copies.sent_now(copy)

    def times_turned(name, slot, left, weights_ref):
        free_parts(slot)

        @pl.loop(0, width // tile)
        def _(order):
            place = pl.ds(pl.multiple_of(order * tile, tile), tile)
            total = contract_cols(left[...], weights_ref[place, :])
            parts_scr[slot, :, :, place] = total.astype(bf16).reshape(blocks, span, tile)

        send_near(name, slot)
        state["near", "of", slot] = state["near", name]

    def forward_out(chunk):
        times_turned(chunk, chunk % 2, product_scr.at[chunk % 2], out_ref)

    def sum_near(name, chunk):
        slot = chunk % 2
        state["near", name].wait_recv()
        add_into(parts_scr.at[slot, pl.ds(0, 2)], near_got.at[slot])
        copy = copies.send(parts_scr.at[slot, 1], far_got.at[chunk], mask_of(far))
        state["far", name] = copy
        state["far", "of", slot] = copy

    block = 32

    def row_blocks(function):
        @pl.loop(0, span // block)
        def _(order):
            function(pl.ds(pl.multiple_of(order * block, block), block))

    def line(index):
        return vector_ref[index : index + 1, :]

    def add_sum(index, rows):
        sums_ref[index : index + 1, :] += jnp.sum(rows, axis=0, keepdims=True)

    def second_norm(chunk):
        slot = chunk % 2
        state["far", chunk].wait_recv()
        loaded(("normed", slot))
        for key in ("low near", "low far"):
            copy = state.pop((key, slot), None)
            if copy is not None:
                copies.sent_now(copy)
        keep_done(("low", slot))

        def body(rows):
            hidden = normed_scr[slot, rows] * line(gain_one) + line(shift_one)
            mlp_branch = parts_scr[slot, 0, rows].astype(f32) + far_got[chunk, rows].astype(f32)
            normed, inverse = norm_rows(deep_alpha * hidden + mlp_branch + line(b_down))
            layer_ref[chunk, rows] = (normed * line(gain_two) + line(shift_two)).astype(bf16)
            grad = cotangent_ref[chunk, rows].astype(f32)
            resid = norm_rows_back(grad, normed, inverse, line(gain_two))
            low = resid.astype(bf16)
            resid_scr[chunk, rows] = resid
            low_scr[slot, rows] = low
            add_sum(3, grad * normed)
            add_sum(4, grad)
            add_sum(5, low.astype(f32))

        row_blocks(body)
        if chunk + 2 < chunks:
            load_normed(chunk + 2)
        source = low_scr.at[slot]
        keep(("low", slot), 4 + slot, source, grad_shared_ref.at[chunk, 0])
        state["low far", slot] = copies.send(source, grad_shared_ref.at[chunk, 1], mask_of(far))
        state["low near", slot] = copies.send(source, grad_shared_ref.at[chunk, 2], mask_of(near))
        state["grad far", chunk] = state["low far", slot]
        state["grad near", chunk] = state["low near", slot]

    def pass_on(chunk):
        state["grad far", chunk].wait_recv()
        part = grad_shared_ref.at[chunk, 1]
        state["grad cross", chunk] = copies.send(
            part, grad_shared_ref.at[chunk, 3], mask_of(near)
        )

    def load_grads(chunk):
        slot = chunk % 2
        keep_done(("low", slot))
        state["grad near", chunk].wait_recv()
        state["grad cross", chunk].wait_recv()
        load(("rows", slot), slot, grad_shared_ref.at[chunk], rows_scr.at[slot])
        keep_done(("save", slot))
        load(("save", slot), 4 + slot, saved_ref.at[chunk], save_scr.at[slot])

    def backward_gate(chunk):
        slot = chunk % 2
        loaded(("rows", slot))
        loaded(("save", slot))
        keep_done("grad in")
        rows = rows_scr.at[slot]

        def columns_of(first, count):
            columns = pl.ds(pl.multiple_of(first * 128, 128), count * 128)
            grad = dot(rows[...].reshape(group_rows, width), out_ref[:, columns])
            for order in range(count):
                part = grad[:, order * 128 : (order + 1) * 128]
                saved = pl.ds(pl.multiple_of((first + order) * 128, 128), 128)
                for which in range(2):
                    low = (part * save_scr[slot, which, :, saved].astype(f32)).astype(bf16)
                    place = pl.ds(
                        pl.multiple_of((2 * (first + order) + which) * 128, 128), 128
                    )
                    grad_in_scr[:, place] = low
                    in_sum_ref[:, place] += jnp.sum(low.astype(f32), axis=0, keepdims=True)

        @pl.loop(0, tiles // 2)
        def _(pair):
            columns_of(2 * pair, 2)

        if tiles % 2:
            columns_of(tiles - 1, 1)
        keep("grad in", 6, grad_in_scr, grad_in_ref.at[chunk])

    def backward_in(chunk):
        times_turned(("back", chunk), chunk % 2, grad_in_scr, in_ref)

    def first_norm(chunk):
        slot = chunk % 2
        state["far", ("back", chunk)].wait_recv()
        loaded(("normed", slot))

        def body(rows):
            grad = parts_scr[slot, 0, rows].astype(f32) + far_got[chunk, rows].astype(f32)
            grad = grad + deep_alpha * resid_scr[chunk, rows]
            normed = normed_scr[slot, rows]
            place = pl.ds(pl.multiple_of(chunk * span + rows.start, block), block)
            resid = norm_rows_back(grad, normed, inverse_ref[place, 0:1], line(gain_one))
            resid_scr[chunk, rows] = resid
            add_sum(0, grad * normed)
            add_sum(1, grad)
            add_sum(2, resid.astype(bf16).astype(f32))

        row_blocks(body)
        if chunk + 2 < chunks:
            load_normed(chunk + 2)
        keep(("resid", chunk), 7 + chunk, resid_scr.at[chunk], resid_ref.at[chunk])

    load_shared(0)
    load_normed(0)
    load_normed(1)
    last = chunks - 1
    for chunk in range(chunks):
        forward_gate(chunk)
        if chunk >= 1:
            sum_near(chunk - 1, chunk - 1)
        if chunk >= 2:
            second_norm(chunk - 2)
        if chunk >= 3:
            pass_on(chunk - 3)
        forward_out(chunk)
    sum_near(last, last)
    second_norm(last - 1)
    pass_on(last - 2)
    waiting = [("norm", last), ("pass", last - 1), ("pass", last)]
    for chunk in range(chunks):
        if chunk == 0:
            load_grads(0)
        backward_gate(chunk)
        spread_block()
        if waiting and waiting[0][0] == "norm":
            second_norm(waiting.pop(0)[1])
            load_normed(0)
            load_normed(1)
        if waiting:
            pass_on(waiting.pop(0)[1])
        if chunk >= 1:
            sum_near(("back", chunk - 1), chunk - 1)
        if chunk >= 2:
            first_norm(chunk - 2)
        if chunk + 1 < chunks:
            if chunk + 1 == last and waiting:
                pass_on(waiting.pop(0)[1])
            load_grads(chunk + 1)
        backward_in(chunk)
    sum_near(("back", last), last)
    first_norm(last - 1)
    first_norm(last)
    wait_all(spread[-1:])
    for name in list(keeps):
        keep_done(name)
    copies.end()


def ff_call(
    item_bits, shared, normed, inverse, cotangent, w_in, w_out, vectors, in_bias, block
):
    chunks, blocks, span, width = shared.shape
    group_rows = blocks * span
    ff_part = w_out.shape[1]
    any_space = pl.BlockSpec(memory_space=pl.ANY)
    near_space = pl.BlockSpec(memory_space=pltpu.VMEM)
    spare = 8 * chunks
    return pl.pallas_call(
        functools.partial(ff_kernel, item_bits),
        in_specs=[any_space, any_space] + [near_space] * 6 + [any_space],
        out_specs=[any_space] * 4 + [near_space, any_space, near_space, near_space, any_space],
        out_shape=[
            jax.ShapeDtypeStruct((chunks, group_rows, ff_part), bf16),
            jax.ShapeDtypeStruct((chunks, 2, group_rows, ff_part), bf16),
            jax.ShapeDtypeStruct((chunks, blocks, span, width), bf16),
            jax.ShapeDtypeStruct((chunks, group_rows, 2 * ff_part), bf16),
            jax.ShapeDtypeStruct((chunks, span, width), bf16),
            jax.ShapeDtypeStruct((chunks, span, width), f32),
            jax.ShapeDtypeStruct((8, width), f32),
            jax.ShapeDtypeStruct((1, 2 * ff_part), f32),
            jax.ShapeDtypeStruct((2 ** len(item_bits),) + block.shape, bf16),
        ],
        scratch_shapes=[
            pltpu.VMEM((2, blocks, span, width), bf16),
            pltpu.VMEM((2, group_rows, ff_part), bf16),
            pltpu.VMEM((2, 2, group_rows, ff_part), bf16),
            pltpu.VMEM((2, blocks, span, width), bf16),
            pltpu.VMEM((2, 2, span, width), bf16),
            pltpu.VMEM((chunks, span, width), bf16),
            pltpu.VMEM((2, span, width), bf16),
            pltpu.VMEM((group_rows, 2 * ff_part), bf16),
            pltpu.VMEM((chunks, span, width), f32),
            pltpu.VMEM((2, span, width), f32),
            pltpu.VMEM((2, group_rows, 256), f32),
            pltpu.SemaphoreType.DMA((spare,)),
            pltpu.SemaphoreType.DMA((spare,)),
            pltpu.SemaphoreType.DMA((6,)),
            pltpu.SemaphoreType.DMA((8 + chunks,)),
        ],
        compiler_params=pltpu.CompilerParams(
            collective_id=3, has_side_effects=True, vmem_limit_bytes=60 * 2**20
        ),
        name="feed_forward",
    )(shared, normed, inverse, cotangent, w_in, w_out, vectors, in_bias, block)


def on_device(
    token_ids,
    masked,
    item_flag,
    prefix,
    cotangent,
    embedding,
    heads_weight,
    heads_bias,
    dense_weight,
    dense_bias,
    first_gain,
    first_bias,
    up_weight,
    up_bias,
    down_weight,
    down_bias,
    second_gain,
    second_bias,
):
    lines = Lines()
    items_here, span = token_ids.shape
    items_size, seq_size = lax.axis_size("items"), lax.axis_size("seq")
    item_place, seq_place = lax.axis_index("items"), lax.axis_index("seq")
    count = items_size * seq_size
    length = span * seq_size
    width = embedding.shape[0] * count
    vocab = embedding.shape[1]
    heads_here = HEADS // seq_size
    packed_width = heads_here * 3 * HEAD
    rows_here = up_weight.shape[0]
    ff_width = down_weight.shape[0]
    members = 4
    groups = count // members
    member = seq_place % members
    ff_part = -(-ff_width // (members * 128)) * 128
    ff_all = members * ff_part

    item_bits, seq_bits = bits_of("items"), bits_of("seq")
    outer_bits = seq_bits[2:]

    input_ids = jnp.where(masked == 1, mask_token, token_ids)
    flat_place = item_place * seq_size + seq_place
    row_count = rows_here + 16
    bias_row = lax.dynamic_update_slice(
        jnp.zeros((16, heads_weight.shape[1]), bf16),
        heads_bias[None],
        (0, flat_place * heads_bias.shape[0]),
    )
    ones_row = jnp.zeros((16, vocab), bf16).at[0].set(1.0)
    def rows_of(part):
        part = part.reshape(-1)
        return jnp.pad(part, (0, -part.shape[0] % 128)).reshape(-1, 128)

    small = [
        embedding,
        ones_row,
        rows_of(input_ids.astype(bf16)),
        rows_of(
            jnp.concatenate(
                [dense_bias, first_gain, first_bias, down_bias, second_gain, second_bias]
            )
        ),
    ]
    ends = [0]
    for part in small:
        ends.append(ends[-1] + part.shape[0])
    small.append(jnp.zeros((-ends[-1] % 16, 128), bf16))
    flat = jnp.concatenate(small, axis=0)

    def by_member(part):
        padded = jnp.pad(part, ((0, 0), (0, ff_all - ff_width)))
        return jnp.transpose(padded.reshape(rows_here, 2, 2, ff_part), (1, 2, 0, 3))

    tiles = ff_part // 128

    def woven(up, gate):
        shape = up.shape[:-1] + (tiles, 128)
        return jnp.stack([up.reshape(shape), gate.reshape(shape)], axis=-2).reshape(
            up.shape[:-1] + (2 * ff_part,)
        )

    def unwoven(both_parts):
        parts = both_parts.reshape(both_parts.shape[:-1] + (tiles, 2, 128))
        shape = both_parts.shape[:-1] + (ff_part,)
        return parts[..., 0, :].reshape(shape), parts[..., 1, :].reshape(shape)

    parts_in = woven(by_member(up_weight[:, :ff_width]), by_member(up_weight[:, ff_width:]))
    parts_out = by_member(down_weight.T)
    everyone, mixed_table, w_block, w_dense, own_in, own_out = first_call(
        item_bits,
        seq_bits,
        flat,
        heads_weight,
        bias_row,
        dense_weight,
        parts_in,
        parts_out,
    )
    w_dense = w_dense.reshape(width, width)
    w_block = w_block[:, :rows_here].reshape(seq_size * rows_here, packed_width)
    pieces = [everyone[:, :, a:b] for a, b in zip(ends[:-1], ends[1:])]
    table = pieces[0].reshape(width, vocab)
    vector_rows = pieces[3].reshape(count, -1)[:, : 6 * rows_here].reshape(count, 6, rows_here)
    vectors = jnp.transpose(vector_rows, (1, 0, 2)).reshape(6, width).astype(f32)
    ids_here = pick(pieces[2], item_place, 0).reshape(seq_size, items_here, span)
    ids_here = jnp.transpose(ids_here, (1, 0, 2)).reshape(items_here, length).astype(jnp.int32)
    in_bias = jnp.pad(
        up_bias.astype(f32).reshape(2, ff_width), ((0, 0), (0, ff_all - ff_width))
    )
    in_bias = lax.dynamic_slice(in_bias, (0, member * ff_part), (2, ff_part))
    in_bias = woven(in_bias[:1], in_bias[1:])

    vocab_index = jnp.arange(vocab, dtype=jnp.int32)
    frequency = np.exp(np.arange(HEAD // 2) * (-2.0 * math.log(10000.0) / HEAD))
    angles = np.arange(length)[:, None] * frequency[None, :]
    cosine, sine_part = np.cos(angles), np.sin(angles)
    cosine = jnp.asarray(np.concatenate([cosine, cosine], axis=1), f32)
    sine_part = jnp.asarray(np.concatenate([-sine_part, sine_part], axis=1), f32)
    visible = jnp.where(item_flag == 1, length, prefix)
    tables = table_halves(mixed_table)
    onehots = (ids_here[:, :, None] == vocab_index).astype(bf16)
    own_onehot = (input_ids.reshape(-1)[:, None] == vocab_index[None, :]).astype(bf16)
    vectors = jnp.concatenate([vectors[1:], vectors[:1], jnp.zeros((2, width), f32)], axis=0)
    context, log_sums, w_in, w_out, shared, normed, inverse = second_call(
        item_bits,
        seq_bits,
        visible,
        onehots,
        tables,
        cosine,
        sine_part,
        own_onehot,
        table,
        vectors,
        w_dense,
        own_in,
        own_out,
    )
    product, _, grad_shared, grad_in, layer_out, grad_resid, sums, in_sum, w_slice = ff_call(
        item_bits,
        shared,
        normed,
        inverse,
        cotangent,
        w_in.reshape(width, 2 * ff_part),
        w_out.reshape(width, ff_part),
        vectors,
        in_bias,
        w_block,
    )
    rows_all = items_here * span
    group_all = members * rows_all
    context = context.reshape(rows_all, width)
    grad_resid = grad_resid.reshape(rows_all, width)
    grad_branch = grad_resid.astype(bf16)
    grad_context = contract_cols(grad_branch, w_dense).astype(bf16)
    core = my_bit(*seq_bits[0])

    def of_core(columns, which):
        parts = columns.reshape(columns.shape[0], count // 2, 2, rows_here)
        return pick(parts, which, 2).reshape(columns.shape[0], -1)

    def row_sums(which):
        grads = of_core(grad_branch, which)
        return jnp.concatenate(
            [
                contract_rows(of_core(context, which), grad_branch).astype(bf16),
                contract_rows(grads, own_onehot).astype(bf16),
                jnp.pad(of_core(sums, which).T, ((0, 0), (0, 120))).astype(bf16),
            ],
            axis=1,
        )

    by_rows = (
        row_sums(core).astype(f32) + lines.swap(row_sums(1 - core), *seq_bits[0]).astype(f32)
    ).astype(bf16)
    row_dims = item_bits[::-1] + seq_bits[:0:-1]
    by_rows = by_rows.reshape((2,) * len(row_dims) + (rows_here, -1))
    in_sum = jnp.concatenate(unwoven(in_sum), axis=0)
    in_all = lax.dynamic_update_slice(
        jnp.zeros((2, ff_all), f32), in_sum, (0, member * ff_part)
    ).reshape(-1, 128)
    w_slice = w_slice.reshape(width, packed_width)
    attention = (
        item_bits,
        seq_bits,
        visible,
        onehots,
        tables,
        cosine,
        sine_part,
        log_sums,
        w_slice.T,
    )
    shared = shared.reshape(group_all, width)
    grad_in = grad_in.reshape(group_all, 2 * ff_part)
    grad_shared = grad_shared.reshape(group_all, width)
    product = product.reshape(group_all, ff_part)
    if len(item_bits) == 2 and len(seq_bits) == 3 and rows_here % 32 == 0:
        spread, token_all, parts, by_rows, in_all = merged_call(
            *attention,
            grad_context.reshape(items_here, span, width),
            shared,
            grad_in,
            grad_shared,
            product,
            by_rows,
            in_all,
        )[:5]
        in_part = jnp.concatenate([parts[1], parts[2]], axis=-1)
        out_part = parts[0]
    else:
        by_head = lax.all_to_all(
            jnp.transpose(
                grad_context.reshape(items_here, span, seq_size, heads_here * HEAD), (0, 2, 1, 3)
            ),
            "seq",
            split_axis=1,
            concat_axis=1,
            tiled=True,
        ).reshape(items_here, length, heads_here * HEAD)
        group_dims = (2,) * (len(item_bits) + len(outer_bits)) + (members * rows_here, -1)
        spread, token_all, in_part, out_part, by_rows, in_all = third_call(
            *attention,
            by_head,
            contract_rows(shared, grad_in).astype(bf16).reshape(group_dims),
            contract_rows(grad_shared, product).astype(bf16).reshape(group_dims),
            by_rows,
            in_all,
        )
    input_grads = spread.astype(f32) + deep_alpha * grad_resid.reshape(spread.shape)
    token_all = jnp.transpose(token_all, (2, 0, 1, 3)).reshape(vocab, -1)

    def from_members(part):
        taken = jnp.transpose(part, (1, 0, 2)).reshape(rows_here, ff_all)
        return taken[:, :ff_width].astype(f32)

    grad_up, grad_gate = (from_members(part) for part in unwoven(in_part))
    grad_down = from_members(out_part)
    by_rows = by_rows.astype(f32)
    grad_dense = by_rows[:, :width]
    token_sum = by_rows[:, width : width + vocab]
    own_vectors = by_rows[:, width + vocab :].T
    in_all = in_all.reshape(2, ff_all)
    grad_up_bias = in_all[:, :ff_width].reshape(-1)

    grad_heads = dot(embedding, token_all)
    grad_heads_bias = lax.dynamic_slice_in_dim(
        jnp.sum(token_all.astype(f32), axis=0),
        (item_place * seq_size + seq_place) * heads_bias.shape[0],
        heads_bias.shape[0],
        0,
    )
    embed_grad = 0.1 * (contract_cols(heads_weight, token_all) + deep_alpha * token_sum)
    return (
        layer_out,
        input_grads,
        embed_grad,
        grad_heads,
        grad_heads_bias,
        grad_dense,
        own_vectors[2],
        own_vectors[0],
        own_vectors[1],
        jnp.concatenate([grad_up, grad_gate], axis=1),
        grad_up_bias,
        grad_down.T,
        own_vectors[5],
        own_vectors[3],
        own_vectors[4],
    )


def solution(mesh):
    in_specs = (
        P("items", "seq"),
        P("items", "seq"),
        P("items"),
        P("items"),
        P("items", "seq", None),
        P(("items", "seq"), None),
        P(("items", "seq"), None),
        P(("items", "seq")),
        P(("items", "seq"), None),
        P(("items", "seq")),
        P(("items", "seq")),
        P(("items", "seq")),
        P(("items", "seq"), None),
        P(),
        P(None, ("items", "seq")),
        P(("items", "seq")),
        P(("items", "seq")),
        P(("items", "seq")),
    )
    out_specs = (
        P("items", "seq", None),
        P("items", "seq", None),
        P(("items", "seq"), None),
        P(("items", "seq"), None),
        P(("items", "seq")),
        P(("items", "seq"), None),
        P(("items", "seq")),
        P(("items", "seq")),
        P(("items", "seq")),
        P(("items", "seq"), None),
        P(),
        P(None, ("items", "seq")),
        P(("items", "seq")),
        P(("items", "seq")),
        P(("items", "seq")),
    )
    return jax.shard_map(
        on_device, mesh=mesh, in_specs=in_specs, out_specs=out_specs, check_vma=False
    )
```

```python
import functools
import math

import jax
import jax.numpy as jnp
import numpy as np
from jax import lax
from jax.experimental import pallas as pl
from jax.experimental.pallas import tpu as pltpu
from jax.sharding import PartitionSpec as P

HEADS = 16
HEAD = 128


deep_alpha = math.sqrt(48.0)
epsilon = 1e-05
mask_token = 3
both = ("items", "seq")
bf16 = jnp.bfloat16
f32 = jnp.float32
score_scale = HEAD ** (-0.5)
exponent_scale = score_scale * math.log2(math.e)


class Lines:
    def __init__(self):
        self.last = {}

    def swap(self, part, axis, bit):
        if (axis, bit) in self.last:
            part, _ = lax.optimization_barrier((part, self.last[axis, bit]))
        size = lax.axis_size(axis)
        got = lax.ppermute(part, axis, [(j, j ^ bit) for j in range(size)])
        self.last[axis, bit] = got
        return got


def bits_of(axis):
    found = []
    bit = 1
    while bit < lax.axis_size(axis):
        found.append((axis, bit))
        bit *= 2
    return found


def my_bit(axis, bit):
    return (lax.axis_index(axis) // bit) % 2


def pick(whole, place, dim):
    return lax.dynamic_index_in_dim(whole, place, dim, keepdims=False)


def moved(masks, axis, bit):
    return (masks[0] ^ (bit if axis == "items" else 0), masks[1] ^ (bit if axis == "seq" else 0))


def contract_rows(left, right):
    return lax.dot_general(left, right, (((0,), (0,)), ((), ())), preferred_element_type=f32)


def contract_cols(left, right):
    return lax.dot_general(left, right, (((1,), (1,)), ((), ())), preferred_element_type=f32)


def dot(left, right):
    return jnp.dot(left, right, preferred_element_type=f32)


def turn(values, cosine, sine_part):
    return values * cosine + pltpu.roll(values, HEAD // 2, 1) * sine_part


def head_parts(onehot_ref, table_ref, cosine, sine_part):
    onehot = onehot_ref[...]
    mixed = dot(jnp.concatenate([onehot, onehot], axis=1), table_ref[...])
    query = turn(mixed[:, :HEAD], cosine, sine_part).astype(bf16)
    key = turn(mixed[:, HEAD : 2 * HEAD], cosine, sine_part).astype(bf16)
    return query, key, mixed[:, 2 * HEAD :].astype(bf16)


def visible_scores(key, query, offset, visible):
    scores = contract_cols(key, query)
    place = offset + lax.broadcasted_iota(jnp.int32, (1, query.shape[0]), 1)
    seen = lax.broadcasted_iota(jnp.int32, scores.shape, 0) < jnp.maximum(place + 1, visible)
    return jnp.where(seen, scores, -1e30)


def table_halves(mixed_table):
    vocab = mixed_table.shape[0]
    by_head = jnp.transpose(mixed_table.reshape(vocab, -1, 3 * HEAD), (1, 0, 2))
    high = lax.reduce_precision(by_head, 8, 7)
    return jnp.concatenate([high.astype(bf16), (by_head - high).astype(bf16)], axis=1)


def norm_rows(rows):
    center = rows - jnp.mean(rows, axis=-1, keepdims=True)
    inverse = lax.rsqrt(jnp.mean(center * center, axis=-1, keepdims=True) + epsilon)
    return center * inverse, inverse


def norm_rows_back(grad, normed, inverse, gain):
    scaled = grad * gain
    return inverse * (
        scaled
        - jnp.mean(scaled, axis=-1, keepdims=True)
        - normed * jnp.mean(scaled * normed, axis=-1, keepdims=True)
    )


MESH = pl.DeviceIdType.MESH


class Copies:
    def __init__(self, send_sems, recv_sems, local_sems):
        self.sems = send_sems, recv_sems, local_sems
        self.sent = {}
        self.moved = 0
        self.count = 0
        self.here = lax.axis_index("items"), lax.axis_index("seq")

    def send(self, source, target, masks):
        order = self.count
        self.count += 1
        copy = pltpu.make_async_remote_copy(
            src_ref=source,
            dst_ref=target,
            send_sem=self.sems[0].at[order],
            recv_sem=self.sems[1].at[order],
            device_id=(self.here[0] ^ masks[0], self.here[1] ^ masks[1]),
            device_id_type=MESH,
        )
        copy.start()
        self.sent[id(copy)] = copy
        return copy

    def move(self, source, target):
        copy = pltpu.make_async_copy(source, target, self.sems[2].at[self.moved])
        self.moved += 1
        copy.start()
        return copy

    def sent_now(self, copy):
        self.sent.pop(id(copy)).wait_send()

    def end(self):
        for copy in self.sent.values():
            copy.wait_send()


def wait_all(copies):
    for copy in copies:
        copy.wait_recv()


def mask_of(step):
    return moved((0, 0), *step)


def greet(masks):
    barrier = pltpu.get_barrier_semaphore()
    here = lax.axis_index("items"), lax.axis_index("seq")
    for mask_i, mask_s in masks:
        pl.semaphore_signal(
            barrier,
            inc=1,
            device_id=(here[0] ^ mask_i, here[1] ^ mask_s),
            device_id_type=MESH,
        )
    pl.semaphore_wait(barrier, len(masks))


def partners(seq_size, item_bits):
    return [(0, mask) for mask in range(1, seq_size)] + [mask_of(step) for step in item_bits]


def aligned(place, size):
    return pl.ds(place // size * size, size)


def first_kernel(
    item_bits,
    seq_bits,
    row_count,
    small_ref,
    heads_ref,
    head_bias_ref,
    dense_ref,
    in_ref,
    out_ref,
    everyone_ref,
    table_ref,
    block_ref,
    dense_all_ref,
    own_in_ref,
    own_out_ref,
    embed_scr,
    block_scr,
    sum_scr,
    got_scr,
    send_sems,
    recv_sems,
    local_sems,
):
    items_size, seq_size = everyone_ref.shape[:2]
    item_place, seq_place = lax.axis_index("items"), lax.axis_index("seq")
    core, chip = seq_place % 2, seq_place // 2
    member = seq_place % 4
    rows = dense_ref.shape[0]
    columns = block_scr.shape[2]
    greet(partners(seq_size, item_bits))
    copies = Copies(send_sems, recv_sems, local_sems)

    def head_columns(place, source):
        return source.at[:, pl.ds(pl.multiple_of(place * columns, 128), columns)]

    head_rows = [
        (heads_ref, pl.ds(0, rows)),
        (head_bias_ref, pl.ds(rows, row_count - rows)),
    ]

    small = [copies.send(small_ref, everyone_ref.at[item_place, seq_place], mask_of(seq_bits[0]))]
    heads = [
        copies.send(
            head_columns(seq_place ^ mask, source), block_scr.at[seq_place, place], (0, mask)
        )
        for mask in range(1, seq_size)
        for source, place in head_rows
    ]
    dense = [
        copies.send(dense_ref, dense_all_ref.at[item_place, chip, core], mask_of(seq_bits[1]))
    ]
    mine = pl.ds(pl.multiple_of(member * rows, rows), rows)
    shares = []

    def share(source, target):
        for mask in range(1, 4):
            other = member ^ mask
            shares.append(
                copies.send(source.at[other // 2, other % 2], target.at[mine], (0, mask))
            )

    local = [
        copies.move(small_ref, everyone_ref.at[item_place, seq_place]),
        copies.move(dense_ref, dense_all_ref.at[item_place, chip, core]),
        copies.move(head_columns(seq_place, heads_ref), block_scr.at[seq_place, head_rows[0][1]]),
        copies.move(
            head_columns(seq_place, head_bias_ref), block_scr.at[seq_place, head_rows[1][1]]
        ),
        copies.move(in_ref.at[member // 2, core], own_in_ref.at[0, mine]),
        copies.move(out_ref.at[member // 2, core], own_out_ref.at[mine]),
    ]
    for copy in local:
        copy.wait()

    for order in range(1, len(seq_bits)):
        if order > 1:
            wait_all(dense[-1:])
            part = dense_all_ref.at[item_place, aligned(chip, 2 ** (order - 1)), core]
            dense.append(copies.send(part, part, mask_of(seq_bits[order])))
        wait_all(small[-1:])
        part = everyone_ref.at[item_place, aligned(seq_place, 2**order)]
        small.append(copies.send(part, part, mask_of(seq_bits[order])))
        if order == 1:
            share(in_ref, own_in_ref.at[0])
    wait_all(small[-1:])
    embed = copies.move(everyone_ref.at[item_place, :, pl.ds(0, row_count)], embed_scr)

    wait_all(heads)
    embed.wait()
    sum_scr[0] = lax.dot_general(
        embed_scr[...].reshape(seq_size * row_count, -1),
        block_scr[...].reshape(seq_size * row_count, columns),
        (((0,), (0,)), ((), ())),
        preferred_element_type=f32,
    )
    sums = copies.send(sum_scr.at[0], got_scr.at[0], mask_of(item_bits[0]))
    block_out = copies.move(block_scr, block_ref)
    part = everyone_ref.at[item_place]
    small.append(copies.send(part, part, mask_of(item_bits[0])))
    share(out_ref, own_out_ref)
    wait_all(dense[-1:])

    def dense_part(mask):
        return dense_all_ref.at[item_place ^ mask, :, core]

    known = [0]
    waves = []
    for step in item_bits[::-1]:
        waves.append([(mask, step) for mask in known])
        known = known + [mask ^ step[1] for mask in known]
    arrived = {}
    for wave in waves:
        part = dense_part(0)
        arrived[wave[0][1][1]] = copies.send(part, part, mask_of(wave[0][1]))
    near = [copies.send(dense_part(0), dense_part(0), mask_of(seq_bits[0]))]
    wait_all(shares[:3])
    outer = []
    if len(seq_bits) == 3:
        first = pl.ds(0, 2 * rows)
        outer.append(
            copies.send(own_in_ref.at[0, first], own_in_ref.at[1, first], mask_of(seq_bits[2]))
        )
    for order, step in enumerate(item_bits):
        sums.wait_recv()
        sum_scr[order + 1] = sum_scr[order] + got_scr[order]
        if order + 1 < len(item_bits):
            sums = copies.send(
                sum_scr.at[order + 1], got_scr.at[order + 1], mask_of(item_bits[order + 1])
            )
            wait_all(small[-1:])
            part = everyone_ref.at[aligned(item_place, 2 ** (order + 1))]
            small.append(copies.send(part, part, mask_of(item_bits[order + 1])))
        if order < len(waves) and order + 1 < len(item_bits):
            wave = waves[order]
            for mask, step in wave:
                arrived[mask ^ step[1]].wait_recv()
                part = dense_part(mask ^ step[1])
                for later in waves[order + 1 :]:
                    arrived[mask ^ step[1] ^ later[0][1][1]] = copies.send(
                        part, part, mask_of(later[0][1])
                    )
                near.append(copies.send(part, part, mask_of(seq_bits[0])))
    table_ref[...] = sum_scr[len(item_bits)]

    for mask, step in waves[-1]:
        arrived[mask ^ step[1]].wait_recv()
        part = dense_part(mask ^ step[1])
        near.append(copies.send(part, part, mask_of(seq_bits[0])))
    wait_all(near)
    wait_all(shares[3:])
    wait_all(outer)
    wait_all(small[-1:])
    block_out.wait()
    copies.end()


def first_call(item_bits, seq_bits, small, heads, head_bias, dense, parts_in, parts_out):
    items_size, seq_size = 2 ** len(item_bits), 2 ** len(seq_bits)
    row_count = heads.shape[0] + head_bias.shape[0]
    rows, width = dense.shape
    vocab = small.shape[1]
    columns = heads.shape[1] // seq_size
    any_space = pl.BlockSpec(memory_space=pl.ANY)
    spare = 8 * (len(item_bits) + len(seq_bits)) + 4 * seq_size + 2 ** (len(item_bits) + 2)
    return pl.pallas_call(
        functools.partial(first_kernel, item_bits, seq_bits, row_count),
        in_specs=[any_space] * 6,
        out_specs=[any_space, pl.BlockSpec(memory_space=pltpu.VMEM)] + [any_space] * 4,
        out_shape=[
            jax.ShapeDtypeStruct((items_size, seq_size) + small.shape, bf16),
            jax.ShapeDtypeStruct((vocab, columns), f32),
            jax.ShapeDtypeStruct((seq_size, row_count, columns), bf16),
            jax.ShapeDtypeStruct((items_size, seq_size // 2, 2, rows, width), bf16),
            jax.ShapeDtypeStruct((2, 4 * rows, parts_in.shape[3]), bf16),
            jax.ShapeDtypeStruct((4 * rows, parts_out.shape[3]), bf16),
        ],
        scratch_shapes=[
            pltpu.VMEM((seq_size, row_count, vocab), bf16),
            pltpu.VMEM((seq_size, row_count, columns), bf16),
            pltpu.VMEM((len(item_bits) + 1, vocab, columns), f32),
            pltpu.VMEM((len(item_bits), vocab, columns), f32),
            pltpu.SemaphoreType.DMA((spare,)),
            pltpu.SemaphoreType.DMA((spare,)),
            pltpu.SemaphoreType.DMA((8,)),
        ],
        compiler_params=pltpu.CompilerParams(
            collective_id=0, has_side_effects=True, vmem_limit_bytes=24 * 2**20
        ),
        name="first",
    )(small, heads, head_bias, dense, parts_in, parts_out)


class Spread:
    def __init__(self, copies, own, whole, outer_bits, item_bits, given=None):
        self.copies, self.own, self.whole, self.given = copies, own, whole, given
        self.outer_bits, self.item_bits = outer_bits, item_bits
        half = own.shape[0] // 2
        self.halves = pl.ds(0, half), pl.ds(half, half)
        self.last = []

    def part(self, masks):
        place = (self.copies.here[0] ^ masks[0]) * lax.axis_size("seq")
        return self.whole.at[(place + (self.copies.here[1] ^ masks[1])) // 4]

    def over(self, masks, step, rows=None):
        source = self.own if masks == (0, 0) else self.part(masks)
        target = self.part(masks)
        if rows is not None:
            source, target = source.at[rows], target.at[rows]
        return self.copies.send(source, target, mask_of(step))

    def start(self):
        self.local = self.copies.move(self.own, self.part((0, 0)))
        self.first = [self.over((0, 0), step) for step in self.item_bits]

    def start_given(self):
        masks = mask_of(self.outer_bits[0])
        target = self.part(masks).at[self.halves[0]]
        self.local_given = self.copies.move(self.given, target)
        self.second = [
            [self.copies.send(self.given, target, mask_of(step)) for step in self.item_bits],
            [],
        ]
        self.outer = [None, self.over((0, 0), self.outer_bits[0], self.halves[1])]

    def start_outer(self):
        self.outer = [self.over((0, 0), self.outer_bits[0], rows) for rows in self.halves]
        self.second = [[], []]

    def cross_own(self):
        one, two = self.item_bits
        self.first[0].wait_recv()
        self.last.append(self.over(moved((0, 0), *one), two, self.halves[0]))
        self.first[1].wait_recv()
        self.last.append(self.over(moved((0, 0), *two), one, self.halves[1]))

    def spread_outer(self, which):
        self.outer[which].wait_recv()
        masks = mask_of(self.outer_bits[0])
        self.second[which] = [
            self.over(masks, step, self.halves[which]) for step in self.item_bits
        ]

    def cross_outer(self, which):
        masks = mask_of(self.outer_bits[0])
        steps = self.item_bits if which == 0 else self.item_bits[::-1]
        copies = self.second[which] if which == 0 else self.second[which][::-1]
        copies[0].wait_recv()
        self.last.append(self.over(moved(masks, *steps[0]), steps[1], self.halves[which]))
        self.last.append(copies[1])

    def plain(self):
        self.local = self.copies.move(self.own, self.part((0, 0)))
        known = [(0, 0)]
        for step in self.outer_bits + self.item_bits:
            wait_all([self.over(masks, step) for masks in known])
            known = known + [moved(masks, *step) for masks in known]

    def end(self):
        wait_all(self.last)
        self.local.wait()
        if self.given is not None:
            self.local_given.wait()


def attend_unit(block, visible, onehot_ref, table_ref, cosine_ref, sine_ref, context_ref, lse_ref):
    query, key, value = head_parts(onehot_ref, table_ref, cosine_ref[...], sine_ref[...])
    value_turned = value.T
    for offset in range(0, query.shape[0], block):
        scores = visible_scores(key, query[offset : offset + block], offset, visible)
        peak = jnp.max(scores, axis=0, keepdims=True)
        expos = jnp.exp2((scores - peak) * exponent_scale)
        total = jnp.sum(expos, axis=0, keepdims=True)
        context = dot(value_turned, expos.astype(bf16)) / total
        context_ref[offset : offset + block, :] = context.T.astype(bf16)
        lse_ref[:, offset : offset + block] = peak * exponent_scale + jnp.log2(total)


def second_kernel(
    item_bits,
    seq_bits,
    visible_ref,
    onehot_ref,
    table_ref,
    cosine_ref,
    sine_ref,
    own_onehot_ref,
    embed_ref,
    vector_ref,
    dense_ref,
    own_in_ref,
    own_out_ref,
    context_ref,
    lse_ref,
    in_ref,
    out_ref,
    shared_ref,
    normed_ref,
    inverse_ref,
    context_scr,
    dense_scr,
    resid_scr,
    low_scr,
    send_sems,
    recv_sems,
    local_sems,
):
    seq_size = 2 ** len(seq_bits)
    items_here, length, features = context_scr.shape
    heads_here = features // HEAD
    span = length // seq_size
    width = dense_ref.shape[0]
    seq_place = lax.axis_index("seq")
    outer_bits = seq_bits[2:]
    greet(partners(seq_size, item_bits))
    copies = Copies(send_sems, recv_sems, local_sems)
    dense_copy = copies.move(dense_ref, dense_scr)
    stepwise = len(outer_bits) == 1 and len(item_bits) == 2
    given = own_in_ref.at[1, pl.ds(0, own_in_ref.shape[1] // 2)] if stepwise else None
    spreads = [
        Spread(copies, own_in_ref.at[0], in_ref, outer_bits, item_bits, given),
        Spread(copies, own_out_ref, out_ref, outer_bits, item_bits),
    ]
    if stepwise:
        spreads[0].start()
        spreads[0].start_given()
    arrivals, local = [], []
    for item in range(items_here):

        @pl.loop(0, heads_here)
        def _(head):
            place = pl.ds(pl.multiple_of(head * HEAD, HEAD), HEAD)
            attend_unit(
                min(256, length),
                visible_ref[item],
                onehot_ref.at[item],
                table_ref.at[head],
                cosine_ref,
                sine_ref,
                context_scr.at[item, :, place],
                lse_ref.at[item, head],
            )

        target = context_ref.at[
            item, :, pl.ds(pl.multiple_of(seq_place * features, HEAD), features)
        ]
        for mask in range(seq_size):
            rows = pl.ds(pl.multiple_of((seq_place ^ mask) * span, span), span)
            source = context_scr.at[item, rows]
            if mask:
                arrivals.append(copies.send(source, target, (0, mask)))
            else:
                local.append(copies.move(source, target))
    if stepwise:
        spreads[0].cross_own()
        spreads[0].cross_outer(0)
        spreads[1].start()
        spreads[0].spread_outer(1)
    wait_all(arrivals)
    for copy in local:
        copy.wait()

    if stepwise:
        spreads[1].start_outer()

    dense_copy.wait()
    rows_all = items_here * span
    tile = 256

    @pl.loop(0, width // tile)
    def _(order):
        place = pl.ds(pl.multiple_of(order * tile, tile), tile)
        branch = dot(context_ref[...].reshape(rows_all, width), dense_scr[:, place])
        inputs = contract_cols(own_onehot_ref[...], embed_ref[place, :])
        resid_scr[:, place] = deep_alpha * inputs + (branch + vector_ref[5:6, place])

    block = 32
    near, far = ("seq", 1), ("seq", 2)
    far_copies, near_copies, own_copies = [], [], []
    for item in range(items_here):

        @pl.loop(0, span // block)
        def _(order):
            start = pl.multiple_of(order * block, block)
            rows = pl.ds(pl.multiple_of(item * span + start, block), block)
            normed, inverse = norm_rows(resid_scr[rows, :])
            normed_ref[rows, :] = normed
            inverse_ref[rows, :] = jnp.broadcast_to(inverse, (block, 128))
            hidden = normed * vector_ref[0:1, :] + vector_ref[1:2, :]
            low_scr[item, pl.ds(start, block), :] = hidden.astype(bf16)

        source = low_scr.at[item]
        far_copies.append(copies.send(source, shared_ref.at[item, 1], mask_of(far)))
        near_copies.append(copies.send(source, shared_ref.at[item, 2], mask_of(near)))
        own_copies.append(copies.move(source, shared_ref.at[item, 0]))

    def pass_on(item):
        far_copies[item].wait_recv()
        part = shared_ref.at[item, 1]
        near_copies.append(copies.send(part, shared_ref.at[item, 3], mask_of(near)))

    if stepwise:
        spreads[1].cross_own()
        spreads[0].cross_outer(1)
    pass_on(0)
    if stepwise:
        spreads[1].spread_outer(0)
    pass_on(1)
    if stepwise:
        spreads[1].spread_outer(1)
        spreads[1].cross_outer(0)
    for item in range(2, items_here):
        pass_on(item)
    if stepwise:
        spreads[1].cross_outer(1)
    else:
        for one in spreads:
            one.plain()
    for one in spreads:
        one.end()
    wait_all(near_copies)
    for copy in own_copies:
        copy.wait()
    copies.end()


def second_call(
    item_bits,
    seq_bits,
    visible,
    onehots,
    tables,
    cosine,
    sine_part,
    own_onehot,
    embed,
    vectors,
    w_dense,
    own_in,
    own_out,
):
    items_here, length, vocab = onehots.shape
    heads_here = tables.shape[0]
    features = heads_here * HEAD
    seq_size = 2 ** len(seq_bits)
    span = length // seq_size
    width = w_dense.shape[0]
    groups = 2 ** (len(item_bits) + len(seq_bits)) // 4
    any_space = pl.BlockSpec(memory_space=pl.ANY)
    near_space = pl.BlockSpec(memory_space=pltpu.VMEM)
    spare = 4 * groups + items_here * (seq_size + 4)
    return pl.pallas_call(
        functools.partial(second_kernel, item_bits, seq_bits),
        in_specs=[pl.BlockSpec(memory_space=pltpu.SMEM)] + [near_space] * 7 + [any_space] * 3,
        out_specs=[near_space] * 2 + [any_space] * 3 + [near_space] * 2,
        out_shape=[
            jax.ShapeDtypeStruct((items_here, span, width), bf16),
            jax.ShapeDtypeStruct((items_here, heads_here, 1, length), f32),
            jax.ShapeDtypeStruct((groups,) + own_in.shape[1:], bf16),
            jax.ShapeDtypeStruct((groups,) + own_out.shape, bf16),
            jax.ShapeDtypeStruct((items_here, 4, span, width), bf16),
            jax.ShapeDtypeStruct((items_here * span, width), f32),
            jax.ShapeDtypeStruct((items_here * span, 128), f32),
        ],
        scratch_shapes=[
            pltpu.VMEM((items_here, length, features), bf16),
            pltpu.VMEM((width, width), bf16),
            pltpu.VMEM((items_here * span, width), f32),
            pltpu.VMEM((items_here, span, width), bf16),
            pltpu.SemaphoreType.DMA((spare,)),
            pltpu.SemaphoreType.DMA((spare,)),
            pltpu.SemaphoreType.DMA((16,)),
        ],
        compiler_params=pltpu.CompilerParams(
            collective_id=1, has_side_effects=True, vmem_limit_bytes=56 * 2**20
        ),
        name="second",
    )(
        visible,
        onehots,
        tables,
        cosine,
        sine_part,
        own_onehot,
        embed,
        vectors,
        w_dense,
        own_in,
        own_out,
    )


def leading(ref):
    return [index for index in np.ndindex(*ref.shape[:-2])]


def add_into(target, source):
    rows = target.shape[-2]
    for index in leading(target):

        @pl.loop(0, rows // 16)
        def _(order):
            place = index + (pl.ds(pl.multiple_of(order * 16, 16), 16),)
            total = target[place].astype(f32) + source[place].astype(f32)
            target[place] = total.astype(target.dtype)


def copy_into(target, source):
    @pl.loop(0, target.shape[0] // 16)
    def _(order):
        place = pl.ds(pl.multiple_of(order * 16, 16), 16)
        target[place] = source[place]


class Reduce:
    def __init__(self, copies, whole, rows, dims, steps, got, stage, stage_sems):
        self.copies, self.whole, self.rows = copies, whole, rows
        self.steps, self.got = steps, got
        self.place = dims.index(steps[0])
        self.stage, self.stage_sems = stage, stage_sems
        self.order = 0

    def first(self, bit, index=()):
        full = (slice(None),) * self.place
        if index:
            full = index[: self.place]
        rest = index[self.place :] if index else ()
        if index:
            return self.whole.at[full + (bit,) + rest + (self.rows,)]
        spare = len(self.whole.shape) - 3 - self.place
        return self.whole.at[full + (bit,) + (slice(None),) * spare + (self.rows,)]

    def start(self):
        step = self.steps[0]
        self.copy = self.copies.send(self.first(1 - my_bit(*step)), self.got[0], mask_of(step))

    def advance(self):
        step = self.steps[self.order]
        self.copy.wait_recv()
        if self.order == 0:
            self.kept = self.got[0]
            rows, columns = self.kept.shape[-2:]
            places = leading(self.kept)

            def load(order):
                return pltpu.make_async_copy(
                    self.first(my_bit(*step), places[order]),
                    self.stage.at[order % 2, pl.ds(0, rows), pl.ds(0, columns)],
                    self.stage_sems.at[order % 2],
                )

            load(0).start()
            for order, place in enumerate(places):
                if order + 1 < len(places):
                    load(order + 1).start()
                load(order).wait()
                add_into(
                    self.kept.at[place],
                    self.stage.at[order % 2, pl.ds(0, rows), pl.ds(0, columns)],
                )
        else:
            self.kept = self.kept.at[my_bit(*step)]
            add_into(self.kept, self.got[self.order])
        self.order += 1
        if self.order < len(self.steps):
            step = self.steps[self.order]
            self.copy = self.copies.send(
                self.kept.at[1 - my_bit(*step)], self.got[self.order], mask_of(step)
            )


def attend_back_unit(
    block,
    visible,
    onehot_ref,
    table_ref,
    cosine_ref,
    sine_ref,
    lse_ref,
    grad_ref,
    mixed_ref,
    sums_ref,
):
    cosine, sine_part = cosine_ref[...], sine_ref[...]
    query, key, value = head_parts(onehot_ref, table_ref, cosine, sine_part)
    key_turned = key.T
    length = query.shape[0]
    grad_key = jnp.zeros((length, HEAD), f32)
    grad_value = jnp.zeros((length, HEAD), f32)
    grad_query = []
    for offset in range(0, length, block):
        query_block = query[offset : offset + block]
        grad_block = grad_ref[offset : offset + block, :]
        scores = visible_scores(key, query_block, offset, visible)
        weights = jnp.exp2(scores * exponent_scale - lse_ref[:, offset : offset + block])
        grad_weights = contract_cols(value, grad_block)
        inner = jnp.sum(weights * grad_weights, axis=0, keepdims=True)
        grad_scores = (weights * (grad_weights - inner)).astype(bf16)
        grad_value = grad_value + dot(weights.astype(bf16), grad_block)
        grad_key = grad_key + dot(grad_scores, query_block)
        grad_query.append(dot(key_turned, grad_scores).T)
    grad_query = jnp.concatenate(grad_query, axis=0)

    def back(grad):
        return turn((grad * score_scale).astype(bf16).astype(f32), cosine, -sine_part).astype(bf16)

    mixed = jnp.concatenate([back(grad_query), back(grad_key), grad_value.astype(bf16)], axis=1)
    mixed_ref[...] = mixed.reshape(mixed_ref.shape)
    sums_ref[...] += dot(onehot_ref[...].T, mixed)


def third_kernel(
    item_bits,
    seq_bits,
    visible_ref,
    onehot_ref,
    table_ref,
    cosine_ref,
    sine_ref,
    lse_ref,
    slice_ref,
    grad_ref,
    in_ref,
    out_ref,
    dense_ref,
    bias_ref,
    spread_ref,
    sums_all_ref,
    in_part_ref,
    out_part_ref,
    dense_part_ref,
    bias_sum_ref,
    mixed_scr,
    other_scr,
    kept_scr,
    step_scrs,
    sums_scr,
    sums_got,
    bias_scr,
    bias_got,
    in_got,
    out_got,
    dense_got,
    in_final,
    out_final,
    stage_scr,
    stage_sems,
    send_sems,
    recv_sems,
    local_sems,
):
    seq_size = 2 ** len(seq_bits)
    items_here, length, features = grad_ref.shape
    heads_here = features // HEAD
    seq_place = lax.axis_index("seq")
    member = seq_place % 4
    outer_bits = seq_bits[2:]
    width = slice_ref.shape[1]
    greet(partners(seq_size, item_bits))
    copies = Copies(send_sems, recv_sems, local_sems)
    dims = item_bits[::-1] + outer_bits[::-1]

    def reducers(whole, got):
        rows = whole.shape[-2]
        if len(item_bits) == 2:
            one, two = item_bits
            ways = [
                (pl.ds(0, rows // 2), [two, one] + outer_bits[::-1]),
                (pl.ds(rows // 2, rows // 2), [one, two] + outer_bits[::-1]),
            ]
        else:
            ways = [(pl.ds(0, rows), dims)]
        return [
            Reduce(copies, whole, part, dims, steps, list(got[order]), stage_scr, stage_sems)
            for order, (part, steps) in enumerate(ways)
        ]

    in_sums = reducers(in_ref, in_got)
    out_sums = reducers(out_ref, out_got)
    dense_steps = item_bits[::-1] + seq_bits[:0:-1]
    dense_sum = Reduce(
        copies,
        dense_ref,
        pl.ds(0, dense_ref.shape[-2]),
        dense_steps,
        dense_steps,
        list(dense_got),
        stage_scr,
        stage_sems,
    )
    for one in in_sums + out_sums:
        one.start()
    sums_scr[...] = jnp.zeros_like(sums_scr)
    tile = 256
    flying = {}
    sums_copy = None

    def next_sum(order):
        nonlocal sums_copy
        sums_copy.wait_recv()
        sums_scr[order + 1] = sums_scr[order] + sums_got[order]
        if order + 1 < len(item_bits):
            sums_copy = copies.send(
                sums_scr.at[order + 1], sums_got.at[order + 1], mask_of(item_bits[order + 1])
            )

    bias_scr[0] = bias_ref[...]
    bias_steps = seq_bits + item_bits
    bias_copies = [copies.send(bias_scr.at[0], bias_got.at[0], mask_of(bias_steps[0]))]
    for stage in range(items_here + len(seq_bits)):
        if stage < items_here:

            @pl.loop(0, heads_here)
            def _(head):
                place = pl.ds(pl.multiple_of(head * HEAD, HEAD), HEAD)
                packed = pl.ds(pl.multiple_of(head * 3 * HEAD, HEAD), 3 * HEAD)
                attend_back_unit(
                    min(256, length),
                    visible_ref[stage],
                    onehot_ref.at[stage],
                    table_ref.at[head],
                    cosine_ref,
                    sine_ref,
                    lse_ref.at[stage, head],
                    grad_ref.at[stage, :, place],
                    mixed_scr.at[:, :, :, packed],
                    sums_scr.at[0, head],
                )

        for order in range(len(seq_bits) - 1, -1, -1):
            item = stage - 1 - order
            if not 0 <= item < items_here:
                continue
            copy, kept = flying[item]
            copy.wait_recv()
            got = step_scrs[order].at[item % 2]
            if order:
                full = (slice(None),) * (len(kept.shape) - 3)
                kept = kept.at[full + (my_bit(*seq_bits[order]),)]
            if order + 1 < len(seq_bits):
                add_into(kept, got)
                step = seq_bits[order + 1]
                full = (slice(None),) * (len(kept.shape) - 3)
                copy = copies.send(
                    kept.at[full + (1 - my_bit(*step),)],
                    step_scrs[order + 1].at[item % 2],
                    mask_of(step),
                )
                flying[item] = copy, kept
                flying["later", item].append(copy)
            else:

                @pl.loop(0, kept.shape[0] // 16)
                def _(block):
                    place = (pl.ds(pl.multiple_of(block * 16, 16), 16),)
                    total = kept[place].astype(f32) + got[place].astype(f32)
                    spread_ref[(item,) + place] = total.astype(bf16)

        if stage < items_here:
            core = my_bit(*seq_bits[0])
            slot = stage % 2
            if stage >= 2:
                copies.sent_now(flying["first", stage - 2])
            kept_slot = stage % len(seq_bits)
            if stage >= len(seq_bits):
                for copy in flying["later", stage - len(seq_bits)]:
                    copies.sent_now(copy)
            half = mixed_scr.shape[0] * mixed_scr.shape[2]
            other = mixed_scr[:, 1 - core].reshape(half, -1)
            mine = mixed_scr[:, core].reshape(half, -1)

            @pl.loop(0, width // tile)
            def _(order):
                place = pl.ds(pl.multiple_of(order * tile, tile), tile)
                weights = slice_ref[:, place]
                target = other_scr.at[slot]
                target[..., place] = dot(other, weights).astype(bf16).reshape(
                    target.shape[:-1] + (tile,)
                )
                target = kept_scr.at[kept_slot]
                target[..., place] = dot(mine, weights).astype(bf16).reshape(
                    target.shape[:-1] + (tile,)
                )

            copy = copies.send(
                other_scr.at[slot], step_scrs[0].at[slot], mask_of(seq_bits[0])
            )
            flying[stage] = copy, kept_scr.at[kept_slot]
            flying["first", stage] = copy
            flying["later", stage] = []
        if stage == 1:
            dense_sum.start()
        if stage == items_here - 1:
            sums_copy = copies.send(sums_scr.at[0], sums_got.at[0], mask_of(item_bits[0]))
        if stage == items_here:
            for one in in_sums:
                one.advance()
        if stage == items_here + 1:
            next_sum(0)
            for one in in_sums:
                one.advance()
            for one in out_sums:
                one.advance()
        if stage == items_here + 2:
            for order in range(1, len(item_bits)):
                next_sum(order)
            for one in out_sums:
                one.advance()

        bias_done = len(bias_copies)
        if bias_done <= len(bias_steps):
            bias_copies[-1].wait_recv()
            bias_scr[bias_done] = bias_scr[bias_done - 1] + bias_got[bias_done - 1]
            if bias_done < len(bias_steps):
                bias_copies.append(
                    copies.send(
                        bias_scr.at[bias_done],
                        bias_got.at[bias_done],
                        mask_of(bias_steps[bias_done]),
                    )
                )
            else:
                bias_copies.append(None)
                bias_sum_ref[...] = bias_scr[bias_done]

    sums_all_ref[seq_place] = sums_scr[len(item_bits)].astype(bf16)
    known = [0]
    arrivals = []
    for axis, bit in seq_bits[::-1]:
        wait_all(arrivals)
        arrivals = []
        for mask in known:
            part = sums_all_ref.at[seq_place ^ mask]
            arrivals.append(copies.send(part, part, (0, bit)))
        known = known + [mask ^ bit for mask in known]
        if dense_sum.order < len(dense_steps):
            dense_sum.advance()

    while in_sums[0].order < len(dims):
        for one in in_sums + out_sums:
            if one.order < len(dims):
                one.advance()
        if dense_sum.order < len(dense_steps):
            dense_sum.advance()
    while out_sums[0].order < len(dims):
        for one in out_sums:
            one.advance()
    wait_all(arrivals)
    shares, local = [], []
    for sums, final, target in (
        (in_sums, in_final, in_part_ref),
        (out_sums, out_final, out_part_ref),
    ):
        rows = target.shape[1]
        first = 0
        for one in sums:
            copy_into(final.at[pl.ds(first, one.kept.shape[0])], one.kept)
            first += one.kept.shape[0]
        for mask in range(4):
            source = final.at[pl.ds(pl.multiple_of((member ^ mask) * rows, 16), rows)]
            if mask:
                shares.append(copies.send(source, target.at[member], (0, mask)))
            else:
                local.append(copies.move(source, target.at[member]))
    while dense_sum.order < len(dense_steps):
        dense_sum.advance()
    dense_part_ref[...] = dense_sum.kept[...]
    wait_all(shares)
    for copy in local:
        copy.wait()
    copies.end()


def third_call(
    item_bits,
    seq_bits,
    visible,
    onehots,
    tables,
    cosine,
    sine_part,
    log_sums,
    w_slice,
    grad_context,
    grad_in,
    grad_out,
    by_rows,
    in_sum,
):
    items_here, length, vocab = onehots.shape
    heads_here = tables.shape[0]
    seq_size = 2 ** len(seq_bits)
    span = length // seq_size
    width = w_slice.shape[1]
    packed = heads_here * 3 * HEAD
    outer = len(seq_bits) - 2
    levels = len(item_bits) + outer
    any_space = pl.BlockSpec(memory_space=pl.ANY)
    near_space = pl.BlockSpec(memory_space=pltpu.VMEM)

    def got_shapes(whole, ways, depth):
        rows, columns = whole.shape[-2:]
        one = tuple(
            pltpu.VMEM((2,) * order + (rows // ways, columns), bf16)
            for order in range(depth - 1, -1, -1)
        )
        return one

    ways = 2 if len(item_bits) == 2 else 1
    group_rows = grad_in.shape[-2]
    rows = group_rows // 4
    dense_depth = len(item_bits) + len(seq_bits) - 1
    spread = (2,) * (len(seq_bits) - 1) + (span, width)
    all_bits = len(item_bits) + len(seq_bits)
    spare = 8 * items_here + 8 * levels + 16 * all_bits
    stage_rows = max(group_rows // ways, by_rows.shape[-2])
    return pl.pallas_call(
        functools.partial(third_kernel, item_bits, seq_bits),
        in_specs=[pl.BlockSpec(memory_space=pltpu.SMEM)]
        + [near_space] * 7
        + [any_space] * 3
        + [near_space],
        out_specs=[near_space, near_space, any_space, any_space, near_space, near_space],
        out_shape=[
            jax.ShapeDtypeStruct((items_here, span, width), bf16),
            jax.ShapeDtypeStruct((seq_size, heads_here, vocab, 3 * HEAD), bf16),
            jax.ShapeDtypeStruct((4, rows, grad_in.shape[-1]), bf16),
            jax.ShapeDtypeStruct((4, rows, grad_out.shape[-1]), bf16),
            jax.ShapeDtypeStruct(by_rows.shape[-2:], bf16),
            jax.ShapeDtypeStruct(in_sum.shape, f32),
        ],
        scratch_shapes=[
            pltpu.VMEM((seq_size // 2, 2, span, packed), bf16),
            pltpu.VMEM((2,) + spread, bf16),
            pltpu.VMEM((len(seq_bits),) + spread, bf16),
            tuple(pltpu.VMEM((2,) + spread[order:], bf16) for order in range(len(seq_bits))),
            pltpu.VMEM((len(item_bits) + 1, heads_here, vocab, 3 * HEAD), f32),
            pltpu.VMEM((len(item_bits), heads_here, vocab, 3 * HEAD), f32),
            pltpu.VMEM((all_bits + 1,) + in_sum.shape, f32),
            pltpu.VMEM((all_bits,) + in_sum.shape, f32),
            tuple(got_shapes(grad_in, ways, levels) for _ in range(ways)),
            tuple(got_shapes(grad_out, ways, levels) for _ in range(ways)),
            got_shapes(by_rows, 1, dense_depth),
            pltpu.VMEM((group_rows, grad_in.shape[-1]), bf16),
            pltpu.VMEM((group_rows, grad_out.shape[-1]), bf16),
            pltpu.VMEM((2, stage_rows, grad_in.shape[-1]), bf16),
            pltpu.SemaphoreType.DMA((2,)),
            pltpu.SemaphoreType.DMA((spare,)),
            pltpu.SemaphoreType.DMA((spare,)),
            pltpu.SemaphoreType.DMA((8,)),
        ],
        compiler_params=pltpu.CompilerParams(
            collective_id=2, has_side_effects=True, vmem_limit_bytes=60 * 2**20
        ),
        name="third",
    )(
        visible,
        onehots,
        tables,
        cosine,
        sine_part,
        log_sums,
        w_slice,
        grad_context,
        grad_in,
        grad_out,
        by_rows,
        in_sum,
    )


def merged_kernel(
    item_bits,
    seq_bits,
    visible_ref,
    onehot_ref,
    table_ref,
    cosine_ref,
    sine_ref,
    lse_ref,
    slice_ref,
    grad_ref,
    shared_ref,
    grad_in_ref,
    grad_shared_ref,
    product_ref,
    dense_ref,
    bias_ref,
    spread_ref,
    sums_all_ref,
    parts_ref,
    dense_part_ref,
    bias_sum_ref,
    land_one_ref,
    land_two_ref,
    land_three_ref,
    mixed_scr,
    other_scr,
    kept_scr,
    step_scrs,
    sums_scr,
    sums_got,
    bias_scr,
    bias_got,
    dense_got,
    rhs_scr,
    lhs_scr,
    turned_scr,
    slot_scr,
    sum_scr,
    stage_scr,
    dense_scr,
    grad_scr,
    stage_sems,
    load_sems,
    send_sems,
    recv_sems,
    local_sems,
):
    seq_size = 2 ** len(seq_bits)
    items_here, length, features = grad_scr.shape
    span = length // seq_size
    heads_here = features // HEAD
    seq_place = lax.axis_index("seq")
    member = seq_place % 4
    outer_bits = seq_bits[2:]
    width = slice_ref.shape[1]
    greet(partners(seq_size, item_bits))
    copies = Copies(send_sems, recv_sems, local_sems)

    one, two = item_bits
    high = outer_bits[0]
    ways = [[two, one, high], [one, two, high]]
    blocks = [(grad_shared_ref, product_ref, 0)]
    ff_part = product_ref.shape[1]
    blocks += [(shared_ref, grad_in_ref, 0), (shared_ref, grad_in_ref, ff_part)]
    group_rows = lhs_scr.shape[2]
    half_rows = group_rows // 2
    pairs = [(two, one), (two,), (one,), ()]

    def masks_of(steps):
        masks = (0, 0)
        for step in steps:
            masks = moved(masks, *step)
        return masks

    def load_rhs(block):
        _, rhs, first = blocks[block]
        return pltpu.make_async_copy(
            rhs.at[:, pl.ds(first, ff_part)], rhs_scr, load_sems.at[0]
        )

    def load_lhs(block, pair, which):
        masks = masks_of(pairs[pair] + ((high,) if which == 0 else ()))
        group = ((copies.here[0] ^ masks[0]) * seq_size + (copies.here[1] ^ masks[1])) // 4
        columns = pl.ds(pl.multiple_of(group * group_rows, 128), group_rows)
        return pltpu.make_async_copy(
            blocks[block][0].at[:, columns], lhs_scr.at[which], load_sems.at[1 + which]
        )

    landed, slots, sends = {}, {}, {}

    def products(block, first):
        if first == 0:
            load_rhs(block).wait()
        for pair, steps in list(enumerate(pairs))[first : first + 2]:
            for which in range(2):
                load_lhs(block, pair, which).wait()
                rows = pl.ds(which * group_rows, group_rows)
                turned_scr[rows, :] = lhs_scr[which].T
            follow = (block, pair + 1) if pair + 1 < len(pairs) else (block + 1, 0)
            if follow[0] < len(blocks):
                for which in range(2):
                    load_lhs(*follow, which).start()
            targets = []
            for which in range(2):
                for way in range(2):
                    away, other = ways[way][:2]
                    place = 2 * (other in steps) + 1 - which
                    if away in steps:
                        if (way, place) in slots:
                            copies.sent_now(slots.pop((way, place)))
                        targets.append(slot_scr.at[way, place])
                    else:
                        targets.append(sum_scr.at[block, way, place])

            def multiply(columns):
                total = dot(turned_scr[...], rhs_scr[:, columns]).astype(bf16)
                for order, target in enumerate(targets):
                    target[:, columns] = total[order * half_rows : (order + 1) * half_rows]

            @pl.loop(0, ff_part // 256)
            def _(order):
                multiply(pl.ds(pl.multiple_of(order * 256, 256), 256))

            if ff_part % 256:
                multiply(pl.ds(ff_part // 256 * 256, ff_part % 256))
            for which in range(2):
                for way in range(2):
                    away, other = ways[way][:2]
                    place = 2 * (other in steps) + 1 - which
                    if away in steps:
                        copy = copies.send(
                            slot_scr.at[way, place],
                            land_one_ref.at[block, way, place],
                            mask_of(away),
                        )
                        slots[way, place] = copy
                        landed[1, block, way, place] = copy
        if first and block + 1 < len(blocks):
            load_rhs(block + 1).start()

    lands = {1: land_one_ref, 2: land_two_ref, 3: land_three_ref}

    def absorb(level, block):
        count = 2 ** (3 - level)
        pending = []

        def finish():
            load, way, place, slot = pending.pop(0)
            load.wait()
            add_into(sum_scr.at[block, way, place], stage_scr.at[slot])
            if level < 3 and place >= count // 2:
                left = place - count // 2
                landed[level + 1, block, way, left] = copies.send(
                    sum_scr.at[block, way, place],
                    lands[level + 1].at[block, way, left],
                    mask_of(ways[way][level]),
                )

        order = 0
        for place in range(count - 1, -1, -1):
            for way in range(2):
                landed[level, block, way, place].wait_recv()
                slot = order % 2
                load = pltpu.make_async_copy(
                    lands[level].at[block, way, place], stage_scr.at[slot], stage_sems.at[slot]
                )
                load.start()
                if pending:
                    finish()
                pending.append((load, way, place, slot))
                order += 1
        finish()

    shares, local = [], []

    def to_members(block):
        rows = parts_ref.shape[2]
        for mask in range(4):
            other = member ^ mask
            source = sum_scr.at[
                block, other // 2, 0, pl.ds(pl.multiple_of(other % 2 * rows, 16), rows)
            ]
            if mask:
                shares.append(copies.send(source, parts_ref.at[block, member], (0, mask)))
            else:
                local.append(copies.move(source, parts_ref.at[block, member]))

    grads = {}

    def send_grads(item):
        target = grad_scr.at[item, pl.ds(pl.multiple_of(seq_place * span, span), span)]
        arriving = []
        for mask in range(seq_size):
            columns = pl.ds(pl.multiple_of((seq_place ^ mask) * features, HEAD), features)
            source = grad_ref.at[item, :, columns]
            if mask:
                arriving.append(copies.send(source, target, (0, mask)))
            else:
                own = copies.move(source, target)
        grads[item] = arriving, own

    send_grads(0)
    load_rhs(0).start()
    for which in range(2):
        load_lhs(0, 0, which).start()
    dense_steps = item_bits[::-1] + seq_bits[:0:-1]
    dense_half = dense_ref.shape[-2] // 2
    dense_sums = [
        Reduce(
            copies,
            dense_ref,
            pl.ds(order * dense_half, dense_half),
            dense_steps,
            steps + dense_steps[2:],
            list(dense_got[order]),
            dense_scr,
            stage_sems,
        )
        for order, steps in enumerate(([two, one], [one, two]))
    ]

    def dense_advance():
        for part in dense_sums:
            part.advance()

    sums_scr[...] = jnp.zeros_like(sums_scr)
    tile = 256
    flying = {}
    sums_copy = None

    def next_sum(order):
        nonlocal sums_copy
        sums_copy.wait_recv()
        sums_scr[order + 1] = sums_scr[order] + sums_got[order]
        if order + 1 < len(item_bits):
            sums_copy = copies.send(
                sums_scr.at[order + 1], sums_got.at[order + 1], mask_of(item_bits[order + 1])
            )

    known, arrivals = [0], []

    def spread_sums():
        nonlocal known, arrivals
        wait_all(arrivals)
        arrivals = []
        bit = seq_size // 2 // len(known)
        for mask in known:
            part = sums_all_ref.at[seq_place ^ mask]
            arrivals.append(copies.send(part, part, (0, bit)))
        known = known + [mask ^ bit for mask in known]

    bias_scr[0] = bias_ref[...]
    bias_steps = seq_bits + item_bits
    bias_copies = [copies.send(bias_scr.at[0], bias_got.at[0], mask_of(bias_steps[0]))]

    def attention(item):
        arriving, own = grads[item]
        wait_all(arriving)
        own.wait()

        @pl.loop(0, heads_here)
        def _(head):
            place = pl.ds(pl.multiple_of(head * HEAD, HEAD), HEAD)
            packed = pl.ds(pl.multiple_of(head * 3 * HEAD, HEAD), 3 * HEAD)
            attend_back_unit(
                min(256, length),
                visible_ref[item],
                onehot_ref.at[item],
                table_ref.at[head],
                cosine_ref,
                sine_ref,
                lse_ref.at[item, head],
                grad_scr.at[item, :, place],
                mixed_scr.at[:, :, :, packed],
                sums_scr.at[0, head],
            )

    def step_on(item, order):
        copy, kept = flying[item]
        copy.wait_recv()
        got = step_scrs[order].at[item % step_scrs[order].shape[0]]
        full = (slice(None),) * (len(kept.shape) - 3)
        if order:
            kept = kept.at[full + (my_bit(*seq_bits[order]),)]
            full = full[1:]
        if order + 1 < len(seq_bits):
            add_into(kept, got)
            step = seq_bits[order + 1]
            target = step_scrs[order + 1]
            copy = copies.send(
                kept.at[full + (1 - my_bit(*step),)],
                target.at[item % target.shape[0]],
                mask_of(step),
            )
            flying[item] = copy, kept
            flying["later", item].append(copy)
        else:
            add_into(kept, got)
            flying["out", item] = copies.move(kept, spread_ref.at[item])

    def partial(item):
        core = my_bit(*seq_bits[0])
        slot = item % 2
        if item >= 1:
            copies.sent_now(flying["first", item - 1])
        kept_slot = item % len(seq_bits)
        if item >= len(seq_bits):
            for copy in flying["later", item - len(seq_bits)]:
                copies.sent_now(copy)
            flying.pop(("out", item - len(seq_bits))).wait()
        half = mixed_scr.shape[0] * mixed_scr.shape[2]
        other = mixed_scr[:, 1 - core].reshape(half, -1)
        mine = mixed_scr[:, core].reshape(half, -1)

        @pl.loop(0, width // tile)
        def _(order):
            place = pl.ds(pl.multiple_of(order * tile, tile), tile)
            weights = slice_ref[:, place]
            target = other_scr
            target[..., place] = dot(other, weights).astype(bf16).reshape(
                target.shape[:-1] + (tile,)
            )
            target = kept_scr.at[kept_slot]
            target[..., place] = dot(mine, weights).astype(bf16).reshape(
                target.shape[:-1] + (tile,)
            )

        copy = copies.send(other_scr, step_scrs[0].at[slot], mask_of(seq_bits[0]))
        flying[item] = copy, kept_scr.at[kept_slot]
        flying["first", item] = copy
        flying["later", item] = []

    def bias_step():
        done = len(bias_copies)
        bias_copies[-1].wait_recv()
        bias_scr[done] = bias_scr[done - 1] + bias_got[done - 1]
        if done < len(bias_steps):
            bias_copies.append(
                copies.send(bias_scr.at[done], bias_got.at[done], mask_of(bias_steps[done]))
            )
        else:
            bias_sum_ref[...] = bias_scr[done]

    products(0, 0)
    for part in dense_sums:
        part.start()
    send_grads(1)
    attention(0)
    partial(0)
    products(0, 2)
    send_grads(2)
    bias_step()
    step_on(0, 0)
    attention(1)
    partial(1)
    products(1, 0)
    send_grads(3)
    step_on(1, 0)
    bias_step()
    step_on(0, 1)
    products(1, 2)
    absorb(1, 0)
    dense_advance()
    attention(2)
    partial(2)
    products(2, 0)
    step_on(2, 0)
    step_on(1, 1)
    bias_step()
    products(2, 2)
    dense_advance()
    absorb(1, 1)
    attention(3)
    absorb(2, 0)
    step_on(0, 2)
    partial(3)
    sums_copy = copies.send(sums_scr.at[0], sums_got.at[0], mask_of(item_bits[0]))
    step_on(2, 1)
    dense_advance()
    step_on(3, 0)
    absorb(1, 2)
    next_sum(0)
    bias_step()
    step_on(1, 2)
    absorb(2, 1)
    dense_advance()
    step_on(3, 1)
    next_sum(1)
    bias_step()
    sums_all_ref[seq_place] = sums_scr[len(item_bits)].astype(bf16)
    spread_sums()
    absorb(2, 2)
    absorb(3, 0)
    to_members(0)
    step_on(2, 2)
    spread_sums()
    absorb(3, 1)
    to_members(1)
    step_on(3, 2)
    spread_sums()
    absorb(3, 2)
    to_members(2)
    for order, part in enumerate(dense_sums):
        dense_part_ref[pl.ds(order * dense_half, dense_half)] = part.kept[...]
    wait_all(arrivals)
    wait_all(shares)
    for item in range(items_here):
        if ("out", item) in flying:
            flying["out", item].wait()
    for copy in local:
        copy.wait()
    copies.end()


def merged_call(
    item_bits,
    seq_bits,
    visible,
    onehots,
    tables,
    cosine,
    sine_part,
    log_sums,
    w_slice,
    grad_context,
    shared,
    grad_in,
    grad_shared,
    product,
    by_rows,
    in_sum,
):
    items_here, length, vocab = onehots.shape
    heads_here = tables.shape[0]
    seq_size = 2 ** len(seq_bits)
    span = length // seq_size
    width = w_slice.shape[1]
    packed = heads_here * 3 * HEAD
    any_space = pl.BlockSpec(memory_space=pl.ANY)
    near_space = pl.BlockSpec(memory_space=pltpu.VMEM)
    ff_part = product.shape[1]
    group_rows = width * 4 // 2 ** (len(item_bits) + len(seq_bits))
    rows = group_rows // 4
    dense_depth = len(item_bits) + len(seq_bits) - 1
    spread = (2,) * (len(seq_bits) - 1) + (span, width)
    all_bits = len(item_bits) + len(seq_bits)
    spare = (8 + seq_size) * items_here + 64 + 16 * all_bits
    half = (group_rows // 2, ff_part)
    return pl.pallas_call(
        functools.partial(merged_kernel, item_bits, seq_bits),
        in_specs=[pl.BlockSpec(memory_space=pltpu.SMEM)]
        + [near_space] * 6
        + [any_space] * 6
        + [near_space],
        out_specs=[any_space, near_space, any_space, near_space, near_space] + [any_space] * 3,
        out_shape=[
            jax.ShapeDtypeStruct((items_here, span, width), bf16),
            jax.ShapeDtypeStruct((seq_size, heads_here, vocab, 3 * HEAD), bf16),
            jax.ShapeDtypeStruct((3, 4, rows, ff_part), bf16),
            jax.ShapeDtypeStruct(by_rows.shape[-2:], bf16),
            jax.ShapeDtypeStruct(in_sum.shape, f32),
            jax.ShapeDtypeStruct((3, 2, 4) + half, bf16),
            jax.ShapeDtypeStruct((3, 2, 2) + half, bf16),
            jax.ShapeDtypeStruct((3, 2, 1) + half, bf16),
        ],
        scratch_shapes=[
            pltpu.VMEM((seq_size // 2, 2, span, packed), bf16),
            pltpu.VMEM(spread, bf16),
            pltpu.VMEM((len(seq_bits),) + spread, bf16),
            tuple(
                pltpu.VMEM((2 if order == 0 else items_here,) + spread[order:], bf16)
                for order in range(len(seq_bits))
            ),
            pltpu.VMEM((len(item_bits) + 1, heads_here, vocab, 3 * HEAD), f32),
            pltpu.VMEM((len(item_bits), heads_here, vocab, 3 * HEAD), f32),
            pltpu.VMEM((all_bits + 1,) + in_sum.shape, f32),
            pltpu.VMEM((all_bits,) + in_sum.shape, f32),
            tuple(
                tuple(
                    pltpu.VMEM((2,) * order + (by_rows.shape[-2] // 2, by_rows.shape[-1]), bf16)
                    for order in range(dense_depth - 1, -1, -1)
                )
                for _ in range(2)
            ),
            pltpu.VMEM((product.shape[0], ff_part), bf16),
            pltpu.VMEM((2, product.shape[0], group_rows), bf16),
            pltpu.VMEM((2 * group_rows, product.shape[0]), bf16),
            pltpu.VMEM((2, 4) + half, bf16),
            pltpu.VMEM((3, 2, 4) + half, bf16),
            pltpu.VMEM((2,) + half, bf16),
            pltpu.VMEM((2,) + by_rows.shape[-2:], bf16),
            pltpu.VMEM((items_here, length, heads_here * HEAD), bf16),
            pltpu.SemaphoreType.DMA((2,)),
            pltpu.SemaphoreType.DMA((3,)),
            pltpu.SemaphoreType.DMA((spare,)),
            pltpu.SemaphoreType.DMA((spare,)),
            pltpu.SemaphoreType.DMA((16,)),
        ],
        compiler_params=pltpu.CompilerParams(
            collective_id=4, has_side_effects=True, vmem_limit_bytes=62 * 2**20
        ),
        name="merged",
    )(
        visible,
        onehots,
        tables,
        cosine,
        sine_part,
        log_sums,
        w_slice,
        grad_context,
        shared,
        grad_in,
        grad_shared,
        product,
        by_rows,
        in_sum,
    )


def weave_kernel(ff_width, members, padded_ref, woven_ref):
    rows = padded_ref.shape[0]
    tiles = woven_ref.shape[2] // 256
    base, shift = ff_width // 128, ff_width % 128
    lane = lax.broadcasted_iota(jnp.int32, (rows, 128), 1)
    last = padded_ref.shape[1] // 128 - 1

    def turned(tile):
        part = padded_ref[:, tile * 128 : (tile + 1) * 128].astype(f32)
        return pltpu.roll(part, (128 - shift) % 128, 1)

    before = turned(base)
    for order in range(members * tiles):
        left = ff_width - order * 128
        if left <= 0:
            up_part = gate = jnp.zeros((rows, 128), bf16)
        else:
            up_part = padded_ref[:, order * 128 : (order + 1) * 128].astype(f32)
            after = turned(min(base + order + 1, last))
            gate = jnp.where(lane < 128 - shift, before, after)
            before = after
            if left < 128:
                up_part = jnp.where(lane < left, up_part, 0.0)
                gate = jnp.where(lane < left, gate, 0.0)
            up_part, gate = up_part.astype(bf16), gate.astype(bf16)
        member, tile = order // tiles, order % tiles
        woven_ref[member, :, tile * 256 : tile * 256 + 128] = up_part
        woven_ref[member, :, tile * 256 + 128 : (tile + 1) * 256] = gate


def weave(up_weight, ff_width, members, ff_part):
    rows, columns = up_weight.shape
    wide = -(-columns // 128) * 128
    padded = jnp.pad(up_weight, ((0, 0), (0, wide - columns)))
    return pl.pallas_call(
        functools.partial(weave_kernel, ff_width, members),
        in_specs=[pl.BlockSpec(memory_space=pltpu.VMEM)],
        out_specs=pl.BlockSpec(memory_space=pltpu.VMEM),
        out_shape=jax.ShapeDtypeStruct((members, rows, 2 * ff_part), bf16),
        compiler_params=pltpu.CompilerParams(vmem_limit_bytes=24 * 2**20),
        name="weave",
    )(padded)


def unweave_kernel(ff_width, woven_ref, whole_ref):
    members, rows, columns = woven_ref.shape
    tiles = columns // 256
    base, shift = ff_width // 128, ff_width % 128
    lane = lax.broadcasted_iota(jnp.int32, (rows, 128), 1)

    def part(order, which):
        first = order % tiles * 256 + which * 128
        return woven_ref[order // tiles, :, first : first + 128].astype(f32)

    for order in range(base):
        whole_ref[:, order * 128 : (order + 1) * 128] = part(order, 0)
    before = part(base, 0)
    width = whole_ref.shape[1]
    for order in range(base, -(-width // 128)):
        if order - base < members * tiles:
            after = pltpu.roll(part(order - base, 1), shift, 1)
        first = order * 128
        count = min(128, width - first)
        whole_ref[:, first : first + count] = jnp.where(lane < shift, before, after)[:, :count]
        before = after


def unweave(woven, ff_width):
    rows = woven.shape[1]
    return pl.pallas_call(
        functools.partial(unweave_kernel, ff_width),
        in_specs=[pl.BlockSpec(memory_space=pltpu.VMEM)],
        out_specs=pl.BlockSpec(memory_space=pltpu.VMEM),
        out_shape=jax.ShapeDtypeStruct((rows, 2 * ff_width), f32),
        compiler_params=pltpu.CompilerParams(vmem_limit_bytes=24 * 2**20),
        name="unweave",
    )(woven)


def ff_kernel(
    item_bits,
    shared_ref,
    normed_ref,
    inverse_ref,
    cotangent_ref,
    in_ref,
    out_ref,
    vector_ref,
    bias_ref,
    block_ref,
    product_ref,
    saved_ref,
    grad_shared_ref,
    grad_in_ref,
    layer_ref,
    resid_ref,
    sums_ref,
    in_sum_ref,
    slices_ref,
    branch_ref,
    rows_scr,
    product_scr,
    save_scr,
    parts_scr,
    near_got,
    far_got,
    low_scr,
    grad_in_scr,
    resid_scr,
    normed_scr,
    gate_scr,
    send_sems,
    recv_sems,
    load_sems,
    keep_sems,
):
    chunks, blocks, span, width = shared_ref.shape
    group_rows = blocks * span
    tiles = product_scr.shape[-1] // 128
    tile = 256
    near, far = ("seq", 1), ("seq", 2)
    greet([mask_of(near), mask_of(far)] + [mask_of(step) for step in item_bits])
    copies = Copies(send_sems, recv_sems, keep_sems)
    item_place = copies.here[0]
    slices = copies.move(block_ref, slices_ref.at[item_place])
    slices.wait()
    spread = []

    def spread_block():
        order = len(spread)
        if order < len(item_bits):
            wait_all(spread[-1:])
            part = slices_ref.at[aligned(item_place, 2**order)]
            spread.append(copies.send(part, part, mask_of(item_bits[order])))

    spread_block()
    keeps, loads = {}, {}
    state = {}
    gain_one, shift_one, b_down, gain_two, shift_two = range(5)
    for line in range(sums_ref.shape[0]):
        sums_ref[line : line + 1, :] = jnp.zeros((1, width), f32)
    in_sum_ref[...] = jnp.zeros_like(in_sum_ref)

    def load(name, slot, source, target):
        copy = pltpu.make_async_copy(source, target, load_sems.at[slot])
        copy.start()
        loads[name] = copy

    def loaded(name):
        loads.pop(name).wait()

    def keep(name, slot, source, target):
        copy = pltpu.make_async_copy(source, target, keep_sems.at[1 + slot])
        copy.start()
        keeps[name] = copy

    def keep_done(name):
        if name in keeps:
            keeps.pop(name).wait()

    def load_shared(chunk):
        slot = chunk % 2
        load(("rows", slot), slot, shared_ref.at[chunk], rows_scr.at[slot])

    def load_normed(chunk):
        slot = chunk % 2
        rows = pl.ds(chunk * span, span)
        load(("normed", slot), 2 + slot, normed_ref.at[rows], normed_scr.at[slot])

    def forward_gate(chunk):
        slot = chunk % 2
        loaded(("rows", slot))
        if chunk + 1 < chunks:
            load_shared(chunk + 1)
        keep_done(("product", slot))
        keep_done(("save", slot))
        rows = rows_scr.at[slot]

        def multiply(order, place):
            columns = pl.ds(pl.multiple_of(order * tile, tile), tile)
            gate_scr[place] = (
                dot(rows[...].reshape(group_rows, width), in_ref[:, columns])
                + bias_ref[:, columns]
            )

        def finish(order, place):
            gate_up = gate_scr[place]
            up_part, gate = gate_up[:, :128], gate_up[:, 128:]
            below = 0.5 * (1.0 + lax.erf(gate * (0.5**0.5)))
            activated = gate * below
            slope = below + gate * jnp.exp(-0.5 * gate * gate) * (1.0 / math.sqrt(2.0 * math.pi))
            columns = pl.ds(pl.multiple_of(order * 128, 128), 128)
            product_scr[slot, :, columns] = (up_part * activated).astype(bf16)
            save_scr[slot, 0, :, columns] = activated.astype(bf16)
            save_scr[slot, 1, :, columns] = (up_part * slope).astype(bf16)

        multiply(0, 0)

        @pl.loop(0, (tiles - 1) // 2)
        def _(pair):
            finish(2 * pair, 0)
            multiply(2 * pair + 1, 1)
            finish(2 * pair + 1, 1)
            multiply(2 * pair + 2, 0)

        if tiles % 2 == 0:
            multiply(tiles - 1, 1)
            finish(tiles - 2, 0)
            finish(tiles - 1, 1)
        else:
            finish(tiles - 1, 0)
        keep(("product", slot), slot, product_scr.at[slot], product_ref.at[chunk])
        keep(("save", slot), 2 + slot, save_scr.at[slot], saved_ref.at[chunk])

    def send_near(name, slot):
        source = parts_scr.at[slot, pl.ds(2, 2)]
        state["near", name] = copies.send(source, near_got.at[slot], mask_of(near))

    def free_parts(slot):
        for key in ("near", "far"):
            copy = state.pop((key, "of", slot), None)
            if copy is not None:
                copies.sent_now(copy)

    def times_turned(name, slot, left, weights_ref):
        free_parts(slot)

        @pl.loop(0, width // tile)
        def _(order):
            place = pl.ds(pl.multiple_of(order * tile, tile), tile)
            total = contract_cols(left[...], weights_ref[place, :])
            parts_scr[slot, :, :, place] = total.astype(bf16).reshape(blocks, span, tile)

        send_near(name, slot)
        state["near", "of", slot] = state["near", name]

    def forward_out(chunk):
        times_turned(chunk, chunk % 2, product_scr.at[chunk % 2], out_ref)

    def sum_near(name, chunk):
        slot = chunk % 2
        state["near", name].wait_recv()
        add_into(parts_scr.at[slot, pl.ds(0, 2)], near_got.at[slot])
        copy = copies.send(parts_scr.at[slot, 1], far_got.at[chunk], mask_of(far))
        state["far", name] = copy
        state["far", "of", slot] = copy

    block = 32

    def row_blocks(function):
        @pl.loop(0, span // block)
        def _(order):
            function(pl.ds(pl.multiple_of(order * block, block), block))

    def line(index):
        return vector_ref[index : index + 1, :]

    def add_sum(index, rows):
        sums_ref[index : index + 1, :] += jnp.sum(rows, axis=0, keepdims=True)

    def second_norm(chunk):
        slot = chunk % 2
        state["far", chunk].wait_recv()
        loaded(("normed", slot))
        for key in ("low near", "low far"):
            copy = state.pop((key, slot), None)
            if copy is not None:
                copies.sent_now(copy)
        keep_done(("low", slot))

        def body(rows):
            hidden = normed_scr[slot, rows] * line(gain_one) + line(shift_one)
            mlp_branch = parts_scr[slot, 0, rows].astype(f32) + far_got[chunk, rows].astype(f32)
            normed, inverse = norm_rows(deep_alpha * hidden + mlp_branch + line(b_down))
            layer_ref[chunk, rows] = (normed * line(gain_two) + line(shift_two)).astype(bf16)
            grad = cotangent_ref[chunk, rows].astype(f32)
            resid = norm_rows_back(grad, normed, inverse, line(gain_two))
            low = resid.astype(bf16)
            resid_scr[chunk, rows] = resid
            low_scr[slot, rows] = low
            add_sum(3, grad * normed)
            add_sum(4, grad)
            add_sum(5, low.astype(f32))

        row_blocks(body)
        if chunk + 2 < chunks:
            load_normed(chunk + 2)
        source = low_scr.at[slot]
        keep(("low", slot), 4 + slot, source, grad_shared_ref.at[chunk, 0])
        state["low far", slot] = copies.send(source, grad_shared_ref.at[chunk, 1], mask_of(far))
        state["low near", slot] = copies.send(source, grad_shared_ref.at[chunk, 2], mask_of(near))
        state["grad far", chunk] = state["low far", slot]
        state["grad near", chunk] = state["low near", slot]

    def pass_on(chunk):
        state["grad far", chunk].wait_recv()
        part = grad_shared_ref.at[chunk, 1]
        state["grad cross", chunk] = copies.send(
            part, grad_shared_ref.at[chunk, 3], mask_of(near)
        )

    def load_grads(chunk):
        slot = chunk % 2
        keep_done(("low", slot))
        state["grad near", chunk].wait_recv()
        state["grad cross", chunk].wait_recv()
        load(("rows", slot), slot, grad_shared_ref.at[chunk], rows_scr.at[slot])
        keep_done(("save", slot))
        load(("save", slot), 4 + slot, saved_ref.at[chunk], save_scr.at[slot])

    def backward_gate(chunk):
        slot = chunk % 2
        loaded(("rows", slot))
        loaded(("save", slot))
        keep_done("grad in")
        rows = rows_scr.at[slot]

        def columns_of(first, count):
            columns = pl.ds(pl.multiple_of(first * 128, 128), count * 128)
            grad = dot(rows[...].reshape(group_rows, width), out_ref[:, columns])
            for order in range(count):
                part = grad[:, order * 128 : (order + 1) * 128]
                saved = pl.ds(pl.multiple_of((first + order) * 128, 128), 128)
                for which in range(2):
                    low = (part * save_scr[slot, which, :, saved].astype(f32)).astype(bf16)
                    place = pl.ds(
                        pl.multiple_of((2 * (first + order) + which) * 128, 128), 128
                    )
                    grad_in_scr[:, place] = low
                    in_sum_ref[:, place] += jnp.sum(low.astype(f32), axis=0, keepdims=True)

        @pl.loop(0, tiles // 2)
        def _(pair):
            columns_of(2 * pair, 2)

        if tiles % 2:
            columns_of(tiles - 1, 1)
        keep("grad in", 6, grad_in_scr, grad_in_ref.at[chunk])

    def backward_in(chunk):
        times_turned(("back", chunk), chunk % 2, grad_in_scr, in_ref)

    def first_norm(chunk):
        slot = chunk % 2
        state["far", ("back", chunk)].wait_recv()
        loaded(("normed", slot))
        for key in ("low near", "low far"):
            copy = state.pop((key, slot), None)
            if copy is not None:
                copies.sent_now(copy)
        keep_done(("branch", slot))

        def body(rows):
            grad = parts_scr[slot, 0, rows].astype(f32) + far_got[chunk, rows].astype(f32)
            grad = grad + deep_alpha * resid_scr[chunk, rows]
            normed = normed_scr[slot, rows]
            place = pl.ds(pl.multiple_of(chunk * span + rows.start, block), block)
            resid = norm_rows_back(grad, normed, inverse_ref[place, 0:1], line(gain_one))
            resid_scr[chunk, rows] = resid
            add_sum(0, grad * normed)
            add_sum(1, grad)
            low = resid.astype(bf16)
            low_scr[slot, rows] = low
            add_sum(2, low.astype(f32))

        row_blocks(body)
        if chunk + 2 < chunks:
            load_normed(chunk + 2)
        keep(("resid", chunk), 7 + chunk, resid_scr.at[chunk], resid_ref.at[chunk])
        keep(("branch", slot), 7 + chunks + slot, low_scr.at[slot], branch_ref.at[chunk])

    load_shared(0)
    load_normed(0)
    load_normed(1)
    last = chunks - 1
    for chunk in range(chunks):
        forward_gate(chunk)
        if chunk >= 1:
            sum_near(chunk - 1, chunk - 1)
        if chunk >= 2:
            second_norm(chunk - 2)
        if chunk >= 3:
            pass_on(chunk - 3)
        forward_out(chunk)
    sum_near(last, last)
    second_norm(last - 1)
    pass_on(last - 2)
    load_grads(0)
    for chunk in range(chunks):
        backward_gate(chunk)
        if chunk >= 2:
            first_norm(chunk - 2)
        backward_in(chunk)
        spread_block()
        if chunk == 0:
            second_norm(last)
            load_normed(0)
            load_normed(1)
        elif chunk + 1 < chunks:
            pass_on(chunk + 1)
        if chunk + 1 < chunks:
            load_grads(chunk + 1)
            sum_near(("back", chunk), chunk)
    sum_near(("back", last), last)
    first_norm(last - 1)
    first_norm(last)
    wait_all(spread[-1:])
    for name in list(keeps):
        keep_done(name)
    copies.end()


def ff_call(
    item_bits, shared, normed, inverse, cotangent, w_in, w_out, vectors, in_bias, block
):
    chunks, blocks, span, width = shared.shape
    group_rows = blocks * span
    ff_part = w_out.shape[1]
    any_space = pl.BlockSpec(memory_space=pl.ANY)
    near_space = pl.BlockSpec(memory_space=pltpu.VMEM)
    spare = 8 * chunks
    return pl.pallas_call(
        functools.partial(ff_kernel, item_bits),
        in_specs=[any_space, any_space] + [near_space] * 6 + [any_space],
        out_specs=[any_space] * 4 + [near_space, any_space, near_space, near_space, any_space, any_space],
        out_shape=[
            jax.ShapeDtypeStruct((chunks, group_rows, ff_part), bf16),
            jax.ShapeDtypeStruct((chunks, 2, group_rows, ff_part), bf16),
            jax.ShapeDtypeStruct((chunks, blocks, span, width), bf16),
            jax.ShapeDtypeStruct((chunks, group_rows, 2 * ff_part), bf16),
            jax.ShapeDtypeStruct((chunks, span, width), bf16),
            jax.ShapeDtypeStruct((chunks, span, width), f32),
            jax.ShapeDtypeStruct((8, width), f32),
            jax.ShapeDtypeStruct((1, 2 * ff_part), f32),
            jax.ShapeDtypeStruct((2 ** len(item_bits),) + block.shape, bf16),
            jax.ShapeDtypeStruct((chunks, span, width), bf16),
        ],
        scratch_shapes=[
            pltpu.VMEM((2, blocks, span, width), bf16),
            pltpu.VMEM((2, group_rows, ff_part), bf16),
            pltpu.VMEM((2, 2, group_rows, ff_part), bf16),
            pltpu.VMEM((2, blocks, span, width), bf16),
            pltpu.VMEM((2, 2, span, width), bf16),
            pltpu.VMEM((chunks, span, width), bf16),
            pltpu.VMEM((2, span, width), bf16),
            pltpu.VMEM((group_rows, 2 * ff_part), bf16),
            pltpu.VMEM((chunks, span, width), f32),
            pltpu.VMEM((2, span, width), f32),
            pltpu.VMEM((2, group_rows, 256), f32),
            pltpu.SemaphoreType.DMA((spare,)),
            pltpu.SemaphoreType.DMA((spare,)),
            pltpu.SemaphoreType.DMA((6,)),
            pltpu.SemaphoreType.DMA((10 + chunks,)),
        ],
        compiler_params=pltpu.CompilerParams(
            collective_id=3, has_side_effects=True, vmem_limit_bytes=60 * 2**20
        ),
        name="feed_forward",
    )(shared, normed, inverse, cotangent, w_in, w_out, vectors, in_bias, block)


def on_device(
    token_ids,
    masked,
    item_flag,
    prefix,
    cotangent,
    embedding,
    heads_weight,
    heads_bias,
    dense_weight,
    dense_bias,
    first_gain,
    first_bias,
    up_weight,
    up_bias,
    down_weight,
    down_bias,
    second_gain,
    second_bias,
):
    lines = Lines()
    items_here, span = token_ids.shape
    items_size, seq_size = lax.axis_size("items"), lax.axis_size("seq")
    item_place, seq_place = lax.axis_index("items"), lax.axis_index("seq")
    count = items_size * seq_size
    length = span * seq_size
    width = embedding.shape[0] * count
    vocab = embedding.shape[1]
    heads_here = HEADS // seq_size
    packed_width = heads_here * 3 * HEAD
    rows_here = up_weight.shape[0]
    ff_width = down_weight.shape[0]
    members = 4
    groups = count // members
    member = seq_place % members
    ff_part = -(-ff_width // (members * 128)) * 128
    ff_all = members * ff_part

    item_bits, seq_bits = bits_of("items"), bits_of("seq")
    outer_bits = seq_bits[2:]

    input_ids = jnp.where(masked == 1, mask_token, token_ids)
    flat_place = item_place * seq_size + seq_place
    row_count = rows_here + 16
    bias_row = lax.dynamic_update_slice(
        jnp.zeros((16, heads_weight.shape[1]), bf16),
        heads_bias[None],
        (0, flat_place * heads_bias.shape[0]),
    )
    ones_row = jnp.zeros((16, vocab), bf16).at[0].set(1.0)
    def rows_of(part):
        part = part.reshape(-1)
        return jnp.pad(part, (0, -part.shape[0] % 128)).reshape(-1, 128)

    small = [
        embedding,
        ones_row,
        rows_of(input_ids.astype(bf16)),
        rows_of(
            jnp.concatenate(
                [dense_bias, first_gain, first_bias, down_bias, second_gain, second_bias]
            )
        ),
    ]
    ends = [0]
    for part in small:
        ends.append(ends[-1] + part.shape[0])
    small.append(jnp.zeros((-ends[-1] % 16, 128), bf16))
    flat = jnp.concatenate(small, axis=0)

    def by_member(part):
        padded = jnp.pad(part, ((0, 0), (0, ff_all - ff_width)))
        return jnp.transpose(padded.reshape(rows_here, 2, 2, ff_part), (1, 2, 0, 3))

    tiles = ff_part // 128

    def woven(up, gate):
        shape = up.shape[:-1] + (tiles, 128)
        return jnp.stack([up.reshape(shape), gate.reshape(shape)], axis=-2).reshape(
            up.shape[:-1] + (2 * ff_part,)
        )

    def unwoven(both_parts):
        parts = both_parts.reshape(both_parts.shape[:-1] + (tiles, 2, 128))
        shape = both_parts.shape[:-1] + (ff_part,)
        return parts[..., 0, :].reshape(shape), parts[..., 1, :].reshape(shape)

    parts_in = weave(up_weight, ff_width, members, ff_part).reshape(
        2, 2, rows_here, 2 * ff_part
    )
    parts_out = by_member(down_weight.T)
    everyone, mixed_table, w_block, w_dense, own_in, own_out = first_call(
        item_bits,
        seq_bits,
        flat,
        heads_weight,
        bias_row,
        dense_weight,
        parts_in,
        parts_out,
    )
    w_dense = w_dense.reshape(width, width)
    w_block = w_block[:, :rows_here].reshape(seq_size * rows_here, packed_width)
    pieces = [everyone[:, :, a:b] for a, b in zip(ends[:-1], ends[1:])]
    table = pieces[0].reshape(width, vocab)
    vector_rows = pieces[3].reshape(count, -1)[:, : 6 * rows_here].reshape(count, 6, rows_here)
    vectors = jnp.transpose(vector_rows, (1, 0, 2)).reshape(6, width).astype(f32)
    ids_here = pick(pieces[2], item_place, 0).reshape(seq_size, items_here, span)
    ids_here = jnp.transpose(ids_here, (1, 0, 2)).reshape(items_here, length).astype(jnp.int32)
    in_bias = jnp.pad(
        up_bias.astype(f32).reshape(2, ff_width), ((0, 0), (0, ff_all - ff_width))
    )
    in_bias = lax.dynamic_slice(in_bias, (0, member * ff_part), (2, ff_part))
    in_bias = woven(in_bias[:1], in_bias[1:])

    vocab_index = jnp.arange(vocab, dtype=jnp.int32)
    frequency = np.exp(np.arange(HEAD // 2) * (-2.0 * math.log(10000.0) / HEAD))
    angles = np.arange(length)[:, None] * frequency[None, :]
    cosine, sine_part = np.cos(angles), np.sin(angles)
    cosine = jnp.asarray(np.concatenate([cosine, cosine], axis=1), f32)
    sine_part = jnp.asarray(np.concatenate([-sine_part, sine_part], axis=1), f32)
    visible = jnp.where(item_flag == 1, length, prefix)
    tables = table_halves(mixed_table)
    onehots = (ids_here[:, :, None] == vocab_index).astype(bf16)
    own_onehot = (input_ids.reshape(-1)[:, None] == vocab_index[None, :]).astype(bf16)
    vectors = jnp.concatenate([vectors[1:], vectors[:1], jnp.zeros((2, width), f32)], axis=0)
    context, log_sums, w_in, w_out, shared, normed, inverse = second_call(
        item_bits,
        seq_bits,
        visible,
        onehots,
        tables,
        cosine,
        sine_part,
        own_onehot,
        table,
        vectors,
        w_dense,
        own_in,
        own_out,
    )
    (
        product,
        _,
        grad_shared,
        grad_in,
        layer_out,
        grad_resid,
        sums,
        in_sum,
        w_slice,
        grad_branch,
    ) = ff_call(
        item_bits,
        shared,
        normed,
        inverse,
        cotangent,
        w_in.reshape(width, 2 * ff_part),
        w_out.reshape(width, ff_part),
        vectors,
        in_bias,
        w_block,
    )
    rows_all = items_here * span
    group_all = members * rows_all
    context = context.reshape(rows_all, width)
    grad_branch = grad_branch.reshape(rows_all, width)
    grad_context = contract_cols(grad_branch, w_dense).astype(bf16)
    core = my_bit(*seq_bits[0])

    def core_sum(whole):
        parts = whole.reshape(count // 2, 2, rows_here, -1)
        got = lines.swap(pick(parts, 1 - core, 1), *seq_bits[0])
        return (pick(parts, core, 1).astype(f32) + got.astype(f32)).astype(bf16)

    small_sums = jnp.concatenate(
        [
            contract_rows(grad_branch, own_onehot).astype(bf16),
            contract_rows(sums.astype(bf16), jnp.eye(8, 128, dtype=bf16)).astype(bf16),
        ],
        axis=1,
    )
    by_rows = jnp.concatenate(
        [core_sum(contract_rows(context, grad_branch).astype(bf16)), core_sum(small_sums)],
        axis=-1,
    )
    row_dims = item_bits[::-1] + seq_bits[:0:-1]
    by_rows = by_rows.reshape((2,) * len(row_dims) + (rows_here, -1))
    in_sum = jnp.concatenate(unwoven(in_sum), axis=0)
    in_all = lax.dynamic_update_slice(
        jnp.zeros((2, ff_all), f32), in_sum, (0, member * ff_part)
    ).reshape(-1, 128)
    w_slice = w_slice.reshape(width, packed_width)
    attention = (
        item_bits,
        seq_bits,
        visible,
        onehots,
        tables,
        cosine,
        sine_part,
        log_sums,
        w_slice.T,
    )
    shared = shared.reshape(group_all, width)
    grad_in = grad_in.reshape(group_all, 2 * ff_part)
    grad_shared = grad_shared.reshape(group_all, width)
    product = product.reshape(group_all, ff_part)
    if len(item_bits) == 2 and len(seq_bits) == 3 and rows_here % 32 == 0:
        spread, token_all, parts, by_rows, in_all = merged_call(
            *attention,
            grad_context.reshape(items_here, span, width),
            shared,
            grad_in,
            grad_shared,
            product,
            by_rows,
            in_all,
        )[:5]
        in_part = jnp.concatenate([parts[1], parts[2]], axis=-1)
        out_part = parts[0]
    else:
        by_head = lax.all_to_all(
            jnp.transpose(
                grad_context.reshape(items_here, span, seq_size, heads_here * HEAD), (0, 2, 1, 3)
            ),
            "seq",
            split_axis=1,
            concat_axis=1,
            tiled=True,
        ).reshape(items_here, length, heads_here * HEAD)
        group_dims = (2,) * (len(item_bits) + len(outer_bits)) + (members * rows_here, -1)
        spread, token_all, in_part, out_part, by_rows, in_all = third_call(
            *attention,
            by_head,
            contract_rows(shared, grad_in).astype(bf16).reshape(group_dims),
            contract_rows(grad_shared, product).astype(bf16).reshape(group_dims),
            by_rows,
            in_all,
        )
    input_grads = spread.astype(f32) + deep_alpha * grad_resid.reshape(spread.shape)
    token_all = jnp.transpose(token_all, (2, 0, 1, 3)).reshape(vocab, -1)

    def from_members(part):
        taken = jnp.transpose(part, (1, 0, 2)).reshape(rows_here, ff_all)
        return taken[:, :ff_width].astype(f32)

    grad_up_weight = unweave(in_part, ff_width)
    grad_down = from_members(out_part)
    by_rows = by_rows.astype(f32)
    grad_dense = by_rows[:, :width]
    token_sum = by_rows[:, width : width + vocab]
    own_vectors = by_rows[:, width + vocab :].T
    in_all = in_all.reshape(2, ff_all)
    grad_up_bias = in_all[:, :ff_width].reshape(-1)

    grad_heads = dot(embedding, token_all)
    grad_heads_bias = lax.dynamic_slice_in_dim(
        jnp.sum(token_all.astype(f32), axis=0),
        (item_place * seq_size + seq_place) * heads_bias.shape[0],
        heads_bias.shape[0],
        0,
    )
    embed_grad = 0.1 * (contract_cols(heads_weight, token_all) + deep_alpha * token_sum)
    return (
        layer_out,
        input_grads,
        embed_grad,
        grad_heads,
        grad_heads_bias,
        grad_dense,
        own_vectors[2],
        own_vectors[0],
        own_vectors[1],
        grad_up_weight,
        grad_up_bias,
        grad_down.T,
        own_vectors[5],
        own_vectors[3],
        own_vectors[4],
    )


def solution(mesh):
    in_specs = (
        P("items", "seq"),
        P("items", "seq"),
        P("items"),
        P("items"),
        P("items", "seq", None),
        P(("items", "seq"), None),
        P(("items", "seq"), None),
        P(("items", "seq")),
        P(("items", "seq"), None),
        P(("items", "seq")),
        P(("items", "seq")),
        P(("items", "seq")),
        P(("items", "seq"), None),
        P(),
        P(None, ("items", "seq")),
        P(("items", "seq")),
        P(("items", "seq")),
        P(("items", "seq")),
    )
    out_specs = (
        P("items", "seq", None),
        P("items", "seq", None),
        P(("items", "seq"), None),
        P(("items", "seq"), None),
        P(("items", "seq")),
        P(("items", "seq"), None),
        P(("items", "seq")),
        P(("items", "seq")),
        P(("items", "seq")),
        P(("items", "seq"), None),
        P(),
        P(None, ("items", "seq")),
        P(("items", "seq")),
        P(("items", "seq")),
        P(("items", "seq")),
    )
    return jax.shard_map(
        on_device, mesh=mesh, in_specs=in_specs, out_specs=out_specs, check_vma=False
    )
```

```python
import functools
import math

import jax
import jax.numpy as jnp
import numpy as np
from jax import lax
from jax.experimental import pallas as pl
from jax.experimental.pallas import tpu as pltpu
from jax.sharding import PartitionSpec as P

HEADS = 16
HEAD = 128


deep_alpha = math.sqrt(48.0)
epsilon = 1e-05
mask_token = 3
both = ("items", "seq")
bf16 = jnp.bfloat16
f32 = jnp.float32
score_scale = HEAD ** (-0.5)
exponent_scale = score_scale * math.log2(math.e)


class Lines:
    def __init__(self):
        self.last = {}

    def swap(self, part, axis, bit):
        if (axis, bit) in self.last:
            part, _ = lax.optimization_barrier((part, self.last[axis, bit]))
        size = lax.axis_size(axis)
        got = lax.ppermute(part, axis, [(j, j ^ bit) for j in range(size)])
        self.last[axis, bit] = got
        return got


def bits_of(axis):
    found = []
    bit = 1
    while bit < lax.axis_size(axis):
        found.append((axis, bit))
        bit *= 2
    return found


def my_bit(axis, bit):
    return (lax.axis_index(axis) // bit) % 2


def pick(whole, place, dim):
    return lax.dynamic_index_in_dim(whole, place, dim, keepdims=False)


def moved(masks, axis, bit):
    return (masks[0] ^ (bit if axis == "items" else 0), masks[1] ^ (bit if axis == "seq" else 0))


def contract_rows(left, right):
    return lax.dot_general(left, right, (((0,), (0,)), ((), ())), preferred_element_type=f32)


def contract_cols(left, right):
    return lax.dot_general(left, right, (((1,), (1,)), ((), ())), preferred_element_type=f32)


def dot(left, right):
    return jnp.dot(left, right, preferred_element_type=f32)


def turn(values, cosine, sine_part):
    return values * cosine + pltpu.roll(values, HEAD // 2, 1) * sine_part


def head_parts(onehot_ref, table_ref, cosine, sine_part):
    onehot = onehot_ref[...]
    mixed = dot(jnp.concatenate([onehot, onehot], axis=1), table_ref[...])
    query = turn(mixed[:, :HEAD], cosine, sine_part).astype(bf16)
    key = turn(mixed[:, HEAD : 2 * HEAD], cosine, sine_part).astype(bf16)
    return query, key, mixed[:, 2 * HEAD :].astype(bf16)


def visible_scores(key, query, offset, visible):
    scores = contract_cols(key, query)
    place = offset + lax.broadcasted_iota(jnp.int32, (1, query.shape[0]), 1)
    seen = lax.broadcasted_iota(jnp.int32, scores.shape, 0) < jnp.maximum(place + 1, visible)
    return jnp.where(seen, scores, -1e30)


def table_halves(mixed_table):
    vocab = mixed_table.shape[0]
    by_head = jnp.transpose(mixed_table.reshape(vocab, -1, 3 * HEAD), (1, 0, 2))
    high = lax.reduce_precision(by_head, 8, 7)
    return jnp.concatenate([high.astype(bf16), (by_head - high).astype(bf16)], axis=1)


def norm_rows(rows):
    center = rows - jnp.mean(rows, axis=-1, keepdims=True)
    inverse = lax.rsqrt(jnp.mean(center * center, axis=-1, keepdims=True) + epsilon)
    return center * inverse, inverse


def norm_rows_back(grad, normed, inverse, gain):
    scaled = grad * gain
    return inverse * (
        scaled
        - jnp.mean(scaled, axis=-1, keepdims=True)
        - normed * jnp.mean(scaled * normed, axis=-1, keepdims=True)
    )


MESH = pl.DeviceIdType.MESH


class Copies:
    def __init__(self, send_sems, recv_sems, local_sems):
        self.sems = send_sems, recv_sems, local_sems
        self.sent = {}
        self.moved = 0
        self.count = 0
        self.here = lax.axis_index("items"), lax.axis_index("seq")

    def send(self, source, target, masks):
        order = self.count
        self.count += 1
        copy = pltpu.make_async_remote_copy(
            src_ref=source,
            dst_ref=target,
            send_sem=self.sems[0].at[order],
            recv_sem=self.sems[1].at[order],
            device_id=(self.here[0] ^ masks[0], self.here[1] ^ masks[1]),
            device_id_type=MESH,
        )
        copy.start()
        self.sent[id(copy)] = copy
        return copy

    def move(self, source, target):
        copy = pltpu.make_async_copy(source, target, self.sems[2].at[self.moved])
        self.moved += 1
        copy.start()
        return copy

    def sent_now(self, copy):
        self.sent.pop(id(copy)).wait_send()

    def end(self):
        for copy in self.sent.values():
            copy.wait_send()


def wait_all(copies):
    for copy in copies:
        copy.wait_recv()


def mask_of(step):
    return moved((0, 0), *step)


def greet(masks):
    barrier = pltpu.get_barrier_semaphore()
    here = lax.axis_index("items"), lax.axis_index("seq")
    for mask_i, mask_s in masks:
        pl.semaphore_signal(
            barrier,
            inc=1,
            device_id=(here[0] ^ mask_i, here[1] ^ mask_s),
            device_id_type=MESH,
        )
    pl.semaphore_wait(barrier, len(masks))


def partners(seq_size, item_bits):
    return [(0, mask) for mask in range(1, seq_size)] + [mask_of(step) for step in item_bits]


def aligned(place, size):
    return pl.ds(place // size * size, size)


def first_kernel(
    item_bits,
    seq_bits,
    row_count,
    small_ref,
    heads_ref,
    head_bias_ref,
    dense_ref,
    in_ref,
    out_ref,
    everyone_ref,
    table_ref,
    block_ref,
    dense_all_ref,
    own_in_ref,
    own_out_ref,
    embed_scr,
    block_scr,
    sum_scr,
    got_scr,
    send_sems,
    recv_sems,
    local_sems,
):
    items_size, seq_size = everyone_ref.shape[:2]
    item_place, seq_place = lax.axis_index("items"), lax.axis_index("seq")
    core, chip = seq_place % 2, seq_place // 2
    member = seq_place % 4
    rows = dense_ref.shape[0]
    columns = block_scr.shape[2]
    greet(partners(seq_size, item_bits))
    copies = Copies(send_sems, recv_sems, local_sems)

    def head_columns(place, source):
        return source.at[:, pl.ds(pl.multiple_of(place * columns, 128), columns)]

    head_rows = [
        (heads_ref, pl.ds(0, rows)),
        (head_bias_ref, pl.ds(rows, row_count - rows)),
    ]

    small = [copies.send(small_ref, everyone_ref.at[item_place, seq_place], mask_of(seq_bits[0]))]
    heads = [
        copies.send(
            head_columns(seq_place ^ mask, source), block_scr.at[seq_place, place], (0, mask)
        )
        for mask in range(1, seq_size)
        for source, place in head_rows
    ]
    dense = [
        copies.send(dense_ref, dense_all_ref.at[item_place, chip, core], mask_of(seq_bits[1]))
    ]
    mine = pl.ds(pl.multiple_of(member * rows, rows), rows)
    shares = []

    def share(source, target):
        for mask in range(1, 4):
            other = member ^ mask
            shares.append(
                copies.send(source.at[other // 2, other % 2], target.at[mine], (0, mask))
            )

    local = [
        copies.move(small_ref, everyone_ref.at[item_place, seq_place]),
        copies.move(dense_ref, dense_all_ref.at[item_place, chip, core]),
        copies.move(head_columns(seq_place, heads_ref), block_scr.at[seq_place, head_rows[0][1]]),
        copies.move(
            head_columns(seq_place, head_bias_ref), block_scr.at[seq_place, head_rows[1][1]]
        ),
        copies.move(in_ref.at[member // 2, core], own_in_ref.at[0, mine]),
        copies.move(out_ref.at[member // 2, core], own_out_ref.at[mine]),
    ]
    for copy in local:
        copy.wait()

    for order in range(1, len(seq_bits)):
        if order > 1:
            wait_all(dense[-1:])
            part = dense_all_ref.at[item_place, aligned(chip, 2 ** (order - 1)), core]
            dense.append(copies.send(part, part, mask_of(seq_bits[order])))
        wait_all(small[-1:])
        part = everyone_ref.at[item_place, aligned(seq_place, 2**order)]
        small.append(copies.send(part, part, mask_of(seq_bits[order])))
        if order == 1:
            share(in_ref, own_in_ref.at[0])
    wait_all(small[-1:])
    embed = copies.move(everyone_ref.at[item_place, :, pl.ds(0, row_count)], embed_scr)

    wait_all(heads)
    embed.wait()
    sum_scr[0] = lax.dot_general(
        embed_scr[...].reshape(seq_size * row_count, -1),
        block_scr[...].reshape(seq_size * row_count, columns),
        (((0,), (0,)), ((), ())),
        preferred_element_type=f32,
    )
    sums = copies.send(sum_scr.at[0], got_scr.at[0], mask_of(item_bits[0]))
    block_out = copies.move(block_scr, block_ref)
    part = everyone_ref.at[item_place]
    small.append(copies.send(part, part, mask_of(item_bits[0])))
    share(out_ref, own_out_ref)
    wait_all(dense[-1:])

    def dense_part(mask):
        return dense_all_ref.at[item_place ^ mask, :, core]

    known = [0]
    waves = []
    for step in item_bits[::-1]:
        waves.append([(mask, step) for mask in known])
        known = known + [mask ^ step[1] for mask in known]
    arrived = {}
    for wave in waves:
        part = dense_part(0)
        arrived[wave[0][1][1]] = copies.send(part, part, mask_of(wave[0][1]))
    near = [copies.send(dense_part(0), dense_part(0), mask_of(seq_bits[0]))]
    wait_all(shares[:3])
    outer = []
    if len(seq_bits) == 3:
        first = pl.ds(0, 2 * rows)
        outer.append(
            copies.send(own_in_ref.at[0, first], own_in_ref.at[1, first], mask_of(seq_bits[2]))
        )
    for order, step in enumerate(item_bits):
        sums.wait_recv()
        sum_scr[order + 1] = sum_scr[order] + got_scr[order]
        if order + 1 < len(item_bits):
            sums = copies.send(
                sum_scr.at[order + 1], got_scr.at[order + 1], mask_of(item_bits[order + 1])
            )
            wait_all(small[-1:])
            part = everyone_ref.at[aligned(item_place, 2 ** (order + 1))]
            small.append(copies.send(part, part, mask_of(item_bits[order + 1])))
        if order < len(waves) and order + 1 < len(item_bits):
            wave = waves[order]
            for mask, step in wave:
                arrived[mask ^ step[1]].wait_recv()
                part = dense_part(mask ^ step[1])
                for later in waves[order + 1 :]:
                    arrived[mask ^ step[1] ^ later[0][1][1]] = copies.send(
                        part, part, mask_of(later[0][1])
                    )
                near.append(copies.send(part, part, mask_of(seq_bits[0])))
    table_ref[...] = sum_scr[len(item_bits)]

    for mask, step in waves[-1]:
        arrived[mask ^ step[1]].wait_recv()
        part = dense_part(mask ^ step[1])
        near.append(copies.send(part, part, mask_of(seq_bits[0])))
    wait_all(near)
    wait_all(shares[3:])
    wait_all(outer)
    wait_all(small[-1:])
    block_out.wait()
    copies.end()


def first_call(item_bits, seq_bits, small, heads, head_bias, dense, parts_in, parts_out):
    items_size, seq_size = 2 ** len(item_bits), 2 ** len(seq_bits)
    row_count = heads.shape[0] + head_bias.shape[0]
    rows, width = dense.shape
    vocab = small.shape[1]
    columns = heads.shape[1] // seq_size
    any_space = pl.BlockSpec(memory_space=pl.ANY)
    spare = 8 * (len(item_bits) + len(seq_bits)) + 4 * seq_size + 2 ** (len(item_bits) + 2)
    return pl.pallas_call(
        functools.partial(first_kernel, item_bits, seq_bits, row_count),
        in_specs=[any_space] * 6,
        out_specs=[any_space, pl.BlockSpec(memory_space=pltpu.VMEM)] + [any_space] * 4,
        out_shape=[
            jax.ShapeDtypeStruct((items_size, seq_size) + small.shape, bf16),
            jax.ShapeDtypeStruct((vocab, columns), f32),
            jax.ShapeDtypeStruct((seq_size, row_count, columns), bf16),
            jax.ShapeDtypeStruct((items_size, seq_size // 2, 2, rows, width), bf16),
            jax.ShapeDtypeStruct((2, 4 * rows, parts_in.shape[3]), bf16),
            jax.ShapeDtypeStruct((4 * rows, parts_out.shape[3]), bf16),
        ],
        scratch_shapes=[
            pltpu.VMEM((seq_size, row_count, vocab), bf16),
            pltpu.VMEM((seq_size, row_count, columns), bf16),
            pltpu.VMEM((len(item_bits) + 1, vocab, columns), f32),
            pltpu.VMEM((len(item_bits), vocab, columns), f32),
            pltpu.SemaphoreType.DMA((spare,)),
            pltpu.SemaphoreType.DMA((spare,)),
            pltpu.SemaphoreType.DMA((8,)),
        ],
        compiler_params=pltpu.CompilerParams(
            collective_id=0, has_side_effects=True, vmem_limit_bytes=24 * 2**20
        ),
        name="first",
    )(small, heads, head_bias, dense, parts_in, parts_out)


class Spread:
    def __init__(self, copies, own, whole, outer_bits, item_bits, given=None):
        self.copies, self.own, self.whole, self.given = copies, own, whole, given
        self.outer_bits, self.item_bits = outer_bits, item_bits
        half = own.shape[0] // 2
        self.halves = pl.ds(0, half), pl.ds(half, half)
        self.last = []

    def part(self, masks):
        place = (self.copies.here[0] ^ masks[0]) * lax.axis_size("seq")
        return self.whole.at[(place + (self.copies.here[1] ^ masks[1])) // 4]

    def over(self, masks, step, rows=None):
        source = self.own if masks == (0, 0) else self.part(masks)
        target = self.part(masks)
        if rows is not None:
            source, target = source.at[rows], target.at[rows]
        return self.copies.send(source, target, mask_of(step))

    def start(self):
        self.local = self.copies.move(self.own, self.part((0, 0)))
        self.first = [self.over((0, 0), step) for step in self.item_bits]

    def start_given(self):
        masks = mask_of(self.outer_bits[0])
        target = self.part(masks).at[self.halves[0]]
        self.local_given = self.copies.move(self.given, target)
        self.second = [
            [self.copies.send(self.given, target, mask_of(step)) for step in self.item_bits],
            [],
        ]
        self.outer = [None, self.over((0, 0), self.outer_bits[0], self.halves[1])]

    def start_outer(self):
        self.outer = [self.over((0, 0), self.outer_bits[0], rows) for rows in self.halves]
        self.second = [[], []]

    def cross_own(self):
        one, two = self.item_bits
        self.first[0].wait_recv()
        self.last.append(self.over(moved((0, 0), *one), two, self.halves[0]))
        self.first[1].wait_recv()
        self.last.append(self.over(moved((0, 0), *two), one, self.halves[1]))

    def spread_outer(self, which):
        self.outer[which].wait_recv()
        masks = mask_of(self.outer_bits[0])
        self.second[which] = [
            self.over(masks, step, self.halves[which]) for step in self.item_bits
        ]

    def cross_outer(self, which):
        masks = mask_of(self.outer_bits[0])
        steps = self.item_bits if which == 0 else self.item_bits[::-1]
        copies = self.second[which] if which == 0 else self.second[which][::-1]
        copies[0].wait_recv()
        self.last.append(self.over(moved(masks, *steps[0]), steps[1], self.halves[which]))
        self.last.append(copies[1])

    def plain(self):
        self.local = self.copies.move(self.own, self.part((0, 0)))
        known = [(0, 0)]
        for step in self.outer_bits + self.item_bits:
            wait_all([self.over(masks, step) for masks in known])
            known = known + [moved(masks, *step) for masks in known]

    def end(self):
        wait_all(self.last)
        self.local.wait()
        if self.given is not None:
            self.local_given.wait()


def attend_unit(block, visible, onehot_ref, table_ref, cosine_ref, sine_ref, context_ref, lse_ref):
    query, key, value = head_parts(onehot_ref, table_ref, cosine_ref[...], sine_ref[...])
    value_turned = value.T
    for offset in range(0, query.shape[0], block):
        scores = visible_scores(key, query[offset : offset + block], offset, visible)
        peak = jnp.max(scores, axis=0, keepdims=True)
        expos = jnp.exp2((scores - peak) * exponent_scale)
        total = jnp.sum(expos, axis=0, keepdims=True)
        context = dot(value_turned, expos.astype(bf16)) / total
        context_ref[offset : offset + block, :] = context.T.astype(bf16)
        lse_ref[:, offset : offset + block] = peak * exponent_scale + jnp.log2(total)


def second_kernel(
    item_bits,
    seq_bits,
    visible_ref,
    onehot_ref,
    table_ref,
    cosine_ref,
    sine_ref,
    own_onehot_ref,
    embed_ref,
    vector_ref,
    dense_ref,
    own_in_ref,
    own_out_ref,
    context_ref,
    lse_ref,
    in_ref,
    out_ref,
    shared_ref,
    normed_ref,
    inverse_ref,
    context_scr,
    dense_scr,
    resid_scr,
    low_scr,
    send_sems,
    recv_sems,
    local_sems,
):
    seq_size = 2 ** len(seq_bits)
    items_here, length, features = context_scr.shape
    heads_here = features // HEAD
    span = length // seq_size
    width = dense_ref.shape[0]
    seq_place = lax.axis_index("seq")
    outer_bits = seq_bits[2:]
    greet(partners(seq_size, item_bits))
    copies = Copies(send_sems, recv_sems, local_sems)
    dense_copy = copies.move(dense_ref, dense_scr)
    stepwise = len(outer_bits) == 1 and len(item_bits) == 2
    given = own_in_ref.at[1, pl.ds(0, own_in_ref.shape[1] // 2)] if stepwise else None
    spreads = [
        Spread(copies, own_in_ref.at[0], in_ref, outer_bits, item_bits, given),
        Spread(copies, own_out_ref, out_ref, outer_bits, item_bits),
    ]
    if stepwise:
        spreads[0].start()
        spreads[0].start_given()
    arrivals, local = [], []
    for item in range(items_here):

        @pl.loop(0, heads_here)
        def _(head):
            place = pl.ds(pl.multiple_of(head * HEAD, HEAD), HEAD)
            attend_unit(
                min(256, length),
                visible_ref[item],
                onehot_ref.at[item],
                table_ref.at[head],
                cosine_ref,
                sine_ref,
                context_scr.at[item, :, place],
                lse_ref.at[item, head],
            )

        target = context_ref.at[
            item, :, pl.ds(pl.multiple_of(seq_place * features, HEAD), features)
        ]
        for mask in range(seq_size):
            rows = pl.ds(pl.multiple_of((seq_place ^ mask) * span, span), span)
            source = context_scr.at[item, rows]
            if mask:
                arrivals.append(copies.send(source, target, (0, mask)))
            else:
                local.append(copies.move(source, target))
    if stepwise:
        spreads[0].cross_own()
        spreads[0].cross_outer(0)
        spreads[1].start()
        spreads[0].spread_outer(1)
    wait_all(arrivals)
    for copy in local:
        copy.wait()

    if stepwise:
        spreads[1].start_outer()

    dense_copy.wait()
    rows_all = items_here * span
    tile = 256

    @pl.loop(0, width // tile)
    def _(order):
        place = pl.ds(pl.multiple_of(order * tile, tile), tile)
        branch = dot(context_ref[...].reshape(rows_all, width), dense_scr[:, place])
        inputs = contract_cols(own_onehot_ref[...], embed_ref[place, :])
        resid_scr[:, place] = deep_alpha * inputs + (branch + vector_ref[5:6, place])

    block = 32
    near, far = ("seq", 1), ("seq", 2)
    far_copies, near_copies, own_copies = [], [], []
    for item in range(items_here):

        @pl.loop(0, span // block)
        def _(order):
            start = pl.multiple_of(order * block, block)
            rows = pl.ds(pl.multiple_of(item * span + start, block), block)
            normed, inverse = norm_rows(resid_scr[rows, :])
            normed_ref[rows, :] = normed
            inverse_ref[rows, :] = jnp.broadcast_to(inverse, (block, 128))
            hidden = normed * vector_ref[0:1, :] + vector_ref[1:2, :]
            low_scr[item, pl.ds(start, block), :] = hidden.astype(bf16)

        source = low_scr.at[item]
        far_copies.append(copies.send(source, shared_ref.at[item, 1], mask_of(far)))
        near_copies.append(copies.send(source, shared_ref.at[item, 2], mask_of(near)))
        own_copies.append(copies.move(source, shared_ref.at[item, 0]))

    def pass_on(item):
        far_copies[item].wait_recv()
        part = shared_ref.at[item, 1]
        near_copies.append(copies.send(part, shared_ref.at[item, 3], mask_of(near)))

    if stepwise:
        spreads[1].cross_own()
        spreads[0].cross_outer(1)
    pass_on(0)
    if stepwise:
        spreads[1].spread_outer(0)
    pass_on(1)
    if stepwise:
        spreads[1].spread_outer(1)
        spreads[1].cross_outer(0)
    for item in range(2, items_here):
        pass_on(item)
    if stepwise:
        spreads[1].cross_outer(1)
    else:
        for one in spreads:
            one.plain()
    for one in spreads:
        one.end()
    wait_all(near_copies)
    for copy in own_copies:
        copy.wait()
    copies.end()


def second_call(
    item_bits,
    seq_bits,
    visible,
    onehots,
    tables,
    cosine,
    sine_part,
    own_onehot,
    embed,
    vectors,
    w_dense,
    own_in,
    own_out,
):
    items_here, length, vocab = onehots.shape
    heads_here = tables.shape[0]
    features = heads_here * HEAD
    seq_size = 2 ** len(seq_bits)
    span = length // seq_size
    width = w_dense.shape[0]
    groups = 2 ** (len(item_bits) + len(seq_bits)) // 4
    any_space = pl.BlockSpec(memory_space=pl.ANY)
    near_space = pl.BlockSpec(memory_space=pltpu.VMEM)
    spare = 4 * groups + items_here * (seq_size + 4)
    return pl.pallas_call(
        functools.partial(second_kernel, item_bits, seq_bits),
        in_specs=[pl.BlockSpec(memory_space=pltpu.SMEM)] + [near_space] * 7 + [any_space] * 3,
        out_specs=[near_space] * 2 + [any_space] * 3 + [near_space] * 2,
        out_shape=[
            jax.ShapeDtypeStruct((items_here, span, width), bf16),
            jax.ShapeDtypeStruct((items_here, heads_here, 1, length), f32),
            jax.ShapeDtypeStruct((groups,) + own_in.shape[1:], bf16),
            jax.ShapeDtypeStruct((groups,) + own_out.shape, bf16),
            jax.ShapeDtypeStruct((items_here, 4, span, width), bf16),
            jax.ShapeDtypeStruct((items_here * span, width), f32),
            jax.ShapeDtypeStruct((items_here * span, 128), f32),
        ],
        scratch_shapes=[
            pltpu.VMEM((items_here, length, features), bf16),
            pltpu.VMEM((width, width), bf16),
            pltpu.VMEM((items_here * span, width), f32),
            pltpu.VMEM((items_here, span, width), bf16),
            pltpu.SemaphoreType.DMA((spare,)),
            pltpu.SemaphoreType.DMA((spare,)),
            pltpu.SemaphoreType.DMA((16,)),
        ],
        compiler_params=pltpu.CompilerParams(
            collective_id=1, has_side_effects=True, vmem_limit_bytes=56 * 2**20
        ),
        name="second",
    )(
        visible,
        onehots,
        tables,
        cosine,
        sine_part,
        own_onehot,
        embed,
        vectors,
        w_dense,
        own_in,
        own_out,
    )


def leading(ref):
    return [index for index in np.ndindex(*ref.shape[:-2])]


def add_into(target, source):
    rows = target.shape[-2]
    for index in leading(target):

        @pl.loop(0, rows // 16)
        def _(order):
            place = index + (pl.ds(pl.multiple_of(order * 16, 16), 16),)
            total = target[place].astype(f32) + source[place].astype(f32)
            target[place] = total.astype(target.dtype)


def copy_into(target, source):
    @pl.loop(0, target.shape[0] // 16)
    def _(order):
        place = pl.ds(pl.multiple_of(order * 16, 16), 16)
        target[place] = source[place]


class Reduce:
    def __init__(self, copies, whole, rows, dims, steps, got, stage, stage_sems):
        self.copies, self.whole, self.rows = copies, whole, rows
        self.steps, self.got = steps, got
        self.place = dims.index(steps[0])
        self.stage, self.stage_sems = stage, stage_sems
        self.order = 0

    def first(self, bit, index=()):
        full = (slice(None),) * self.place
        if index:
            full = index[: self.place]
        rest = index[self.place :] if index else ()
        if index:
            return self.whole.at[full + (bit,) + rest + (self.rows,)]
        spare = len(self.whole.shape) - 3 - self.place
        return self.whole.at[full + (bit,) + (slice(None),) * spare + (self.rows,)]

    def start(self):
        step = self.steps[0]
        self.copy = self.copies.send(self.first(1 - my_bit(*step)), self.got[0], mask_of(step))

    def advance(self):
        step = self.steps[self.order]
        self.copy.wait_recv()
        if self.order == 0:
            self.kept = self.got[0]
            rows, columns = self.kept.shape[-2:]
            places = leading(self.kept)

            def load(order):
                return pltpu.make_async_copy(
                    self.first(my_bit(*step), places[order]),
                    self.stage.at[order % 2, pl.ds(0, rows), pl.ds(0, columns)],
                    self.stage_sems.at[order % 2],
                )

            load(0).start()
            for order, place in enumerate(places):
                if order + 1 < len(places):
                    load(order + 1).start()
                load(order).wait()
                add_into(
                    self.kept.at[place],
                    self.stage.at[order % 2, pl.ds(0, rows), pl.ds(0, columns)],
                )
        else:
            self.kept = self.kept.at[my_bit(*step)]
            add_into(self.kept, self.got[self.order])
        self.order += 1
        if self.order < len(self.steps):
            step = self.steps[self.order]
            self.copy = self.copies.send(
                self.kept.at[1 - my_bit(*step)], self.got[self.order], mask_of(step)
            )


def attend_back_unit(
    block,
    visible,
    onehot_ref,
    table_ref,
    cosine_ref,
    sine_ref,
    lse_ref,
    grad_ref,
    mixed_ref,
    sums_ref,
):
    cosine, sine_part = cosine_ref[...], sine_ref[...]
    query, key, value = head_parts(onehot_ref, table_ref, cosine, sine_part)
    key_turned = key.T
    length = query.shape[0]
    grad_key = jnp.zeros((length, HEAD), f32)
    grad_value = jnp.zeros((length, HEAD), f32)
    grad_query = []
    for offset in range(0, length, block):
        query_block = query[offset : offset + block]
        grad_block = grad_ref[offset : offset + block, :]
        scores = visible_scores(key, query_block, offset, visible)
        weights = jnp.exp2(scores * exponent_scale - lse_ref[:, offset : offset + block])
        grad_weights = contract_cols(value, grad_block)
        inner = jnp.sum(weights * grad_weights, axis=0, keepdims=True)
        grad_scores = (weights * (grad_weights - inner)).astype(bf16)
        grad_value = grad_value + dot(weights.astype(bf16), grad_block)
        grad_key = grad_key + dot(grad_scores, query_block)
        grad_query.append(dot(key_turned, grad_scores).T)
    grad_query = jnp.concatenate(grad_query, axis=0)

    def back(grad):
        return turn((grad * score_scale).astype(bf16).astype(f32), cosine, -sine_part).astype(bf16)

    mixed = jnp.concatenate([back(grad_query), back(grad_key), grad_value.astype(bf16)], axis=1)
    mixed_ref[...] = mixed.reshape(mixed_ref.shape)
    sums_ref[...] += dot(onehot_ref[...].T, mixed)


def third_kernel(
    item_bits,
    seq_bits,
    visible_ref,
    onehot_ref,
    table_ref,
    cosine_ref,
    sine_ref,
    lse_ref,
    slice_ref,
    grad_ref,
    in_ref,
    out_ref,
    dense_ref,
    bias_ref,
    spread_ref,
    sums_all_ref,
    in_part_ref,
    out_part_ref,
    dense_part_ref,
    bias_sum_ref,
    mixed_scr,
    other_scr,
    kept_scr,
    step_scrs,
    sums_scr,
    sums_got,
    bias_scr,
    bias_got,
    in_got,
    out_got,
    dense_got,
    in_final,
    out_final,
    stage_scr,
    stage_sems,
    send_sems,
    recv_sems,
    local_sems,
):
    seq_size = 2 ** len(seq_bits)
    items_here, length, features = grad_ref.shape
    heads_here = features // HEAD
    seq_place = lax.axis_index("seq")
    member = seq_place % 4
    outer_bits = seq_bits[2:]
    width = slice_ref.shape[0]
    greet(partners(seq_size, item_bits))
    copies = Copies(send_sems, recv_sems, local_sems)
    dims = item_bits[::-1] + outer_bits[::-1]

    def reducers(whole, got):
        rows = whole.shape[-2]
        if len(item_bits) == 2:
            one, two = item_bits
            ways = [
                (pl.ds(0, rows // 2), [two, one] + outer_bits[::-1]),
                (pl.ds(rows // 2, rows // 2), [one, two] + outer_bits[::-1]),
            ]
        else:
            ways = [(pl.ds(0, rows), dims)]
        return [
            Reduce(copies, whole, part, dims, steps, list(got[order]), stage_scr, stage_sems)
            for order, (part, steps) in enumerate(ways)
        ]

    in_sums = reducers(in_ref, in_got)
    out_sums = reducers(out_ref, out_got)
    dense_steps = item_bits[::-1] + seq_bits[:0:-1]
    dense_sum = Reduce(
        copies,
        dense_ref,
        pl.ds(0, dense_ref.shape[-2]),
        dense_steps,
        dense_steps,
        list(dense_got),
        stage_scr,
        stage_sems,
    )
    for one in in_sums + out_sums:
        one.start()
    sums_scr[...] = jnp.zeros_like(sums_scr)
    tile = 256
    flying = {}
    sums_copy = None

    def next_sum(order):
        nonlocal sums_copy
        sums_copy.wait_recv()
        sums_scr[order + 1] = sums_scr[order] + sums_got[order]
        if order + 1 < len(item_bits):
            sums_copy = copies.send(
                sums_scr.at[order + 1], sums_got.at[order + 1], mask_of(item_bits[order + 1])
            )

    bias_scr[0] = bias_ref[...]
    bias_steps = seq_bits + item_bits
    bias_copies = [copies.send(bias_scr.at[0], bias_got.at[0], mask_of(bias_steps[0]))]
    for stage in range(items_here + len(seq_bits)):
        if stage < items_here:

            @pl.loop(0, heads_here)
            def _(head):
                place = pl.ds(pl.multiple_of(head * HEAD, HEAD), HEAD)
                packed = pl.ds(pl.multiple_of(head * 3 * HEAD, HEAD), 3 * HEAD)
                attend_back_unit(
                    min(256, length),
                    visible_ref[stage],
                    onehot_ref.at[stage],
                    table_ref.at[head],
                    cosine_ref,
                    sine_ref,
                    lse_ref.at[stage, head],
                    grad_ref.at[stage, :, place],
                    mixed_scr.at[:, :, :, packed],
                    sums_scr.at[0, head],
                )

        for order in range(len(seq_bits) - 1, -1, -1):
            item = stage - 1 - order
            if not 0 <= item < items_here:
                continue
            copy, kept = flying[item]
            copy.wait_recv()
            got = step_scrs[order].at[item % 2]
            if order:
                full = (slice(None),) * (len(kept.shape) - 3)
                kept = kept.at[full + (my_bit(*seq_bits[order]),)]
            if order + 1 < len(seq_bits):
                add_into(kept, got)
                step = seq_bits[order + 1]
                full = (slice(None),) * (len(kept.shape) - 3)
                copy = copies.send(
                    kept.at[full + (1 - my_bit(*step),)],
                    step_scrs[order + 1].at[item % 2],
                    mask_of(step),
                )
                flying[item] = copy, kept
                flying["later", item].append(copy)
            else:

                @pl.loop(0, kept.shape[0] // 16)
                def _(block):
                    place = (pl.ds(pl.multiple_of(block * 16, 16), 16),)
                    total = kept[place].astype(f32) + got[place].astype(f32)
                    spread_ref[(item,) + place] = total.astype(bf16)

        if stage < items_here:
            core = my_bit(*seq_bits[0])
            slot = stage % 2
            if stage >= 2:
                copies.sent_now(flying["first", stage - 2])
            kept_slot = stage % len(seq_bits)
            if stage >= len(seq_bits):
                for copy in flying["later", stage - len(seq_bits)]:
                    copies.sent_now(copy)
            half = mixed_scr.shape[0] * mixed_scr.shape[2]
            other = mixed_scr[:, 1 - core].reshape(half, -1)
            mine = mixed_scr[:, core].reshape(half, -1)

            @pl.loop(0, width // tile)
            def _(order):
                place = pl.ds(pl.multiple_of(order * tile, tile), tile)
                weights = slice_ref[place, :]
                target = other_scr.at[slot]
                target[..., place] = contract_cols(other, weights).astype(bf16).reshape(
                    target.shape[:-1] + (tile,)
                )
                target = kept_scr.at[kept_slot]
                target[..., place] = contract_cols(mine, weights).astype(bf16).reshape(
                    target.shape[:-1] + (tile,)
                )

            copy = copies.send(
                other_scr.at[slot], step_scrs[0].at[slot], mask_of(seq_bits[0])
            )
            flying[stage] = copy, kept_scr.at[kept_slot]
            flying["first", stage] = copy
            flying["later", stage] = []
        if stage == 1:
            dense_sum.start()
        if stage == items_here - 1:
            sums_copy = copies.send(sums_scr.at[0], sums_got.at[0], mask_of(item_bits[0]))
        if stage == items_here:
            for one in in_sums:
                one.advance()
        if stage == items_here + 1:
            next_sum(0)
            for one in in_sums:
                one.advance()
            for one in out_sums:
                one.advance()
        if stage == items_here + 2:
            for order in range(1, len(item_bits)):
                next_sum(order)
            for one in out_sums:
                one.advance()

        bias_done = len(bias_copies)
        if bias_done <= len(bias_steps):
            bias_copies[-1].wait_recv()
            bias_scr[bias_done] = bias_scr[bias_done - 1] + bias_got[bias_done - 1]
            if bias_done < len(bias_steps):
                bias_copies.append(
                    copies.send(
                        bias_scr.at[bias_done],
                        bias_got.at[bias_done],
                        mask_of(bias_steps[bias_done]),
                    )
                )
            else:
                bias_copies.append(None)
                bias_sum_ref[...] = bias_scr[bias_done]

    sums_all_ref[seq_place] = sums_scr[len(item_bits)].astype(bf16)
    known = [0]
    arrivals = []
    for axis, bit in seq_bits[::-1]:
        wait_all(arrivals)
        arrivals = []
        for mask in known:
            part = sums_all_ref.at[seq_place ^ mask]
            arrivals.append(copies.send(part, part, (0, bit)))
        known = known + [mask ^ bit for mask in known]
        if dense_sum.order < len(dense_steps):
            dense_sum.advance()

    while in_sums[0].order < len(dims):
        for one in in_sums + out_sums:
            if one.order < len(dims):
                one.advance()
        if dense_sum.order < len(dense_steps):
            dense_sum.advance()
    while out_sums[0].order < len(dims):
        for one in out_sums:
            one.advance()
    wait_all(arrivals)
    shares, local = [], []
    for sums, final, target in (
        (in_sums, in_final, in_part_ref),
        (out_sums, out_final, out_part_ref),
    ):
        rows = target.shape[1]
        first = 0
        for one in sums:
            copy_into(final.at[pl.ds(first, one.kept.shape[0])], one.kept)
            first += one.kept.shape[0]
        for mask in range(4):
            source = final.at[pl.ds(pl.multiple_of((member ^ mask) * rows, 16), rows)]
            if mask:
                shares.append(copies.send(source, target.at[member], (0, mask)))
            else:
                local.append(copies.move(source, target.at[member]))
    while dense_sum.order < len(dense_steps):
        dense_sum.advance()
    dense_part_ref[...] = dense_sum.kept[...]
    wait_all(shares)
    for copy in local:
        copy.wait()
    copies.end()


def third_call(
    item_bits,
    seq_bits,
    visible,
    onehots,
    tables,
    cosine,
    sine_part,
    log_sums,
    w_slice,
    grad_context,
    grad_in,
    grad_out,
    by_rows,
    in_sum,
):
    items_here, length, vocab = onehots.shape
    heads_here = tables.shape[0]
    seq_size = 2 ** len(seq_bits)
    span = length // seq_size
    width = w_slice.shape[0]
    packed = heads_here * 3 * HEAD
    outer = len(seq_bits) - 2
    levels = len(item_bits) + outer
    any_space = pl.BlockSpec(memory_space=pl.ANY)
    near_space = pl.BlockSpec(memory_space=pltpu.VMEM)

    def got_shapes(whole, ways, depth):
        rows, columns = whole.shape[-2:]
        one = tuple(
            pltpu.VMEM((2,) * order + (rows // ways, columns), bf16)
            for order in range(depth - 1, -1, -1)
        )
        return one

    ways = 2 if len(item_bits) == 2 else 1
    group_rows = grad_in.shape[-2]
    rows = group_rows // 4
    dense_depth = len(item_bits) + len(seq_bits) - 1
    spread = (2,) * (len(seq_bits) - 1) + (span, width)
    all_bits = len(item_bits) + len(seq_bits)
    spare = 8 * items_here + 8 * levels + 16 * all_bits
    stage_rows = max(group_rows // ways, by_rows.shape[-2])
    return pl.pallas_call(
        functools.partial(third_kernel, item_bits, seq_bits),
        in_specs=[pl.BlockSpec(memory_space=pltpu.SMEM)]
        + [near_space] * 7
        + [any_space] * 3
        + [near_space],
        out_specs=[near_space, near_space, any_space, any_space, near_space, near_space],
        out_shape=[
            jax.ShapeDtypeStruct((items_here, span, width), bf16),
            jax.ShapeDtypeStruct((seq_size, heads_here, vocab, 3 * HEAD), bf16),
            jax.ShapeDtypeStruct((4, rows, grad_in.shape[-1]), bf16),
            jax.ShapeDtypeStruct((4, rows, grad_out.shape[-1]), bf16),
            jax.ShapeDtypeStruct(by_rows.shape[-2:], bf16),
            jax.ShapeDtypeStruct(in_sum.shape, f32),
        ],
        scratch_shapes=[
            pltpu.VMEM((seq_size // 2, 2, span, packed), bf16),
            pltpu.VMEM((2,) + spread, bf16),
            pltpu.VMEM((len(seq_bits),) + spread, bf16),
            tuple(pltpu.VMEM((2,) + spread[order:], bf16) for order in range(len(seq_bits))),
            pltpu.VMEM((len(item_bits) + 1, heads_here, vocab, 3 * HEAD), f32),
            pltpu.VMEM((len(item_bits), heads_here, vocab, 3 * HEAD), f32),
            pltpu.VMEM((all_bits + 1,) + in_sum.shape, f32),
            pltpu.VMEM((all_bits,) + in_sum.shape, f32),
            tuple(got_shapes(grad_in, ways, levels) for _ in range(ways)),
            tuple(got_shapes(grad_out, ways, levels) for _ in range(ways)),
            got_shapes(by_rows, 1, dense_depth),
            pltpu.VMEM((group_rows, grad_in.shape[-1]), bf16),
            pltpu.VMEM((group_rows, grad_out.shape[-1]), bf16),
            pltpu.VMEM((2, stage_rows, grad_in.shape[-1]), bf16),
            pltpu.SemaphoreType.DMA((2,)),
            pltpu.SemaphoreType.DMA((spare,)),
            pltpu.SemaphoreType.DMA((spare,)),
            pltpu.SemaphoreType.DMA((8,)),
        ],
        compiler_params=pltpu.CompilerParams(
            collective_id=2, has_side_effects=True, vmem_limit_bytes=60 * 2**20
        ),
        name="third",
    )(
        visible,
        onehots,
        tables,
        cosine,
        sine_part,
        log_sums,
        w_slice,
        grad_context,
        grad_in,
        grad_out,
        by_rows,
        in_sum,
    )


def merged_kernel(
    item_bits,
    seq_bits,
    visible_ref,
    onehot_ref,
    table_ref,
    cosine_ref,
    sine_ref,
    lse_ref,
    slice_ref,
    grad_ref,
    shared_ref,
    grad_in_ref,
    grad_shared_ref,
    product_ref,
    dense_ref,
    bias_ref,
    spread_ref,
    sums_all_ref,
    parts_ref,
    dense_part_ref,
    bias_sum_ref,
    land_one_ref,
    land_two_ref,
    land_three_ref,
    mixed_scr,
    other_scr,
    kept_scr,
    step_scrs,
    sums_scr,
    sums_got,
    bias_scr,
    bias_got,
    dense_got,
    rhs_scr,
    lhs_scr,
    turned_scr,
    slot_scr,
    sum_scr,
    stage_scr,
    dense_scr,
    grad_scr,
    stage_sems,
    load_sems,
    send_sems,
    recv_sems,
    local_sems,
):
    seq_size = 2 ** len(seq_bits)
    items_here, length, features = grad_scr.shape
    span = length // seq_size
    heads_here = features // HEAD
    seq_place = lax.axis_index("seq")
    member = seq_place % 4
    outer_bits = seq_bits[2:]
    width = slice_ref.shape[0]
    greet(partners(seq_size, item_bits))
    copies = Copies(send_sems, recv_sems, local_sems)

    one, two = item_bits
    high = outer_bits[0]
    ways = [[two, one, high], [one, two, high]]
    blocks = [(grad_shared_ref, product_ref, 0)]
    ff_part = product_ref.shape[1]
    blocks += [(shared_ref, grad_in_ref, 0), (shared_ref, grad_in_ref, ff_part)]
    group_rows = lhs_scr.shape[2]
    half_rows = group_rows // 2
    pairs = [(two, one), (two,), (one,), ()]

    def masks_of(steps):
        masks = (0, 0)
        for step in steps:
            masks = moved(masks, *step)
        return masks

    def load_rhs(block):
        _, rhs, first = blocks[block]
        return pltpu.make_async_copy(
            rhs.at[:, pl.ds(first, ff_part)], rhs_scr, load_sems.at[0]
        )

    def load_lhs(block, pair, which):
        masks = masks_of(pairs[pair] + ((high,) if which == 0 else ()))
        group = ((copies.here[0] ^ masks[0]) * seq_size + (copies.here[1] ^ masks[1])) // 4
        columns = pl.ds(pl.multiple_of(group * group_rows, 128), group_rows)
        return pltpu.make_async_copy(
            blocks[block][0].at[:, columns], lhs_scr.at[which], load_sems.at[1 + which]
        )

    landed, slots, sends = {}, {}, {}

    def products(block, first):
        if first == 0:
            load_rhs(block).wait()
        for pair, steps in list(enumerate(pairs))[first : first + 2]:
            for which in range(2):
                load_lhs(block, pair, which).wait()
                rows = pl.ds(which * group_rows, group_rows)
                turned_scr[rows, :] = lhs_scr[which].T
            follow = (block, pair + 1) if pair + 1 < len(pairs) else (block + 1, 0)
            if follow[0] < len(blocks):
                for which in range(2):
                    load_lhs(*follow, which).start()
            targets = []
            for which in range(2):
                for way in range(2):
                    away, other = ways[way][:2]
                    place = 2 * (other in steps) + 1 - which
                    if away in steps:
                        if (way, place) in slots:
                            copies.sent_now(slots.pop((way, place)))
                        targets.append(slot_scr.at[way, place])
                    else:
                        targets.append(sum_scr.at[block, way, place])

            def multiply(columns):
                total = dot(turned_scr[...], rhs_scr[:, columns]).astype(bf16)
                for order, target in enumerate(targets):
                    target[:, columns] = total[order * half_rows : (order + 1) * half_rows]

            @pl.loop(0, ff_part // 256)
            def _(order):
                multiply(pl.ds(pl.multiple_of(order * 256, 256), 256))

            if ff_part % 256:
                multiply(pl.ds(ff_part // 256 * 256, ff_part % 256))
            for which in range(2):
                for way in range(2):
                    away, other = ways[way][:2]
                    place = 2 * (other in steps) + 1 - which
                    if away in steps:
                        copy = copies.send(
                            slot_scr.at[way, place],
                            land_one_ref.at[block, way, place],
                            mask_of(away),
                        )
                        slots[way, place] = copy
                        landed[1, block, way, place] = copy
        if first and block + 1 < len(blocks):
            load_rhs(block + 1).start()

    lands = {1: land_one_ref, 2: land_two_ref, 3: land_three_ref}

    def absorb(level, block):
        count = 2 ** (3 - level)
        pending = []

        def finish():
            load, way, place, slot = pending.pop(0)
            load.wait()
            add_into(sum_scr.at[block, way, place], stage_scr.at[slot])
            if level < 3 and place >= count // 2:
                left = place - count // 2
                landed[level + 1, block, way, left] = copies.send(
                    sum_scr.at[block, way, place],
                    lands[level + 1].at[block, way, left],
                    mask_of(ways[way][level]),
                )

        order = 0
        for place in range(count - 1, -1, -1):
            for way in range(2):
                landed[level, block, way, place].wait_recv()
                slot = order % 2
                load = pltpu.make_async_copy(
                    lands[level].at[block, way, place], stage_scr.at[slot], stage_sems.at[slot]
                )
                load.start()
                if pending:
                    finish()
                pending.append((load, way, place, slot))
                order += 1
        finish()

    shares, local = [], []

    def to_members(block):
        rows = parts_ref.shape[2]
        for mask in range(4):
            other = member ^ mask
            source = sum_scr.at[
                block, other // 2, 0, pl.ds(pl.multiple_of(other % 2 * rows, 16), rows)
            ]
            if mask:
                shares.append(copies.send(source, parts_ref.at[block, member], (0, mask)))
            else:
                local.append(copies.move(source, parts_ref.at[block, member]))

    grads = {}

    def send_grads(item):
        target = grad_scr.at[item, pl.ds(pl.multiple_of(seq_place * span, span), span)]
        arriving = []
        for mask in range(seq_size):
            columns = pl.ds(pl.multiple_of((seq_place ^ mask) * features, HEAD), features)
            source = grad_ref.at[item, :, columns]
            if mask:
                arriving.append(copies.send(source, target, (0, mask)))
            else:
                own = copies.move(source, target)
        grads[item] = arriving, own

    send_grads(0)
    load_rhs(0).start()
    for which in range(2):
        load_lhs(0, 0, which).start()
    dense_steps = item_bits[::-1] + seq_bits[:0:-1]
    dense_half = dense_ref.shape[-2] // 2
    dense_sums = [
        Reduce(
            copies,
            dense_ref,
            pl.ds(order * dense_half, dense_half),
            dense_steps,
            steps + dense_steps[2:],
            list(dense_got[order]),
            dense_scr,
            stage_sems,
        )
        for order, steps in enumerate(([two, one], [one, two]))
    ]

    def dense_advance():
        for part in dense_sums:
            part.advance()

    sums_scr[...] = jnp.zeros_like(sums_scr)
    tile = 256
    flying = {}
    sums_copy = None

    def next_sum(order):
        nonlocal sums_copy
        sums_copy.wait_recv()
        sums_scr[order + 1] = sums_scr[order] + sums_got[order]
        if order + 1 < len(item_bits):
            sums_copy = copies.send(
                sums_scr.at[order + 1], sums_got.at[order + 1], mask_of(item_bits[order + 1])
            )

    known, arrivals = [0], []

    def spread_sums():
        nonlocal known, arrivals
        wait_all(arrivals)
        arrivals = []
        bit = seq_size // 2 // len(known)
        for mask in known:
            part = sums_all_ref.at[seq_place ^ mask]
            arrivals.append(copies.send(part, part, (0, bit)))
        known = known + [mask ^ bit for mask in known]

    bias_scr[0] = bias_ref[...]
    bias_steps = seq_bits + item_bits
    bias_copies = [copies.send(bias_scr.at[0], bias_got.at[0], mask_of(bias_steps[0]))]

    def attention(item):
        arriving, own = grads[item]
        wait_all(arriving)
        own.wait()

        @pl.loop(0, heads_here)
        def _(head):
            place = pl.ds(pl.multiple_of(head * HEAD, HEAD), HEAD)
            packed = pl.ds(pl.multiple_of(head * 3 * HEAD, HEAD), 3 * HEAD)
            attend_back_unit(
                min(256, length),
                visible_ref[item],
                onehot_ref.at[item],
                table_ref.at[head],
                cosine_ref,
                sine_ref,
                lse_ref.at[item, head],
                grad_scr.at[item, :, place],
                mixed_scr.at[:, :, :, packed],
                sums_scr.at[0, head],
            )

    def step_on(item, order):
        copy, kept = flying[item]
        copy.wait_recv()
        got = step_scrs[order].at[item % step_scrs[order].shape[0]]
        full = (slice(None),) * (len(kept.shape) - 3)
        if order:
            kept = kept.at[full + (my_bit(*seq_bits[order]),)]
            full = full[1:]
        if order + 1 < len(seq_bits):
            add_into(kept, got)
            step = seq_bits[order + 1]
            target = step_scrs[order + 1]
            copy = copies.send(
                kept.at[full + (1 - my_bit(*step),)],
                target.at[item % target.shape[0]],
                mask_of(step),
            )
            flying[item] = copy, kept
            flying["later", item].append(copy)
        else:
            add_into(kept, got)
            flying["out", item] = copies.move(kept, spread_ref.at[item])

    def partial(item):
        core = my_bit(*seq_bits[0])
        slot = item % 2
        if item >= 1:
            copies.sent_now(flying["first", item - 1])
        kept_slot = item % len(seq_bits)
        if item >= len(seq_bits):
            for copy in flying["later", item - len(seq_bits)]:
                copies.sent_now(copy)
            flying.pop(("out", item - len(seq_bits))).wait()
        half = mixed_scr.shape[0] * mixed_scr.shape[2]
        other = mixed_scr[:, 1 - core].reshape(half, -1)
        mine = mixed_scr[:, core].reshape(half, -1)

        @pl.loop(0, width // tile)
        def _(order):
            place = pl.ds(pl.multiple_of(order * tile, tile), tile)
            weights = slice_ref[place, :]
            target = other_scr
            target[..., place] = contract_cols(other, weights).astype(bf16).reshape(
                target.shape[:-1] + (tile,)
            )
            target = kept_scr.at[kept_slot]
            target[..., place] = contract_cols(mine, weights).astype(bf16).reshape(
                target.shape[:-1] + (tile,)
            )

        copy = copies.send(other_scr, step_scrs[0].at[slot], mask_of(seq_bits[0]))
        flying[item] = copy, kept_scr.at[kept_slot]
        flying["first", item] = copy
        flying["later", item] = []

    def bias_step():
        done = len(bias_copies)
        bias_copies[-1].wait_recv()
        bias_scr[done] = bias_scr[done - 1] + bias_got[done - 1]
        if done < len(bias_steps):
            bias_copies.append(
                copies.send(bias_scr.at[done], bias_got.at[done], mask_of(bias_steps[done]))
            )
        else:
            bias_sum_ref[...] = bias_scr[done]

    products(0, 0)
    for part in dense_sums:
        part.start()
    send_grads(1)
    attention(0)
    partial(0)
    products(0, 2)
    send_grads(2)
    bias_step()
    step_on(0, 0)
    attention(1)
    partial(1)
    products(1, 0)
    send_grads(3)
    step_on(1, 0)
    bias_step()
    step_on(0, 1)
    products(1, 2)
    absorb(1, 0)
    dense_advance()
    attention(2)
    partial(2)
    products(2, 0)
    step_on(2, 0)
    step_on(1, 1)
    bias_step()
    products(2, 2)
    dense_advance()
    absorb(1, 1)
    attention(3)
    absorb(2, 0)
    step_on(0, 2)
    partial(3)
    sums_copy = copies.send(sums_scr.at[0], sums_got.at[0], mask_of(item_bits[0]))
    step_on(2, 1)
    dense_advance()
    step_on(3, 0)
    absorb(1, 2)
    next_sum(0)
    bias_step()
    step_on(1, 2)
    absorb(2, 1)
    dense_advance()
    step_on(3, 1)
    next_sum(1)
    bias_step()
    sums_all_ref[seq_place] = sums_scr[len(item_bits)].astype(bf16)
    spread_sums()
    absorb(2, 2)
    absorb(3, 0)
    to_members(0)
    step_on(2, 2)
    spread_sums()
    absorb(3, 1)
    to_members(1)
    step_on(3, 2)
    spread_sums()
    absorb(3, 2)
    to_members(2)
    for order, part in enumerate(dense_sums):
        dense_part_ref[pl.ds(order * dense_half, dense_half)] = part.kept[...]
    wait_all(arrivals)
    wait_all(shares)
    for item in range(items_here):
        if ("out", item) in flying:
            flying["out", item].wait()
    for copy in local:
        copy.wait()
    copies.end()


def merged_call(
    item_bits,
    seq_bits,
    visible,
    onehots,
    tables,
    cosine,
    sine_part,
    log_sums,
    w_slice,
    grad_context,
    shared,
    grad_in,
    grad_shared,
    product,
    by_rows,
    in_sum,
):
    items_here, length, vocab = onehots.shape
    heads_here = tables.shape[0]
    seq_size = 2 ** len(seq_bits)
    span = length // seq_size
    width = w_slice.shape[0]
    packed = heads_here * 3 * HEAD
    any_space = pl.BlockSpec(memory_space=pl.ANY)
    near_space = pl.BlockSpec(memory_space=pltpu.VMEM)
    ff_part = product.shape[1]
    group_rows = width * 4 // 2 ** (len(item_bits) + len(seq_bits))
    rows = group_rows // 4
    dense_depth = len(item_bits) + len(seq_bits) - 1
    spread = (2,) * (len(seq_bits) - 1) + (span, width)
    all_bits = len(item_bits) + len(seq_bits)
    spare = (8 + seq_size) * items_here + 64 + 16 * all_bits
    half = (group_rows // 2, ff_part)
    return pl.pallas_call(
        functools.partial(merged_kernel, item_bits, seq_bits),
        in_specs=[pl.BlockSpec(memory_space=pltpu.SMEM)]
        + [near_space] * 6
        + [any_space] * 6
        + [near_space],
        out_specs=[any_space, near_space, any_space, near_space, near_space] + [any_space] * 3,
        out_shape=[
            jax.ShapeDtypeStruct((items_here, span, width), bf16),
            jax.ShapeDtypeStruct((seq_size, heads_here, vocab, 3 * HEAD), bf16),
            jax.ShapeDtypeStruct((3, 4, rows, ff_part), bf16),
            jax.ShapeDtypeStruct(by_rows.shape[-2:], bf16),
            jax.ShapeDtypeStruct(in_sum.shape, f32),
            jax.ShapeDtypeStruct((3, 2, 4) + half, bf16),
            jax.ShapeDtypeStruct((3, 2, 2) + half, bf16),
            jax.ShapeDtypeStruct((3, 2, 1) + half, bf16),
        ],
        scratch_shapes=[
            pltpu.VMEM((seq_size // 2, 2, span, packed), bf16),
            pltpu.VMEM(spread, bf16),
            pltpu.VMEM((len(seq_bits),) + spread, bf16),
            tuple(
                pltpu.VMEM((2 if order == 0 else items_here,) + spread[order:], bf16)
                for order in range(len(seq_bits))
            ),
            pltpu.VMEM((len(item_bits) + 1, heads_here, vocab, 3 * HEAD), f32),
            pltpu.VMEM((len(item_bits), heads_here, vocab, 3 * HEAD), f32),
            pltpu.VMEM((all_bits + 1,) + in_sum.shape, f32),
            pltpu.VMEM((all_bits,) + in_sum.shape, f32),
            tuple(
                tuple(
                    pltpu.VMEM((2,) * order + (by_rows.shape[-2] // 2, by_rows.shape[-1]), bf16)
                    for order in range(dense_depth - 1, -1, -1)
                )
                for _ in range(2)
            ),
            pltpu.VMEM((product.shape[0], ff_part), bf16),
            pltpu.VMEM((2, product.shape[0], group_rows), bf16),
            pltpu.VMEM((2 * group_rows, product.shape[0]), bf16),
            pltpu.VMEM((2, 4) + half, bf16),
            pltpu.VMEM((3, 2, 4) + half, bf16),
            pltpu.VMEM((2,) + half, bf16),
            pltpu.VMEM((2,) + by_rows.shape[-2:], bf16),
            pltpu.VMEM((items_here, length, heads_here * HEAD), bf16),
            pltpu.SemaphoreType.DMA((2,)),
            pltpu.SemaphoreType.DMA((3,)),
            pltpu.SemaphoreType.DMA((spare,)),
            pltpu.SemaphoreType.DMA((spare,)),
            pltpu.SemaphoreType.DMA((16,)),
        ],
        compiler_params=pltpu.CompilerParams(
            collective_id=4, has_side_effects=True, vmem_limit_bytes=62 * 2**20
        ),
        name="merged",
    )(
        visible,
        onehots,
        tables,
        cosine,
        sine_part,
        log_sums,
        w_slice,
        grad_context,
        shared,
        grad_in,
        grad_shared,
        product,
        by_rows,
        in_sum,
    )


def weave_kernel(ff_width, members, padded_ref, woven_ref):
    rows = padded_ref.shape[0]
    tiles = woven_ref.shape[2] // 256
    base, shift = ff_width // 128, ff_width % 128
    lane = lax.broadcasted_iota(jnp.int32, (rows, 128), 1)
    last = padded_ref.shape[1] // 128 - 1

    def turned(tile):
        part = padded_ref[:, tile * 128 : (tile + 1) * 128].astype(f32)
        return pltpu.roll(part, (128 - shift) % 128, 1)

    before = turned(base)
    for order in range(members * tiles):
        left = ff_width - order * 128
        if left <= 0:
            up_part = gate = jnp.zeros((rows, 128), bf16)
        else:
            up_part = padded_ref[:, order * 128 : (order + 1) * 128].astype(f32)
            after = turned(min(base + order + 1, last))
            gate = jnp.where(lane < 128 - shift, before, after)
            before = after
            if left < 128:
                up_part = jnp.where(lane < left, up_part, 0.0)
                gate = jnp.where(lane < left, gate, 0.0)
            up_part, gate = up_part.astype(bf16), gate.astype(bf16)
        member, tile = order // tiles, order % tiles
        woven_ref[member, :, tile * 256 : tile * 256 + 128] = up_part
        woven_ref[member, :, tile * 256 + 128 : (tile + 1) * 256] = gate


def weave(up_weight, ff_width, members, ff_part):
    rows, columns = up_weight.shape
    wide = -(-columns // 128) * 128
    padded = jnp.pad(up_weight, ((0, 0), (0, wide - columns)))
    return pl.pallas_call(
        functools.partial(weave_kernel, ff_width, members),
        in_specs=[pl.BlockSpec(memory_space=pltpu.VMEM)],
        out_specs=pl.BlockSpec(memory_space=pltpu.VMEM),
        out_shape=jax.ShapeDtypeStruct((members, rows, 2 * ff_part), bf16),
        compiler_params=pltpu.CompilerParams(vmem_limit_bytes=24 * 2**20),
        name="weave",
    )(padded)


def unweave_kernel(ff_width, woven_ref, whole_ref):
    members, rows, columns = woven_ref.shape
    tiles = columns // 256
    base, shift = ff_width // 128, ff_width % 128
    lane = lax.broadcasted_iota(jnp.int32, (rows, 128), 1)

    def part(order, which):
        first = order % tiles * 256 + which * 128
        return woven_ref[order // tiles, :, first : first + 128].astype(f32)

    for order in range(base):
        whole_ref[:, order * 128 : (order + 1) * 128] = part(order, 0)
    before = part(base, 0)
    width = whole_ref.shape[1]
    for order in range(base, -(-width // 128)):
        if order - base < members * tiles:
            after = pltpu.roll(part(order - base, 1), shift, 1)
        first = order * 128
        count = min(128, width - first)
        whole_ref[:, first : first + count] = jnp.where(lane < shift, before, after)[:, :count]
        before = after


def unweave(woven, ff_width):
    rows = woven.shape[1]
    return pl.pallas_call(
        functools.partial(unweave_kernel, ff_width),
        in_specs=[pl.BlockSpec(memory_space=pltpu.VMEM)],
        out_specs=pl.BlockSpec(memory_space=pltpu.VMEM),
        out_shape=jax.ShapeDtypeStruct((rows, 2 * ff_width), f32),
        compiler_params=pltpu.CompilerParams(vmem_limit_bytes=24 * 2**20),
        name="unweave",
    )(woven)


def dense_back_kernel(rows_here, core_ref, context_ref, grad_ref, dense_ref, back_ref, mine_ref, other_ref):
    core = core_ref[0]
    back_ref[...] = contract_cols(grad_ref[...], dense_ref[...]).astype(bf16)
    products = contract_rows(context_ref[...], grad_ref[...]).astype(bf16)
    for order in range(products.shape[0] // (2 * rows_here)):
        first, second = (
            products[start : start + rows_here]
            for start in (2 * order * rows_here, (2 * order + 1) * rows_here)
        )
        rows = slice(order * rows_here, (order + 1) * rows_here)
        mine_ref[rows, :] = jnp.where(core == 0, first, second)
        other_ref[rows, :] = jnp.where(core == 0, second, first)


def dense_back(core, context, grad_branch, w_dense, rows_here):
    rows, width = context.shape
    tile = 256
    grid_spec = pltpu.PrefetchScalarGridSpec(
        num_scalar_prefetch=1,
        grid=(width // tile,),
        in_specs=[
            pl.BlockSpec((rows, tile), lambda i, c: (0, i)),
            pl.BlockSpec((rows, width), lambda i, c: (0, 0)),
            pl.BlockSpec((tile, width), lambda i, c: (i, 0)),
        ],
        out_specs=[
            pl.BlockSpec((rows, tile), lambda i, c: (0, i)),
            pl.BlockSpec((tile // 2, width), lambda i, c: (i, 0)),
            pl.BlockSpec((tile // 2, width), lambda i, c: (i, 0)),
        ],
    )
    return pl.pallas_call(
        functools.partial(dense_back_kernel, rows_here),
        grid_spec=grid_spec,
        out_shape=[
            jax.ShapeDtypeStruct((rows, width), bf16),
            jax.ShapeDtypeStruct((width // 2, width), bf16),
            jax.ShapeDtypeStruct((width // 2, width), bf16),
        ],
        compiler_params=pltpu.CompilerParams(vmem_limit_bytes=32 * 2**20),
        cost_estimate=pl.CostEstimate(
            flops=4 * rows * width * width, bytes_accessed=6 * width * width, transcendentals=0
        ),
        name="dense_back",
    )(core, context, grad_branch, w_dense)


def ff_kernel(
    item_bits,
    shared_ref,
    normed_ref,
    inverse_ref,
    cotangent_ref,
    in_ref,
    out_ref,
    vector_ref,
    bias_ref,
    block_ref,
    product_ref,
    saved_ref,
    grad_shared_ref,
    grad_in_ref,
    layer_ref,
    resid_ref,
    sums_ref,
    in_sum_ref,
    slices_ref,
    branch_ref,
    rows_scr,
    product_scr,
    save_scr,
    parts_scr,
    near_got,
    far_got,
    low_scr,
    grad_in_scr,
    resid_scr,
    normed_scr,
    gate_scr,
    send_sems,
    recv_sems,
    load_sems,
    keep_sems,
):
    chunks, blocks, span, width = shared_ref.shape
    group_rows = blocks * span
    tiles = product_scr.shape[-1] // 128
    tile = 256
    near, far = ("seq", 1), ("seq", 2)
    greet([mask_of(near), mask_of(far)] + [mask_of(step) for step in item_bits])
    copies = Copies(send_sems, recv_sems, keep_sems)
    item_place = copies.here[0]
    slices = copies.move(block_ref, slices_ref.at[item_place])
    slices.wait()
    spread = []

    def spread_block():
        order = len(spread)
        if order < len(item_bits):
            wait_all(spread[-1:])
            part = slices_ref.at[aligned(item_place, 2**order)]
            spread.append(copies.send(part, part, mask_of(item_bits[order])))

    spread_block()
    keeps, loads = {}, {}
    state = {}
    gain_one, shift_one, b_down, gain_two, shift_two = range(5)
    for line in range(sums_ref.shape[0]):
        sums_ref[line : line + 1, :] = jnp.zeros((1, width), f32)
    in_sum_ref[...] = jnp.zeros_like(in_sum_ref)

    def load(name, slot, source, target):
        copy = pltpu.make_async_copy(source, target, load_sems.at[slot])
        copy.start()
        loads[name] = copy

    def loaded(name):
        loads.pop(name).wait()

    def keep(name, slot, source, target):
        copy = pltpu.make_async_copy(source, target, keep_sems.at[1 + slot])
        copy.start()
        keeps[name] = copy

    def keep_done(name):
        if name in keeps:
            keeps.pop(name).wait()

    def load_shared(chunk):
        slot = chunk % 2
        load(("rows", slot), slot, shared_ref.at[chunk], rows_scr.at[slot])

    def load_normed(chunk):
        slot = chunk % 2
        rows = pl.ds(chunk * span, span)
        load(("normed", slot), 2 + slot, normed_ref.at[rows], normed_scr.at[slot])

    def forward_gate(chunk):
        slot = chunk % 2
        loaded(("rows", slot))
        if chunk + 1 < chunks:
            load_shared(chunk + 1)
        keep_done(("product", slot))
        keep_done(("save", slot))
        rows = rows_scr.at[slot]

        def multiply(order, place):
            columns = pl.ds(pl.multiple_of(order * tile, tile), tile)
            gate_scr[place] = (
                dot(rows[...].reshape(group_rows, width), in_ref[:, columns])
                + bias_ref[:, columns]
            )

        def finish(order, place):
            gate_up = gate_scr[place]
            up_part, gate = gate_up[:, :128], gate_up[:, 128:]
            below = 0.5 * (1.0 + lax.erf(gate * (0.5**0.5)))
            activated = gate * below
            slope = below + gate * jnp.exp(-0.5 * gate * gate) * (1.0 / math.sqrt(2.0 * math.pi))
            columns = pl.ds(pl.multiple_of(order * 128, 128), 128)
            product_scr[slot, :, columns] = (up_part * activated).astype(bf16)
            save_scr[slot, 0, :, columns] = activated.astype(bf16)
            save_scr[slot, 1, :, columns] = (up_part * slope).astype(bf16)

        multiply(0, 0)

        @pl.loop(0, (tiles - 1) // 2)
        def _(pair):
            finish(2 * pair, 0)
            multiply(2 * pair + 1, 1)
            finish(2 * pair + 1, 1)
            multiply(2 * pair + 2, 0)

        if tiles % 2 == 0:
            multiply(tiles - 1, 1)
            finish(tiles - 2, 0)
            finish(tiles - 1, 1)
        else:
            finish(tiles - 1, 0)
        keep(("product", slot), slot, product_scr.at[slot], product_ref.at[chunk])
        keep(("save", slot), 2 + slot, save_scr.at[slot], saved_ref.at[chunk])

    def send_near(name, slot):
        source = parts_scr.at[slot, pl.ds(2, 2)]
        state["near", name] = copies.send(source, near_got.at[slot], mask_of(near))

    def free_parts(slot):
        for key in ("near", "far"):
            copy = state.pop((key, "of", slot), None)
            if copy is not None:
                copies.sent_now(copy)

    def times_turned(name, slot, left, weights_ref):
        free_parts(slot)

        @pl.loop(0, width // tile)
        def _(order):
            place = pl.ds(pl.multiple_of(order * tile, tile), tile)
            total = contract_cols(left[...], weights_ref[place, :])
            parts_scr[slot, :, :, place] = total.astype(bf16).reshape(blocks, span, tile)

        send_near(name, slot)
        state["near", "of", slot] = state["near", name]

    def forward_out(chunk):
        times_turned(chunk, chunk % 2, product_scr.at[chunk % 2], out_ref)

    def sum_near(name, chunk):
        slot = chunk % 2
        state["near", name].wait_recv()
        add_into(parts_scr.at[slot, pl.ds(0, 2)], near_got.at[slot])
        copy = copies.send(parts_scr.at[slot, 1], far_got.at[chunk], mask_of(far))
        state["far", name] = copy
        state["far", "of", slot] = copy

    block = 32

    def row_blocks(function):
        @pl.loop(0, span // block)
        def _(order):
            function(pl.ds(pl.multiple_of(order * block, block), block))

    def line(index):
        return vector_ref[index : index + 1, :]

    def add_sum(index, rows):
        sums_ref[index : index + 1, :] += jnp.sum(rows, axis=0, keepdims=True)

    def second_norm(chunk):
        slot = chunk % 2
        state["far", chunk].wait_recv()
        loaded(("normed", slot))
        for key in ("low near", "low far"):
            copy = state.pop((key, slot), None)
            if copy is not None:
                copies.sent_now(copy)
        keep_done(("low", slot))

        def body(rows):
            hidden = normed_scr[slot, rows] * line(gain_one) + line(shift_one)
            mlp_branch = parts_scr[slot, 0, rows].astype(f32) + far_got[chunk, rows].astype(f32)
            normed, inverse = norm_rows(deep_alpha * hidden + mlp_branch + line(b_down))
            layer_ref[chunk, rows] = (normed * line(gain_two) + line(shift_two)).astype(bf16)
            grad = cotangent_ref[chunk, rows].astype(f32)
            resid = norm_rows_back(grad, normed, inverse, line(gain_two))
            low = resid.astype(bf16)
            resid_scr[chunk, rows] = resid
            low_scr[slot, rows] = low
            add_sum(3, grad * normed)
            add_sum(4, grad)
            add_sum(5, low.astype(f32))

        row_blocks(body)
        if chunk + 2 < chunks:
            load_normed(chunk + 2)
        source = low_scr.at[slot]
        keep(("low", slot), 4 + slot, source, grad_shared_ref.at[chunk, 0])
        state["low far", slot] = copies.send(source, grad_shared_ref.at[chunk, 1], mask_of(far))
        state["low near", slot] = copies.send(source, grad_shared_ref.at[chunk, 2], mask_of(near))
        state["grad far", chunk] = state["low far", slot]
        state["grad near", chunk] = state["low near", slot]

    def pass_on(chunk):
        state["grad far", chunk].wait_recv()
        part = grad_shared_ref.at[chunk, 1]
        state["grad cross", chunk] = copies.send(
            part, grad_shared_ref.at[chunk, 3], mask_of(near)
        )

    def load_grads(chunk):
        slot = chunk % 2
        keep_done(("low", slot))
        state["grad near", chunk].wait_recv()
        state["grad cross", chunk].wait_recv()
        load(("rows", slot), slot, grad_shared_ref.at[chunk], rows_scr.at[slot])
        keep_done(("save", slot))
        load(("save", slot), 4 + slot, saved_ref.at[chunk], save_scr.at[slot])

    def backward_gate(chunk):
        slot = chunk % 2
        loaded(("rows", slot))
        loaded(("save", slot))
        keep_done("grad in")
        rows = rows_scr.at[slot]

        def columns_of(first, count):
            columns = pl.ds(pl.multiple_of(first * 128, 128), count * 128)
            grad = dot(rows[...].reshape(group_rows, width), out_ref[:, columns])
            for order in range(count):
                part = grad[:, order * 128 : (order + 1) * 128]
                saved = pl.ds(pl.multiple_of((first + order) * 128, 128), 128)
                for which in range(2):
                    low = (part * save_scr[slot, which, :, saved].astype(f32)).astype(bf16)
                    place = pl.ds(
                        pl.multiple_of((2 * (first + order) + which) * 128, 128), 128
                    )
                    grad_in_scr[:, place] = low
                    in_sum_ref[:, place] += jnp.sum(low.astype(f32), axis=0, keepdims=True)

        @pl.loop(0, tiles // 2)
        def _(pair):
            columns_of(2 * pair, 2)

        if tiles % 2:
            columns_of(tiles - 1, 1)
        keep("grad in", 6, grad_in_scr, grad_in_ref.at[chunk])

    def backward_in(chunk):
        times_turned(("back", chunk), chunk % 2, grad_in_scr, in_ref)

    def first_norm(chunk):
        slot = chunk % 2
        state["far", ("back", chunk)].wait_recv()
        loaded(("normed", slot))
        for key in ("low near", "low far"):
            copy = state.pop((key, slot), None)
            if copy is not None:
                copies.sent_now(copy)
        keep_done(("branch", slot))

        def body(rows):
            grad = parts_scr[slot, 0, rows].astype(f32) + far_got[chunk, rows].astype(f32)
            grad = grad + deep_alpha * resid_scr[chunk, rows]
            normed = normed_scr[slot, rows]
            place = pl.ds(pl.multiple_of(chunk * span + rows.start, block), block)
            resid = norm_rows_back(grad, normed, inverse_ref[place, 0:1], line(gain_one))
            resid_scr[chunk, rows] = resid
            add_sum(0, grad * normed)
            add_sum(1, grad)
            low = resid.astype(bf16)
            low_scr[slot, rows] = low
            add_sum(2, low.astype(f32))

        row_blocks(body)
        if chunk + 2 < chunks:
            load_normed(chunk + 2)
        keep(("resid", chunk), 7 + chunk, resid_scr.at[chunk], resid_ref.at[chunk])
        keep(("branch", slot), 7 + chunks + slot, low_scr.at[slot], branch_ref.at[chunk])

    load_shared(0)
    load_normed(0)
    load_normed(1)
    last = chunks - 1
    for chunk in range(chunks):
        forward_gate(chunk)
        if chunk >= 1:
            sum_near(chunk - 1, chunk - 1)
        if chunk >= 2:
            second_norm(chunk - 2)
        if chunk >= 3:
            pass_on(chunk - 3)
        forward_out(chunk)
    sum_near(last, last)
    second_norm(last - 1)
    pass_on(last - 2)
    load_grads(0)
    for chunk in range(chunks):
        backward_gate(chunk)
        if chunk >= 2:
            first_norm(chunk - 2)
        backward_in(chunk)
        spread_block()
        if chunk == 0:
            second_norm(last)
            load_normed(0)
            load_normed(1)
        elif chunk + 1 < chunks:
            pass_on(chunk + 1)
        if chunk + 1 < chunks:
            load_grads(chunk + 1)
            sum_near(("back", chunk), chunk)
    sum_near(("back", last), last)
    first_norm(last - 1)
    first_norm(last)
    wait_all(spread[-1:])
    for name in list(keeps):
        keep_done(name)
    copies.end()


def ff_call(
    item_bits, shared, normed, inverse, cotangent, w_in, w_out, vectors, in_bias, block
):
    chunks, blocks, span, width = shared.shape
    group_rows = blocks * span
    ff_part = w_out.shape[1]
    any_space = pl.BlockSpec(memory_space=pl.ANY)
    near_space = pl.BlockSpec(memory_space=pltpu.VMEM)
    spare = 8 * chunks
    return pl.pallas_call(
        functools.partial(ff_kernel, item_bits),
        in_specs=[any_space, any_space] + [near_space] * 6 + [any_space],
        out_specs=[any_space] * 4 + [near_space, any_space, near_space, near_space, any_space, any_space],
        out_shape=[
            jax.ShapeDtypeStruct((chunks, group_rows, ff_part), bf16),
            jax.ShapeDtypeStruct((chunks, 2, group_rows, ff_part), bf16),
            jax.ShapeDtypeStruct((chunks, blocks, span, width), bf16),
            jax.ShapeDtypeStruct((chunks, group_rows, 2 * ff_part), bf16),
            jax.ShapeDtypeStruct((chunks, span, width), bf16),
            jax.ShapeDtypeStruct((chunks, span, width), f32),
            jax.ShapeDtypeStruct((8, width), f32),
            jax.ShapeDtypeStruct((1, 2 * ff_part), f32),
            jax.ShapeDtypeStruct((2 ** len(item_bits),) + block.shape, bf16),
            jax.ShapeDtypeStruct((chunks, span, width), bf16),
        ],
        scratch_shapes=[
            pltpu.VMEM((2, blocks, span, width), bf16),
            pltpu.VMEM((2, group_rows, ff_part), bf16),
            pltpu.VMEM((2, 2, group_rows, ff_part), bf16),
            pltpu.VMEM((2, blocks, span, width), bf16),
            pltpu.VMEM((2, 2, span, width), bf16),
            pltpu.VMEM((chunks, span, width), bf16),
            pltpu.VMEM((2, span, width), bf16),
            pltpu.VMEM((group_rows, 2 * ff_part), bf16),
            pltpu.VMEM((chunks, span, width), f32),
            pltpu.VMEM((2, span, width), f32),
            pltpu.VMEM((2, group_rows, 256), f32),
            pltpu.SemaphoreType.DMA((spare,)),
            pltpu.SemaphoreType.DMA((spare,)),
            pltpu.SemaphoreType.DMA((6,)),
            pltpu.SemaphoreType.DMA((10 + chunks,)),
        ],
        compiler_params=pltpu.CompilerParams(
            collective_id=3, has_side_effects=True, vmem_limit_bytes=60 * 2**20
        ),
        name="feed_forward",
    )(shared, normed, inverse, cotangent, w_in, w_out, vectors, in_bias, block)


def on_device(
    token_ids,
    masked,
    item_flag,
    prefix,
    cotangent,
    embedding,
    heads_weight,
    heads_bias,
    dense_weight,
    dense_bias,
    first_gain,
    first_bias,
    up_weight,
    up_bias,
    down_weight,
    down_bias,
    second_gain,
    second_bias,
):
    lines = Lines()
    items_here, span = token_ids.shape
    items_size, seq_size = lax.axis_size("items"), lax.axis_size("seq")
    item_place, seq_place = lax.axis_index("items"), lax.axis_index("seq")
    count = items_size * seq_size
    length = span * seq_size
    width = embedding.shape[0] * count
    vocab = embedding.shape[1]
    heads_here = HEADS // seq_size
    packed_width = heads_here * 3 * HEAD
    rows_here = up_weight.shape[0]
    ff_width = down_weight.shape[0]
    members = 4
    groups = count // members
    member = seq_place % members
    ff_part = -(-ff_width // (members * 128)) * 128
    ff_all = members * ff_part

    item_bits, seq_bits = bits_of("items"), bits_of("seq")
    outer_bits = seq_bits[2:]

    input_ids = jnp.where(masked == 1, mask_token, token_ids)
    flat_place = item_place * seq_size + seq_place
    row_count = rows_here + 16
    bias_row = lax.dynamic_update_slice(
        jnp.zeros((16, heads_weight.shape[1]), bf16),
        heads_bias[None],
        (0, flat_place * heads_bias.shape[0]),
    )
    ones_row = jnp.zeros((16, vocab), bf16).at[0].set(1.0)
    def rows_of(part):
        part = part.reshape(-1)
        return jnp.pad(part, (0, -part.shape[0] % 128)).reshape(-1, 128)

    small = [
        embedding,
        ones_row,
        rows_of(input_ids.astype(bf16)),
        rows_of(
            jnp.concatenate(
                [dense_bias, first_gain, first_bias, down_bias, second_gain, second_bias]
            )
        ),
    ]
    ends = [0]
    for part in small:
        ends.append(ends[-1] + part.shape[0])
    small.append(jnp.zeros((-ends[-1] % 16, 128), bf16))
    flat = jnp.concatenate(small, axis=0)

    def by_member(part):
        padded = jnp.pad(part, ((0, 0), (0, ff_all - ff_width)))
        return jnp.transpose(padded.reshape(rows_here, 2, 2, ff_part), (1, 2, 0, 3))

    tiles = ff_part // 128

    def woven(up, gate):
        shape = up.shape[:-1] + (tiles, 128)
        return jnp.stack([up.reshape(shape), gate.reshape(shape)], axis=-2).reshape(
            up.shape[:-1] + (2 * ff_part,)
        )

    def unwoven(both_parts):
        parts = both_parts.reshape(both_parts.shape[:-1] + (tiles, 2, 128))
        shape = both_parts.shape[:-1] + (ff_part,)
        return parts[..., 0, :].reshape(shape), parts[..., 1, :].reshape(shape)

    parts_in = weave(up_weight, ff_width, members, ff_part).reshape(
        2, 2, rows_here, 2 * ff_part
    )
    parts_out = by_member(down_weight.T)
    everyone, mixed_table, w_block, w_dense, own_in, own_out = first_call(
        item_bits,
        seq_bits,
        flat,
        heads_weight,
        bias_row,
        dense_weight,
        parts_in,
        parts_out,
    )
    w_dense = w_dense.reshape(width, width)
    w_block = w_block[:, :rows_here].reshape(seq_size * rows_here, packed_width)
    pieces = [everyone[:, :, a:b] for a, b in zip(ends[:-1], ends[1:])]
    table = pieces[0].reshape(width, vocab)
    vector_rows = pieces[3].reshape(count, -1)[:, : 6 * rows_here].reshape(count, 6, rows_here)
    vectors = jnp.transpose(vector_rows, (1, 0, 2)).reshape(6, width).astype(f32)
    ids_here = pick(pieces[2], item_place, 0).reshape(seq_size, items_here, span)
    ids_here = jnp.transpose(ids_here, (1, 0, 2)).reshape(items_here, length).astype(jnp.int32)
    in_bias = jnp.pad(
        up_bias.astype(f32).reshape(2, ff_width), ((0, 0), (0, ff_all - ff_width))
    )
    in_bias = lax.dynamic_slice(in_bias, (0, member * ff_part), (2, ff_part))
    in_bias = woven(in_bias[:1], in_bias[1:])

    vocab_index = jnp.arange(vocab, dtype=jnp.int32)
    frequency = np.exp(np.arange(HEAD // 2) * (-2.0 * math.log(10000.0) / HEAD))
    angles = np.arange(length)[:, None] * frequency[None, :]
    cosine, sine_part = np.cos(angles), np.sin(angles)
    cosine = jnp.asarray(np.concatenate([cosine, cosine], axis=1), f32)
    sine_part = jnp.asarray(np.concatenate([-sine_part, sine_part], axis=1), f32)
    visible = jnp.where(item_flag == 1, length, prefix)
    tables = table_halves(mixed_table)
    onehots = (ids_here[:, :, None] == vocab_index).astype(bf16)
    own_onehot = (input_ids.reshape(-1)[:, None] == vocab_index[None, :]).astype(bf16)
    vectors = jnp.concatenate([vectors[1:], vectors[:1], jnp.zeros((2, width), f32)], axis=0)
    context, log_sums, w_in, w_out, shared, normed, inverse = second_call(
        item_bits,
        seq_bits,
        visible,
        onehots,
        tables,
        cosine,
        sine_part,
        own_onehot,
        table,
        vectors,
        w_dense,
        own_in,
        own_out,
    )
    (
        product,
        _,
        grad_shared,
        grad_in,
        layer_out,
        grad_resid,
        sums,
        in_sum,
        w_slice,
        grad_branch,
    ) = ff_call(
        item_bits,
        shared,
        normed,
        inverse,
        cotangent,
        w_in.reshape(width, 2 * ff_part),
        w_out.reshape(width, ff_part),
        vectors,
        in_bias,
        w_block,
    )
    rows_all = items_here * span
    group_all = members * rows_all
    context = context.reshape(rows_all, width)
    grad_branch = grad_branch.reshape(rows_all, width)
    core = my_bit(*seq_bits[0])
    grad_context, dense_mine, dense_other = dense_back(
        core.astype(jnp.int32).reshape(1), context, grad_branch, w_dense, rows_here
    )
    def core_sum(whole):
        parts = whole.reshape(count // 2, 2, rows_here, -1)
        got = lines.swap(pick(parts, 1 - core, 1), *seq_bits[0])
        return (pick(parts, core, 1).astype(f32) + got.astype(f32)).astype(bf16)

    small_sums = jnp.concatenate(
        [
            contract_rows(grad_branch, own_onehot).astype(bf16),
            contract_rows(sums.astype(bf16), jnp.eye(8, 128, dtype=bf16)).astype(bf16),
        ],
        axis=1,
    )
    by_rows = jnp.concatenate(
        [
            (
                dense_mine.astype(f32)
                + lines.swap(dense_other, *seq_bits[0]).astype(f32)
            ).astype(bf16),
            core_sum(small_sums).reshape(width // 2, 256),
        ],
        axis=-1,
    )
    row_dims = item_bits[::-1] + seq_bits[:0:-1]
    by_rows = by_rows.reshape((2,) * len(row_dims) + (rows_here, -1))
    in_sum = jnp.concatenate(unwoven(in_sum), axis=0)
    in_all = lax.dynamic_update_slice(
        jnp.zeros((2, ff_all), f32), in_sum, (0, member * ff_part)
    ).reshape(-1, 128)
    w_slice = w_slice.reshape(width, packed_width)
    attention = (
        item_bits,
        seq_bits,
        visible,
        onehots,
        tables,
        cosine,
        sine_part,
        log_sums,
        w_slice,
    )
    shared = shared.reshape(group_all, width)
    grad_in = grad_in.reshape(group_all, 2 * ff_part)
    grad_shared = grad_shared.reshape(group_all, width)
    product = product.reshape(group_all, ff_part)
    if len(item_bits) == 2 and len(seq_bits) == 3 and rows_here % 32 == 0:
        spread, token_all, parts, by_rows, in_all = merged_call(
            *attention,
            grad_context.reshape(items_here, span, width),
            shared,
            grad_in,
            grad_shared,
            product,
            by_rows,
            in_all,
        )[:5]
        in_part = jnp.concatenate([parts[1], parts[2]], axis=-1)
        out_part = parts[0]
    else:
        by_head = lax.all_to_all(
            jnp.transpose(
                grad_context.reshape(items_here, span, seq_size, heads_here * HEAD), (0, 2, 1, 3)
            ),
            "seq",
            split_axis=1,
            concat_axis=1,
            tiled=True,
        ).reshape(items_here, length, heads_here * HEAD)
        group_dims = (2,) * (len(item_bits) + len(outer_bits)) + (members * rows_here, -1)
        spread, token_all, in_part, out_part, by_rows, in_all = third_call(
            *attention,
            by_head,
            contract_rows(shared, grad_in).astype(bf16).reshape(group_dims),
            contract_rows(grad_shared, product).astype(bf16).reshape(group_dims),
            by_rows,
            in_all,
        )
    input_grads = spread.astype(f32) + deep_alpha * grad_resid.reshape(spread.shape)
    token_all = jnp.transpose(token_all, (2, 0, 1, 3)).reshape(vocab, -1)

    def from_members(part):
        taken = jnp.transpose(part, (1, 0, 2)).reshape(rows_here, ff_all)
        return taken[:, :ff_width].astype(f32)

    grad_up_weight = unweave(in_part, ff_width)
    grad_down = from_members(out_part)
    by_rows = by_rows.astype(f32)
    grad_dense = by_rows[:, :width]
    token_sum = by_rows[:, width : width + vocab]
    own_vectors = by_rows[:, width + vocab :].T
    in_all = in_all.reshape(2, ff_all)
    grad_up_bias = in_all[:, :ff_width].reshape(-1)

    grad_heads = dot(embedding, token_all)
    grad_heads_bias = lax.dynamic_slice_in_dim(
        jnp.sum(token_all.astype(f32), axis=0),
        (item_place * seq_size + seq_place) * heads_bias.shape[0],
        heads_bias.shape[0],
        0,
    )
    embed_grad = 0.1 * (contract_cols(heads_weight, token_all) + deep_alpha * token_sum)
    return (
        layer_out,
        input_grads,
        embed_grad,
        grad_heads,
        grad_heads_bias,
        grad_dense,
        own_vectors[2],
        own_vectors[0],
        own_vectors[1],
        grad_up_weight,
        grad_up_bias,
        grad_down.T,
        own_vectors[5],
        own_vectors[3],
        own_vectors[4],
    )


def solution(mesh):
    in_specs = (
        P("items", "seq"),
        P("items", "seq"),
        P("items"),
        P("items"),
        P("items", "seq", None),
        P(("items", "seq"), None),
        P(("items", "seq"), None),
        P(("items", "seq")),
        P(("items", "seq"), None),
        P(("items", "seq")),
        P(("items", "seq")),
        P(("items", "seq")),
        P(("items", "seq"), None),
        P(),
        P(None, ("items", "seq")),
        P(("items", "seq")),
        P(("items", "seq")),
        P(("items", "seq")),
    )
    out_specs = (
        P("items", "seq", None),
        P("items", "seq", None),
        P(("items", "seq"), None),
        P(("items", "seq"), None),
        P(("items", "seq")),
        P(("items", "seq"), None),
        P(("items", "seq")),
        P(("items", "seq")),
        P(("items", "seq")),
        P(("items", "seq"), None),
        P(),
        P(None, ("items", "seq")),
        P(("items", "seq")),
        P(("items", "seq")),
        P(("items", "seq")),
    )
    return jax.shard_map(
        on_device, mesh=mesh, in_specs=in_specs, out_specs=out_specs, check_vma=False
    )
```

```python
import functools
import math

import jax
import jax.numpy as jnp
import numpy as np
from jax import lax
from jax.experimental import pallas as pl
from jax.experimental.pallas import tpu as pltpu
from jax.sharding import PartitionSpec as P

HEADS = 16
HEAD = 128


deep_alpha = math.sqrt(48.0)
epsilon = 1e-05
mask_token = 3
both = ("items", "seq")
bf16 = jnp.bfloat16
f32 = jnp.float32
score_scale = HEAD ** (-0.5)
exponent_scale = score_scale * math.log2(math.e)


class Lines:
    def __init__(self):
        self.last = {}

    def swap(self, part, axis, bit):
        if (axis, bit) in self.last:
            part, _ = lax.optimization_barrier((part, self.last[axis, bit]))
        size = lax.axis_size(axis)
        got = lax.ppermute(part, axis, [(j, j ^ bit) for j in range(size)])
        self.last[axis, bit] = got
        return got


def bits_of(axis):
    found = []
    bit = 1
    while bit < lax.axis_size(axis):
        found.append((axis, bit))
        bit *= 2
    return found


def my_bit(axis, bit):
    return (lax.axis_index(axis) // bit) % 2


def pick(whole, place, dim):
    return lax.dynamic_index_in_dim(whole, place, dim, keepdims=False)


def moved(masks, axis, bit):
    return (masks[0] ^ (bit if axis == "items" else 0), masks[1] ^ (bit if axis == "seq" else 0))


def contract_rows(left, right):
    return lax.dot_general(left, right, (((0,), (0,)), ((), ())), preferred_element_type=f32)


def contract_cols(left, right):
    return lax.dot_general(left, right, (((1,), (1,)), ((), ())), preferred_element_type=f32)


def dot(left, right):
    return jnp.dot(left, right, preferred_element_type=f32)


def turn(values, cosine, sine_part):
    return values * cosine + pltpu.roll(values, HEAD // 2, 1) * sine_part


def head_parts(onehot_ref, table_ref, cosine, sine_part):
    onehot = onehot_ref[...]
    mixed = dot(jnp.concatenate([onehot, onehot], axis=1), table_ref[...])
    query = turn(mixed[:, :HEAD], cosine, sine_part).astype(bf16)
    key = turn(mixed[:, HEAD : 2 * HEAD], cosine, sine_part).astype(bf16)
    return query, key, mixed[:, 2 * HEAD :].astype(bf16)


def visible_scores(key, query, offset, visible):
    scores = contract_cols(key, query)
    place = offset + lax.broadcasted_iota(jnp.int32, (1, query.shape[0]), 1)
    seen = lax.broadcasted_iota(jnp.int32, scores.shape, 0) < jnp.maximum(place + 1, visible)
    return jnp.where(seen, scores, -1e30)


def table_halves(mixed_table):
    vocab = mixed_table.shape[0]
    by_head = jnp.transpose(mixed_table.reshape(vocab, -1, 3 * HEAD), (1, 0, 2))
    high = lax.reduce_precision(by_head, 8, 7)
    return jnp.concatenate([high.astype(bf16), (by_head - high).astype(bf16)], axis=1)


def norm_rows(rows):
    center = rows - jnp.mean(rows, axis=-1, keepdims=True)
    inverse = lax.rsqrt(jnp.mean(center * center, axis=-1, keepdims=True) + epsilon)
    return center * inverse, inverse


def norm_rows_back(grad, normed, inverse, gain):
    scaled = grad * gain
    return inverse * (
        scaled
        - jnp.mean(scaled, axis=-1, keepdims=True)
        - normed * jnp.mean(scaled * normed, axis=-1, keepdims=True)
    )


MESH = pl.DeviceIdType.MESH


class Copies:
    def __init__(self, send_sems, recv_sems, local_sems):
        self.sems = send_sems, recv_sems, local_sems
        self.sent = {}
        self.moved = 0
        self.count = 0
        self.here = lax.axis_index("items"), lax.axis_index("seq")

    def send(self, source, target, masks):
        order = self.count
        self.count += 1
        copy = pltpu.make_async_remote_copy(
            src_ref=source,
            dst_ref=target,
            send_sem=self.sems[0].at[order],
            recv_sem=self.sems[1].at[order],
            device_id=(self.here[0] ^ masks[0], self.here[1] ^ masks[1]),
            device_id_type=MESH,
        )
        copy.start()
        self.sent[id(copy)] = copy
        return copy

    def move(self, source, target):
        copy = pltpu.make_async_copy(source, target, self.sems[2].at[self.moved])
        self.moved += 1
        copy.start()
        return copy

    def sent_now(self, copy):
        self.sent.pop(id(copy)).wait_send()

    def end(self):
        for copy in self.sent.values():
            copy.wait_send()


def wait_all(copies):
    for copy in copies:
        copy.wait_recv()


def mask_of(step):
    return moved((0, 0), *step)


def greet(masks):
    barrier = pltpu.get_barrier_semaphore()
    here = lax.axis_index("items"), lax.axis_index("seq")
    for mask_i, mask_s in masks:
        pl.semaphore_signal(
            barrier,
            inc=1,
            device_id=(here[0] ^ mask_i, here[1] ^ mask_s),
            device_id_type=MESH,
        )
    pl.semaphore_wait(barrier, len(masks))


def partners(seq_size, item_bits):
    return [(0, mask) for mask in range(1, seq_size)] + [mask_of(step) for step in item_bits]


def aligned(place, size):
    return pl.ds(place // size * size, size)


def first_kernel(
    item_bits,
    seq_bits,
    row_count,
    small_ref,
    heads_ref,
    head_bias_ref,
    dense_ref,
    in_ref,
    out_ref,
    everyone_ref,
    table_ref,
    block_ref,
    dense_all_ref,
    own_in_ref,
    own_out_ref,
    embed_scr,
    block_scr,
    sum_scr,
    got_scr,
    send_sems,
    recv_sems,
    local_sems,
):
    items_size, seq_size = everyone_ref.shape[:2]
    item_place, seq_place = lax.axis_index("items"), lax.axis_index("seq")
    core, chip = seq_place % 2, seq_place // 2
    member = seq_place % 4
    rows = dense_ref.shape[0]
    columns = block_scr.shape[2]
    greet(partners(seq_size, item_bits))
    copies = Copies(send_sems, recv_sems, local_sems)

    def head_columns(place, source):
        return source.at[:, pl.ds(pl.multiple_of(place * columns, 128), columns)]

    head_rows = [
        (heads_ref, pl.ds(0, rows)),
        (head_bias_ref, pl.ds(rows, row_count - rows)),
    ]

    small = [copies.send(small_ref, everyone_ref.at[item_place, seq_place], mask_of(seq_bits[0]))]
    heads = [
        copies.send(
            head_columns(seq_place ^ mask, source), block_scr.at[seq_place, place], (0, mask)
        )
        for mask in range(1, seq_size)
        for source, place in head_rows
    ]
    dense = [
        copies.send(dense_ref, dense_all_ref.at[item_place, chip, core], mask_of(seq_bits[1]))
    ]
    mine = pl.ds(pl.multiple_of(member * rows, rows), rows)
    shares = []

    def share(source, target):
        for mask in range(1, 4):
            other = member ^ mask
            shares.append(
                copies.send(source.at[other // 2, other % 2], target.at[mine], (0, mask))
            )

    local = [
        copies.move(small_ref, everyone_ref.at[item_place, seq_place]),
        copies.move(dense_ref, dense_all_ref.at[item_place, chip, core]),
        copies.move(head_columns(seq_place, heads_ref), block_scr.at[seq_place, head_rows[0][1]]),
        copies.move(
            head_columns(seq_place, head_bias_ref), block_scr.at[seq_place, head_rows[1][1]]
        ),
        copies.move(in_ref.at[member // 2, core], own_in_ref.at[0, mine]),
        copies.move(out_ref.at[member // 2, core], own_out_ref.at[mine]),
    ]
    for copy in local:
        copy.wait()

    for order in range(1, len(seq_bits)):
        if order > 1:
            wait_all(dense[-1:])
            part = dense_all_ref.at[item_place, aligned(chip, 2 ** (order - 1)), core]
            dense.append(copies.send(part, part, mask_of(seq_bits[order])))
        wait_all(small[-1:])
        part = everyone_ref.at[item_place, aligned(seq_place, 2**order)]
        small.append(copies.send(part, part, mask_of(seq_bits[order])))
        if order == 1:
            share(in_ref, own_in_ref.at[0])
    wait_all(small[-1:])
    embed = copies.move(everyone_ref.at[item_place, :, pl.ds(0, row_count)], embed_scr)

    wait_all(heads)
    embed.wait()
    sum_scr[0] = lax.dot_general(
        embed_scr[...].reshape(seq_size * row_count, -1),
        block_scr[...].reshape(seq_size * row_count, columns),
        (((0,), (0,)), ((), ())),
        preferred_element_type=f32,
    )
    sums = copies.send(sum_scr.at[0], got_scr.at[0], mask_of(item_bits[0]))
    block_out = copies.move(block_scr, block_ref)
    part = everyone_ref.at[item_place]
    small.append(copies.send(part, part, mask_of(item_bits[0])))
    share(out_ref, own_out_ref)
    wait_all(dense[-1:])

    def dense_part(mask):
        return dense_all_ref.at[item_place ^ mask, :, core]

    known = [0]
    waves = []
    for step in item_bits[::-1]:
        waves.append([(mask, step) for mask in known])
        known = known + [mask ^ step[1] for mask in known]
    arrived = {}
    for wave in waves:
        part = dense_part(0)
        arrived[wave[0][1][1]] = copies.send(part, part, mask_of(wave[0][1]))
    near = [copies.send(dense_part(0), dense_part(0), mask_of(seq_bits[0]))]
    wait_all(shares[:3])
    outer = []
    if len(seq_bits) == 3:
        first = pl.ds(0, 2 * rows)
        outer.append(
            copies.send(own_in_ref.at[0, first], own_in_ref.at[1, first], mask_of(seq_bits[2]))
        )
    for order, step in enumerate(item_bits):
        sums.wait_recv()
        sum_scr[order + 1] = sum_scr[order] + got_scr[order]
        if order + 1 < len(item_bits):
            sums = copies.send(
                sum_scr.at[order + 1], got_scr.at[order + 1], mask_of(item_bits[order + 1])
            )
            wait_all(small[-1:])
            part = everyone_ref.at[aligned(item_place, 2 ** (order + 1))]
            small.append(copies.send(part, part, mask_of(item_bits[order + 1])))
        if order < len(waves) and order + 1 < len(item_bits):
            wave = waves[order]
            for mask, step in wave:
                arrived[mask ^ step[1]].wait_recv()
                part = dense_part(mask ^ step[1])
                for later in waves[order + 1 :]:
                    arrived[mask ^ step[1] ^ later[0][1][1]] = copies.send(
                        part, part, mask_of(later[0][1])
                    )
                near.append(copies.send(part, part, mask_of(seq_bits[0])))
    table_ref[...] = sum_scr[len(item_bits)]

    for mask, step in waves[-1]:
        arrived[mask ^ step[1]].wait_recv()
        part = dense_part(mask ^ step[1])
        near.append(copies.send(part, part, mask_of(seq_bits[0])))
    wait_all(near)
    wait_all(shares[3:])
    wait_all(outer)
    wait_all(small[-1:])
    block_out.wait()
    copies.end()


def first_call(item_bits, seq_bits, small, heads, head_bias, dense, parts_in, parts_out):
    items_size, seq_size = 2 ** len(item_bits), 2 ** len(seq_bits)
    row_count = heads.shape[0] + head_bias.shape[0]
    rows, width = dense.shape
    vocab = small.shape[1]
    columns = heads.shape[1] // seq_size
    any_space = pl.BlockSpec(memory_space=pl.ANY)
    spare = 8 * (len(item_bits) + len(seq_bits)) + 4 * seq_size + 2 ** (len(item_bits) + 2)
    return pl.pallas_call(
        functools.partial(first_kernel, item_bits, seq_bits, row_count),
        in_specs=[any_space] * 6,
        out_specs=[any_space, pl.BlockSpec(memory_space=pltpu.VMEM)] + [any_space] * 4,
        out_shape=[
            jax.ShapeDtypeStruct((items_size, seq_size) + small.shape, bf16),
            jax.ShapeDtypeStruct((vocab, columns), f32),
            jax.ShapeDtypeStruct((seq_size, row_count, columns), bf16),
            jax.ShapeDtypeStruct((items_size, seq_size // 2, 2, rows, width), bf16),
            jax.ShapeDtypeStruct((2, 4 * rows, parts_in.shape[3]), bf16),
            jax.ShapeDtypeStruct((4 * rows, parts_out.shape[3]), bf16),
        ],
        scratch_shapes=[
            pltpu.VMEM((seq_size, row_count, vocab), bf16),
            pltpu.VMEM((seq_size, row_count, columns), bf16),
            pltpu.VMEM((len(item_bits) + 1, vocab, columns), f32),
            pltpu.VMEM((len(item_bits), vocab, columns), f32),
            pltpu.SemaphoreType.DMA((spare,)),
            pltpu.SemaphoreType.DMA((spare,)),
            pltpu.SemaphoreType.DMA((8,)),
        ],
        compiler_params=pltpu.CompilerParams(
            collective_id=0, has_side_effects=True, vmem_limit_bytes=24 * 2**20
        ),
        name="first",
    )(small, heads, head_bias, dense, parts_in, parts_out)


class Spread:
    def __init__(self, copies, own, whole, outer_bits, item_bits, given=None):
        self.copies, self.own, self.whole, self.given = copies, own, whole, given
        self.outer_bits, self.item_bits = outer_bits, item_bits
        half = own.shape[0] // 2
        self.halves = pl.ds(0, half), pl.ds(half, half)
        self.last = []

    def part(self, masks):
        place = (self.copies.here[0] ^ masks[0]) * lax.axis_size("seq")
        return self.whole.at[(place + (self.copies.here[1] ^ masks[1])) // 4]

    def over(self, masks, step, rows=None):
        source = self.own if masks == (0, 0) else self.part(masks)
        target = self.part(masks)
        if rows is not None:
            source, target = source.at[rows], target.at[rows]
        return self.copies.send(source, target, mask_of(step))

    def start(self):
        self.local = self.copies.move(self.own, self.part((0, 0)))
        self.first = [self.over((0, 0), step) for step in self.item_bits]

    def start_given(self):
        masks = mask_of(self.outer_bits[0])
        target = self.part(masks).at[self.halves[0]]
        self.local_given = self.copies.move(self.given, target)
        self.second = [
            [self.copies.send(self.given, target, mask_of(step)) for step in self.item_bits],
            [],
        ]
        self.outer = [None, self.over((0, 0), self.outer_bits[0], self.halves[1])]

    def start_outer(self):
        self.outer = [self.over((0, 0), self.outer_bits[0], rows) for rows in self.halves]
        self.second = [[], []]

    def cross_own(self):
        one, two = self.item_bits
        self.first[0].wait_recv()
        self.last.append(self.over(moved((0, 0), *one), two, self.halves[0]))
        self.first[1].wait_recv()
        self.last.append(self.over(moved((0, 0), *two), one, self.halves[1]))

    def spread_outer(self, which):
        self.outer[which].wait_recv()
        masks = mask_of(self.outer_bits[0])
        self.second[which] = [
            self.over(masks, step, self.halves[which]) for step in self.item_bits
        ]

    def cross_outer(self, which):
        masks = mask_of(self.outer_bits[0])
        steps = self.item_bits if which == 0 else self.item_bits[::-1]
        copies = self.second[which] if which == 0 else self.second[which][::-1]
        copies[0].wait_recv()
        self.last.append(self.over(moved(masks, *steps[0]), steps[1], self.halves[which]))
        self.last.append(copies[1])

    def plain(self):
        self.local = self.copies.move(self.own, self.part((0, 0)))
        known = [(0, 0)]
        for step in self.outer_bits + self.item_bits:
            wait_all([self.over(masks, step) for masks in known])
            known = known + [moved(masks, *step) for masks in known]

    def end(self):
        wait_all(self.last)
        self.local.wait()
        if self.given is not None:
            self.local_given.wait()


def attend_unit(block, visible, onehot_ref, table_ref, cosine_ref, sine_ref, context_ref, lse_ref):
    query, key, value = head_parts(onehot_ref, table_ref, cosine_ref[...], sine_ref[...])
    value_turned = value.T
    for offset in range(0, query.shape[0], block):
        scores = visible_scores(key, query[offset : offset + block], offset, visible)
        peak = jnp.max(scores, axis=0, keepdims=True)
        expos = jnp.exp2((scores - peak) * exponent_scale)
        total = jnp.sum(expos, axis=0, keepdims=True)
        context = dot(value_turned, expos.astype(bf16)) / total
        context_ref[offset : offset + block, :] = context.T.astype(bf16)
        lse_ref[:, offset : offset + block] = peak * exponent_scale + jnp.log2(total)


def second_kernel(
    item_bits,
    seq_bits,
    visible_ref,
    onehot_ref,
    table_ref,
    cosine_ref,
    sine_ref,
    own_onehot_ref,
    embed_ref,
    vector_ref,
    dense_ref,
    own_in_ref,
    own_out_ref,
    context_ref,
    lse_ref,
    in_ref,
    out_ref,
    shared_ref,
    normed_ref,
    inverse_ref,
    context_scr,
    dense_scr,
    resid_scr,
    low_scr,
    send_sems,
    recv_sems,
    local_sems,
):
    seq_size = 2 ** len(seq_bits)
    items_here, length, features = context_scr.shape
    heads_here = features // HEAD
    span = length // seq_size
    width = dense_ref.shape[0]
    seq_place = lax.axis_index("seq")
    outer_bits = seq_bits[2:]
    greet(partners(seq_size, item_bits))
    copies = Copies(send_sems, recv_sems, local_sems)
    dense_copy = copies.move(dense_ref, dense_scr)
    stepwise = len(outer_bits) == 1 and len(item_bits) == 2
    given = own_in_ref.at[1, pl.ds(0, own_in_ref.shape[1] // 2)] if stepwise else None
    spreads = [
        Spread(copies, own_in_ref.at[0], in_ref, outer_bits, item_bits, given),
        Spread(copies, own_out_ref, out_ref, outer_bits, item_bits),
    ]
    if stepwise:
        spreads[0].start()
        spreads[0].start_given()
    arrivals, local = [], []
    for item in range(items_here):

        @pl.loop(0, heads_here)
        def _(head):
            place = pl.ds(pl.multiple_of(head * HEAD, HEAD), HEAD)
            attend_unit(
                min(256, length),
                visible_ref[item],
                onehot_ref.at[item],
                table_ref.at[head],
                cosine_ref,
                sine_ref,
                context_scr.at[item, :, place],
                lse_ref.at[item, head],
            )

        target = context_ref.at[
            item, :, pl.ds(pl.multiple_of(seq_place * features, HEAD), features)
        ]
        for mask in range(seq_size):
            rows = pl.ds(pl.multiple_of((seq_place ^ mask) * span, span), span)
            source = context_scr.at[item, rows]
            if mask:
                arrivals.append(copies.send(source, target, (0, mask)))
            else:
                local.append(copies.move(source, target))
    if stepwise:
        spreads[0].cross_own()
        spreads[0].cross_outer(0)
        spreads[1].start()
        spreads[0].spread_outer(1)
    wait_all(arrivals)
    for copy in local:
        copy.wait()

    if stepwise:
        spreads[1].start_outer()

    dense_copy.wait()
    rows_all = items_here * span
    tile = 256

    @pl.loop(0, width // tile)
    def _(order):
        place = pl.ds(pl.multiple_of(order * tile, tile), tile)
        branch = dot(context_ref[...].reshape(rows_all, width), dense_scr[:, place])
        inputs = contract_cols(own_onehot_ref[...], embed_ref[place, :])
        resid_scr[:, place] = deep_alpha * inputs + (branch + vector_ref[5:6, place])

    block = 32
    near, far = ("seq", 1), ("seq", 2)
    far_copies, near_copies, own_copies = [], [], []
    for item in range(items_here):

        @pl.loop(0, span // block)
        def _(order):
            start = pl.multiple_of(order * block, block)
            rows = pl.ds(pl.multiple_of(item * span + start, block), block)
            normed, inverse = norm_rows(resid_scr[rows, :])
            normed_ref[rows, :] = normed
            inverse_ref[rows, :] = jnp.broadcast_to(inverse, (block, 128))
            hidden = normed * vector_ref[0:1, :] + vector_ref[1:2, :]
            low_scr[item, pl.ds(start, block), :] = hidden.astype(bf16)

        source = low_scr.at[item]
        far_copies.append(copies.send(source, shared_ref.at[item, 1], mask_of(far)))
        near_copies.append(copies.send(source, shared_ref.at[item, 2], mask_of(near)))
        own_copies.append(copies.move(source, shared_ref.at[item, 0]))

    def pass_on(item):
        far_copies[item].wait_recv()
        part = shared_ref.at[item, 1]
        near_copies.append(copies.send(part, shared_ref.at[item, 3], mask_of(near)))

    if stepwise:
        spreads[1].cross_own()
        spreads[0].cross_outer(1)
    pass_on(0)
    if stepwise:
        spreads[1].spread_outer(0)
    pass_on(1)
    if stepwise:
        spreads[1].spread_outer(1)
        spreads[1].cross_outer(0)
    for item in range(2, items_here):
        pass_on(item)
    if stepwise:
        spreads[1].cross_outer(1)
    else:
        for one in spreads:
            one.plain()
    for one in spreads:
        one.end()
    wait_all(near_copies)
    for copy in own_copies:
        copy.wait()
    copies.end()


def second_call(
    item_bits,
    seq_bits,
    visible,
    onehots,
    tables,
    cosine,
    sine_part,
    own_onehot,
    embed,
    vectors,
    w_dense,
    own_in,
    own_out,
):
    items_here, length, vocab = onehots.shape
    heads_here = tables.shape[0]
    features = heads_here * HEAD
    seq_size = 2 ** len(seq_bits)
    span = length // seq_size
    width = w_dense.shape[0]
    groups = 2 ** (len(item_bits) + len(seq_bits)) // 4
    any_space = pl.BlockSpec(memory_space=pl.ANY)
    near_space = pl.BlockSpec(memory_space=pltpu.VMEM)
    spare = 4 * groups + items_here * (seq_size + 4)
    return pl.pallas_call(
        functools.partial(second_kernel, item_bits, seq_bits),
        in_specs=[pl.BlockSpec(memory_space=pltpu.SMEM)] + [near_space] * 7 + [any_space] * 3,
        out_specs=[near_space] * 2 + [any_space] * 3 + [near_space] * 2,
        out_shape=[
            jax.ShapeDtypeStruct((items_here, span, width), bf16),
            jax.ShapeDtypeStruct((items_here, heads_here, 1, length), f32),
            jax.ShapeDtypeStruct((groups,) + own_in.shape[1:], bf16),
            jax.ShapeDtypeStruct((groups,) + own_out.shape, bf16),
            jax.ShapeDtypeStruct((items_here, 4, span, width), bf16),
            jax.ShapeDtypeStruct((items_here * span, width), f32),
            jax.ShapeDtypeStruct((items_here * span, 128), f32),
        ],
        scratch_shapes=[
            pltpu.VMEM((items_here, length, features), bf16),
            pltpu.VMEM((width, width), bf16),
            pltpu.VMEM((items_here * span, width), f32),
            pltpu.VMEM((items_here, span, width), bf16),
            pltpu.SemaphoreType.DMA((spare,)),
            pltpu.SemaphoreType.DMA((spare,)),
            pltpu.SemaphoreType.DMA((16,)),
        ],
        compiler_params=pltpu.CompilerParams(
            collective_id=1, has_side_effects=True, vmem_limit_bytes=56 * 2**20
        ),
        name="second",
    )(
        visible,
        onehots,
        tables,
        cosine,
        sine_part,
        own_onehot,
        embed,
        vectors,
        w_dense,
        own_in,
        own_out,
    )


def leading(ref):
    return [index for index in np.ndindex(*ref.shape[:-2])]


def add_into(target, source):
    rows = target.shape[-2]
    for index in leading(target):

        @pl.loop(0, rows // 16)
        def _(order):
            place = index + (pl.ds(pl.multiple_of(order * 16, 16), 16),)
            total = target[place].astype(f32) + source[place].astype(f32)
            target[place] = total.astype(target.dtype)


def copy_into(target, source):
    @pl.loop(0, target.shape[0] // 16)
    def _(order):
        place = pl.ds(pl.multiple_of(order * 16, 16), 16)
        target[place] = source[place]


class Reduce:
    def __init__(self, copies, whole, rows, dims, steps, got, stage, stage_sems):
        self.copies, self.whole, self.rows = copies, whole, rows
        self.steps, self.got = steps, got
        self.place = dims.index(steps[0])
        self.stage, self.stage_sems = stage, stage_sems
        self.order = 0

    def first(self, bit, index=()):
        full = (slice(None),) * self.place
        if index:
            full = index[: self.place]
        rest = index[self.place :] if index else ()
        if index:
            return self.whole.at[full + (bit,) + rest + (self.rows,)]
        spare = len(self.whole.shape) - 3 - self.place
        return self.whole.at[full + (bit,) + (slice(None),) * spare + (self.rows,)]

    def start(self):
        step = self.steps[0]
        self.copy = self.copies.send(self.first(1 - my_bit(*step)), self.got[0], mask_of(step))

    def advance(self):
        step = self.steps[self.order]
        self.copy.wait_recv()
        if self.order == 0:
            self.kept = self.got[0]
            rows, columns = self.kept.shape[-2:]
            places = leading(self.kept)

            def load(order):
                return pltpu.make_async_copy(
                    self.first(my_bit(*step), places[order]),
                    self.stage.at[order % 2, pl.ds(0, rows), pl.ds(0, columns)],
                    self.stage_sems.at[order % 2],
                )

            load(0).start()
            for order, place in enumerate(places):
                if order + 1 < len(places):
                    load(order + 1).start()
                load(order).wait()
                add_into(
                    self.kept.at[place],
                    self.stage.at[order % 2, pl.ds(0, rows), pl.ds(0, columns)],
                )
        else:
            self.kept = self.kept.at[my_bit(*step)]
            add_into(self.kept, self.got[self.order])
        self.order += 1
        if self.order < len(self.steps):
            step = self.steps[self.order]
            self.copy = self.copies.send(
                self.kept.at[1 - my_bit(*step)], self.got[self.order], mask_of(step)
            )


def attend_back_unit(
    block,
    visible,
    onehot_ref,
    table_ref,
    cosine_ref,
    sine_ref,
    lse_ref,
    grad_ref,
    mixed_ref,
    sums_ref,
):
    cosine, sine_part = cosine_ref[...], sine_ref[...]
    query, key, value = head_parts(onehot_ref, table_ref, cosine, sine_part)
    key_turned = key.T
    length = query.shape[0]
    grad_key = jnp.zeros((length, HEAD), f32)
    grad_value = jnp.zeros((length, HEAD), f32)
    grad_query = []
    for offset in range(0, length, block):
        query_block = query[offset : offset + block]
        grad_block = grad_ref[offset : offset + block, :]
        scores = visible_scores(key, query_block, offset, visible)
        weights = jnp.exp2(scores * exponent_scale - lse_ref[:, offset : offset + block])
        grad_weights = contract_cols(value, grad_block)
        inner = jnp.sum(weights * grad_weights, axis=0, keepdims=True)
        grad_scores = (weights * (grad_weights - inner)).astype(bf16)
        grad_value = grad_value + dot(weights.astype(bf16), grad_block)
        grad_key = grad_key + dot(grad_scores, query_block)
        grad_query.append(dot(key_turned, grad_scores).T)
    grad_query = jnp.concatenate(grad_query, axis=0)

    def back(grad):
        return turn((grad * score_scale).astype(bf16).astype(f32), cosine, -sine_part).astype(bf16)

    mixed = jnp.concatenate([back(grad_query), back(grad_key), grad_value.astype(bf16)], axis=1)
    mixed_ref[...] = mixed.reshape(mixed_ref.shape)
    sums_ref[...] += dot(onehot_ref[...].T, mixed)


def third_kernel(
    item_bits,
    seq_bits,
    visible_ref,
    onehot_ref,
    table_ref,
    cosine_ref,
    sine_ref,
    lse_ref,
    slice_ref,
    grad_ref,
    in_ref,
    out_ref,
    dense_ref,
    bias_ref,
    spread_ref,
    sums_all_ref,
    in_part_ref,
    out_part_ref,
    dense_part_ref,
    bias_sum_ref,
    mixed_scr,
    other_scr,
    kept_scr,
    step_scrs,
    sums_scr,
    sums_got,
    bias_scr,
    bias_got,
    in_got,
    out_got,
    dense_got,
    in_final,
    out_final,
    stage_scr,
    stage_sems,
    send_sems,
    recv_sems,
    local_sems,
):
    seq_size = 2 ** len(seq_bits)
    items_here, length, features = grad_ref.shape
    heads_here = features // HEAD
    seq_place = lax.axis_index("seq")
    member = seq_place % 4
    outer_bits = seq_bits[2:]
    width = slice_ref.shape[0]
    greet(partners(seq_size, item_bits))
    copies = Copies(send_sems, recv_sems, local_sems)
    dims = item_bits[::-1] + outer_bits[::-1]

    def reducers(whole, got):
        rows = whole.shape[-2]
        if len(item_bits) == 2:
            one, two = item_bits
            ways = [
                (pl.ds(0, rows // 2), [two, one] + outer_bits[::-1]),
                (pl.ds(rows // 2, rows // 2), [one, two] + outer_bits[::-1]),
            ]
        else:
            ways = [(pl.ds(0, rows), dims)]
        return [
            Reduce(copies, whole, part, dims, steps, list(got[order]), stage_scr, stage_sems)
            for order, (part, steps) in enumerate(ways)
        ]

    in_sums = reducers(in_ref, in_got)
    out_sums = reducers(out_ref, out_got)
    dense_steps = item_bits[::-1] + seq_bits[:0:-1]
    dense_sum = Reduce(
        copies,
        dense_ref,
        pl.ds(0, dense_ref.shape[-2]),
        dense_steps,
        dense_steps,
        list(dense_got),
        stage_scr,
        stage_sems,
    )
    for one in in_sums + out_sums:
        one.start()
    sums_scr[...] = jnp.zeros_like(sums_scr)
    tile = 256
    flying = {}
    sums_copy = None

    def next_sum(order):
        nonlocal sums_copy
        sums_copy.wait_recv()
        sums_scr[order + 1] = sums_scr[order] + sums_got[order]
        if order + 1 < len(item_bits):
            sums_copy = copies.send(
                sums_scr.at[order + 1], sums_got.at[order + 1], mask_of(item_bits[order + 1])
            )

    bias_scr[0] = bias_ref[...]
    bias_steps = seq_bits + item_bits
    bias_copies = [copies.send(bias_scr.at[0], bias_got.at[0], mask_of(bias_steps[0]))]
    for stage in range(items_here + len(seq_bits)):
        if stage < items_here:

            @pl.loop(0, heads_here)
            def _(head):
                place = pl.ds(pl.multiple_of(head * HEAD, HEAD), HEAD)
                packed = pl.ds(pl.multiple_of(head * 3 * HEAD, HEAD), 3 * HEAD)
                attend_back_unit(
                    min(256, length),
                    visible_ref[stage],
                    onehot_ref.at[stage],
                    table_ref.at[head],
                    cosine_ref,
                    sine_ref,
                    lse_ref.at[stage, head],
                    grad_ref.at[stage, :, place],
                    mixed_scr.at[:, :, :, packed],
                    sums_scr.at[0, head],
                )

        for order in range(len(seq_bits) - 1, -1, -1):
            item = stage - 1 - order
            if not 0 <= item < items_here:
                continue
            copy, kept = flying[item]
            copy.wait_recv()
            got = step_scrs[order].at[item % 2]
            if order:
                full = (slice(None),) * (len(kept.shape) - 3)
                kept = kept.at[full + (my_bit(*seq_bits[order]),)]
            if order + 1 < len(seq_bits):
                add_into(kept, got)
                step = seq_bits[order + 1]
                full = (slice(None),) * (len(kept.shape) - 3)
                copy = copies.send(
                    kept.at[full + (1 - my_bit(*step),)],
                    step_scrs[order + 1].at[item % 2],
                    mask_of(step),
                )
                flying[item] = copy, kept
                flying["later", item].append(copy)
            else:

                @pl.loop(0, kept.shape[0] // 16)
                def _(block):
                    place = (pl.ds(pl.multiple_of(block * 16, 16), 16),)
                    total = kept[place].astype(f32) + got[place].astype(f32)
                    spread_ref[(item,) + place] = total.astype(bf16)

        if stage < items_here:
            core = my_bit(*seq_bits[0])
            slot = stage % 2
            if stage >= 2:
                copies.sent_now(flying["first", stage - 2])
            kept_slot = stage % len(seq_bits)
            if stage >= len(seq_bits):
                for copy in flying["later", stage - len(seq_bits)]:
                    copies.sent_now(copy)
            half = mixed_scr.shape[0] * mixed_scr.shape[2]
            other = mixed_scr[:, 1 - core].reshape(half, -1)
            mine = mixed_scr[:, core].reshape(half, -1)

            @pl.loop(0, width // tile)
            def _(order):
                place = pl.ds(pl.multiple_of(order * tile, tile), tile)
                weights = slice_ref[place, :]
                target = other_scr.at[slot]
                target[..., place] = contract_cols(other, weights).astype(bf16).reshape(
                    target.shape[:-1] + (tile,)
                )
                target = kept_scr.at[kept_slot]
                target[..., place] = contract_cols(mine, weights).astype(bf16).reshape(
                    target.shape[:-1] + (tile,)
                )

            copy = copies.send(
                other_scr.at[slot], step_scrs[0].at[slot], mask_of(seq_bits[0])
            )
            flying[stage] = copy, kept_scr.at[kept_slot]
            flying["first", stage] = copy
            flying["later", stage] = []
        if stage == 1:
            dense_sum.start()
        if stage == items_here - 1:
            sums_copy = copies.send(sums_scr.at[0], sums_got.at[0], mask_of(item_bits[0]))
        if stage == items_here:
            for one in in_sums:
                one.advance()
        if stage == items_here + 1:
            next_sum(0)
            for one in in_sums:
                one.advance()
            for one in out_sums:
                one.advance()
        if stage == items_here + 2:
            for order in range(1, len(item_bits)):
                next_sum(order)
            for one in out_sums:
                one.advance()

        bias_done = len(bias_copies)
        if bias_done <= len(bias_steps):
            bias_copies[-1].wait_recv()
            bias_scr[bias_done] = bias_scr[bias_done - 1] + bias_got[bias_done - 1]
            if bias_done < len(bias_steps):
                bias_copies.append(
                    copies.send(
                        bias_scr.at[bias_done],
                        bias_got.at[bias_done],
                        mask_of(bias_steps[bias_done]),
                    )
                )
            else:
                bias_copies.append(None)
                bias_sum_ref[...] = bias_scr[bias_done]

    sums_all_ref[seq_place] = sums_scr[len(item_bits)].astype(bf16)
    known = [0]
    arrivals = []
    for axis, bit in seq_bits[::-1]:
        wait_all(arrivals)
        arrivals = []
        for mask in known:
            part = sums_all_ref.at[seq_place ^ mask]
            arrivals.append(copies.send(part, part, (0, bit)))
        known = known + [mask ^ bit for mask in known]
        if dense_sum.order < len(dense_steps):
            dense_sum.advance()

    while in_sums[0].order < len(dims):
        for one in in_sums + out_sums:
            if one.order < len(dims):
                one.advance()
        if dense_sum.order < len(dense_steps):
            dense_sum.advance()
    while out_sums[0].order < len(dims):
        for one in out_sums:
            one.advance()
    wait_all(arrivals)
    shares, local = [], []
    for sums, final, target in (
        (in_sums, in_final, in_part_ref),
        (out_sums, out_final, out_part_ref),
    ):
        rows = target.shape[1]
        first = 0
        for one in sums:
            copy_into(final.at[pl.ds(first, one.kept.shape[0])], one.kept)
            first += one.kept.shape[0]
        for mask in range(4):
            source = final.at[pl.ds(pl.multiple_of((member ^ mask) * rows, 16), rows)]
            if mask:
                shares.append(copies.send(source, target.at[member], (0, mask)))
            else:
                local.append(copies.move(source, target.at[member]))
    while dense_sum.order < len(dense_steps):
        dense_sum.advance()
    dense_part_ref[...] = dense_sum.kept[...]
    wait_all(shares)
    for copy in local:
        copy.wait()
    copies.end()


def third_call(
    item_bits,
    seq_bits,
    visible,
    onehots,
    tables,
    cosine,
    sine_part,
    log_sums,
    w_slice,
    grad_context,
    grad_in,
    grad_out,
    by_rows,
    in_sum,
):
    items_here, length, vocab = onehots.shape
    heads_here = tables.shape[0]
    seq_size = 2 ** len(seq_bits)
    span = length // seq_size
    width = w_slice.shape[0]
    packed = heads_here * 3 * HEAD
    outer = len(seq_bits) - 2
    levels = len(item_bits) + outer
    any_space = pl.BlockSpec(memory_space=pl.ANY)
    near_space = pl.BlockSpec(memory_space=pltpu.VMEM)

    def got_shapes(whole, ways, depth):
        rows, columns = whole.shape[-2:]
        one = tuple(
            pltpu.VMEM((2,) * order + (rows // ways, columns), bf16)
            for order in range(depth - 1, -1, -1)
        )
        return one

    ways = 2 if len(item_bits) == 2 else 1
    group_rows = grad_in.shape[-2]
    rows = group_rows // 4
    dense_depth = len(item_bits) + len(seq_bits) - 1
    spread = (2,) * (len(seq_bits) - 1) + (span, width)
    all_bits = len(item_bits) + len(seq_bits)
    spare = 8 * items_here + 8 * levels + 16 * all_bits
    stage_rows = max(group_rows // ways, by_rows.shape[-2])
    return pl.pallas_call(
        functools.partial(third_kernel, item_bits, seq_bits),
        in_specs=[pl.BlockSpec(memory_space=pltpu.SMEM)]
        + [near_space] * 7
        + [any_space] * 3
        + [near_space],
        out_specs=[near_space, near_space, any_space, any_space, near_space, near_space],
        out_shape=[
            jax.ShapeDtypeStruct((items_here, span, width), bf16),
            jax.ShapeDtypeStruct((seq_size, heads_here, vocab, 3 * HEAD), bf16),
            jax.ShapeDtypeStruct((4, rows, grad_in.shape[-1]), bf16),
            jax.ShapeDtypeStruct((4, rows, grad_out.shape[-1]), bf16),
            jax.ShapeDtypeStruct(by_rows.shape[-2:], bf16),
            jax.ShapeDtypeStruct(in_sum.shape, f32),
        ],
        scratch_shapes=[
            pltpu.VMEM((seq_size // 2, 2, span, packed), bf16),
            pltpu.VMEM((2,) + spread, bf16),
            pltpu.VMEM((len(seq_bits),) + spread, bf16),
            tuple(pltpu.VMEM((2,) + spread[order:], bf16) for order in range(len(seq_bits))),
            pltpu.VMEM((len(item_bits) + 1, heads_here, vocab, 3 * HEAD), f32),
            pltpu.VMEM((len(item_bits), heads_here, vocab, 3 * HEAD), f32),
            pltpu.VMEM((all_bits + 1,) + in_sum.shape, f32),
            pltpu.VMEM((all_bits,) + in_sum.shape, f32),
            tuple(got_shapes(grad_in, ways, levels) for _ in range(ways)),
            tuple(got_shapes(grad_out, ways, levels) for _ in range(ways)),
            got_shapes(by_rows, 1, dense_depth),
            pltpu.VMEM((group_rows, grad_in.shape[-1]), bf16),
            pltpu.VMEM((group_rows, grad_out.shape[-1]), bf16),
            pltpu.VMEM((2, stage_rows, grad_in.shape[-1]), bf16),
            pltpu.SemaphoreType.DMA((2,)),
            pltpu.SemaphoreType.DMA((spare,)),
            pltpu.SemaphoreType.DMA((spare,)),
            pltpu.SemaphoreType.DMA((8,)),
        ],
        compiler_params=pltpu.CompilerParams(
            collective_id=2, has_side_effects=True, vmem_limit_bytes=60 * 2**20
        ),
        name="third",
    )(
        visible,
        onehots,
        tables,
        cosine,
        sine_part,
        log_sums,
        w_slice,
        grad_context,
        grad_in,
        grad_out,
        by_rows,
        in_sum,
    )


def merged_kernel(
    item_bits,
    seq_bits,
    visible_ref,
    onehot_ref,
    table_ref,
    cosine_ref,
    sine_ref,
    lse_ref,
    slice_ref,
    grad_ref,
    shared_ref,
    grad_in_ref,
    grad_shared_ref,
    product_ref,
    dense_ref,
    bias_ref,
    spread_ref,
    sums_all_ref,
    parts_ref,
    dense_part_ref,
    bias_sum_ref,
    land_one_ref,
    land_two_ref,
    land_three_ref,
    mixed_scr,
    other_scr,
    kept_scr,
    step_scrs,
    sums_scr,
    sums_got,
    bias_scr,
    bias_got,
    dense_got,
    rhs_scr,
    lhs_scr,
    turned_scr,
    slot_scr,
    sum_scr,
    stage_scr,
    dense_scr,
    grad_scr,
    stage_sems,
    load_sems,
    send_sems,
    recv_sems,
    local_sems,
):
    seq_size = 2 ** len(seq_bits)
    items_here, length, features = grad_scr.shape
    span = length // seq_size
    heads_here = features // HEAD
    seq_place = lax.axis_index("seq")
    member = seq_place % 4
    outer_bits = seq_bits[2:]
    width = slice_ref.shape[0]
    greet(partners(seq_size, item_bits))
    copies = Copies(send_sems, recv_sems, local_sems)

    one, two = item_bits
    high = outer_bits[0]
    ways = [[two, one, high], [one, two, high]]
    blocks = [(grad_shared_ref, product_ref, 0)]
    ff_part = product_ref.shape[1]
    blocks += [(shared_ref, grad_in_ref, 0), (shared_ref, grad_in_ref, ff_part)]
    group_rows = lhs_scr.shape[2]
    half_rows = group_rows // 2
    pairs = [(two, one), (two,), (one,), ()]

    def masks_of(steps):
        masks = (0, 0)
        for step in steps:
            masks = moved(masks, *step)
        return masks

    def load_rhs(block):
        _, rhs, first = blocks[block]
        return pltpu.make_async_copy(
            rhs.at[:, pl.ds(first, ff_part)], rhs_scr, load_sems.at[0]
        )

    def load_lhs(block, pair, which):
        masks = masks_of(pairs[pair] + ((high,) if which == 0 else ()))
        group = ((copies.here[0] ^ masks[0]) * seq_size + (copies.here[1] ^ masks[1])) // 4
        columns = pl.ds(pl.multiple_of(group * group_rows, 128), group_rows)
        return pltpu.make_async_copy(
            blocks[block][0].at[:, columns], lhs_scr.at[which], load_sems.at[1 + which]
        )

    landed, slots, sends = {}, {}, {}

    def products(block, first):
        if first == 0:
            load_rhs(block).wait()
        for pair, steps in list(enumerate(pairs))[first : first + 2]:
            for which in range(2):
                load_lhs(block, pair, which).wait()
                rows = pl.ds(which * group_rows, group_rows)
                turned_scr[rows, :] = lhs_scr[which].T
            follow = (block, pair + 1) if pair + 1 < len(pairs) else (block + 1, 0)
            if follow[0] < len(blocks):
                for which in range(2):
                    load_lhs(*follow, which).start()
            targets = []
            for which in range(2):
                for way in range(2):
                    away, other = ways[way][:2]
                    place = 2 * (other in steps) + 1 - which
                    if away in steps:
                        if (way, place) in slots:
                            copies.sent_now(slots.pop((way, place)))
                        targets.append(slot_scr.at[way, place])
                    else:
                        targets.append(sum_scr.at[block, way, place])

            def multiply(columns):
                total = dot(turned_scr[...], rhs_scr[:, columns]).astype(bf16)
                for order, target in enumerate(targets):
                    target[:, columns] = total[order * half_rows : (order + 1) * half_rows]

            @pl.loop(0, ff_part // 256)
            def _(order):
                multiply(pl.ds(pl.multiple_of(order * 256, 256), 256))

            if ff_part % 256:
                multiply(pl.ds(ff_part // 256 * 256, ff_part % 256))
            for which in range(2):
                for way in range(2):
                    away, other = ways[way][:2]
                    place = 2 * (other in steps) + 1 - which
                    if away in steps:
                        copy = copies.send(
                            slot_scr.at[way, place],
                            land_one_ref.at[block, way, place],
                            mask_of(away),
                        )
                        slots[way, place] = copy
                        landed[1, block, way, place] = copy
        if first and block + 1 < len(blocks):
            load_rhs(block + 1).start()

    lands = {1: land_one_ref, 2: land_two_ref, 3: land_three_ref}

    def absorb(level, block):
        count = 2 ** (3 - level)
        pending = []

        def finish():
            load, way, place, slot = pending.pop(0)
            load.wait()
            add_into(sum_scr.at[block, way, place], stage_scr.at[slot])
            if level < 3 and place >= count // 2:
                left = place - count // 2
                landed[level + 1, block, way, left] = copies.send(
                    sum_scr.at[block, way, place],
                    lands[level + 1].at[block, way, left],
                    mask_of(ways[way][level]),
                )

        order = 0
        for place in range(count - 1, -1, -1):
            for way in range(2):
                landed[level, block, way, place].wait_recv()
                slot = order % 2
                load = pltpu.make_async_copy(
                    lands[level].at[block, way, place], stage_scr.at[slot], stage_sems.at[slot]
                )
                load.start()
                if pending:
                    finish()
                pending.append((load, way, place, slot))
                order += 1
        finish()

    shares, local = [], []

    def to_members(block):
        rows = parts_ref.shape[2]
        for mask in range(4):
            other = member ^ mask
            source = sum_scr.at[
                block, other // 2, 0, pl.ds(pl.multiple_of(other % 2 * rows, 16), rows)
            ]
            if mask:
                shares.append(copies.send(source, parts_ref.at[block, member], (0, mask)))
            else:
                local.append(copies.move(source, parts_ref.at[block, member]))

    grads = {}

    def send_grads(item):
        target = grad_scr.at[item, pl.ds(pl.multiple_of(seq_place * span, span), span)]
        arriving = []
        for mask in range(seq_size):
            columns = pl.ds(pl.multiple_of((seq_place ^ mask) * features, HEAD), features)
            source = grad_ref.at[item, :, columns]
            if mask:
                arriving.append(copies.send(source, target, (0, mask)))
            else:
                own = copies.move(source, target)
        grads[item] = arriving, own

    send_grads(0)
    load_rhs(0).start()
    for which in range(2):
        load_lhs(0, 0, which).start()
    dense_steps = item_bits[::-1] + seq_bits[:0:-1]
    dense_half = dense_ref.shape[-2] // 2
    dense_sums = [
        Reduce(
            copies,
            dense_ref,
            pl.ds(order * dense_half, dense_half),
            dense_steps,
            steps + dense_steps[2:],
            list(dense_got[order]),
            dense_scr,
            stage_sems,
        )
        for order, steps in enumerate(([two, one], [one, two]))
    ]

    def dense_advance():
        for part in dense_sums:
            part.advance()

    sums_scr[...] = jnp.zeros_like(sums_scr)
    tile = 256
    flying = {}
    sums_copy = None

    def next_sum(order):
        nonlocal sums_copy
        sums_copy.wait_recv()
        sums_scr[order + 1] = sums_scr[order] + sums_got[order]
        if order + 1 < len(item_bits):
            sums_copy = copies.send(
                sums_scr.at[order + 1], sums_got.at[order + 1], mask_of(item_bits[order + 1])
            )

    known, arrivals = [0], []

    def spread_sums():
        nonlocal known, arrivals
        wait_all(arrivals)
        arrivals = []
        bit = seq_size // 2 // len(known)
        for mask in known:
            part = sums_all_ref.at[seq_place ^ mask]
            arrivals.append(copies.send(part, part, (0, bit)))
        known = known + [mask ^ bit for mask in known]

    bias_scr[0] = bias_ref[...]
    bias_steps = seq_bits + item_bits
    bias_copies = [copies.send(bias_scr.at[0], bias_got.at[0], mask_of(bias_steps[0]))]

    def attention(item):
        arriving, own = grads[item]
        wait_all(arriving)
        own.wait()

        @pl.loop(0, heads_here)
        def _(head):
            place = pl.ds(pl.multiple_of(head * HEAD, HEAD), HEAD)
            packed = pl.ds(pl.multiple_of(head * 3 * HEAD, HEAD), 3 * HEAD)
            attend_back_unit(
                min(256, length),
                visible_ref[item],
                onehot_ref.at[item],
                table_ref.at[head],
                cosine_ref,
                sine_ref,
                lse_ref.at[item, head],
                grad_scr.at[item, :, place],
                mixed_scr.at[:, :, :, packed],
                sums_scr.at[0, head],
            )

    def step_on(item, order):
        copy, kept = flying[item]
        copy.wait_recv()
        got = step_scrs[order].at[item % step_scrs[order].shape[0]]
        full = (slice(None),) * (len(kept.shape) - 3)
        if order:
            kept = kept.at[full + (my_bit(*seq_bits[order]),)]
            full = full[1:]
        if order + 1 < len(seq_bits):
            add_into(kept, got)
            step = seq_bits[order + 1]
            target = step_scrs[order + 1]
            copy = copies.send(
                kept.at[full + (1 - my_bit(*step),)],
                target.at[item % target.shape[0]],
                mask_of(step),
            )
            flying[item] = copy, kept
            flying["later", item].append(copy)
        else:
            add_into(kept, got)
            flying["out", item] = copies.move(kept, spread_ref.at[item])

    def partial(item):
        core = my_bit(*seq_bits[0])
        slot = item % 2
        if item >= 1:
            copies.sent_now(flying["first", item - 1])
        kept_slot = item % len(seq_bits)
        if item >= len(seq_bits):
            for copy in flying["later", item - len(seq_bits)]:
                copies.sent_now(copy)
            flying.pop(("out", item - len(seq_bits))).wait()
        half = mixed_scr.shape[0] * mixed_scr.shape[2]
        other = mixed_scr[:, 1 - core].reshape(half, -1)
        mine = mixed_scr[:, core].reshape(half, -1)

        @pl.loop(0, width // tile)
        def _(order):
            place = pl.ds(pl.multiple_of(order * tile, tile), tile)
            weights = slice_ref[place, :]
            target = other_scr
            target[..., place] = contract_cols(other, weights).astype(bf16).reshape(
                target.shape[:-1] + (tile,)
            )
            target = kept_scr.at[kept_slot]
            target[..., place] = contract_cols(mine, weights).astype(bf16).reshape(
                target.shape[:-1] + (tile,)
            )

        copy = copies.send(other_scr, step_scrs[0].at[slot], mask_of(seq_bits[0]))
        flying[item] = copy, kept_scr.at[kept_slot]
        flying["first", item] = copy
        flying["later", item] = []

    def bias_step():
        done = len(bias_copies)
        bias_copies[-1].wait_recv()
        bias_scr[done] = bias_scr[done - 1] + bias_got[done - 1]
        if done < len(bias_steps):
            bias_copies.append(
                copies.send(bias_scr.at[done], bias_got.at[done], mask_of(bias_steps[done]))
            )
        else:
            bias_sum_ref[...] = bias_scr[done]

    products(0, 0)
    for part in dense_sums:
        part.start()
    send_grads(1)
    attention(0)
    partial(0)
    products(0, 2)
    send_grads(2)
    bias_step()
    step_on(0, 0)
    attention(1)
    partial(1)
    products(1, 0)
    send_grads(3)
    step_on(1, 0)
    bias_step()
    step_on(0, 1)
    products(1, 2)
    absorb(1, 0)
    dense_advance()
    attention(2)
    partial(2)
    products(2, 0)
    step_on(2, 0)
    step_on(1, 1)
    bias_step()
    products(2, 2)
    dense_advance()
    absorb(1, 1)
    attention(3)
    absorb(2, 0)
    step_on(0, 2)
    partial(3)
    sums_copy = copies.send(sums_scr.at[0], sums_got.at[0], mask_of(item_bits[0]))
    step_on(2, 1)
    dense_advance()
    step_on(3, 0)
    absorb(1, 2)
    next_sum(0)
    bias_step()
    step_on(1, 2)
    absorb(2, 1)
    dense_advance()
    step_on(3, 1)
    next_sum(1)
    bias_step()
    sums_all_ref[seq_place] = sums_scr[len(item_bits)].astype(bf16)
    spread_sums()
    absorb(2, 2)
    absorb(3, 0)
    to_members(0)
    step_on(2, 2)
    spread_sums()
    absorb(3, 1)
    to_members(1)
    step_on(3, 2)
    spread_sums()
    absorb(3, 2)
    to_members(2)
    for order, part in enumerate(dense_sums):
        dense_part_ref[pl.ds(order * dense_half, dense_half)] = part.kept[...]
    wait_all(arrivals)
    wait_all(shares)
    for item in range(items_here):
        if ("out", item) in flying:
            flying["out", item].wait()
    for copy in local:
        copy.wait()
    copies.end()


def merged_call(
    item_bits,
    seq_bits,
    visible,
    onehots,
    tables,
    cosine,
    sine_part,
    log_sums,
    w_slice,
    grad_context,
    shared,
    grad_in,
    grad_shared,
    product,
    by_rows,
    in_sum,
):
    items_here, length, vocab = onehots.shape
    heads_here = tables.shape[0]
    seq_size = 2 ** len(seq_bits)
    span = length // seq_size
    width = w_slice.shape[0]
    packed = heads_here * 3 * HEAD
    any_space = pl.BlockSpec(memory_space=pl.ANY)
    near_space = pl.BlockSpec(memory_space=pltpu.VMEM)
    ff_part = product.shape[1]
    group_rows = width * 4 // 2 ** (len(item_bits) + len(seq_bits))
    rows = group_rows // 4
    dense_depth = len(item_bits) + len(seq_bits) - 1
    spread = (2,) * (len(seq_bits) - 1) + (span, width)
    all_bits = len(item_bits) + len(seq_bits)
    spare = (8 + seq_size) * items_here + 64 + 16 * all_bits
    half = (group_rows // 2, ff_part)
    return pl.pallas_call(
        functools.partial(merged_kernel, item_bits, seq_bits),
        in_specs=[pl.BlockSpec(memory_space=pltpu.SMEM)]
        + [near_space] * 6
        + [any_space] * 6
        + [near_space],
        out_specs=[any_space, near_space, any_space, near_space, near_space] + [any_space] * 3,
        out_shape=[
            jax.ShapeDtypeStruct((items_here, span, width), bf16),
            jax.ShapeDtypeStruct((seq_size, heads_here, vocab, 3 * HEAD), bf16),
            jax.ShapeDtypeStruct((3, 4, rows, ff_part), bf16),
            jax.ShapeDtypeStruct(by_rows.shape[-2:], bf16),
            jax.ShapeDtypeStruct(in_sum.shape, f32),
            jax.ShapeDtypeStruct((3, 2, 4) + half, bf16),
            jax.ShapeDtypeStruct((3, 2, 2) + half, bf16),
            jax.ShapeDtypeStruct((3, 2, 1) + half, bf16),
        ],
        scratch_shapes=[
            pltpu.VMEM((seq_size // 2, 2, span, packed), bf16),
            pltpu.VMEM(spread, bf16),
            pltpu.VMEM((len(seq_bits),) + spread, bf16),
            tuple(
                pltpu.VMEM((2 if order == 0 else items_here,) + spread[order:], bf16)
                for order in range(len(seq_bits))
            ),
            pltpu.VMEM((len(item_bits) + 1, heads_here, vocab, 3 * HEAD), f32),
            pltpu.VMEM((len(item_bits), heads_here, vocab, 3 * HEAD), f32),
            pltpu.VMEM((all_bits + 1,) + in_sum.shape, f32),
            pltpu.VMEM((all_bits,) + in_sum.shape, f32),
            tuple(
                tuple(
                    pltpu.VMEM((2,) * order + (by_rows.shape[-2] // 2, by_rows.shape[-1]), bf16)
                    for order in range(dense_depth - 1, -1, -1)
                )
                for _ in range(2)
            ),
            pltpu.VMEM((product.shape[0], ff_part), bf16),
            pltpu.VMEM((2, product.shape[0], group_rows), bf16),
            pltpu.VMEM((2 * group_rows, product.shape[0]), bf16),
            pltpu.VMEM((2, 4) + half, bf16),
            pltpu.VMEM((3, 2, 4) + half, bf16),
            pltpu.VMEM((2,) + half, bf16),
            pltpu.VMEM((2,) + by_rows.shape[-2:], bf16),
            pltpu.VMEM((items_here, length, heads_here * HEAD), bf16),
            pltpu.SemaphoreType.DMA((2,)),
            pltpu.SemaphoreType.DMA((3,)),
            pltpu.SemaphoreType.DMA((spare,)),
            pltpu.SemaphoreType.DMA((spare,)),
            pltpu.SemaphoreType.DMA((16,)),
        ],
        compiler_params=pltpu.CompilerParams(
            collective_id=4, has_side_effects=True, vmem_limit_bytes=62 * 2**20
        ),
        name="merged",
    )(
        visible,
        onehots,
        tables,
        cosine,
        sine_part,
        log_sums,
        w_slice,
        grad_context,
        shared,
        grad_in,
        grad_shared,
        product,
        by_rows,
        in_sum,
    )


def weave_kernel(ff_width, members, padded_ref, woven_ref):
    rows = padded_ref.shape[0]
    tiles = woven_ref.shape[2] // 256
    base, shift = ff_width // 128, ff_width % 128
    lane = lax.broadcasted_iota(jnp.int32, (rows, 128), 1)
    last = padded_ref.shape[1] // 128 - 1

    def turned(tile):
        part = padded_ref[:, tile * 128 : (tile + 1) * 128].astype(f32)
        return pltpu.roll(part, (128 - shift) % 128, 1)

    before = turned(base)
    for order in range(members * tiles):
        left = ff_width - order * 128
        if left <= 0:
            up_part = gate = jnp.zeros((rows, 128), bf16)
        else:
            up_part = padded_ref[:, order * 128 : (order + 1) * 128].astype(f32)
            after = turned(min(base + order + 1, last))
            gate = jnp.where(lane < 128 - shift, before, after)
            before = after
            if left < 128:
                up_part = jnp.where(lane < left, up_part, 0.0)
                gate = jnp.where(lane < left, gate, 0.0)
            up_part, gate = up_part.astype(bf16), gate.astype(bf16)
        member, tile = order // tiles, order % tiles
        woven_ref[member, :, tile * 256 : tile * 256 + 128] = up_part
        woven_ref[member, :, tile * 256 + 128 : (tile + 1) * 256] = gate


def weave(up_weight, ff_width, members, ff_part):
    rows, columns = up_weight.shape
    wide = -(-columns // 128) * 128
    padded = jnp.pad(up_weight, ((0, 0), (0, wide - columns)))
    return pl.pallas_call(
        functools.partial(weave_kernel, ff_width, members),
        in_specs=[pl.BlockSpec(memory_space=pltpu.VMEM)],
        out_specs=pl.BlockSpec(memory_space=pltpu.VMEM),
        out_shape=jax.ShapeDtypeStruct((members, rows, 2 * ff_part), bf16),
        compiler_params=pltpu.CompilerParams(vmem_limit_bytes=24 * 2**20),
        name="weave",
    )(padded)


def unweave_kernel(ff_width, woven_ref, whole_ref):
    members, rows, columns = woven_ref.shape
    tiles = columns // 256
    base, shift = ff_width // 128, ff_width % 128
    lane = lax.broadcasted_iota(jnp.int32, (rows, 128), 1)

    def part(order, which):
        first = order % tiles * 256 + which * 128
        return woven_ref[order // tiles, :, first : first + 128].astype(f32)

    for order in range(base):
        whole_ref[:, order * 128 : (order + 1) * 128] = part(order, 0)
    before = part(base, 0)
    width = whole_ref.shape[1]
    for order in range(base, -(-width // 128)):
        if order - base < members * tiles:
            after = pltpu.roll(part(order - base, 1), shift, 1)
        first = order * 128
        count = min(128, width - first)
        whole_ref[:, first : first + count] = jnp.where(lane < shift, before, after)[:, :count]
        before = after


def unweave(woven, ff_width):
    rows = woven.shape[1]
    return pl.pallas_call(
        functools.partial(unweave_kernel, ff_width),
        in_specs=[pl.BlockSpec(memory_space=pltpu.VMEM)],
        out_specs=pl.BlockSpec(memory_space=pltpu.VMEM),
        out_shape=jax.ShapeDtypeStruct((rows, 2 * ff_width), f32),
        compiler_params=pltpu.CompilerParams(vmem_limit_bytes=24 * 2**20),
        name="unweave",
    )(woven)


def dense_back_kernel(rows_here, core_ref, context_ref, grad_ref, dense_ref, back_ref, mine_ref, other_ref):
    core = core_ref[0]
    back_ref[...] = contract_cols(grad_ref[...], dense_ref[...]).astype(bf16)
    products = contract_rows(context_ref[...], grad_ref[...]).astype(bf16)
    for order in range(products.shape[0] // (2 * rows_here)):
        first, second = (
            products[start : start + rows_here]
            for start in (2 * order * rows_here, (2 * order + 1) * rows_here)
        )
        rows = slice(order * rows_here, (order + 1) * rows_here)
        mine_ref[rows, :] = jnp.where(core == 0, first, second)
        other_ref[rows, :] = jnp.where(core == 0, second, first)


def dense_back(core, context, grad_branch, w_dense, rows_here):
    rows, width = context.shape
    tile = 256
    grid_spec = pltpu.PrefetchScalarGridSpec(
        num_scalar_prefetch=1,
        grid=(width // tile,),
        in_specs=[
            pl.BlockSpec((rows, tile), lambda i, c: (0, i)),
            pl.BlockSpec((rows, width), lambda i, c: (0, 0)),
            pl.BlockSpec((tile, width), lambda i, c: (i, 0)),
        ],
        out_specs=[
            pl.BlockSpec((rows, tile), lambda i, c: (0, i)),
            pl.BlockSpec((tile // 2, width), lambda i, c: (i, 0)),
            pl.BlockSpec((tile // 2, width), lambda i, c: (i, 0)),
        ],
    )
    return pl.pallas_call(
        functools.partial(dense_back_kernel, rows_here),
        grid_spec=grid_spec,
        out_shape=[
            jax.ShapeDtypeStruct((rows, width), bf16),
            jax.ShapeDtypeStruct((width // 2, width), bf16),
            jax.ShapeDtypeStruct((width // 2, width), bf16),
        ],
        compiler_params=pltpu.CompilerParams(vmem_limit_bytes=32 * 2**20),
        cost_estimate=pl.CostEstimate(
            flops=4 * rows * width * width, bytes_accessed=6 * width * width, transcendentals=0
        ),
        name="dense_back",
    )(core, context, grad_branch, w_dense)


def ff_kernel(
    item_bits,
    shared_ref,
    normed_ref,
    inverse_ref,
    cotangent_ref,
    in_all_ref,
    out_all_ref,
    vector_ref,
    bias_ref,
    block_ref,
    product_ref,
    saved_ref,
    grad_shared_ref,
    grad_in_ref,
    layer_ref,
    resid_ref,
    sums_ref,
    in_sum_ref,
    slices_ref,
    branch_ref,
    rows_scr,
    product_scr,
    save_scr,
    parts_scr,
    near_got,
    far_got,
    low_scr,
    grad_in_scr,
    resid_scr,
    normed_scr,
    gate_scr,
    in_ref,
    out_ref,
    weight_sems,
    send_sems,
    recv_sems,
    load_sems,
    keep_sems,
):
    chunks, blocks, span, width = shared_ref.shape
    group_rows = blocks * span
    tiles = product_scr.shape[-1] // 128
    tile = 256
    near, far = ("seq", 1), ("seq", 2)
    in_copy = pltpu.make_async_copy(in_all_ref, in_ref, weight_sems.at[0])
    out_copy = pltpu.make_async_copy(out_all_ref, out_ref, weight_sems.at[1])
    in_copy.start()
    out_copy.start()
    greet([mask_of(near), mask_of(far)] + [mask_of(step) for step in item_bits])
    copies = Copies(send_sems, recv_sems, keep_sems)
    item_place = copies.here[0]
    slices = copies.move(block_ref, slices_ref.at[item_place])
    slices.wait()
    spread = []

    def spread_block():
        order = len(spread)
        if order < len(item_bits):
            wait_all(spread[-1:])
            part = slices_ref.at[aligned(item_place, 2**order)]
            spread.append(copies.send(part, part, mask_of(item_bits[order])))

    spread_block()
    keeps, loads = {}, {}
    state = {}
    gain_one, shift_one, b_down, gain_two, shift_two = range(5)
    for line in range(sums_ref.shape[0]):
        sums_ref[line : line + 1, :] = jnp.zeros((1, width), f32)
    in_sum_ref[...] = jnp.zeros_like(in_sum_ref)

    def load(name, slot, source, target):
        copy = pltpu.make_async_copy(source, target, load_sems.at[slot])
        copy.start()
        loads[name] = copy

    def loaded(name):
        loads.pop(name).wait()

    def keep(name, slot, source, target):
        copy = pltpu.make_async_copy(source, target, keep_sems.at[1 + slot])
        copy.start()
        keeps[name] = copy

    def keep_done(name):
        if name in keeps:
            keeps.pop(name).wait()

    def load_shared(chunk):
        slot = chunk % 2
        load(("rows", slot), slot, shared_ref.at[chunk], rows_scr.at[slot])

    def load_normed(chunk):
        slot = chunk % 2
        rows = pl.ds(chunk * span, span)
        load(("normed", slot), 2 + slot, normed_ref.at[rows], normed_scr.at[slot])

    def forward_gate(chunk):
        slot = chunk % 2
        loaded(("rows", slot))
        if chunk + 1 < chunks:
            load_shared(chunk + 1)
        keep_done(("product", slot))
        keep_done(("save", slot))
        rows = rows_scr.at[slot]

        def multiply(order, place):
            columns = pl.ds(pl.multiple_of(order * tile, tile), tile)
            gate_scr[place] = (
                dot(rows[...].reshape(group_rows, width), in_ref[:, columns])
                + bias_ref[:, columns]
            )

        def finish(order, place):
            gate_up = gate_scr[place]
            up_part, gate = gate_up[:, :128], gate_up[:, 128:]
            below = 0.5 * (1.0 + lax.erf(gate * (0.5**0.5)))
            activated = gate * below
            slope = below + gate * jnp.exp(-0.5 * gate * gate) * (1.0 / math.sqrt(2.0 * math.pi))
            columns = pl.ds(pl.multiple_of(order * 128, 128), 128)
            product_scr[slot, :, columns] = (up_part * activated).astype(bf16)
            save_scr[slot, 0, :, columns] = activated.astype(bf16)
            save_scr[slot, 1, :, columns] = (up_part * slope).astype(bf16)

        multiply(0, 0)

        @pl.loop(0, (tiles - 1) // 2)
        def _(pair):
            finish(2 * pair, 0)
            multiply(2 * pair + 1, 1)
            finish(2 * pair + 1, 1)
            multiply(2 * pair + 2, 0)

        if tiles % 2 == 0:
            multiply(tiles - 1, 1)
            finish(tiles - 2, 0)
            finish(tiles - 1, 1)
        else:
            finish(tiles - 1, 0)
        keep(("product", slot), slot, product_scr.at[slot], product_ref.at[chunk])
        keep(("save", slot), 2 + slot, save_scr.at[slot], saved_ref.at[chunk])

    def send_near(name, slot):
        source = parts_scr.at[slot, pl.ds(2, 2)]
        state["near", name] = copies.send(source, near_got.at[slot], mask_of(near))

    def free_parts(slot):
        for key in ("near", "far"):
            copy = state.pop((key, "of", slot), None)
            if copy is not None:
                copies.sent_now(copy)

    def times_turned(name, slot, left, weights_ref):
        free_parts(slot)

        @pl.loop(0, width // tile)
        def _(order):
            place = pl.ds(pl.multiple_of(order * tile, tile), tile)
            total = contract_cols(left[...], weights_ref[place, :])
            parts_scr[slot, :, :, place] = total.astype(bf16).reshape(blocks, span, tile)

        send_near(name, slot)
        state["near", "of", slot] = state["near", name]

    def forward_out(chunk):
        times_turned(chunk, chunk % 2, product_scr.at[chunk % 2], out_ref)

    def sum_near(name, chunk):
        slot = chunk % 2
        state["near", name].wait_recv()
        add_into(parts_scr.at[slot, pl.ds(0, 2)], near_got.at[slot])
        copy = copies.send(parts_scr.at[slot, 1], far_got.at[chunk], mask_of(far))
        state["far", name] = copy
        state["far", "of", slot] = copy

    block = 32

    def row_blocks(function):
        @pl.loop(0, span // block)
        def _(order):
            function(pl.ds(pl.multiple_of(order * block, block), block))

    def line(index):
        return vector_ref[index : index + 1, :]

    def add_sum(index, rows):
        sums_ref[index : index + 1, :] += jnp.sum(rows, axis=0, keepdims=True)

    def second_norm(chunk):
        slot = chunk % 2
        state["far", chunk].wait_recv()
        loaded(("normed", slot))
        for key in ("low near", "low far"):
            copy = state.pop((key, slot), None)
            if copy is not None:
                copies.sent_now(copy)
        keep_done(("low", slot))

        def body(rows):
            hidden = normed_scr[slot, rows] * line(gain_one) + line(shift_one)
            mlp_branch = parts_scr[slot, 0, rows].astype(f32) + far_got[chunk, rows].astype(f32)
            normed, inverse = norm_rows(deep_alpha * hidden + mlp_branch + line(b_down))
            layer_ref[chunk, rows] = (normed * line(gain_two) + line(shift_two)).astype(bf16)
            grad = cotangent_ref[chunk, rows].astype(f32)
            resid = norm_rows_back(grad, normed, inverse, line(gain_two))
            low = resid.astype(bf16)
            resid_scr[chunk, rows] = resid
            low_scr[slot, rows] = low
            add_sum(3, grad * normed)
            add_sum(4, grad)
            add_sum(5, low.astype(f32))

        row_blocks(body)
        if chunk + 2 < chunks:
            load_normed(chunk + 2)
        source = low_scr.at[slot]
        keep(("low", slot), 4 + slot, source, grad_shared_ref.at[chunk, 0])
        state["low far", slot] = copies.send(source, grad_shared_ref.at[chunk, 1], mask_of(far))
        state["low near", slot] = copies.send(source, grad_shared_ref.at[chunk, 2], mask_of(near))
        state["grad far", chunk] = state["low far", slot]
        state["grad near", chunk] = state["low near", slot]

    def pass_on(chunk):
        state["grad far", chunk].wait_recv()
        part = grad_shared_ref.at[chunk, 1]
        state["grad cross", chunk] = copies.send(
            part, grad_shared_ref.at[chunk, 3], mask_of(near)
        )

    def load_grads(chunk):
        slot = chunk % 2
        keep_done(("low", slot))
        state["grad near", chunk].wait_recv()
        state["grad cross", chunk].wait_recv()
        load(("rows", slot), slot, grad_shared_ref.at[chunk], rows_scr.at[slot])
        keep_done(("save", slot))
        load(("save", slot), 4 + slot, saved_ref.at[chunk], save_scr.at[slot])

    def backward_gate(chunk):
        slot = chunk % 2
        loaded(("rows", slot))
        loaded(("save", slot))
        keep_done("grad in")
        rows = rows_scr.at[slot]

        def columns_of(first, count):
            columns = pl.ds(pl.multiple_of(first * 128, 128), count * 128)
            grad = dot(rows[...].reshape(group_rows, width), out_ref[:, columns])
            for order in range(count):
                part = grad[:, order * 128 : (order + 1) * 128]
                saved = pl.ds(pl.multiple_of((first + order) * 128, 128), 128)
                for which in range(2):
                    low = (part * save_scr[slot, which, :, saved].astype(f32)).astype(bf16)
                    place = pl.ds(
                        pl.multiple_of((2 * (first + order) + which) * 128, 128), 128
                    )
                    grad_in_scr[:, place] = low
                    in_sum_ref[:, place] += jnp.sum(low.astype(f32), axis=0, keepdims=True)

        @pl.loop(0, tiles // 2)
        def _(pair):
            columns_of(2 * pair, 2)

        if tiles % 2:
            columns_of(tiles - 1, 1)
        keep("grad in", 6, grad_in_scr, grad_in_ref.at[chunk])

    def backward_in(chunk):
        times_turned(("back", chunk), chunk % 2, grad_in_scr, in_ref)

    def first_norm(chunk):
        slot = chunk % 2
        state["far", ("back", chunk)].wait_recv()
        loaded(("normed", slot))
        for key in ("low near", "low far"):
            copy = state.pop((key, slot), None)
            if copy is not None:
                copies.sent_now(copy)
        keep_done(("branch", slot))

        def body(rows):
            grad = parts_scr[slot, 0, rows].astype(f32) + far_got[chunk, rows].astype(f32)
            grad = grad + deep_alpha * resid_scr[chunk, rows]
            normed = normed_scr[slot, rows]
            place = pl.ds(pl.multiple_of(chunk * span + rows.start, block), block)
            resid = norm_rows_back(grad, normed, inverse_ref[place, 0:1], line(gain_one))
            resid_scr[chunk, rows] = resid
            add_sum(0, grad * normed)
            add_sum(1, grad)
            low = resid.astype(bf16)
            low_scr[slot, rows] = low
            add_sum(2, low.astype(f32))

        row_blocks(body)
        if chunk + 2 < chunks:
            load_normed(chunk + 2)
        keep(("resid", chunk), 7 + chunk, resid_scr.at[chunk], resid_ref.at[chunk])
        keep(("branch", slot), 7 + chunks + slot, low_scr.at[slot], branch_ref.at[chunk])

    load_shared(0)
    load_normed(0)
    load_normed(1)
    last = chunks - 1
    in_copy.wait()
    for chunk in range(chunks):
        forward_gate(chunk)
        if chunk == 0:
            out_copy.wait()
        if chunk == last:
            pass_on(0)
        forward_out(chunk)
        sum_near(chunk, chunk)
        if chunk:
            second_norm(chunk - 1)
    pass_on(1)
    load_grads(0)
    for chunk in range(chunks):
        backward_gate(chunk)
        if chunk == 0:
            load_grads(1)
        if chunk >= 2:
            first_norm(chunk - 2)
        backward_in(chunk)
        sum_near(("back", chunk), chunk)
        spread_block()
        if chunk == 0:
            second_norm(last)
            load_normed(0)
            load_normed(1)
        elif chunk + 1 < chunks:
            pass_on(chunk + 1)
            load_grads(chunk + 1)
    first_norm(last - 1)
    first_norm(last)
    wait_all(spread[-1:])
    for name in list(keeps):
        keep_done(name)
    copies.end()


def ff_call(
    item_bits, shared, normed, inverse, cotangent, w_in, w_out, vectors, in_bias, block
):
    chunks, blocks, span, width = shared.shape
    group_rows = blocks * span
    ff_part = w_out.shape[1]
    any_space = pl.BlockSpec(memory_space=pl.ANY)
    near_space = pl.BlockSpec(memory_space=pltpu.VMEM)
    spare = 8 * chunks
    return pl.pallas_call(
        functools.partial(ff_kernel, item_bits),
        in_specs=[any_space] * 2 + [near_space] * 2 + [any_space] * 2 + [near_space] * 2 + [any_space],
        out_specs=[any_space] * 4 + [near_space, any_space, near_space, near_space, any_space, any_space],
        out_shape=[
            jax.ShapeDtypeStruct((chunks, group_rows, ff_part), bf16),
            jax.ShapeDtypeStruct((chunks, 2, group_rows, ff_part), bf16),
            jax.ShapeDtypeStruct((chunks, blocks, span, width), bf16),
            jax.ShapeDtypeStruct((chunks, group_rows, 2 * ff_part), bf16),
            jax.ShapeDtypeStruct((chunks, span, width), bf16),
            jax.ShapeDtypeStruct((chunks, span, width), f32),
            jax.ShapeDtypeStruct((8, width), f32),
            jax.ShapeDtypeStruct((1, 2 * ff_part), f32),
            jax.ShapeDtypeStruct((2 ** len(item_bits),) + block.shape, bf16),
            jax.ShapeDtypeStruct((chunks, span, width), bf16),
        ],
        scratch_shapes=[
            pltpu.VMEM((2, blocks, span, width), bf16),
            pltpu.VMEM((2, group_rows, ff_part), bf16),
            pltpu.VMEM((2, 2, group_rows, ff_part), bf16),
            pltpu.VMEM((2, blocks, span, width), bf16),
            pltpu.VMEM((2, 2, span, width), bf16),
            pltpu.VMEM((chunks, span, width), bf16),
            pltpu.VMEM((2, span, width), bf16),
            pltpu.VMEM((group_rows, 2 * ff_part), bf16),
            pltpu.VMEM((chunks, span, width), f32),
            pltpu.VMEM((2, span, width), f32),
            pltpu.VMEM((2, group_rows, 256), f32),
            pltpu.VMEM(w_in.shape, bf16),
            pltpu.VMEM(w_out.shape, bf16),
            pltpu.SemaphoreType.DMA((2,)),
            pltpu.SemaphoreType.DMA((spare,)),
            pltpu.SemaphoreType.DMA((spare,)),
            pltpu.SemaphoreType.DMA((6,)),
            pltpu.SemaphoreType.DMA((10 + chunks,)),
        ],
        compiler_params=pltpu.CompilerParams(
            collective_id=3, has_side_effects=True, vmem_limit_bytes=60 * 2**20
        ),
        name="feed_forward",
    )(shared, normed, inverse, cotangent, w_in, w_out, vectors, in_bias, block)


def on_device(
    token_ids,
    masked,
    item_flag,
    prefix,
    cotangent,
    embedding,
    heads_weight,
    heads_bias,
    dense_weight,
    dense_bias,
    first_gain,
    first_bias,
    up_weight,
    up_bias,
    down_weight,
    down_bias,
    second_gain,
    second_bias,
):
    lines = Lines()
    items_here, span = token_ids.shape
    items_size, seq_size = lax.axis_size("items"), lax.axis_size("seq")
    item_place, seq_place = lax.axis_index("items"), lax.axis_index("seq")
    count = items_size * seq_size
    length = span * seq_size
    width = embedding.shape[0] * count
    vocab = embedding.shape[1]
    heads_here = HEADS // seq_size
    packed_width = heads_here * 3 * HEAD
    rows_here = up_weight.shape[0]
    ff_width = down_weight.shape[0]
    members = 4
    groups = count // members
    member = seq_place % members
    ff_part = -(-ff_width // (members * 128)) * 128
    ff_all = members * ff_part

    item_bits, seq_bits = bits_of("items"), bits_of("seq")
    outer_bits = seq_bits[2:]

    input_ids = jnp.where(masked == 1, mask_token, token_ids)
    flat_place = item_place * seq_size + seq_place
    row_count = rows_here + 16
    bias_row = lax.dynamic_update_slice(
        jnp.zeros((16, heads_weight.shape[1]), bf16),
        heads_bias[None],
        (0, flat_place * heads_bias.shape[0]),
    )
    ones_row = jnp.zeros((16, vocab), bf16).at[0].set(1.0)
    def rows_of(part):
        part = part.reshape(-1)
        return jnp.pad(part, (0, -part.shape[0] % 128)).reshape(-1, 128)

    small = [
        embedding,
        ones_row,
        rows_of(input_ids.astype(bf16)),
        rows_of(
            jnp.concatenate(
                [dense_bias, first_gain, first_bias, down_bias, second_gain, second_bias]
            )
        ),
    ]
    ends = [0]
    for part in small:
        ends.append(ends[-1] + part.shape[0])
    small.append(jnp.zeros((-ends[-1] % 16, 128), bf16))
    flat = jnp.concatenate(small, axis=0)

    def by_member(part):
        padded = jnp.pad(part, ((0, 0), (0, ff_all - ff_width)))
        return jnp.transpose(padded.reshape(rows_here, 2, 2, ff_part), (1, 2, 0, 3))

    tiles = ff_part // 128

    def woven(up, gate):
        shape = up.shape[:-1] + (tiles, 128)
        return jnp.stack([up.reshape(shape), gate.reshape(shape)], axis=-2).reshape(
            up.shape[:-1] + (2 * ff_part,)
        )

    def unwoven(both_parts):
        parts = both_parts.reshape(both_parts.shape[:-1] + (tiles, 2, 128))
        shape = both_parts.shape[:-1] + (ff_part,)
        return parts[..., 0, :].reshape(shape), parts[..., 1, :].reshape(shape)

    parts_in = weave(up_weight, ff_width, members, ff_part).reshape(
        2, 2, rows_here, 2 * ff_part
    )
    parts_out = by_member(down_weight.T)
    everyone, mixed_table, w_block, w_dense, own_in, own_out = first_call(
        item_bits,
        seq_bits,
        flat,
        heads_weight,
        bias_row,
        dense_weight,
        parts_in,
        parts_out,
    )
    w_dense = w_dense.reshape(width, width)
    w_block = w_block[:, :rows_here].reshape(seq_size * rows_here, packed_width)
    pieces = [everyone[:, :, a:b] for a, b in zip(ends[:-1], ends[1:])]
    table = pieces[0].reshape(width, vocab)
    vector_rows = pieces[3].reshape(count, -1)[:, : 6 * rows_here].reshape(count, 6, rows_here)
    vectors = jnp.transpose(vector_rows, (1, 0, 2)).reshape(6, width).astype(f32)
    ids_here = pick(pieces[2], item_place, 0).reshape(seq_size, items_here, span)
    ids_here = jnp.transpose(ids_here, (1, 0, 2)).reshape(items_here, length).astype(jnp.int32)
    in_bias = jnp.pad(
        up_bias.astype(f32).reshape(2, ff_width), ((0, 0), (0, ff_all - ff_width))
    )
    in_bias = lax.dynamic_slice(in_bias, (0, member * ff_part), (2, ff_part))
    in_bias = woven(in_bias[:1], in_bias[1:])

    vocab_index = jnp.arange(vocab, dtype=jnp.int32)
    frequency = np.exp(np.arange(HEAD // 2) * (-2.0 * math.log(10000.0) / HEAD))
    angles = np.arange(length)[:, None] * frequency[None, :]
    cosine, sine_part = np.cos(angles), np.sin(angles)
    cosine = jnp.asarray(np.concatenate([cosine, cosine], axis=1), f32)
    sine_part = jnp.asarray(np.concatenate([-sine_part, sine_part], axis=1), f32)
    visible = jnp.where(item_flag == 1, length, prefix)
    tables = table_halves(mixed_table)
    onehots = (ids_here[:, :, None] == vocab_index).astype(bf16)
    own_onehot = (input_ids.reshape(-1)[:, None] == vocab_index[None, :]).astype(bf16)
    vectors = jnp.concatenate([vectors[1:], vectors[:1], jnp.zeros((2, width), f32)], axis=0)
    context, log_sums, w_in, w_out, shared, normed, inverse = second_call(
        item_bits,
        seq_bits,
        visible,
        onehots,
        tables,
        cosine,
        sine_part,
        own_onehot,
        table,
        vectors,
        w_dense,
        own_in,
        own_out,
    )
    (
        product,
        _,
        grad_shared,
        grad_in,
        layer_out,
        grad_resid,
        sums,
        in_sum,
        w_slice,
        grad_branch,
    ) = ff_call(
        item_bits,
        shared,
        normed,
        inverse,
        cotangent,
        w_in.reshape(width, 2 * ff_part),
        w_out.reshape(width, ff_part),
        vectors,
        in_bias,
        w_block,
    )
    rows_all = items_here * span
    group_all = members * rows_all
    context = context.reshape(rows_all, width)
    grad_branch = grad_branch.reshape(rows_all, width)
    core = my_bit(*seq_bits[0])
    grad_context, dense_mine, dense_other = dense_back(
        core.astype(jnp.int32).reshape(1), context, grad_branch, w_dense, rows_here
    )
    def core_sum(whole):
        parts = whole.reshape(count // 2, 2, rows_here, -1)
        got = lines.swap(pick(parts, 1 - core, 1), *seq_bits[0])
        return (pick(parts, core, 1).astype(f32) + got.astype(f32)).astype(bf16)

    small_sums = jnp.concatenate(
        [
            contract_rows(grad_branch, own_onehot).astype(bf16),
            contract_rows(sums.astype(bf16), jnp.eye(8, 128, dtype=bf16)).astype(bf16),
        ],
        axis=1,
    )
    by_rows = jnp.concatenate(
        [
            (
                dense_mine.astype(f32)
                + lines.swap(dense_other, *seq_bits[0]).astype(f32)
            ).astype(bf16),
            core_sum(small_sums).reshape(width // 2, 256),
        ],
        axis=-1,
    )
    row_dims = item_bits[::-1] + seq_bits[:0:-1]
    by_rows = by_rows.reshape((2,) * len(row_dims) + (rows_here, -1))
    in_sum = jnp.concatenate(unwoven(in_sum), axis=0)
    in_all = lax.dynamic_update_slice(
        jnp.zeros((2, ff_all), f32), in_sum, (0, member * ff_part)
    ).reshape(-1, 128)
    w_slice = w_slice.reshape(width, packed_width)
    attention = (
        item_bits,
        seq_bits,
        visible,
        onehots,
        tables,
        cosine,
        sine_part,
        log_sums,
        w_slice,
    )
    shared = shared.reshape(group_all, width)
    grad_in = grad_in.reshape(group_all, 2 * ff_part)
    grad_shared = grad_shared.reshape(group_all, width)
    product = product.reshape(group_all, ff_part)
    if len(item_bits) == 2 and len(seq_bits) == 3 and rows_here % 32 == 0:
        spread, token_all, parts, by_rows, in_all = merged_call(
            *attention,
            grad_context.reshape(items_here, span, width),
            shared,
            grad_in,
            grad_shared,
            product,
            by_rows,
            in_all,
        )[:5]
        in_part = jnp.concatenate([parts[1], parts[2]], axis=-1)
        out_part = parts[0]
    else:
        by_head = lax.all_to_all(
            jnp.transpose(
                grad_context.reshape(items_here, span, seq_size, heads_here * HEAD), (0, 2, 1, 3)
            ),
            "seq",
            split_axis=1,
            concat_axis=1,
            tiled=True,
        ).reshape(items_here, length, heads_here * HEAD)
        group_dims = (2,) * (len(item_bits) + len(outer_bits)) + (members * rows_here, -1)
        spread, token_all, in_part, out_part, by_rows, in_all = third_call(
            *attention,
            by_head,
            contract_rows(shared, grad_in).astype(bf16).reshape(group_dims),
            contract_rows(grad_shared, product).astype(bf16).reshape(group_dims),
            by_rows,
            in_all,
        )
    input_grads = spread.astype(f32) + deep_alpha * grad_resid.reshape(spread.shape)
    token_all = jnp.transpose(token_all, (2, 0, 1, 3)).reshape(vocab, -1)

    def from_members(part):
        taken = jnp.transpose(part, (1, 0, 2)).reshape(rows_here, ff_all)
        return taken[:, :ff_width].astype(f32)

    grad_up_weight = unweave(in_part, ff_width)
    grad_down = from_members(out_part)
    by_rows = by_rows.astype(f32)
    grad_dense = by_rows[:, :width]
    token_sum = by_rows[:, width : width + vocab]
    own_vectors = by_rows[:, width + vocab :].T
    in_all = in_all.reshape(2, ff_all)
    grad_up_bias = in_all[:, :ff_width].reshape(-1)

    grad_heads = dot(embedding, token_all)
    grad_heads_bias = lax.dynamic_slice_in_dim(
        jnp.sum(token_all.astype(f32), axis=0),
        (item_place * seq_size + seq_place) * heads_bias.shape[0],
        heads_bias.shape[0],
        0,
    )
    embed_grad = 0.1 * (contract_cols(heads_weight, token_all) + deep_alpha * token_sum)
    return (
        layer_out,
        input_grads,
        embed_grad,
        grad_heads,
        grad_heads_bias,
        grad_dense,
        own_vectors[2],
        own_vectors[0],
        own_vectors[1],
        grad_up_weight,
        grad_up_bias,
        grad_down.T,
        own_vectors[5],
        own_vectors[3],
        own_vectors[4],
    )


def solution(mesh):
    in_specs = (
        P("items", "seq"),
        P("items", "seq"),
        P("items"),
        P("items"),
        P("items", "seq", None),
        P(("items", "seq"), None),
        P(("items", "seq"), None),
        P(("items", "seq")),
        P(("items", "seq"), None),
        P(("items", "seq")),
        P(("items", "seq")),
        P(("items", "seq")),
        P(("items", "seq"), None),
        P(),
        P(None, ("items", "seq")),
        P(("items", "seq")),
        P(("items", "seq")),
        P(("items", "seq")),
    )
    out_specs = (
        P("items", "seq", None),
        P("items", "seq", None),
        P(("items", "seq"), None),
        P(("items", "seq"), None),
        P(("items", "seq")),
        P(("items", "seq"), None),
        P(("items", "seq")),
        P(("items", "seq")),
        P(("items", "seq")),
        P(("items", "seq"), None),
        P(),
        P(None, ("items", "seq")),
        P(("items", "seq")),
        P(("items", "seq")),
        P(("items", "seq")),
    )
    return jax.shard_map(
        on_device, mesh=mesh, in_specs=in_specs, out_specs=out_specs, check_vma=False
    )
```
